32 devices in a mesh: row: 4 (over y, x), col: 8 (over z, core).
Axes of the slice: x: 2, y: 2, z: 4, core: 2. Of those that a mesh axis runs over, the one named last changes fastest.
Arguments:
- field_real: float32 [4096, 4096], P('row', 'col'), may hold values from -6 to 6
- field_imag: float32 [4096, 4096], P('row', 'col'), may hold values from -6 to 6
Outputs:
- slm_real: float32 [4096, 4096], P('row', 'col')
- slm_imag: float32 [4096, 4096], P('row', 'col')
The draws below stay inside these ranges and needn't reach their ends.
All inputs are finite; a program needn't handle non-finite values.
Results may differ from the reference program's by a relative error of at most 0.0003.
Values sent between devices are 32-bit elements; how exact they have to be, the bound alone decides.
No kernel may reach another device: no remote copies, remote signals or barrier semaphores. Data moves between devices by JAX's collectives and lax.ppermute only.
A program may use at most 128 MiB of HBM per device.

```python
import math
import jax
import jax.numpy as jnp
from jax import lax

N = 4096


def block_levels(stream_key, shape, split, low, high):
    level = 1.0
    for dim, blocks in split:
        draws = jax.random.uniform(jax.random.fold_in(jax.random.fold_in(stream_key, 6), dim), (blocks,), jnp.float32, low / len(split), high / len(split))
        level = level * jnp.repeat(jnp.exp(draws), shape[dim] // blocks).reshape((-1,) + (1,) * (len(shape) - 1 - dim))
    return level


def normal_values(key, dims, deviation, bound, shards=(), kind=jnp.bfloat16):
    drawn = deviation * jax.random.normal(key, dims, jnp.float32)
    if shards:
        drawn = drawn * block_levels(key, dims, shards, -0.22, 0.18)
    return jnp.clip(drawn, -bound, bound).astype(kind)


def setup_inputs(seed: int = 0) -> dict:
    streams_of = jax.random.split(jax.random.key(seed), 3)
    return {
        "field_real": normal_values(streams_of[0], (N, N), 1.0, 6.0, ((0, 4), (1, 8)), jnp.float32),
        "field_imag": normal_values(streams_of[1], (N, N), 1.0, 6.0, ((0, 4), (1, 8)), jnp.float32),
    }


wavelength = 5.2e-07
distance = 0.2

def optics(padded_side):
    pitch = 2e-06 * math.sqrt(8192.0 / padded_side)
    extent = padded_side * pitch
    ratio_sq = (wavelength / extent) ** 2
    band_limit = extent / (wavelength * math.sqrt((2.0 * distance / extent) ** 2 + 1.0))
    return (ratio_sq, band_limit)

def signed_index(index_ids, modulus):
    return jnp.where(index_ids >= modulus // 2, index_ids - modulus, index_ids)

def transfer(row_signed, col_signed, ratio_sq, band_limit):
    square = row_signed[:, None] * row_signed[:, None] + col_signed[None, :] * col_signed[None, :]
    scaled = ratio_sq * square
    phase_angle = -2.0 * math.pi * distance / wavelength * scaled / (1.0 + jnp.sqrt(1.0 - scaled))
    gauss_gain = jnp.exp(square * (-2.0 / (band_limit * band_limit)))
    inside = (jnp.abs(row_signed)[:, None] < band_limit) & (jnp.abs(col_signed)[None, :] < band_limit)
    total_gain = jnp.where(inside, gauss_gain, 0.0)
    return (total_gain * jnp.cos(phase_angle), total_gain * jnp.sin(phase_angle))

def encode(near_real, near_imag, amplitude, peak, even_cell):
    amp_level = 0.8 * amplitude / peak
    amp_floor = jnp.maximum(amplitude, 0.05 * peak)
    unit_real = near_real / amp_floor
    unit_imag = near_imag / amp_floor
    lift_part = jnp.sqrt(1.0 - amp_level * amp_level)
    cell_sign = jnp.where(even_cell, 1.0, -1.0)
    out_real = unit_real * amp_level + cell_sign * unit_imag * lift_part
    out_imag = unit_imag * amp_level - cell_sign * unit_real * lift_part
    return (out_real, out_imag)

def reference(field_real, field_imag):
    padded_side = 2 * N
    quarter = padded_side // 4
    complex_field = lax.complex(field_real, field_imag)
    padded = jnp.pad(complex_field, ((quarter, quarter), (quarter, quarter)))
    spectrum = jnp.fft.fft2(padded)
    ratio_sq, band_limit = optics(padded_side)
    col_signed = signed_index(jnp.arange(padded_side, dtype=jnp.int32), padded_side).astype(jnp.float32)
    blocks = spectrum.reshape(padded_side // 512, 512, padded_side)
    starts = jnp.arange(padded_side // 512, dtype=jnp.int32) * 512

    def filter_block(block_pair):
        row_block, row_start = block_pair
        row_ids = row_start + jnp.arange(512, dtype=jnp.int32)
        row_signed = signed_index(row_ids, padded_side).astype(jnp.float32)
        gain_real, gain_imag = transfer(row_signed, col_signed, ratio_sq, band_limit)
        return row_block * lax.complex(gain_real, gain_imag)
    filtered = lax.map(filter_block, (blocks, starts)).reshape(padded_side, padded_side)
    row_part = jnp.fft.ifft(filtered, axis=0)[quarter:quarter + N]
    propagated = jnp.fft.ifft(row_part, axis=1)[:, quarter:quarter + N]
    sum_scale = float(padded_side) * float(padded_side)
    near_real = jnp.real(propagated) * sum_scale
    near_imag = jnp.imag(propagated) * sum_scale
    amplitude = jnp.sqrt(near_real * near_real + near_imag * near_imag)
    peak = jnp.max(amplitude)
    row_ids = jnp.arange(N, dtype=jnp.int32)
    even_cell = (row_ids[:, None] + row_ids[None, :]) % 2 == 0
    slm_real, slm_imag = encode(near_real, near_imag, amplitude, peak, even_cell)
    return (slm_real.astype(jnp.float32), slm_imag.astype(jnp.float32))
```

```python
from functools import partial
import math

import jax
import jax.numpy as jnp
import ml_dtypes
import numpy as np
from jax import lax
from jax.experimental import pallas as pl
from jax.experimental.pallas import tpu as pltpu
from jax.sharding import PartitionSpec as P

N = 4096
PAD = 2 * N
wavelength = 5.2e-07
distance = 0.2
INNER = 256
SLABS = N // INNER
RES = PAD // INNER
HALF = 40
VMEM = 56 * 1024 * 1024


def optics(padded_side):
    pitch = 2e-06 * math.sqrt(8192.0 / padded_side)
    extent = padded_side * pitch
    ratio_sq = (wavelength / extent) ** 2
    band_limit = extent / (wavelength * math.sqrt((2.0 * distance / extent) ** 2 + 1.0))
    return (ratio_sq, band_limit)


RATIO_SQ, LIMIT = optics(PAD)
assert RES * HALF - RES // 2 + RES > LIMIT and RES * HALF + RES // 2 > LIMIT


def residue(u):
    return u if u < RES // 2 else u - RES


def split16(table):
    table = np.asarray(table, np.float64)
    high = table.astype(np.float32).astype(ml_dtypes.bfloat16)
    low = (table - high.astype(np.float64)).astype(np.float32).astype(ml_dtypes.bfloat16)
    return high, low


def row_order(groups):
    rows = []
    for group in range(groups):
        for part in range(2):
            for s in range(8):
                rows.append((part, group * 8 + s - HALF))
    return rows


def column_tables(groups):
    q = np.arange(INNER)
    rows = row_order(groups)
    forward = np.zeros((len(rows), 2 * INNER))
    inverse = np.zeros((2 * INNER, len(rows)))
    for at, (part, k1) in enumerate(rows):
        if abs(k1) > HALF:
            continue
        angle = 2.0 * np.pi * ((k1 * q) % INNER) / INNER
        c, s = np.cos(angle), np.sin(angle)
        if part == 0:
            forward[at, :INNER], forward[at, INNER:] = c, s
            inverse[:INNER, at], inverse[INNER:, at] = c, s
        else:
            forward[at, :INNER], forward[at, INNER:] = -s, c
            inverse[:INNER, at], inverse[INNER:, at] = -s, c
    return split16(forward) + split16(inverse)


def line_tables():
    q = np.arange(INNER)
    forward = np.zeros((2 * INNER, 256))
    inverse = np.zeros((256, 2 * INNER))
    for lane in range(2 * HALF + 1):
        angle = 2.0 * np.pi * (((lane - HALF) * q) % INNER) / INNER
        c, s = np.cos(angle), np.sin(angle)
        forward[:INNER, lane], forward[INNER:, lane] = c, s
        forward[:INNER, 128 + lane], forward[INNER:, 128 + lane] = -s, c
        inverse[lane, :INNER], inverse[lane, INNER:] = c, s
        inverse[128 + lane, :INNER], inverse[128 + lane, INNER:] = -s, c
    return split16(forward) + split16(inverse)


def twist_table():
    q = np.arange(INNER) + N // 2
    k0 = np.array([residue(u) for u in range(RES)])
    angle = 2.0 * np.pi * ((k0[:, None] * q[None, :]) % PAD) / PAD
    return np.cos(angle).astype(np.float32), (-np.sin(angle)).astype(np.float32)


def turn(value, num, den):
    re, im = value
    num = num % den
    eighth = 8 * num
    if num == 0:
        return re, im
    if 2 * num == den:
        return -re, -im
    if 4 * num == den:
        return -im, re
    if 4 * num == 3 * den:
        return im, -re
    if eighth % den == 0:
        root = np.float32(math.sqrt(0.5))
        kind = eighth // den
        if kind == 1:
            return (re - im) * root, (re + im) * root
        if kind == 3:
            return (re + im) * (-root), (re - im) * root
        if kind == 5:
            return (im - re) * root, (re + im) * (-root)
        return (re + im) * root, (im - re) * root
    c = np.float32(math.cos(2.0 * math.pi * num / den))
    s = np.float32(math.sin(2.0 * math.pi * num / den))
    return re * c - im * s, re * s + im * c


def small_dft(get, ids, sign):
    count = len(ids)
    if count == 1:
        return [get(ids[0])]
    even = small_dft(get, ids[0::2], sign)
    odd = small_dft(get, ids[1::2], sign)
    half = count // 2
    first, second = [], []
    for j in range(half):
        re, im = even[j]
        t_re, t_im = turn(odd[j], sign * j, count)
        first.append((re + t_re, im + t_im))
        second.append((re - t_re, im - t_im))
    return first + second


def forward_slabs(get, put):
    ids = list(range(SLABS))
    for v, value in enumerate(small_dft(get, ids, -1)):
        put(2 * v, value)
    for v, value in enumerate(small_dft(lambda n: turn(get(n), -n, RES), ids, -1)):
        put(2 * v + 1, value)


def inverse_slabs(get, put):
    even = small_dft(get, list(range(0, RES, 2)), 1)
    odd = small_dft(get, list(range(1, RES, 2)), 1)
    for n in range(SLABS):
        t_re, t_im = turn(odd[n], n, RES)
        put(n, (even[n][0] + t_re, even[n][1] + t_im))


def high_low(value):
    high = value.astype(jnp.bfloat16)
    low = (value - high.astype(jnp.float32)).astype(jnp.bfloat16)
    return high, low


def dot16(left, right):
    return jnp.dot(left, right, preferred_element_type=jnp.float32)


def column_forward_kernel(field, twist, mat_high, mat_low, out, high, low):
    width = field.shape[-1]
    per_source = field.shape[2] // INNER
    pair = high.shape[2] // width

    def step(t, carry):
        q0 = pl.multiple_of(t * 16, 16)

        def get(n):
            source, block = divmod(n, per_source)
            rows = pl.ds(block * INNER + q0, 16)
            return field[source, 0, rows, :], field[source, 1, rows, :]

        def put(u, value):
            re, im = value
            c = twist[pl.ds(q0, 16), u : u + 1]
            s = twist[pl.ds(q0, 16), RES + u : RES + u + 1]
            lanes = pl.ds((u % pair) * width, width)
            for part, item in enumerate((re * c - im * s, re * s + im * c)):
                rows = pl.ds(part * INNER + q0, 16)
                high[u // pair, rows, lanes], low[u // pair, rows, lanes] = high_low(item)

        forward_slabs(get, put)
        return carry

    lax.fori_loop(0, INNER // 16, step, 0)

    def product(p, carry):
        done = (
            dot16(mat_high[...], high[p])
            + dot16(mat_high[...], low[p])
            + dot16(mat_low[...], high[p])
        )
        for part in range(pair):
            out[p * pair + part] = done[:, part * width : (part + 1) * width]
        return carry

    lax.fori_loop(0, RES // pair, product, 0)


def column_inverse_kernel(lines, twist, mat_high, mat_low, out, top, back):
    width = lines.shape[-1]
    per_dest = out.shape[2] // INNER
    pair = 2 if width == 128 else 1

    def product(p, carry):
        blocks = [lines[p * pair + part] for part in range(pair)]
        high, low = high_low(jnp.concatenate(blocks, axis=1) if pair > 1 else blocks[0])
        done = (
            dot16(mat_high[...], high) + dot16(mat_high[...], low) + dot16(mat_low[...], high)
        )
        for part in range(pair):
            back[p * pair + part] = done[:, part * width : (part + 1) * width]
        return carry

    lax.fori_loop(0, RES // pair, product, 0)
    top[...] = jnp.zeros_like(top)

    def step(t, carry):
        q0 = pl.multiple_of(t * 8, 8)
        largest = []

        def get(u):
            re = back[u, pl.ds(q0, 8), :]
            im = back[u, pl.ds(INNER + q0, 8), :]
            c = twist[pl.ds(q0, 8), u : u + 1]
            s = twist[pl.ds(q0, 8), RES + u : RES + u + 1]
            return re * c + im * s, im * c - re * s

        def put(n, value):
            dest, block = divmod(n, per_dest)
            rows = pl.ds(block * INNER + q0, 8)
            out[dest, 0, rows, :], out[dest, 1, rows, :] = value
            largest.append(value[0] * value[0] + value[1] * value[1])

        inverse_slabs(get, put)
        while len(largest) > 1:
            largest = [jnp.maximum(a, b) for a, b in zip(largest[0::2], largest[1::2])]
        top[...] = jnp.maximum(top[...], largest[0])
        return carry

    lax.fori_loop(0, INNER // 8, step, 0)


def line_kernel(
    order, lines, gain_re, gain_im, twist, fwd_high, fwd_low, inv_high, inv_low, out, high, low, back
):
    for side in range(2):
        lanes = pl.ds(side * 128, 128)
        waiting = {}

        def get(m):
            block = order[2 * m + side]
            return lines[block, 0:8, :], lines[block, 8:16, :]

        def put(u, value):
            re, im = value
            c = twist[u : u + 1, lanes]
            s = twist[RES + u : RES + u + 1, lanes]
            waiting[u] = (re * c - im * s, re * s + im * c)
            v = (u + RES // 2) % RES
            if v in waiting:
                low_u = min(u, v)
                rows = pl.ds(low_u * 16, 16)
                for part in range(2):
                    item = jnp.concatenate([waiting[low_u][part], waiting[low_u + RES // 2][part]], axis=0)
                    at = pl.ds(part * INNER + side * 128, 128)
                    high[rows, at], low[rows, at] = high_low(item)

        forward_slabs(get, put)

    spec = (
        dot16(high[...], fwd_high[...]) + dot16(high[...], fwd_low[...]) + dot16(low[...], fwd_high[...])
    )
    spec_re, spec_im = spec[:, :128], spec[:, 128:]
    mixed = jnp.concatenate(
        [
            spec_re * gain_re[0] - spec_im * gain_im[0],
            spec_re * gain_im[0] + spec_im * gain_re[0],
        ],
        axis=1,
    )
    mixed_high, mixed_low = high_low(mixed)
    back[...] = (
        dot16(mixed_high, inv_high[...])
        + dot16(mixed_high, inv_low[...])
        + dot16(mixed_low, inv_high[...])
    )

    for side in range(2):
        lanes = pl.ds(side * 128, 128)

        def get(u):
            rows = pl.ds((u % (RES // 2)) * 16 + (u // (RES // 2)) * 8, 8)
            re = back[rows, pl.ds(side * 128, 128)]
            im = back[rows, pl.ds(INNER + side * 128, 128)]
            c = twist[u : u + 1, lanes]
            s = twist[RES + u : RES + u + 1, lanes]
            return re * c + im * s, im * c - re * s

        def put(m, value):
            block = order[2 * m + side]
            out[block, 0:8, :], out[block, 8:16, :] = value

        inverse_slabs(get, put)


def gain_kernel(place, gain_re, gain_im):
    k0 = place[0]
    group = place[1] + pl.program_id(0)
    down = lax.broadcasted_iota(jnp.int32, (8, 128), 0)
    across = lax.broadcasted_iota(jnp.int32, (8, 128), 1)
    row = (k0 + RES * (group * 8 + down - HALF)).astype(jnp.float32)
    row_sq = row * row
    row_in = jnp.abs(row) < LIMIT
    for u in range(RES):
        col = (residue(u) + RES * (across - HALF)).astype(jnp.float32)
        square = row_sq + col * col
        scaled = RATIO_SQ * square
        phase = -2.0 * math.pi * distance / wavelength * scaled / (1.0 + jnp.sqrt(1.0 - scaled))
        total = jnp.where(
            row_in & (jnp.abs(col) < LIMIT), jnp.exp(square * (-2.0 / (LIMIT * LIMIT))), 0.0
        )
        quarter = jnp.floor(phase * (2.0 / math.pi) + 0.5)
        left = phase - quarter * 1.5703125
        left = left - quarter * 4.837512969970703125e-4
        left = left - quarter * 7.549789954891882e-8
        sq = left * left
        sine = ((-1.9515295891e-4 * sq + 8.3321608736e-3) * sq - 1.6666654611e-1) * sq * left + left
        cosine = (
            (2.443315711809948e-5 * sq - 1.388731625493765e-3) * sq + 4.166664568298827e-2
        ) * sq * sq - 0.5 * sq + 1.0
        which = quarter.astype(jnp.int32) & 3
        swap = (which & 1) == 1
        cos_part = jnp.where(swap, sine, cosine)
        sin_part = jnp.where(swap, cosine, sine)
        cos_part = jnp.where((which == 1) | (which == 2), -cos_part, cos_part)
        sin_part = jnp.where(which >= 2, -sin_part, sin_part)
        at = (u % (RES // 2)) * 16 + (u // (RES // 2)) * 8
        gain_re[0, at : at + 8, :] = total * cos_part
        gain_im[0, at : at + 8, :] = total * sin_part


def encode(near_real, near_imag, peak, even_cell):
    amplitude = jnp.sqrt(near_real * near_real + near_imag * near_imag)
    amp_level = 0.8 * amplitude / peak
    amp_floor = jnp.maximum(amplitude, 0.05 * peak)
    unit_real = near_real / amp_floor
    unit_imag = near_imag / amp_floor
    lift_part = jnp.sqrt(1.0 - amp_level * amp_level)
    cell_sign = jnp.where(even_cell, 1.0, -1.0)
    out_real = unit_real * amp_level + cell_sign * unit_imag * lift_part
    out_imag = unit_imag * amp_level - cell_sign * unit_real * lift_part
    return (out_real, out_imag)


def encode_kernel(peak, near, slm_real, slm_imag):
    shape = slm_real.shape
    cell = lax.broadcasted_iota(jnp.int32, shape, 0) + lax.broadcasted_iota(jnp.int32, shape, 1)
    slm_real[...], slm_imag[...] = encode(near[0, 0], near[0, 1], peak[0], (cell & 1) == 0)


def params():
    return pltpu.CompilerParams(vmem_limit_bytes=VMEM)


def whole(memory=pltpu.VMEM):
    return pl.BlockSpec(memory_space=memory)


def body(field_real, field_imag):
    row_total, col_total = lax.axis_size("row"), lax.axis_size("col")
    devices = row_total * col_total
    device = lax.axis_index("row") * col_total + lax.axis_index("col")
    height, tile_width = field_real.shape
    width = tile_width // row_total
    parts = max(1, devices // RES)
    groups = -(-(2 * HALF + 1) // (8 * parts)) * parts
    own = groups // parts
    pair = 2 if width == 128 else 1

    fwd_high, fwd_low, inv_high, inv_low = column_tables(groups)
    line_fh, line_fl, line_ih, line_il = line_tables()
    twist_c, twist_s = twist_table()
    twist_line = np.concatenate([twist_c, twist_s], axis=0)
    twist_col = np.concatenate([twist_c, twist_s], axis=0).T.copy()
    twist_col = np.pad(twist_col, ((0, 0), (0, 128 - 2 * RES)))

    u = device // parts
    k0 = jnp.where(u >= RES // 2, u - RES, u)
    place = jnp.stack([k0, (device % parts) * own]).astype(jnp.int32)
    gain_shape = jax.ShapeDtypeStruct((own, RES * 8, 128), jnp.float32)
    gain_spec = pl.BlockSpec((1, RES * 8, 128), lambda g: (g, 0, 0))
    gain_re, gain_im = pl.pallas_call(
        gain_kernel,
        grid=(own,),
        in_specs=[whole(pltpu.SMEM)],
        out_specs=[gain_spec, gain_spec],
        out_shape=[gain_shape, gain_shape],
        compiler_params=params(),
        name="gain",
    )(place)

    packed = jnp.stack([field_real, field_imag])
    packed = packed.reshape(2, height, row_total, width).transpose(2, 0, 1, 3)
    columns = lax.all_to_all(packed, "row", split_axis=0, concat_axis=0, tiled=True)

    lines_shape = jax.ShapeDtypeStruct((RES, groups * 16, width), jnp.float32)
    slab = pltpu.VMEM((RES // pair, 2 * INNER, pair * width), jnp.bfloat16)
    lines = pl.pallas_call(
        column_forward_kernel,
        in_specs=[whole()] * 4,
        out_specs=whole(),
        out_shape=lines_shape,
        scratch_shapes=[slab, slab],
        compiler_params=params(),
        name="column_forward",
    )(columns, twist_col, fwd_high, fwd_low)

    lines = lines.reshape(devices, own * 16, width)
    lines = lax.all_to_all(lines, ("row", "col"), split_axis=0, concat_axis=0, tiled=True)
    if width == 128:
        order = tuple((b % row_total) * col_total + b // row_total for b in range(N // 128))
    else:
        order = tuple(range(N // 128))
        lines = lines.reshape(row_total, col_total, own * 16, width).transpose(2, 1, 0, 3)
        lines = lines.reshape(own * 16, N // 128, 128).transpose(1, 0, 2)

    lines_spec = pl.BlockSpec((N // 128, 16, 128), lambda g: (0, g, 0))
    gain_spec = pl.BlockSpec((1, RES * 8, 128), lambda g: (g, 0, 0))
    lines = pl.pallas_call(
        partial(line_kernel, order),
        grid=(own,),
        in_specs=[lines_spec, gain_spec, gain_spec] + [whole()] * 5,
        out_specs=lines_spec,
        out_shape=jax.ShapeDtypeStruct((N // 128, own * 16, 128), jnp.float32),
        scratch_shapes=[
            pltpu.VMEM((RES * 8, 2 * INNER), jnp.bfloat16),
            pltpu.VMEM((RES * 8, 2 * INNER), jnp.bfloat16),
            pltpu.VMEM((RES * 8, 2 * INNER), jnp.float32),
        ],
        compiler_params=params(),
        name="line",
    )(lines, gain_re, gain_im, twist_line, line_fh, line_fl, line_ih, line_il)

    if width != 128:
        lines = lines.transpose(1, 0, 2).reshape(own * 16, col_total, row_total, width)
        lines = lines.transpose(2, 1, 0, 3).reshape(devices, own * 16, width)
    lines = lax.all_to_all(lines, ("row", "col"), split_axis=0, concat_axis=0, tiled=True)
    lines = lines.reshape(RES, groups * 16, width)

    near, top = pl.pallas_call(
        column_inverse_kernel,
        in_specs=[whole()] * 4,
        out_specs=[whole(), whole()],
        out_shape=[
            jax.ShapeDtypeStruct((row_total, 2, height, width), jnp.float32),
            jax.ShapeDtypeStruct((8, width), jnp.float32),
        ],
        scratch_shapes=[pltpu.VMEM((RES, 2 * INNER, width), jnp.float32)],
        compiler_params=params(),
        name="column_inverse",
    )(lines, twist_col, inv_high, inv_low)

    peak = jnp.sqrt(lax.pmax(jnp.max(top), ("row", "col")))
    near = lax.all_to_all(near, "row", split_axis=0, concat_axis=0, tiled=True)
    if width != 128:
        near = near.transpose(1, 2, 0, 3).reshape(2, height, tile_width)
        even_cell = (jnp.arange(height)[:, None] + jnp.arange(tile_width)[None, :]) % 2 == 0
        return encode(near[0], near[1], peak, even_cell)
    rows = 256
    tile_spec = pl.BlockSpec((rows, width), lambda i, r: (i, r))
    tile_shape = jax.ShapeDtypeStruct((height, tile_width), jnp.float32)
    return pl.pallas_call(
        encode_kernel,
        grid=(height // rows, row_total),
        in_specs=[
            whole(pltpu.SMEM),
            pl.BlockSpec((1, 2, rows, width), lambda i, r: (r, 0, i, 0)),
        ],
        out_specs=[tile_spec, tile_spec],
        out_shape=[tile_shape, tile_shape],
        compiler_params=params(),
        name="encode",
    )(peak.reshape(1), near)


def solution(mesh):
    in_specs = (P("row", "col"), P("row", "col"))
    out_specs = (P("row", "col"), P("row", "col"))
    return jax.shard_map(body, mesh=mesh, in_specs=in_specs, out_specs=out_specs, check_vma=False)
```

```python
from functools import partial
import math

import jax
import jax.numpy as jnp
import ml_dtypes
import numpy as np
from jax import lax
from jax.experimental import pallas as pl
from jax.experimental.pallas import tpu as pltpu
from jax.sharding import PartitionSpec as P

N = 4096
PAD = 2 * N
wavelength = 5.2e-07
distance = 0.2
INNER = 256
SLABS = N // INNER
RES = PAD // INNER
HALF = 40
VMEM = 56 * 1024 * 1024


def optics(padded_side):
    pitch = 2e-06 * math.sqrt(8192.0 / padded_side)
    extent = padded_side * pitch
    ratio_sq = (wavelength / extent) ** 2
    band_limit = extent / (wavelength * math.sqrt((2.0 * distance / extent) ** 2 + 1.0))
    return (ratio_sq, band_limit)


RATIO_SQ, LIMIT = optics(PAD)
assert RES * HALF - RES // 2 + RES > LIMIT and RES * HALF + RES // 2 > LIMIT


def residue(u):
    return u if u < RES // 2 else u - RES


def split16(table):
    table = np.asarray(table, np.float64)
    high = table.astype(np.float32).astype(ml_dtypes.bfloat16)
    low = (table - high.astype(np.float64)).astype(np.float32).astype(ml_dtypes.bfloat16)
    return high, low


def row_order(groups):
    rows = []
    for group in range(groups):
        for part in range(2):
            for s in range(8):
                rows.append((part, group * 8 + s - HALF))
    return rows


def column_tables(groups):
    q = np.arange(INNER)
    rows = row_order(groups)
    forward = np.zeros((len(rows), 2 * INNER))
    inverse = np.zeros((2 * INNER, len(rows)))
    for at, (part, k1) in enumerate(rows):
        if abs(k1) > HALF:
            continue
        angle = 2.0 * np.pi * ((k1 * q) % INNER) / INNER
        c, s = np.cos(angle), np.sin(angle)
        if part == 0:
            forward[at, :INNER], forward[at, INNER:] = c, s
            inverse[:INNER, at], inverse[INNER:, at] = c, s
        else:
            forward[at, :INNER], forward[at, INNER:] = -s, c
            inverse[:INNER, at], inverse[INNER:, at] = -s, c
    chunk = INNER // 2
    forward = forward.reshape(-1, 2, 2, chunk).transpose(2, 0, 1, 3).reshape(2, -1, 2 * chunk)
    inverse = inverse.reshape(2, 2, chunk, -1).transpose(1, 0, 2, 3).reshape(2, 2 * chunk, -1)
    return (
        np.concatenate(split16(forward), axis=1),
        np.concatenate(split16(inverse), axis=1),
    )


def line_tables():
    q = np.arange(INNER)
    forward = np.zeros((2 * INNER, 256))
    inverse = np.zeros((256, 2 * INNER))
    for lane in range(2 * HALF + 1):
        angle = 2.0 * np.pi * (((lane - HALF) * q) % INNER) / INNER
        c, s = np.cos(angle), np.sin(angle)
        forward[:INNER, lane], forward[INNER:, lane] = c, s
        forward[:INNER, 128 + lane], forward[INNER:, 128 + lane] = -s, c
        inverse[lane, :INNER], inverse[lane, INNER:] = c, s
        inverse[128 + lane, :INNER], inverse[128 + lane, INNER:] = -s, c
    return split16(forward) + split16(inverse)


def twist_table():
    q = np.arange(INNER) + N // 2
    k0 = np.array([residue(u) for u in range(RES)])
    angle = 2.0 * np.pi * ((k0[:, None] * q[None, :]) % PAD) / PAD
    return np.cos(angle).astype(np.float32), (-np.sin(angle)).astype(np.float32)


def turn(value, num, den):
    re, im = value
    num = num % den
    eighth = 8 * num
    if num == 0:
        return re, im
    if 2 * num == den:
        return -re, -im
    if 4 * num == den:
        return -im, re
    if 4 * num == 3 * den:
        return im, -re
    if eighth % den == 0:
        root = np.float32(math.sqrt(0.5))
        kind = eighth // den
        if kind == 1:
            return (re - im) * root, (re + im) * root
        if kind == 3:
            return (re + im) * (-root), (re - im) * root
        if kind == 5:
            return (im - re) * root, (re + im) * (-root)
        return (re + im) * root, (im - re) * root
    c = np.float32(math.cos(2.0 * math.pi * num / den))
    s = np.float32(math.sin(2.0 * math.pi * num / den))
    return re * c - im * s, re * s + im * c


def small_dft(get, ids, sign):
    count = len(ids)
    if count == 1:
        return [get(ids[0])]
    even = small_dft(get, ids[0::2], sign)
    odd = small_dft(get, ids[1::2], sign)
    half = count // 2
    first, second = [], []
    for j in range(half):
        re, im = even[j]
        t_re, t_im = turn(odd[j], sign * j, count)
        first.append((re + t_re, im + t_im))
        second.append((re - t_re, im - t_im))
    return first + second


def forward_slabs(get, put):
    ids = list(range(SLABS))
    for v, value in enumerate(small_dft(get, ids, -1)):
        put(2 * v, value)
    for v, value in enumerate(small_dft(lambda n: turn(get(n), -n, RES), ids, -1)):
        put(2 * v + 1, value)


def inverse_slabs(get, put):
    even = small_dft(get, list(range(0, RES, 2)), 1)
    odd = small_dft(get, list(range(1, RES, 2)), 1)
    for n in range(SLABS):
        t_re, t_im = turn(odd[n], n, RES)
        put(n, (even[n][0] + t_re, even[n][1] + t_im))


def high_low(value):
    high = value.astype(jnp.bfloat16)
    low = (value - high.astype(jnp.float32)).astype(jnp.bfloat16)
    return high, low


def dot16(left, right):
    return jnp.dot(left, right, preferred_element_type=jnp.float32)


def three_left(stacked, count, high, low):
    both = dot16(stacked[...], high)
    return both[:count] + both[count:] + dot16(stacked[:count], low)


def three_right(stacked, count, high, low):
    both = dot16(stacked, high)
    return both[:count] + both[count:] + dot16(stacked[:count], low)


def column_forward_kernel(field, twist, matrix, out, high, low):
    width = field.shape[-1]
    per_source = field.shape[2]
    chunk = field.shape[3]
    pair = high.shape[-1] // width
    rows_out = out.shape[1]
    tiles = chunk // 16
    pairs = RES // pair
    now = pl.program_id(0)
    steps = INNER // chunk

    def butterflies(t):
        q0 = pl.multiple_of(t * 16, 16)
        slot = now % 2

        def get(n):
            source, block = divmod(n, per_source)
            rows = pl.ds(q0, 16)
            return field[source, 0, block, rows, :], field[source, 1, block, rows, :]

        def put(u, value):
            re, im = value
            c = twist[pl.ds(q0, 16), u : u + 1]
            s = twist[pl.ds(q0, 16), RES + u : RES + u + 1]
            lanes = pl.ds((u % pair) * width, width)
            for part, item in enumerate((re * c - im * s, re * s + im * c)):
                rows = pl.ds(part * chunk + q0, 16)
                at = (slot, u // pair, rows, lanes)
                high[at], low[at] = high_low(item)

        forward_slabs(get, put)

    def product(p, first):
        slot = (now + 1) % 2
        done = three_left(matrix.at[0], rows_out, high[slot, p], low[slot, p])
        for part in range(pair):
            item = done[:, part * width : (part + 1) * width]
            at = p * pair + part
            out[at] = item if first else out[at] + item

    @pl.when(now == 0)
    def _():
        pl.loop(0, tiles)(butterflies)

    for step in range(1, steps + 1):

        @pl.when(now == step)
        def _():
            @pl.loop(0, tiles)
            def _(t):
                for part in range(pairs // tiles):
                    product(t * (pairs // tiles) + part, step == 1)
                if step < steps:
                    butterflies(t)


def column_inverse_kernel(lines, twist, matrix, out, top, high, low, back):
    width = lines.shape[-1]
    per_dest = out.shape[2]
    chunk = out.shape[3]
    pair = high.shape[-1] // width
    tiles = chunk // 8
    pairs = RES // pair
    now = pl.program_id(0)
    steps = INNER // chunk

    def product(p):
        done = three_left(matrix.at[0], 2 * chunk, high[p], low[p])
        slot = now % 2
        for part in range(pair):
            back[slot, p * pair + part] = done[:, part * width : (part + 1) * width]

    def butterflies(t):
        q0 = pl.multiple_of(t * 8, 8)
        slot = (now + 1) % 2
        largest = []

        def get(u):
            re = back[slot, u, pl.ds(q0, 8), :]
            im = back[slot, u, pl.ds(chunk + q0, 8), :]
            c = twist[pl.ds(q0, 8), u : u + 1]
            s = twist[pl.ds(q0, 8), RES + u : RES + u + 1]
            return re * c + im * s, im * c - re * s

        def put(n, value):
            dest, block = divmod(n, per_dest)
            rows = pl.ds(q0, 8)
            out[dest, 0, block, rows, :], out[dest, 1, block, rows, :] = value
            largest.append(value[0] * value[0] + value[1] * value[1])

        inverse_slabs(get, put)
        while len(largest) > 1:
            largest = [jnp.maximum(a, b) for a, b in zip(largest[0::2], largest[1::2])]
        top[...] = jnp.maximum(top[...], largest[0])

    @pl.when(now == 0)
    def _():
        top[...] = jnp.zeros_like(top)

        @pl.loop(0, pairs)
        def _(p):
            blocks = [lines[p * pair + part] for part in range(pair)]
            joined = jnp.concatenate(blocks, axis=1) if pair > 1 else blocks[0]
            high[p], low[p] = high_low(joined)
            product(p)

    for step in range(1, steps + 1):

        @pl.when(now == step)
        def _():
            @pl.loop(0, tiles)
            def _(t):
                butterflies(t)
                if step < steps:
                    for part in range(pairs // tiles):
                        product(t * (pairs // tiles) + part)


def line_kernel(
    order, lines, gain_re, gain_im, twist, fwd_high, fwd_low, inv_high, inv_low, out, stacked, back
):
    half = RES * 8

    for side in range(2):
        lanes = pl.ds(side * 128, 128)

        def get(u):
            rows = pl.ds((u % (RES // 2)) * 16 + (u // (RES // 2)) * 8, 8)
            re = back[rows, pl.ds(side * 128, 128)]
            im = back[rows, pl.ds(INNER + side * 128, 128)]
            c = twist[u : u + 1, lanes]
            s = twist[RES + u : RES + u + 1, lanes]
            return re * c + im * s, im * c - re * s

        def put(m, value):
            block = order[2 * m + side]
            out[block, 0:8, :], out[block, 8:16, :] = value

        inverse_slabs(get, put)

    spec = three_right(stacked[...], half, fwd_high[...], fwd_low[...])
    spec_re, spec_im = spec[:, :128], spec[:, 128:]
    mixed = jnp.concatenate(
        [
            spec_re * gain_re[0] - spec_im * gain_im[0],
            spec_re * gain_im[0] + spec_im * gain_re[0],
        ],
        axis=1,
    )
    mixed = jnp.concatenate(high_low(mixed), axis=0)
    back[...] = three_right(mixed, half, inv_high[...], inv_low[...])

    for side in range(2):
        lanes = pl.ds(side * 128, 128)
        waiting = {}

        def get(m):
            block = order[2 * m + side]
            return lines[block, 0:8, :], lines[block, 8:16, :]

        def put(u, value):
            re, im = value
            c = twist[u : u + 1, lanes]
            s = twist[RES + u : RES + u + 1, lanes]
            waiting[u] = (re * c - im * s, re * s + im * c)
            v = (u + RES // 2) % RES
            if v in waiting:
                first = min(u, v)
                rows = pl.ds(first * 16, 16)
                rows_low = pl.ds(half + first * 16, 16)
                for part in range(2):
                    item = jnp.concatenate(
                        [waiting[first][part], waiting[first + RES // 2][part]], axis=0
                    )
                    at = pl.ds(part * INNER + side * 128, 128)
                    stacked[rows, at], stacked[rows_low, at] = high_low(item)

        forward_slabs(get, put)


def gain_kernel(place, gain_re, gain_im):
    k0 = place[0]
    group = place[1] + pl.program_id(0)
    down = lax.broadcasted_iota(jnp.int32, (8, 128), 0)
    across = lax.broadcasted_iota(jnp.int32, (8, 128), 1)
    row = (k0 + RES * (group * 8 + down - HALF)).astype(jnp.float32)
    row_sq = row * row
    row_in = jnp.abs(row) < LIMIT
    for u in range(RES):
        col = (residue(u) + RES * (across - HALF)).astype(jnp.float32)
        square = row_sq + col * col
        scaled = RATIO_SQ * square
        phase = -2.0 * math.pi * distance / wavelength * scaled / (1.0 + jnp.sqrt(1.0 - scaled))
        total = jnp.where(
            row_in & (jnp.abs(col) < LIMIT), jnp.exp(square * (-2.0 / (LIMIT * LIMIT))), 0.0
        )
        quarter = jnp.floor(phase * (2.0 / math.pi) + 0.5)
        left = phase - quarter * 1.5703125
        left = left - quarter * 4.837512969970703125e-4
        left = left - quarter * 7.549789954891882e-8
        sq = left * left
        sine = ((-1.9515295891e-4 * sq + 8.3321608736e-3) * sq - 1.6666654611e-1) * sq * left + left
        cosine = (
            (2.443315711809948e-5 * sq - 1.388731625493765e-3) * sq + 4.166664568298827e-2
        ) * sq * sq - 0.5 * sq + 1.0
        which = quarter.astype(jnp.int32) & 3
        swap = (which & 1) == 1
        cos_part = jnp.where(swap, sine, cosine)
        sin_part = jnp.where(swap, cosine, sine)
        cos_part = jnp.where((which == 1) | (which == 2), -cos_part, cos_part)
        sin_part = jnp.where(which >= 2, -sin_part, sin_part)
        at = (u % (RES // 2)) * 16 + (u // (RES // 2)) * 8
        gain_re[0, at : at + 8, :] = total * cos_part
        gain_im[0, at : at + 8, :] = total * sin_part


def inverse_root(value):
    root = lax.rsqrt(value)
    return root * (1.5 - 0.5 * (value * root) * root)


def encode(near_real, near_imag, peak, even_cell):
    square = near_real * near_real + near_imag * near_imag
    root = inverse_root(jnp.maximum(square, 1.2e-38))
    amp_level = (square * root) * (0.8 / peak)
    unit = jnp.minimum(root, 20.0 / peak)
    rest = 1.0 - amp_level * amp_level
    lift_part = rest * inverse_root(rest)
    level = unit * amp_level
    lift = jnp.where(even_cell, unit * lift_part, -(unit * lift_part))
    return (near_real * level + near_imag * lift, near_imag * level - near_real * lift)


def encode_kernel(peak, near, slm_real, slm_imag):
    shape = slm_real.shape
    cell = lax.broadcasted_iota(jnp.int32, shape, 0) + lax.broadcasted_iota(jnp.int32, shape, 1)
    slm_real[...], slm_imag[...] = encode(near[0, 0], near[0, 1], peak[0], (cell & 1) == 0)


def pack_kernel(field_real, field_imag, packed):
    packed[0, 0] = field_real[...]
    packed[0, 1] = field_imag[...]


def params():
    return pltpu.CompilerParams(vmem_limit_bytes=VMEM)


def whole(memory=pltpu.VMEM):
    return pl.BlockSpec(memory_space=memory)


def body(field_real, field_imag):
    row_total, col_total = lax.axis_size("row"), lax.axis_size("col")
    devices = row_total * col_total
    device = lax.axis_index("row") * col_total + lax.axis_index("col")
    height, tile_width = field_real.shape
    width = tile_width // row_total
    parts = max(1, devices // RES)
    groups = -(-(2 * HALF + 1) // (8 * parts)) * parts
    own = groups // parts
    pair = 2 if width == 128 else 1

    fwd_col, inv_col = column_tables(groups)
    line_fh, line_fl, line_ih, line_il = line_tables()
    twist_c, twist_s = twist_table()
    twist_line = np.concatenate([twist_c, twist_s], axis=0)
    twist_col = np.concatenate([twist_c, twist_s], axis=0).T.copy()
    twist_col = np.pad(twist_col, ((0, 0), (0, 128 - 2 * RES)))

    u = device // parts
    k0 = jnp.where(u >= RES // 2, u - RES, u)
    place = jnp.stack([k0, (device % parts) * own]).astype(jnp.int32)
    gain_shape = jax.ShapeDtypeStruct((own, RES * 8, 128), jnp.float32)
    gain_spec = pl.BlockSpec((1, RES * 8, 128), lambda g: (g, 0, 0))
    gain_re, gain_im = pl.pallas_call(
        gain_kernel,
        grid=(own,),
        in_specs=[whole(pltpu.SMEM)],
        out_specs=[gain_spec, gain_spec],
        out_shape=[gain_shape, gain_shape],
        compiler_params=params(),
        name="gain",
    )(place)

    if width == 128:
        rows = min(height, 512)
        packed = pl.pallas_call(
            pack_kernel,
            grid=(row_total, height // rows),
            in_specs=[pl.BlockSpec((rows, width), lambda r, i: (i, r))] * 2,
            out_specs=pl.BlockSpec((1, 2, rows, width), lambda r, i: (r, 0, i, 0)),
            out_shape=jax.ShapeDtypeStruct((row_total, 2, height, width), jnp.float32),
            compiler_params=params(),
            name="pack",
        )(field_real, field_imag)
    else:
        packed = jnp.stack([field_real, field_imag])
        packed = packed.reshape(2, height, row_total, width).transpose(2, 0, 1, 3)
    columns = lax.all_to_all(packed, "row", split_axis=0, concat_axis=0, tiled=True)

    blocks = height // INNER
    chunk = INNER // 2
    steps = INNER // chunk
    columns = columns.reshape(row_total, 2, blocks, INNER, width)
    tall = (row_total, 2, blocks, chunk, width)
    slab = pltpu.VMEM((2, RES // pair, 2 * chunk, pair * width), jnp.bfloat16)
    lines = pl.pallas_call(
        column_forward_kernel,
        grid=(steps + 1,),
        in_specs=[
            pl.BlockSpec(tall, lambda i: (0, 0, 0, jnp.minimum(i, steps - 1), 0)),
            pl.BlockSpec((chunk, 128), lambda i: (jnp.minimum(i, steps - 1), 0)),
            pl.BlockSpec((1, 2 * groups * 16, 2 * chunk), lambda i: (jnp.maximum(i - 1, 0), 0, 0)),
        ],
        out_specs=whole(),
        out_shape=jax.ShapeDtypeStruct((RES, groups * 16, width), jnp.float32),
        scratch_shapes=[slab, slab],
        compiler_params=params(),
        name="column_forward",
    )(columns, twist_col, fwd_col)

    lines = lines.reshape(devices, own * 16, width)
    lines = lax.all_to_all(lines, ("row", "col"), split_axis=0, concat_axis=0, tiled=True)
    if width == 128:
        order = tuple((b % row_total) * col_total + b // row_total for b in range(N // 128))
    else:
        order = tuple(range(N // 128))
        lines = lines.reshape(row_total, col_total, own * 16, width).transpose(2, 1, 0, 3)
        lines = lines.reshape(own * 16, N // 128, 128).transpose(1, 0, 2)

    last = own - 1
    line_grain = (N // 128, 16, 128)
    gain_grain = (1, RES * 8, 128)
    lines = pl.pallas_call(
        partial(line_kernel, order),
        grid=(own + 2,),
        in_specs=[pl.BlockSpec(line_grain, lambda i: (0, jnp.minimum(i, last), 0))]
        + [pl.BlockSpec(gain_grain, lambda i: (jnp.clip(i - 1, 0, last), 0, 0))] * 2
        + [whole()] * 5,
        out_specs=pl.BlockSpec(line_grain, lambda i: (0, jnp.clip(i - 2, 0, last), 0)),
        out_shape=jax.ShapeDtypeStruct((N // 128, own * 16, 128), jnp.float32),
        scratch_shapes=[
            pltpu.VMEM((2 * RES * 8, 2 * INNER), jnp.bfloat16),
            pltpu.VMEM((RES * 8, 2 * INNER), jnp.float32),
        ],
        compiler_params=params(),
        name="line",
    )(lines, gain_re, gain_im, twist_line, line_fh, line_fl, line_ih, line_il)

    if width != 128:
        lines = lines.transpose(1, 0, 2).reshape(own * 16, col_total, row_total, width)
        lines = lines.transpose(2, 1, 0, 3).reshape(devices, own * 16, width)
    lines = lax.all_to_all(lines, ("row", "col"), split_axis=0, concat_axis=0, tiled=True)
    lines = lines.reshape(RES, groups * 16, width)

    slab = pltpu.VMEM((RES // pair, groups * 16, pair * width), jnp.bfloat16)
    near, top = pl.pallas_call(
        column_inverse_kernel,
        grid=(steps + 1,),
        in_specs=[
            whole(),
            pl.BlockSpec((chunk, 128), lambda i: (jnp.maximum(i - 1, 0), 0)),
            pl.BlockSpec(
                (1, 4 * chunk, groups * 16), lambda i: (jnp.minimum(i, steps - 1), 0, 0)
            ),
        ],
        out_specs=[
            pl.BlockSpec(tall, lambda i: (0, 0, 0, jnp.maximum(i - 1, 0), 0)),
            whole(),
        ],
        out_shape=[
            jax.ShapeDtypeStruct((row_total, 2, blocks, INNER, width), jnp.float32),
            jax.ShapeDtypeStruct((8, width), jnp.float32),
        ],
        scratch_shapes=[slab, slab, pltpu.VMEM((2, RES, 2 * chunk, width), jnp.float32)],
        compiler_params=params(),
        name="column_inverse",
    )(lines, twist_col, inv_col)

    near = near.reshape(row_total, 2, height, width)
    near = lax.all_to_all(near, "row", split_axis=0, concat_axis=0, tiled=True)
    peak = jnp.max(top)
    for axis, total in (("row", row_total), ("col", col_total)):
        shift = 1
        while shift < total:
            partner = [(i, i ^ shift) for i in range(total)]
            peak = jnp.maximum(peak, lax.ppermute(peak, axis, partner))
            shift *= 2
    peak = jnp.sqrt(peak)
    if width != 128:
        near = near.transpose(1, 2, 0, 3).reshape(2, height, tile_width)
        even_cell = (jnp.arange(height)[:, None] + jnp.arange(tile_width)[None, :]) % 2 == 0
        return encode(near[0], near[1], peak, even_cell)
    rows = min(height, 512)
    tile_spec = pl.BlockSpec((rows, width), lambda i, r: (i, r))
    tile_shape = jax.ShapeDtypeStruct((height, tile_width), jnp.float32)
    return pl.pallas_call(
        encode_kernel,
        grid=(height // rows, row_total),
        in_specs=[
            whole(pltpu.SMEM),
            pl.BlockSpec((1, 2, rows, width), lambda i, r: (r, 0, i, 0)),
        ],
        out_specs=[tile_spec, tile_spec],
        out_shape=[tile_shape, tile_shape],
        compiler_params=params(),
        name="encode",
    )(peak.reshape(1), near)


def solution(mesh):
    in_specs = (P("row", "col"), P("row", "col"))
    out_specs = (P("row", "col"), P("row", "col"))
    return jax.shard_map(body, mesh=mesh, in_specs=in_specs, out_specs=out_specs, check_vma=False)
```

```python
from functools import partial
import math

import jax
import jax.numpy as jnp
import ml_dtypes
import numpy as np
from jax import lax
from jax.experimental import pallas as pl
from jax.experimental.pallas import tpu as pltpu
from jax.sharding import PartitionSpec as P

N = 4096
PAD = 2 * N
wavelength = 5.2e-07
distance = 0.2
INNER = 256
SLABS = N // INNER
RES = PAD // INNER
HALF = 40
CHUNKS = 2
CHUNK = INNER // CHUNKS
VMEM = 56 * 1024 * 1024


def optics(padded_side):
    pitch = 2e-06 * math.sqrt(8192.0 / padded_side)
    extent = padded_side * pitch
    ratio_sq = (wavelength / extent) ** 2
    band_limit = extent / (wavelength * math.sqrt((2.0 * distance / extent) ** 2 + 1.0))
    return (ratio_sq, band_limit)


RATIO_SQ, LIMIT = optics(PAD)
assert RES * HALF - RES // 2 + RES > LIMIT and RES * HALF + RES // 2 > LIMIT


def residue(u):
    return u if u < RES // 2 else u - RES


def split16(table):
    table = np.asarray(table, np.float64)
    high = table.astype(np.float32).astype(ml_dtypes.bfloat16)
    low = (table - high.astype(np.float64)).astype(np.float32).astype(ml_dtypes.bfloat16)
    return high, low


def row_order(groups, tail):
    rows = []
    for group in range(groups):
        size = 4 if tail and group == groups - 1 else 8
        for part in range(2):
            for s in range(size):
                rows.append((part, group * 8 + s - HALF))
    return rows


def column_tables(groups, tail):
    q = np.arange(INNER)
    rows = row_order(groups, tail)
    forward = np.zeros((len(rows), 2, INNER))
    inverse = np.zeros((2, INNER, len(rows)))
    for at, (part, k1) in enumerate(rows):
        if abs(k1) > HALF:
            continue
        angle = 2.0 * np.pi * ((k1 * q) % INNER) / INNER
        c, s = np.cos(angle), np.sin(angle)
        forward[at] = (c, s) if part == 0 else (-s, c)
        inverse[:, :, at] = (c, s) if part == 0 else (-s, c)
    forward = forward.reshape(-1, 2, CHUNKS, CHUNK // 8, 8).transpose(2, 0, 3, 1, 4)
    forward = np.concatenate(split16(forward.reshape(CHUNKS, len(rows), 2 * CHUNK)), axis=1)
    inverse = inverse.reshape(2, CHUNKS, CHUNK, -1).transpose(1, 0, 2, 3)
    high, low = split16(inverse.reshape(CHUNKS, 2 * CHUNK, len(rows)))
    inverse = np.concatenate([high, high, low], axis=2)
    inverse = np.pad(inverse, ((0, 0), (0, 0), (0, -3 * len(rows) % 16)))
    return forward, inverse


def line_tables():
    q = np.arange(INNER)
    forward = np.zeros((2 * INNER, 256))
    inverse = np.zeros((256, 2 * INNER))
    for lane in range(2 * HALF + 1):
        angle = 2.0 * np.pi * (((lane - HALF) * q) % INNER) / INNER
        c, s = np.cos(angle), np.sin(angle)
        forward[:INNER, lane], forward[INNER:, lane] = c, s
        forward[:INNER, 128 + lane], forward[INNER:, 128 + lane] = -s, c
        inverse[lane, :INNER], inverse[lane, INNER:] = c, s
        inverse[128 + lane, :INNER], inverse[128 + lane, INNER:] = -s, c
    return split16(forward) + split16(inverse)


def twist_table():
    q = np.arange(INNER) + N // 2
    k0 = np.arange(RES // 2 + 1)
    angle = 2.0 * np.pi * ((k0[:, None] * q[None, :]) % PAD) / PAD
    return np.cos(angle).astype(np.float32), (-np.sin(angle)).astype(np.float32)


def turn(value, num, den):
    re, im = value
    num = num % den
    eighth = 8 * num
    if num == 0:
        return re, im
    if 2 * num == den:
        return -re, -im
    if 4 * num == den:
        return -im, re
    if 4 * num == 3 * den:
        return im, -re
    if eighth % den == 0:
        root = np.float32(math.sqrt(0.5))
        kind = eighth // den
        if kind == 1:
            return (re - im) * root, (re + im) * root
        if kind == 3:
            return (re + im) * (-root), (re - im) * root
        if kind == 5:
            return (im - re) * root, (re + im) * (-root)
        return (re + im) * root, (im - re) * root
    c = np.float32(math.cos(2.0 * math.pi * num / den))
    s = np.float32(math.sin(2.0 * math.pi * num / den))
    return re * c - im * s, re * s + im * c


def small_dft(get, ids, sign):
    count = len(ids)
    if count == 1:
        return [get(ids[0])]
    even = small_dft(get, ids[0::2], sign)
    odd = small_dft(get, ids[1::2], sign)
    half = count // 2
    first, second = [], []
    for j in range(half):
        re, im = even[j]
        t_re, t_im = turn(odd[j], sign * j, count)
        first.append((re + t_re, im + t_im))
        second.append((re - t_re, im - t_im))
    return first + second


def forward_slabs(get, put):
    ids = list(range(SLABS))
    for v, value in enumerate(small_dft(get, ids, -1)):
        put(2 * v, value)
    for v, value in enumerate(small_dft(lambda n: turn(get(n), -n, RES), ids, -1)):
        put(2 * v + 1, value)


def inverse_slabs(get, put):
    even = small_dft(get, list(range(0, RES, 2)), 1)
    odd = small_dft(get, list(range(1, RES, 2)), 1)
    for n in range(SLABS):
        t_re, t_im = turn(odd[n], n, RES)
        put(n, (even[n][0] + t_re, even[n][1] + t_im))


def twisted(value, u, sign, read):
    re, im = value
    k0 = residue(u)
    if k0 == 0:
        return value
    c, s = read(abs(k0))
    if (k0 < 0) == (sign > 0):
        return re * c + im * s, im * c - re * s
    return re * c - im * s, re * s + im * c


def high_low(value):
    high = value.astype(jnp.bfloat16)
    low = (value - high.astype(jnp.float32)).astype(jnp.bfloat16)
    return high, low


def dot16(left, right):
    return jnp.dot(left, right, preferred_element_type=jnp.float32)


def three_left(stacked, count, high, low):
    both = dot16(stacked[...], high)
    return both[:count] + both[count:] + dot16(stacked[:count], low)


def three_right(stacked, count, high, low):
    both = dot16(stacked, high)
    return both[:count] + both[count:] + dot16(stacked[:count], low)


def interleave(tiles, products, butterflies, product):
    steps = min(tiles, products)

    @pl.loop(0, steps)
    def _(t):
        if product is not None:
            for part in range(products // steps):
                product(t * (products // steps) + part)
        if butterflies is not None:
            for part in range(tiles // steps):
                butterflies(t * (tiles // steps) + part)


def column_twist(twist, q0):
    def read(k):
        rows = pl.ds(q0, 8)
        return twist[rows, k : k + 1], twist[rows, 64 + k : 65 + k]

    return read


def column_forward_kernel(field, twist, matrix, out, high, low):
    width = field.shape[-1]
    per_source = field.shape[2]
    many = high.shape[-1] // width
    rows_out = out.shape[1]
    now = pl.program_id(0)

    def butterflies(t):
        q0 = pl.multiple_of(t * 8, 8)
        slot = now % 2

        def get(n):
            source, block = divmod(n, per_source)
            rows = pl.ds(q0, 8)
            return field[source, 0, block, rows, :], field[source, 1, block, rows, :]

        def put(u, value):
            item = jnp.concatenate(twisted(value, u, 1, column_twist(twist, q0)), axis=0)
            at = (slot, u // many, pl.ds(pl.multiple_of(t * 16, 16), 16), pl.ds((u % many) * width, width))
            high[at], low[at] = high_low(item)

        forward_slabs(get, put)

    def product(p, first):
        slot = (now + 1) % 2
        done = three_left(matrix.at[0], rows_out, high[slot, p], low[slot, p])
        for part in range(many):
            item = done[:, part * width : (part + 1) * width]
            at = p * many + part
            out[at] = item if first else out[at] + item

    for step in range(CHUNKS + 1):

        @pl.when(now == step)
        def _():
            interleave(
                CHUNK // 8,
                RES // many,
                butterflies if step < CHUNKS else None,
                partial(product, first=step == 1) if step > 0 else None,
            )


def column_inverse_kernel(lines, twist, matrix, out, top, deep, back):
    width = lines.shape[-1]
    rows_in = lines.shape[1]
    per_dest = out.shape[2]
    many = deep.shape[-1] // width
    now = pl.program_id(0)

    def product(p):
        done = dot16(matrix[0], deep[p])
        slot = now % 2
        for part in range(many):
            back[slot, p * many + part] = done[:, part * width : (part + 1) * width]

    def prepare(p):
        blocks = [lines[p * many + part] for part in range(many)]
        joined = jnp.concatenate(blocks, axis=1) if many > 1 else blocks[0]
        high = joined.astype(jnp.bfloat16).astype(jnp.float32)
        parts = [high, joined - high, high]
        if deep.shape[1] > 3 * rows_in:
            parts.append(jnp.zeros((deep.shape[1] - 3 * rows_in, many * width), jnp.float32))
        deep[p] = jnp.concatenate(parts, axis=0).astype(jnp.bfloat16)
        product(p)

    def butterflies(t):
        q0 = pl.multiple_of(t * 8, 8)
        slot = (now + 1) % 2
        largest = []

        def get(u):
            re = back[slot, u, pl.ds(q0, 8), :]
            im = back[slot, u, pl.ds(CHUNK + q0, 8), :]
            return twisted((re, im), u, -1, column_twist(twist, q0))

        def put(n, value):
            dest, block = divmod(n, per_dest)
            rows = pl.ds(q0, 8)
            out[dest, 0, block, rows, :], out[dest, 1, block, rows, :] = value
            largest.append(value[0] * value[0] + value[1] * value[1])

        inverse_slabs(get, put)
        while len(largest) > 1:
            largest = [jnp.maximum(a, b) for a, b in zip(largest[0::2], largest[1::2])]
        top[...] = jnp.maximum(top[...], largest[0])

    @pl.when(now == 0)
    def _():
        top[...] = jnp.zeros_like(top)
        pl.loop(0, RES // many)(prepare)

    for step in range(1, CHUNKS + 1):

        @pl.when(now == step)
        def _():
            interleave(
                CHUNK // 8, RES // many, butterflies, product if step < CHUNKS else None
            )


def line_kernel(
    order, tail, lines, gain_re, gain_im, twist, fwd_high, fwd_low, inv_high, inv_low, out, *scratch
):
    half = RES * 8
    at_tail = pl.program_id(0) == pl.num_programs(0) - 1

    def line_twist(side):
        def read(k):
            lanes = pl.ds(side * 128, 128)
            return twist[0, k, :, lanes], twist[1, k, :, lanes]

        return read

    def forward(group, stacked):
        for side in range(2):
            waiting = {}

            def get(m):
                block = order[2 * m + side]
                at = group * 16
                return lines[block, at : at + 8, :], lines[block, at + 8 : at + 16, :]

            def put(u, value):
                waiting[u] = twisted(value, u, 1, line_twist(side))
                v = (u + RES // 2) % RES
                if v in waiting:
                    first = min(u, v)
                    rows = pl.ds(first * 16, 16)
                    rows_low = pl.ds(half + first * 16, 16)
                    for part in range(2):
                        item = jnp.concatenate(
                            [waiting[first][part], waiting[first + RES // 2][part]], axis=0
                        )
                        at = pl.ds(part * INNER + side * 128, 128)
                        stacked[rows, at], stacked[rows_low, at] = high_low(item)

            forward_slabs(get, put)

    def middle(group, stacked, back):
        spec = three_right(stacked[...], half, fwd_high[...], fwd_low[...])
        spec_re, spec_im = spec[:, :128], spec[:, 128:]
        g_re, g_im = gain_re[group], gain_im[group]
        mixed = jnp.concatenate(
            [spec_re * g_re - spec_im * g_im, spec_re * g_im + spec_im * g_re], axis=1
        )
        mixed = jnp.concatenate(high_low(mixed), axis=0)
        back[...] = three_right(mixed, half, inv_high[...], inv_low[...])

    def inverse(group, back):
        for side in range(2):

            def get(u):
                rows = pl.ds((u % (RES // 2)) * 16 + (u // (RES // 2)) * 8, 8)
                re = back[rows, pl.ds(side * 128, 128)]
                im = back[rows, pl.ds(INNER + side * 128, 128)]
                return twisted((re, im), u, -1, line_twist(side))

            def put(m, value):
                block = order[2 * m + side]
                at = group * 16
                out[block, at : at + 8, :], out[block, at + 8 : at + 16, :] = value

            inverse_slabs(get, put)

    if tail:

        @pl.when(at_tail)
        def _():
            for block in range(N // 128):
                lines[block, 8:12, :] = lines[block, 4:8, :]

    groups = len(scratch) // 2
    for group in range(groups):
        forward(group, scratch[group])
    for group in range(groups):
        middle(group, scratch[group], scratch[groups + group])
    for group in range(groups):
        inverse(group, scratch[groups + group])

    if tail:

        @pl.when(at_tail)
        def _():
            for block in range(N // 128):
                out[block, 4:8, :] = out[block, 8:12, :]


def gain_kernel(place, gain_re, gain_im):
    k0 = place[0]
    group = place[1] + pl.program_id(0)
    down = lax.broadcasted_iota(jnp.int32, (8, 128), 0)
    across = lax.broadcasted_iota(jnp.int32, (8, 128), 1)
    row = (k0 + RES * (group * 8 + down - HALF)).astype(jnp.float32)
    row_sq = row * row
    row_in = jnp.abs(row) < LIMIT
    for u in range(RES):
        col = (residue(u) + RES * (across - HALF)).astype(jnp.float32)
        square = row_sq + col * col
        scaled = RATIO_SQ * square
        phase = -2.0 * math.pi * distance / wavelength * scaled / (1.0 + jnp.sqrt(1.0 - scaled))
        total = jnp.where(
            row_in & (jnp.abs(col) < LIMIT), jnp.exp(square * (-2.0 / (LIMIT * LIMIT))), 0.0
        )
        quarter = jnp.floor(phase * (2.0 / math.pi) + 0.5)
        left = phase - quarter * 1.5703125
        left = left - quarter * 4.837512969970703125e-4
        left = left - quarter * 7.549789954891882e-8
        sq = left * left
        sine = ((-1.9515295891e-4 * sq + 8.3321608736e-3) * sq - 1.6666654611e-1) * sq * left + left
        cosine = (
            (2.443315711809948e-5 * sq - 1.388731625493765e-3) * sq + 4.166664568298827e-2
        ) * sq * sq - 0.5 * sq + 1.0
        which = quarter.astype(jnp.int32) & 3
        swap = (which & 1) == 1
        cos_part = jnp.where(swap, sine, cosine)
        sin_part = jnp.where(swap, cosine, sine)
        cos_part = jnp.where((which == 1) | (which == 2), -cos_part, cos_part)
        sin_part = jnp.where(which >= 2, -sin_part, sin_part)
        at = (u % (RES // 2)) * 16 + (u // (RES // 2)) * 8
        gain_re[0, at : at + 8, :] = total * cos_part
        gain_im[0, at : at + 8, :] = total * sin_part


def inverse_root(value):
    root = lax.rsqrt(value)
    return root * (1.5 - 0.5 * (value * root) * root)


def encode(near_real, near_imag, peak, even_cell):
    square = near_real * near_real + near_imag * near_imag
    root = inverse_root(jnp.maximum(square, 1.2e-38))
    amp_level = (square * root) * (0.8 / peak)
    unit = jnp.minimum(root, 20.0 / peak)
    rest = 1.0 - amp_level * amp_level
    lift_part = rest * inverse_root(rest)
    level = unit * amp_level
    lift = jnp.where(even_cell, unit * lift_part, -(unit * lift_part))
    return (near_real * level + near_imag * lift, near_imag * level - near_real * lift)


def encode_kernel(peak, near, slm_real, slm_imag):
    rows, width = near.shape[2:]
    cell = lax.broadcasted_iota(jnp.int32, (rows, width), 0)
    cell = cell + lax.broadcasted_iota(jnp.int32, (rows, width), 1)
    for r in range(near.shape[0]):
        lanes = pl.ds(r * width, width)
        slm_real[:, lanes], slm_imag[:, lanes] = encode(
            near[r, 0], near[r, 1], peak[0], (cell & 1) == 0
        )


def pack_kernel(field_real, field_imag, packed):
    width = packed.shape[-1]
    for r in range(packed.shape[0]):
        lanes = pl.ds(r * width, width)
        packed[r, 0] = field_real[:, lanes]
        packed[r, 1] = field_imag[:, lanes]


def params():
    return pltpu.CompilerParams(vmem_limit_bytes=VMEM)


def whole(memory=pltpu.VMEM):
    return pl.BlockSpec(memory_space=memory)


def body(field_real, field_imag):
    row_total, col_total = lax.axis_size("row"), lax.axis_size("col")
    devices = row_total * col_total
    device = lax.axis_index("row") * col_total + lax.axis_index("col")
    height, tile_width = field_real.shape
    width = tile_width // row_total
    parts = max(1, devices // RES)
    groups = -(-(2 * HALF + 1) // (8 * parts)) * parts
    own = groups // parts
    tail = parts == 1
    total_rows = groups * 16 - (8 if tail else 0)
    own_rows = total_rows // parts
    many = 4 if width == 128 else 1

    fwd_col, inv_col = column_tables(groups, tail)
    line_fh, line_fl, line_ih, line_il = line_tables()
    twist = np.stack(twist_table())
    twist_line = np.ascontiguousarray(np.broadcast_to(twist[:, :, None], twist.shape[:2] + (8, INNER)))
    twist_col = np.pad(twist, ((0, 0), (0, 64 - twist.shape[1]), (0, 0)))
    twist_col = twist_col.reshape(128, INNER).T.copy()

    u = device // parts
    k0 = jnp.where(u >= RES // 2, u - RES, u)
    place = jnp.stack([k0, (device % parts) * own]).astype(jnp.int32)
    gain_shape = jax.ShapeDtypeStruct((own, RES * 8, 128), jnp.float32)
    gain_spec = pl.BlockSpec((1, RES * 8, 128), lambda g: (g, 0, 0))
    gain_re, gain_im = pl.pallas_call(
        gain_kernel,
        grid=(own,),
        in_specs=[whole(pltpu.SMEM)],
        out_specs=[gain_spec, gain_spec],
        out_shape=[gain_shape, gain_shape],
        compiler_params=params(),
        name="gain",
    )(place)

    pack_rows = min(height, 256)
    if width == 128:
        packed = pl.pallas_call(
            pack_kernel,
            grid=(height // pack_rows,),
            in_specs=[pl.BlockSpec((pack_rows, tile_width), lambda i: (i, 0))] * 2,
            out_specs=pl.BlockSpec((row_total, 2, pack_rows, width), lambda i: (0, 0, i, 0)),
            out_shape=jax.ShapeDtypeStruct((row_total, 2, height, width), jnp.float32),
            compiler_params=params(),
            name="pack",
        )(field_real, field_imag)
    else:
        packed = jnp.stack([field_real, field_imag])
        packed = packed.reshape(2, height, row_total, width).transpose(2, 0, 1, 3)
    columns = lax.all_to_all(packed, "row", split_axis=0, concat_axis=0, tiled=True)

    blocks = height // INNER
    columns = columns.reshape(row_total, 2, blocks, INNER, width)
    tall = (row_total, 2, blocks, CHUNK, width)
    slab = pltpu.VMEM((2, RES // many, 2 * CHUNK, many * width), jnp.bfloat16)
    lines = pl.pallas_call(
        column_forward_kernel,
        grid=(CHUNKS + 1,),
        in_specs=[
            pl.BlockSpec(tall, lambda i: (0, 0, 0, jnp.minimum(i, CHUNKS - 1), 0)),
            pl.BlockSpec((CHUNK, 128), lambda i: (jnp.minimum(i, CHUNKS - 1), 0)),
            pl.BlockSpec((1, 2 * total_rows, 2 * CHUNK), lambda i: (jnp.maximum(i - 1, 0), 0, 0)),
        ],
        out_specs=whole(),
        out_shape=jax.ShapeDtypeStruct((RES, total_rows, width), jnp.float32),
        scratch_shapes=[slab, slab],
        compiler_params=params(),
        name="column_forward",
    )(columns, twist_col, fwd_col)

    lines = lines.reshape(devices, own_rows, width)
    lines = lax.all_to_all(lines, ("row", "col"), split_axis=0, concat_axis=0, tiled=True)
    if width == 128:
        order = tuple((b % row_total) * col_total + b // row_total for b in range(N // 128))
    else:
        order = tuple(range(N // 128))
        lines = lines.reshape(row_total, col_total, own_rows, width).transpose(2, 1, 0, 3)
        lines = lines.reshape(own_rows, N // 128, 128).transpose(1, 0, 2)

    at_once = 2
    line_grain = pl.BlockSpec((N // 128, 16 * at_once, 128), lambda i: (0, i, 0))
    gain_grain = pl.BlockSpec((at_once, RES * 8, 128), lambda i: (i, 0, 0))
    lines = pl.pallas_call(
        partial(line_kernel, order, tail),
        grid=(-(-own // at_once),),
        in_specs=[line_grain, gain_grain, gain_grain] + [whole()] * 5,
        out_specs=line_grain,
        out_shape=jax.ShapeDtypeStruct((N // 128, own_rows, 128), jnp.float32),
        scratch_shapes=[pltpu.VMEM((2 * RES * 8, 2 * INNER), jnp.bfloat16)] * at_once
        + [pltpu.VMEM((RES * 8, 2 * INNER), jnp.float32)] * at_once,
        compiler_params=params(),
        name="line",
    )(lines, gain_re, gain_im, twist_line, line_fh, line_fl, line_ih, line_il)

    if width != 128:
        lines = lines.transpose(1, 0, 2).reshape(own_rows, col_total, row_total, width)
        lines = lines.transpose(2, 1, 0, 3).reshape(devices, own_rows, width)
    lines = lax.all_to_all(lines, ("row", "col"), split_axis=0, concat_axis=0, tiled=True)
    lines = lines.reshape(RES, total_rows, width)

    near, top = pl.pallas_call(
        column_inverse_kernel,
        grid=(CHUNKS + 1,),
        in_specs=[
            whole(),
            pl.BlockSpec((CHUNK, 128), lambda i: (jnp.maximum(i - 1, 0), 0)),
            pl.BlockSpec((1,) + inv_col.shape[1:], lambda i: (jnp.minimum(i, CHUNKS - 1), 0, 0)),
        ],
        out_specs=[
            pl.BlockSpec(tall, lambda i: (0, 0, 0, jnp.maximum(i - 1, 0), 0)),
            whole(),
        ],
        out_shape=[
            jax.ShapeDtypeStruct((row_total, 2, blocks, INNER, width), jnp.float32),
            jax.ShapeDtypeStruct((8, width), jnp.float32),
        ],
        scratch_shapes=[
            pltpu.VMEM((RES // many, inv_col.shape[2], many * width), jnp.bfloat16),
            pltpu.VMEM((2, RES, 2 * CHUNK, width), jnp.float32),
        ],
        compiler_params=params(),
        name="column_inverse",
    )(lines, twist_col, inv_col)

    near = near.reshape(row_total, 2, height, width)
    near = lax.all_to_all(near, "row", split_axis=0, concat_axis=0, tiled=True)
    peak = jnp.max(top)
    for axis, total in (("row", row_total), ("col", col_total)):
        shift = 1
        while shift < total:
            partner = [(i, i ^ shift) for i in range(total)]
            peak = jnp.maximum(peak, lax.ppermute(peak, axis, partner))
            shift *= 2
    peak = jnp.sqrt(peak)
    if width != 128:
        near = near.transpose(1, 2, 0, 3).reshape(2, height, tile_width)
        even_cell = (jnp.arange(height)[:, None] + jnp.arange(tile_width)[None, :]) % 2 == 0
        return encode(near[0], near[1], peak, even_cell)
    tile_spec = pl.BlockSpec((pack_rows, tile_width), lambda i: (i, 0))
    tile_shape = jax.ShapeDtypeStruct((height, tile_width), jnp.float32)
    return pl.pallas_call(
        encode_kernel,
        grid=(height // pack_rows,),
        in_specs=[
            whole(pltpu.SMEM),
            pl.BlockSpec((row_total, 2, pack_rows, width), lambda i: (0, 0, i, 0)),
        ],
        out_specs=[tile_spec, tile_spec],
        out_shape=[tile_shape, tile_shape],
        compiler_params=params(),
        name="encode",
    )(peak.reshape(1), near)


def solution(mesh):
    in_specs = (P("row", "col"), P("row", "col"))
    out_specs = (P("row", "col"), P("row", "col"))
    return jax.shard_map(body, mesh=mesh, in_specs=in_specs, out_specs=out_specs, check_vma=False)
```

```python
from functools import partial
import math

import jax
import jax.numpy as jnp
import ml_dtypes
import numpy as np
from jax import lax
from jax.experimental import pallas as pl
from jax.experimental.pallas import tpu as pltpu
from jax.sharding import PartitionSpec as P

N = 4096
PAD = 2 * N
wavelength = 5.2e-07
distance = 0.2
INNER = 256
SLABS = N // INNER
RES = PAD // INNER
HALF = 40
CHUNKS = 2
CHUNK = INNER // CHUNKS
VMEM = 56 * 1024 * 1024


def optics(padded_side):
    pitch = 2e-06 * math.sqrt(8192.0 / padded_side)
    extent = padded_side * pitch
    ratio_sq = (wavelength / extent) ** 2
    band_limit = extent / (wavelength * math.sqrt((2.0 * distance / extent) ** 2 + 1.0))
    return (ratio_sq, band_limit)


RATIO_SQ, LIMIT = optics(PAD)
assert RES * HALF - RES // 2 + RES > LIMIT and RES * HALF + RES // 2 > LIMIT


def residue(u):
    return u if u < RES // 2 else u - RES


def split16(table):
    table = np.asarray(table, np.float64)
    high = table.astype(np.float32).astype(ml_dtypes.bfloat16)
    low = (table - high.astype(np.float64)).astype(np.float32).astype(ml_dtypes.bfloat16)
    return high, low


def row_order(groups, tail):
    rows = []
    for group in range(groups):
        size = 4 if tail and group == groups - 1 else 8
        for part in range(2):
            for s in range(size):
                rows.append((part, group * 8 + s - HALF))
    return rows


def column_tables(groups, tail):
    q = np.arange(INNER)
    rows = row_order(groups, tail)
    forward = np.zeros((len(rows), 2, INNER))
    inverse = np.zeros((2, INNER, len(rows)))
    for at, (part, k1) in enumerate(rows):
        if abs(k1) > HALF:
            continue
        angle = 2.0 * np.pi * ((k1 * q) % INNER) / INNER
        c, s = np.cos(angle), np.sin(angle)
        forward[at] = (c, s) if part == 0 else (-s, c)
        inverse[:, :, at] = (c, s) if part == 0 else (-s, c)
    forward = forward.reshape(-1, 2, CHUNKS, CHUNK // 8, 8).transpose(2, 0, 3, 1, 4)
    forward = np.concatenate(split16(forward.reshape(CHUNKS, len(rows), 2 * CHUNK)), axis=1)
    inverse = inverse.reshape(2, CHUNKS, CHUNK, -1).transpose(1, 0, 2, 3)
    high, low = split16(inverse.reshape(CHUNKS, 2 * CHUNK, len(rows)))
    inverse = np.concatenate([high, high, low], axis=2)
    inverse = np.pad(inverse, ((0, 0), (0, 0), (0, -3 * len(rows) % 16)))
    return forward, inverse


def line_tables():
    q = np.arange(INNER)
    forward = np.zeros((2 * INNER, 256))
    inverse = np.zeros((256, 2 * INNER))
    for lane in range(2 * HALF + 1):
        angle = 2.0 * np.pi * (((lane - HALF) * q) % INNER) / INNER
        c, s = np.cos(angle), np.sin(angle)
        forward[:INNER, lane], forward[INNER:, lane] = c, s
        forward[:INNER, 128 + lane], forward[INNER:, 128 + lane] = -s, c
        inverse[lane, :INNER], inverse[lane, INNER:] = c, s
        inverse[128 + lane, :INNER], inverse[128 + lane, INNER:] = -s, c
    return split16(forward) + split16(inverse)


def twist_table():
    q = np.arange(INNER) + N // 2
    k0 = np.arange(RES // 2 + 1)
    angle = 2.0 * np.pi * ((k0[:, None] * q[None, :]) % PAD) / PAD
    return np.cos(angle).astype(np.float32), (-np.sin(angle)).astype(np.float32)


def turn(value, num, den):
    re, im = value
    num = num % den
    eighth = 8 * num
    if num == 0:
        return re, im
    if 2 * num == den:
        return -re, -im
    if 4 * num == den:
        return -im, re
    if 4 * num == 3 * den:
        return im, -re
    if eighth % den == 0:
        root = np.float32(math.sqrt(0.5))
        kind = eighth // den
        if kind == 1:
            return (re - im) * root, (re + im) * root
        if kind == 3:
            return (re + im) * (-root), (re - im) * root
        if kind == 5:
            return (im - re) * root, (re + im) * (-root)
        return (re + im) * root, (im - re) * root
    c = np.float32(math.cos(2.0 * math.pi * num / den))
    s = np.float32(math.sin(2.0 * math.pi * num / den))
    return re * c - im * s, re * s + im * c


def small_dft(get, ids, sign):
    count = len(ids)
    if count == 1:
        return [get(ids[0])]
    even = small_dft(get, ids[0::2], sign)
    odd = small_dft(get, ids[1::2], sign)
    half = count // 2
    first, second = [], []
    for j in range(half):
        re, im = even[j]
        t_re, t_im = turn(odd[j], sign * j, count)
        first.append((re + t_re, im + t_im))
        second.append((re - t_re, im - t_im))
    return first + second


def forward_slabs(get, put):
    ids = list(range(SLABS))
    for v, value in enumerate(small_dft(get, ids, -1)):
        put(2 * v, value)
    for v, value in enumerate(small_dft(lambda n: turn(get(n), -n, RES), ids, -1)):
        put(2 * v + 1, value)


def inverse_slabs(get, put):
    even = small_dft(get, list(range(0, RES, 2)), 1)
    odd = small_dft(get, list(range(1, RES, 2)), 1)
    for n in range(SLABS):
        t_re, t_im = turn(odd[n], n, RES)
        put(n, (even[n][0] + t_re, even[n][1] + t_im))


def twisted(value, u, sign, read):
    re, im = value
    k0 = residue(u)
    if k0 == 0:
        return value
    c, s = read(abs(k0))
    if (k0 < 0) == (sign > 0):
        return re * c + im * s, im * c - re * s
    return re * c - im * s, re * s + im * c


def high_low(value):
    high = value.astype(jnp.bfloat16)
    low = (value - high.astype(jnp.float32)).astype(jnp.bfloat16)
    return high, low


def dot16(left, right):
    return jnp.dot(left, right, preferred_element_type=jnp.float32)


def three_left(stacked, count, high, low):
    both = dot16(stacked[...], high)
    return both[:count] + both[count:] + dot16(stacked[:count], low)


def three_right(stacked, count, high, low):
    both = dot16(stacked, high)
    return both[:count] + both[count:] + dot16(stacked[:count], low)


def column_twist(twist, q0):
    def read(k):
        rows = pl.ds(q0, 8)
        return twist[rows, k : k + 1], twist[rows, 64 + k : 65 + k]

    return read


def column_forward_kernel(count, place, twist, matrix, *refs):
    pieces, refs = refs[:count], refs[count:]
    before, (out, field, high, low, sems) = refs[:-5], refs[-5:]
    width = field.shape[-1]
    per_source = field.shape[2]
    many = high.shape[-1] // width
    rows_out = out.shape[1]
    copies = [
        pltpu.make_async_copy(piece, field.at[place[0] ^ j], sems.at[j])
        for j, piece in enumerate(pieces)
    ]
    copies += [pltpu.make_async_copy(item, out, sems.at[count]) for item in before]
    for copy in copies:
        copy.start()
    for copy in copies[:count]:
        copy.wait()

    @pl.loop(0, CHUNK // 8)
    def _(t):
        q0 = pl.multiple_of(t * 8, 8)

        def get(n):
            source, block = divmod(n, per_source)
            rows = pl.ds(q0, 8)
            return field[source, 0, block, rows, :], field[source, 1, block, rows, :]

        def put(u, value):
            item = jnp.concatenate(twisted(value, u, 1, column_twist(twist, q0)), axis=0)
            rows = pl.ds(pl.multiple_of(t * 16, 16), 16)
            at = (u // many, rows, pl.ds((u % many) * width, width))
            high[at], low[at] = high_low(item)

        forward_slabs(get, put)

    for copy in copies[count:]:
        copy.wait()

    @pl.loop(0, RES // many)
    def _(p):
        done = three_left(matrix, rows_out, high[p], low[p])
        for part in range(many):
            item = done[:, part * width : (part + 1) * width]
            at = p * many + part
            out[at] = out[at] + item if before else item


def column_inverse_kernel(count, place, lines, twist, matrix, *refs):
    pieces, (top, near, deep, back, sems) = refs[:count], refs[count:]
    width = lines.shape[-1]
    rows_in = lines.shape[1]
    per_dest = near.shape[2]
    many = deep.shape[-1] // width

    @pl.loop(0, RES // many)
    def _(p):
        blocks = [lines[p * many + part] for part in range(many)]
        joined = jnp.concatenate(blocks, axis=1) if many > 1 else blocks[0]
        high = joined.astype(jnp.bfloat16).astype(jnp.float32)
        parts = [high, joined - high, high]
        if deep.shape[1] > 3 * rows_in:
            parts.append(jnp.zeros((deep.shape[1] - 3 * rows_in, many * width), jnp.float32))
        deep[p] = jnp.concatenate(parts, axis=0).astype(jnp.bfloat16)
        done = dot16(matrix[...], deep[p])
        for part in range(many):
            back[p * many + part] = done[:, part * width : (part + 1) * width]

    top[...] = jnp.zeros_like(top)

    @pl.loop(0, CHUNK // 8)
    def _(t):
        q0 = pl.multiple_of(t * 8, 8)
        largest = []

        def get(u):
            re = back[u, pl.ds(q0, 8), :]
            im = back[u, pl.ds(CHUNK + q0, 8), :]
            return twisted((re, im), u, -1, column_twist(twist, q0))

        def put(n, value):
            dest, block = divmod(n, per_dest)
            rows = pl.ds(q0, 8)
            near[dest, 0, block, rows, :], near[dest, 1, block, rows, :] = value
            largest.append(value[0] * value[0] + value[1] * value[1])

        inverse_slabs(get, put)
        while len(largest) > 1:
            largest = [jnp.maximum(a, b) for a, b in zip(largest[0::2], largest[1::2])]
        top[...] = jnp.maximum(top[...], largest[0])

    copies = [
        pltpu.make_async_copy(near.at[place[0] ^ j], piece, sems.at[j])
        for j, piece in enumerate(pieces)
    ]
    for copy in copies:
        copy.start()
    for copy in copies:
        copy.wait()


def line_kernel(
    order, tail, lines, gain_re, gain_im, twist, fwd_high, fwd_low, inv_high, inv_low, out, *scratch
):
    half = RES * 8
    at_tail = pl.program_id(0) == pl.num_programs(0) - 1

    def line_twist(side):
        def read(k):
            lanes = pl.ds(side * 128, 128)
            return twist[0, k, :, lanes], twist[1, k, :, lanes]

        return read

    def forward(group, stacked):
        for side in range(2):
            waiting = {}

            def get(m):
                block = order[2 * m + side]
                at = group * 16
                return lines[block, at : at + 8, :], lines[block, at + 8 : at + 16, :]

            def put(u, value):
                waiting[u] = twisted(value, u, 1, line_twist(side))
                v = (u + RES // 2) % RES
                if v in waiting:
                    first = min(u, v)
                    rows = pl.ds(first * 16, 16)
                    rows_low = pl.ds(half + first * 16, 16)
                    for part in range(2):
                        item = jnp.concatenate(
                            [waiting[first][part], waiting[first + RES // 2][part]], axis=0
                        )
                        at = pl.ds(part * INNER + side * 128, 128)
                        stacked[rows, at], stacked[rows_low, at] = high_low(item)

            forward_slabs(get, put)

    def middle(group, stacked, back):
        spec = three_right(stacked[...], half, fwd_high[...], fwd_low[...])
        spec_re, spec_im = spec[:, :128], spec[:, 128:]
        g_re, g_im = gain_re[group], gain_im[group]
        mixed = jnp.concatenate(
            [spec_re * g_re - spec_im * g_im, spec_re * g_im + spec_im * g_re], axis=1
        )
        mixed = jnp.concatenate(high_low(mixed), axis=0)
        back[...] = three_right(mixed, half, inv_high[...], inv_low[...])

    def inverse(group, back):
        for side in range(2):

            def get(u):
                rows = pl.ds((u % (RES // 2)) * 16 + (u // (RES // 2)) * 8, 8)
                re = back[rows, pl.ds(side * 128, 128)]
                im = back[rows, pl.ds(INNER + side * 128, 128)]
                return twisted((re, im), u, -1, line_twist(side))

            def put(m, value):
                block = order[2 * m + side]
                at = group * 16
                out[block, at : at + 8, :], out[block, at + 8 : at + 16, :] = value

            inverse_slabs(get, put)

    if tail:

        @pl.when(at_tail)
        def _():
            for block in range(N // 128):
                lines[block, 8:12, :] = lines[block, 4:8, :]

    groups = len(scratch) // 2
    for group in range(groups):
        forward(group, scratch[group])
    for group in range(groups):
        middle(group, scratch[group], scratch[groups + group])
    for group in range(groups):
        inverse(group, scratch[groups + group])

    if tail:

        @pl.when(at_tail)
        def _():
            for block in range(N // 128):
                out[block, 4:8, :] = out[block, 8:12, :]


def gain_kernel(place, gain_re, gain_im):
    k0 = place[0]
    group = place[1] + pl.program_id(0)
    down = lax.broadcasted_iota(jnp.int32, (8, 128), 0)
    across = lax.broadcasted_iota(jnp.int32, (8, 128), 1)
    row = (k0 + RES * (group * 8 + down - HALF)).astype(jnp.float32)
    row_sq = row * row
    row_in = jnp.abs(row) < LIMIT
    for u in range(RES):
        col = (residue(u) + RES * (across - HALF)).astype(jnp.float32)
        square = row_sq + col * col
        scaled = RATIO_SQ * square
        phase = -2.0 * math.pi * distance / wavelength * scaled / (1.0 + jnp.sqrt(1.0 - scaled))
        total = jnp.where(
            row_in & (jnp.abs(col) < LIMIT), jnp.exp(square * (-2.0 / (LIMIT * LIMIT))), 0.0
        )
        quarter = jnp.floor(phase * (2.0 / math.pi) + 0.5)
        left = phase - quarter * 1.5703125
        left = left - quarter * 4.837512969970703125e-4
        left = left - quarter * 7.549789954891882e-8
        sq = left * left
        sine = ((-1.9515295891e-4 * sq + 8.3321608736e-3) * sq - 1.6666654611e-1) * sq * left + left
        cosine = (
            (2.443315711809948e-5 * sq - 1.388731625493765e-3) * sq + 4.166664568298827e-2
        ) * sq * sq - 0.5 * sq + 1.0
        which = quarter.astype(jnp.int32) & 3
        swap = (which & 1) == 1
        cos_part = jnp.where(swap, sine, cosine)
        sin_part = jnp.where(swap, cosine, sine)
        cos_part = jnp.where((which == 1) | (which == 2), -cos_part, cos_part)
        sin_part = jnp.where(which >= 2, -sin_part, sin_part)
        at = (u % (RES // 2)) * 16 + (u // (RES // 2)) * 8
        gain_re[0, at : at + 8, :] = total * cos_part
        gain_im[0, at : at + 8, :] = total * sin_part


def inverse_root(value):
    root = lax.rsqrt(value)
    return root * (1.5 - 0.5 * (value * root) * root)


def encode(near_real, near_imag, peak, even_cell):
    square = near_real * near_real + near_imag * near_imag
    root = inverse_root(jnp.maximum(square, 1.2e-38))
    amp_level = (square * root) * (0.8 / peak)
    unit = jnp.minimum(root, 20.0 / peak)
    rest = 1.0 - amp_level * amp_level
    lift_part = rest * inverse_root(rest)
    level = unit * amp_level
    lift = jnp.where(even_cell, unit * lift_part, -(unit * lift_part))
    return (near_real * level + near_imag * lift, near_imag * level - near_real * lift)


def encode_kernel(place, peak, *refs):
    pieces, (slm_real, slm_imag) = refs[:-2], refs[-2:]
    width = pieces[0].shape[-1]
    count = len(pieces) // CHUNKS
    cell = lax.broadcasted_iota(jnp.int32, (CHUNK, width), 0)
    cell = cell + lax.broadcasted_iota(jnp.int32, (CHUNK, width), 1)
    for at, piece in enumerate(pieces):
        chunk, j = divmod(at, count)
        rows = pl.ds(chunk * CHUNK, CHUNK)
        lanes = pl.ds(pl.multiple_of((place[0] ^ j) * width, width), width)
        slm_real[rows, lanes], slm_imag[rows, lanes] = encode(
            piece[0, 0], piece[1, 0], peak[0], (cell & 1) == 0
        )


def pack_kernel(place, field_real, field_imag, *pieces):
    width = pieces[0].shape[-1]
    for j, piece in enumerate(pieces):
        lanes = pl.ds(pl.multiple_of((place[0] ^ j) * width, width), width)
        piece[0, 0] = field_real[:, lanes]
        piece[1, 0] = field_imag[:, lanes]


def exchange(pieces, axis):
    total = len(pieces)
    return [pieces[0]] + [
        lax.ppermute(pieces[j], axis, [(i, i ^ j) for i in range(total)]) for j in range(1, total)
    ]


def params():
    return pltpu.CompilerParams(vmem_limit_bytes=VMEM)


def cost(megabytes):
    return pl.CostEstimate(flops=0, bytes_accessed=megabytes << 20, transcendentals=0)


def whole(memory=pltpu.VMEM):
    return pl.BlockSpec(memory_space=memory)


def body(field_real, field_imag):
    row_total, col_total = lax.axis_size("row"), lax.axis_size("col")
    devices = row_total * col_total
    device = lax.axis_index("row") * col_total + lax.axis_index("col")
    height, tile_width = field_real.shape
    width = tile_width // row_total
    parts = max(1, devices // RES)
    groups = -(-(2 * HALF + 1) // (8 * parts)) * parts
    own = groups // parts
    tail = parts == 1
    total_rows = groups * 16 - (8 if tail else 0)
    own_rows = total_rows // parts
    many = 4 if width == 128 else 1

    fwd_col, inv_col = column_tables(groups, tail)
    line_fh, line_fl, line_ih, line_il = line_tables()
    twist = np.stack(twist_table())
    twist_line = np.ascontiguousarray(np.broadcast_to(twist[:, :, None], twist.shape[:2] + (8, INNER)))
    twist_col = np.pad(twist, ((0, 0), (0, 64 - twist.shape[1]), (0, 0)))
    twist_col = twist_col.reshape(128, INNER).T.copy()

    u = device // parts
    k0 = jnp.where(u >= RES // 2, u - RES, u)
    place = jnp.stack([k0, (device % parts) * own]).astype(jnp.int32)
    gain_shape = jax.ShapeDtypeStruct((own, RES * 8, 128), jnp.float32)
    gain_spec = pl.BlockSpec((1, RES * 8, 128), lambda g: (g, 0, 0))
    gain_re, gain_im = pl.pallas_call(
        gain_kernel,
        grid=(own,),
        in_specs=[whole(pltpu.SMEM)],
        out_specs=[gain_spec, gain_spec],
        out_shape=[gain_shape, gain_shape],
        compiler_params=params(),
        name="gain",
    )(place)

    place_row = lax.axis_index("row").reshape(1).astype(jnp.int32)
    blocks = height // INNER
    piece = (2, blocks, CHUNK, width)
    piece_shape = jax.ShapeDtypeStruct(piece, jnp.float32)
    anywhere = whole(pl.ANY)
    if width != 128:
        packed = jnp.stack([field_real, field_imag])
        packed = packed.reshape(2, blocks, CHUNKS, CHUNK, row_total, width).transpose(2, 4, 0, 1, 3, 5)
        packed = jnp.take(packed, jnp.arange(row_total) ^ place_row[0], axis=1)
    lines = []
    for chunk in range(CHUNKS):
        if width == 128:
            pieces = pl.pallas_call(
                pack_kernel,
                grid=(blocks,),
                in_specs=[whole(pltpu.SMEM)]
                + [pl.BlockSpec((CHUNK, tile_width), lambda i: (i * CHUNKS + chunk, 0))] * 2,
                out_specs=[pl.BlockSpec((2, 1, CHUNK, width), lambda i: (0, i, 0, 0))] * row_total,
                out_shape=[piece_shape] * row_total,
                compiler_params=params(),
                cost_estimate=cost(4),
                name="pack",
            )(place_row, field_real, field_imag)
        else:
            pieces = [packed[chunk, j] for j in range(row_total)]
        pieces = exchange(pieces, "row")
        rows = slice(chunk * CHUNK, (chunk + 1) * CHUNK)
        slab = pltpu.VMEM((RES // many, 2 * CHUNK, many * width), jnp.bfloat16)
        lines = [
            pl.pallas_call(
                partial(column_forward_kernel, row_total),
                in_specs=[whole(pltpu.SMEM)] + [whole()] * 2 + [anywhere] * (row_total + len(lines)),
                out_specs=whole(),
                out_shape=jax.ShapeDtypeStruct((RES, total_rows, width), jnp.float32),
                scratch_shapes=[
                    pltpu.VMEM((row_total,) + piece, jnp.float32),
                    slab,
                    slab,
                    pltpu.SemaphoreType.DMA((row_total + 1,)),
                ],
                compiler_params=params(),
                cost_estimate=cost(20),
                name="column_forward",
            )(place_row, twist_col[rows], fwd_col[chunk], *pieces, *lines)
        ]
    (lines,) = lines

    lines = lines.reshape(devices, own_rows, width)
    lines = lax.all_to_all(lines, ("row", "col"), split_axis=0, concat_axis=0, tiled=True)
    if width == 128:
        order = tuple((b % row_total) * col_total + b // row_total for b in range(N // 128))
    else:
        order = tuple(range(N // 128))
        lines = lines.reshape(row_total, col_total, own_rows, width).transpose(2, 1, 0, 3)
        lines = lines.reshape(own_rows, N // 128, 128).transpose(1, 0, 2)

    at_once = 2
    line_grain = pl.BlockSpec((N // 128, 16 * at_once, 128), lambda i: (0, i, 0))
    gain_grain = pl.BlockSpec((at_once, RES * 8, 128), lambda i: (i, 0, 0))
    lines = pl.pallas_call(
        partial(line_kernel, order, tail),
        grid=(-(-own // at_once),),
        in_specs=[line_grain, gain_grain, gain_grain] + [whole()] * 5,
        out_specs=line_grain,
        out_shape=jax.ShapeDtypeStruct((N // 128, own_rows, 128), jnp.float32),
        scratch_shapes=[pltpu.VMEM((2 * RES * 8, 2 * INNER), jnp.bfloat16)] * at_once
        + [pltpu.VMEM((RES * 8, 2 * INNER), jnp.float32)] * at_once,
        compiler_params=params(),
        name="line",
    )(lines, gain_re, gain_im, twist_line, line_fh, line_fl, line_ih, line_il)

    if width != 128:
        lines = lines.transpose(1, 0, 2).reshape(own_rows, col_total, row_total, width)
        lines = lines.transpose(2, 1, 0, 3).reshape(devices, own_rows, width)
    lines = lax.all_to_all(lines, ("row", "col"), split_axis=0, concat_axis=0, tiled=True)
    lines = lines.reshape(RES, total_rows, width)

    near, tops = [], []
    for chunk in range(CHUNKS):
        rows = slice(chunk * CHUNK, (chunk + 1) * CHUNK)
        *pieces, top = pl.pallas_call(
            partial(column_inverse_kernel, row_total),
            in_specs=[whole(pltpu.SMEM)] + [whole()] * 3,
            out_specs=[anywhere] * row_total + [whole()],
            out_shape=[piece_shape] * row_total + [jax.ShapeDtypeStruct((8, width), jnp.float32)],
            scratch_shapes=[
                pltpu.VMEM((row_total,) + piece, jnp.float32),
                pltpu.VMEM((RES // many, inv_col.shape[2], many * width), jnp.bfloat16),
                pltpu.VMEM((RES, 2 * CHUNK, width), jnp.float32),
                pltpu.SemaphoreType.DMA((row_total,)),
            ],
            compiler_params=params(),
            cost_estimate=cost(20),
            name="column_inverse",
        )(place_row, lines, twist_col[rows], inv_col[chunk])
        near += exchange(pieces, "row")
        tops.append(top)
    peak = jnp.max(jnp.stack(tops))
    for axis, total in (("row", row_total), ("col", col_total)):
        peak = jnp.max(jnp.stack(exchange([peak] * total, axis)))
    peak = jnp.sqrt(peak)

    if width != 128:
        near = jnp.stack(near).reshape((CHUNKS, row_total) + piece)
        near = jnp.take(near, jnp.arange(row_total) ^ place_row[0], axis=1)
        near = near.transpose(2, 3, 0, 4, 1, 5).reshape(2, height, tile_width)
        even_cell = (jnp.arange(height)[:, None] + jnp.arange(tile_width)[None, :]) % 2 == 0
        return encode(near[0], near[1], peak, even_cell)
    tile_spec = pl.BlockSpec((INNER, tile_width), lambda i: (i, 0))
    tile_shape = jax.ShapeDtypeStruct((height, tile_width), jnp.float32)
    return pl.pallas_call(
        encode_kernel,
        grid=(blocks,),
        in_specs=[whole(pltpu.SMEM)] * 2
        + [pl.BlockSpec((2, 1, CHUNK, width), lambda i: (0, i, 0, 0))] * len(near),
        out_specs=[tile_spec, tile_spec],
        out_shape=[tile_shape, tile_shape],
        compiler_params=params(),
        name="encode",
    )(place_row, peak.reshape(1), *near)


def solution(mesh):
    in_specs = (P("row", "col"), P("row", "col"))
    out_specs = (P("row", "col"), P("row", "col"))
    return jax.shard_map(body, mesh=mesh, in_specs=in_specs, out_specs=out_specs, check_vma=False)
```

```python
from functools import partial
import math

import jax
import jax.numpy as jnp
import ml_dtypes
import numpy as np
from jax import lax
from jax.experimental import pallas as pl
from jax.experimental.pallas import tpu as pltpu
from jax.sharding import PartitionSpec as P

N = 4096
PAD = 2 * N
wavelength = 5.2e-07
distance = 0.2
INNER = 256
SLABS = N // INNER
RES = PAD // INNER
HALF = 40
CHUNKS = 2
CHUNK = INNER // CHUNKS
VMEM = 56 * 1024 * 1024


def optics(padded_side):
    pitch = 2e-06 * math.sqrt(8192.0 / padded_side)
    extent = padded_side * pitch
    ratio_sq = (wavelength / extent) ** 2
    band_limit = extent / (wavelength * math.sqrt((2.0 * distance / extent) ** 2 + 1.0))
    return (ratio_sq, band_limit)


RATIO_SQ, LIMIT = optics(PAD)
assert RES * HALF - RES // 2 + RES > LIMIT and RES * HALF + RES // 2 > LIMIT


def residue(u):
    return u if u < RES // 2 else u - RES


def split16(table):
    table = np.asarray(table, np.float64)
    high = table.astype(np.float32).astype(ml_dtypes.bfloat16)
    low = (table - high.astype(np.float64)).astype(np.float32).astype(ml_dtypes.bfloat16)
    return high, low


def row_order(groups, tail):
    rows = []
    for group in range(groups):
        size = 4 if tail and group == groups - 1 else 8
        for part in range(2):
            for s in range(size):
                rows.append((part, group * 8 + s - HALF))
    return rows


def column_tables(groups, tail):
    q = np.arange(INNER)
    rows = row_order(groups, tail)
    forward = np.zeros((len(rows), 2, INNER))
    inverse = np.zeros((2, INNER, len(rows)))
    for at, (part, k1) in enumerate(rows):
        if abs(k1) > HALF:
            continue
        angle = 2.0 * np.pi * ((k1 * q) % INNER) / INNER
        c, s = np.cos(angle), np.sin(angle)
        forward[at] = (c, s) if part == 0 else (-s, c)
        inverse[:, :, at] = (c, s) if part == 0 else (-s, c)
    forward = forward.reshape(-1, 2, CHUNKS, CHUNK // 8, 8).transpose(2, 0, 3, 1, 4)
    forward = np.concatenate(split16(forward.reshape(CHUNKS, len(rows), 2 * CHUNK)), axis=1)
    inverse = inverse.reshape(2, CHUNKS, CHUNK, -1).transpose(1, 0, 2, 3)
    high, low = split16(inverse.reshape(CHUNKS, 2 * CHUNK, len(rows)))
    inverse = np.concatenate([high, high, low], axis=2)
    inverse = np.pad(inverse, ((0, 0), (0, 0), (0, -3 * len(rows) % 16)))
    return forward, inverse


def line_tables():
    q = np.arange(INNER)
    forward = np.zeros((2 * INNER, 256))
    inverse = np.zeros((256, 2 * INNER))
    for lane in range(2 * HALF + 1):
        angle = 2.0 * np.pi * (((lane - HALF) * q) % INNER) / INNER
        c, s = np.cos(angle), np.sin(angle)
        forward[:INNER, lane], forward[INNER:, lane] = c, s
        forward[:INNER, 128 + lane], forward[INNER:, 128 + lane] = -s, c
        inverse[lane, :INNER], inverse[lane, INNER:] = c, s
        inverse[128 + lane, :INNER], inverse[128 + lane, INNER:] = -s, c
    return split16(forward) + split16(inverse)


def twist_table():
    q = np.arange(INNER) + N // 2
    k0 = np.arange(RES // 2 + 1)
    angle = 2.0 * np.pi * ((k0[:, None] * q[None, :]) % PAD) / PAD
    return np.cos(angle).astype(np.float32), (-np.sin(angle)).astype(np.float32)


def turn(value, num, den):
    re, im = value
    num = num % den
    eighth = 8 * num
    if num == 0:
        return re, im
    if 2 * num == den:
        return -re, -im
    if 4 * num == den:
        return -im, re
    if 4 * num == 3 * den:
        return im, -re
    if eighth % den == 0:
        root = np.float32(math.sqrt(0.5))
        kind = eighth // den
        if kind == 1:
            return (re - im) * root, (re + im) * root
        if kind == 3:
            return (re + im) * (-root), (re - im) * root
        if kind == 5:
            return (im - re) * root, (re + im) * (-root)
        return (re + im) * root, (im - re) * root
    c = np.float32(math.cos(2.0 * math.pi * num / den))
    s = np.float32(math.sin(2.0 * math.pi * num / den))
    return re * c - im * s, re * s + im * c


def small_dft(get, ids, sign):
    count = len(ids)
    if count == 1:
        return [get(ids[0])]
    even = small_dft(get, ids[0::2], sign)
    odd = small_dft(get, ids[1::2], sign)
    half = count // 2
    first, second = [], []
    for j in range(half):
        re, im = even[j]
        t_re, t_im = turn(odd[j], sign * j, count)
        first.append((re + t_re, im + t_im))
        second.append((re - t_re, im - t_im))
    return first + second


def forward_slabs(get, put):
    ids = list(range(SLABS))
    for v, value in enumerate(small_dft(get, ids, -1)):
        put(2 * v, value)
    for v, value in enumerate(small_dft(lambda n: turn(get(n), -n, RES), ids, -1)):
        put(2 * v + 1, value)


def inverse_slabs(get, put):
    even = small_dft(get, list(range(0, RES, 2)), 1)
    odd = small_dft(get, list(range(1, RES, 2)), 1)
    for n in range(SLABS):
        t_re, t_im = turn(odd[n], n, RES)
        put(n, (even[n][0] + t_re, even[n][1] + t_im))


def twisted(value, u, sign, read):
    re, im = value
    k0 = residue(u)
    if k0 == 0:
        return value
    c, s = read(abs(k0))
    if (k0 < 0) == (sign > 0):
        return re * c + im * s, im * c - re * s
    return re * c - im * s, re * s + im * c


def high_low(value):
    high = value.astype(jnp.bfloat16)
    low = (value - high.astype(jnp.float32)).astype(jnp.bfloat16)
    return high, low


def dot16(left, right):
    return jnp.dot(left, right, preferred_element_type=jnp.float32)


def three_left(stacked, count, high, low):
    both = dot16(stacked[...], high)
    return both[:count] + both[count:] + dot16(stacked[:count], low)


def three_right(stacked, count, high, low):
    both = dot16(stacked, high)
    return both[:count] + both[count:] + dot16(stacked[:count], low)


def column_twist(twist, q0):
    def read(k):
        rows = pl.ds(q0, 8)
        return twist[rows, k : k + 1], twist[rows, 64 + k : 65 + k]

    return read


def column_forward_kernel(count, place, twist, matrix, *refs):
    pieces, refs = refs[:count], refs[count:]
    before, (out, field, high, low, sems) = refs[:-5], refs[-5:]
    width = field.shape[-1]
    per_source = field.shape[2]
    many = high.shape[-1] // width
    rows_out = out.shape[1]
    copies = [
        pltpu.make_async_copy(piece, field.at[place[0] ^ j], sems.at[j])
        for j, piece in enumerate(pieces)
    ]
    copies += [pltpu.make_async_copy(item, out, sems.at[count]) for item in before]
    for copy in copies:
        copy.start()
    for copy in copies[:count]:
        copy.wait()

    @pl.loop(0, CHUNK // 8)
    def _(t):
        q0 = pl.multiple_of(t * 8, 8)

        def get(n):
            source, block = divmod(n, per_source)
            rows = pl.ds(q0, 8)
            return field[source, 0, block, rows, :], field[source, 1, block, rows, :]

        def put(u, value):
            item = jnp.concatenate(twisted(value, u, 1, column_twist(twist, q0)), axis=0)
            rows = pl.ds(pl.multiple_of(t * 16, 16), 16)
            at = (u // many, rows, pl.ds((u % many) * width, width))
            high[at], low[at] = high_low(item)

        forward_slabs(get, put)

    for copy in copies[count:]:
        copy.wait()

    @pl.loop(0, RES // many)
    def _(p):
        done = three_left(matrix, rows_out, high[p], low[p])
        for part in range(many):
            item = done[:, part * width : (part + 1) * width]
            at = p * many + part
            out[at] = out[at] + item if before else item


def interleave(tiles, products, butterflies, product):
    steps = min(tiles, products)

    @pl.loop(0, steps)
    def _(t):
        if product is not None:
            for part in range(products // steps):
                product(t * (products // steps) + part)
        if butterflies is not None:
            for part in range(tiles // steps):
                butterflies(t * (tiles // steps) + part)


def column_inverse_kernel(lines, twist, matrix, out, top, deep, back):
    width = lines.shape[-1]
    rows_in = lines.shape[1]
    per_dest = out.shape[2]
    many = deep.shape[-1] // width
    now = pl.program_id(0)

    def product(p):
        done = dot16(matrix[0], deep[p])
        slot = now % 2
        for part in range(many):
            back[slot, p * many + part] = done[:, part * width : (part + 1) * width]

    def prepare(p):
        blocks = [lines[p * many + part] for part in range(many)]
        joined = jnp.concatenate(blocks, axis=1) if many > 1 else blocks[0]
        high = joined.astype(jnp.bfloat16).astype(jnp.float32)
        parts = [high, joined - high, high]
        if deep.shape[1] > 3 * rows_in:
            parts.append(jnp.zeros((deep.shape[1] - 3 * rows_in, many * width), jnp.float32))
        deep[p] = jnp.concatenate(parts, axis=0).astype(jnp.bfloat16)
        product(p)

    def butterflies(t):
        q0 = pl.multiple_of(t * 8, 8)
        slot = (now + 1) % 2
        largest = []

        def get(u):
            re = back[slot, u, pl.ds(q0, 8), :]
            im = back[slot, u, pl.ds(CHUNK + q0, 8), :]
            return twisted((re, im), u, -1, column_twist(twist, q0))

        def put(n, value):
            dest, block = divmod(n, per_dest)
            rows = pl.ds(q0, 8)
            out[dest, 0, block, rows, :], out[dest, 1, block, rows, :] = value
            largest.append(value[0] * value[0] + value[1] * value[1])

        inverse_slabs(get, put)
        while len(largest) > 1:
            largest = [jnp.maximum(a, b) for a, b in zip(largest[0::2], largest[1::2])]
        top[...] = jnp.maximum(top[...], largest[0])

    @pl.when(now == 0)
    def _():
        top[...] = jnp.zeros_like(top)
        pl.loop(0, RES // many)(prepare)

    for step in range(1, CHUNKS + 1):

        @pl.when(now == step)
        def _():
            interleave(
                CHUNK // 8, RES // many, butterflies, product if step < CHUNKS else None
            )


def line_kernel(
    order, tail, lines, gain_re, gain_im, twist, fwd_high, fwd_low, inv_high, inv_low, out, *scratch
):
    half = RES * 8
    at_tail = pl.program_id(0) == pl.num_programs(0) - 1

    def line_twist(side):
        def read(k):
            lanes = pl.ds(side * 128, 128)
            return twist[0, k, :, lanes], twist[1, k, :, lanes]

        return read

    def forward(group, stacked):
        for side in range(2):
            waiting = {}

            def get(m):
                block = order[2 * m + side]
                at = group * 16
                return lines[block, at : at + 8, :], lines[block, at + 8 : at + 16, :]

            def put(u, value):
                waiting[u] = twisted(value, u, 1, line_twist(side))
                v = (u + RES // 2) % RES
                if v in waiting:
                    first = min(u, v)
                    rows = pl.ds(first * 16, 16)
                    rows_low = pl.ds(half + first * 16, 16)
                    for part in range(2):
                        item = jnp.concatenate(
                            [waiting[first][part], waiting[first + RES // 2][part]], axis=0
                        )
                        at = pl.ds(part * INNER + side * 128, 128)
                        stacked[rows, at], stacked[rows_low, at] = high_low(item)

            forward_slabs(get, put)

    def middle(group, stacked, back):
        spec = three_right(stacked[...], half, fwd_high[...], fwd_low[...])
        spec_re, spec_im = spec[:, :128], spec[:, 128:]
        g_re, g_im = gain_re[group], gain_im[group]
        mixed = jnp.concatenate(
            [spec_re * g_re - spec_im * g_im, spec_re * g_im + spec_im * g_re], axis=1
        )
        mixed = jnp.concatenate(high_low(mixed), axis=0)
        back[...] = three_right(mixed, half, inv_high[...], inv_low[...])

    def inverse(group, back):
        for side in range(2):

            def get(u):
                rows = pl.ds((u % (RES // 2)) * 16 + (u // (RES // 2)) * 8, 8)
                re = back[rows, pl.ds(side * 128, 128)]
                im = back[rows, pl.ds(INNER + side * 128, 128)]
                return twisted((re, im), u, -1, line_twist(side))

            def put(m, value):
                block = order[2 * m + side]
                at = group * 16
                out[block, at : at + 8, :], out[block, at + 8 : at + 16, :] = value

            inverse_slabs(get, put)

    if tail:

        @pl.when(at_tail)
        def _():
            for block in range(N // 128):
                lines[block, 8:12, :] = lines[block, 4:8, :]

    groups = len(scratch) // 2
    for group in range(groups):
        forward(group, scratch[group])
    for group in range(groups):
        middle(group, scratch[group], scratch[groups + group])
    for group in range(groups):
        inverse(group, scratch[groups + group])

    if tail:

        @pl.when(at_tail)
        def _():
            for block in range(N // 128):
                out[block, 4:8, :] = out[block, 8:12, :]


def gain_kernel(place, gain_re, gain_im):
    k0 = place[0]
    group = place[1] + pl.program_id(0)
    down = lax.broadcasted_iota(jnp.int32, (8, 128), 0)
    across = lax.broadcasted_iota(jnp.int32, (8, 128), 1)
    row = (k0 + RES * (group * 8 + down - HALF)).astype(jnp.float32)
    row_sq = row * row
    row_in = jnp.abs(row) < LIMIT
    for u in range(RES):
        col = (residue(u) + RES * (across - HALF)).astype(jnp.float32)
        square = row_sq + col * col
        scaled = RATIO_SQ * square
        phase = -2.0 * math.pi * distance / wavelength * scaled / (1.0 + jnp.sqrt(1.0 - scaled))
        total = jnp.where(
            row_in & (jnp.abs(col) < LIMIT), jnp.exp(square * (-2.0 / (LIMIT * LIMIT))), 0.0
        )
        quarter = jnp.floor(phase * (2.0 / math.pi) + 0.5)
        left = phase - quarter * 1.5703125
        left = left - quarter * 4.837512969970703125e-4
        left = left - quarter * 7.549789954891882e-8
        sq = left * left
        sine = ((-1.9515295891e-4 * sq + 8.3321608736e-3) * sq - 1.6666654611e-1) * sq * left + left
        cosine = (
            (2.443315711809948e-5 * sq - 1.388731625493765e-3) * sq + 4.166664568298827e-2
        ) * sq * sq - 0.5 * sq + 1.0
        which = quarter.astype(jnp.int32) & 3
        swap = (which & 1) == 1
        cos_part = jnp.where(swap, sine, cosine)
        sin_part = jnp.where(swap, cosine, sine)
        cos_part = jnp.where((which == 1) | (which == 2), -cos_part, cos_part)
        sin_part = jnp.where(which >= 2, -sin_part, sin_part)
        at = (u % (RES // 2)) * 16 + (u // (RES // 2)) * 8
        gain_re[0, at : at + 8, :] = total * cos_part
        gain_im[0, at : at + 8, :] = total * sin_part


def inverse_root(value):
    root = lax.rsqrt(value)
    return root * (1.5 - 0.5 * (value * root) * root)


def encode(near_real, near_imag, peak, even_cell):
    square = near_real * near_real + near_imag * near_imag
    root = inverse_root(jnp.maximum(square, 1.2e-38))
    amp_level = (square * root) * (0.8 / peak)
    unit = jnp.minimum(root, 20.0 / peak)
    rest = 1.0 - amp_level * amp_level
    lift_part = rest * inverse_root(rest)
    level = unit * amp_level
    lift = jnp.where(even_cell, unit * lift_part, -(unit * lift_part))
    return (near_real * level + near_imag * lift, near_imag * level - near_real * lift)


def encode_kernel(peak, near, slm_real, slm_imag):
    rows, width = near.shape[2:]
    cell = lax.broadcasted_iota(jnp.int32, (rows, width), 0)
    cell = cell + lax.broadcasted_iota(jnp.int32, (rows, width), 1)
    for r in range(near.shape[0]):
        lanes = pl.ds(r * width, width)
        slm_real[:, lanes], slm_imag[:, lanes] = encode(
            near[r, 0], near[r, 1], peak[0], (cell & 1) == 0
        )


def pack_kernel(place, field_real, field_imag, *pieces):
    width = pieces[0].shape[-1]
    for j, piece in enumerate(pieces):
        lanes = pl.ds(pl.multiple_of((place[0] ^ j) * width, width), width)
        piece[0, 0] = field_real[:, lanes]
        piece[1, 0] = field_imag[:, lanes]


def exchange(pieces, axis):
    total = len(pieces)
    return [pieces[0]] + [
        lax.ppermute(pieces[j], axis, [(i, i ^ j) for i in range(total)]) for j in range(1, total)
    ]


def params():
    return pltpu.CompilerParams(vmem_limit_bytes=VMEM)


def cost(megabytes):
    return pl.CostEstimate(flops=0, bytes_accessed=megabytes << 20, transcendentals=0)


def whole(memory=pltpu.VMEM):
    return pl.BlockSpec(memory_space=memory)


def body(field_real, field_imag):
    row_total, col_total = lax.axis_size("row"), lax.axis_size("col")
    devices = row_total * col_total
    device = lax.axis_index("row") * col_total + lax.axis_index("col")
    height, tile_width = field_real.shape
    width = tile_width // row_total
    parts = max(1, devices // RES)
    groups = -(-(2 * HALF + 1) // (8 * parts)) * parts
    own = groups // parts
    tail = parts == 1
    total_rows = groups * 16 - (8 if tail else 0)
    own_rows = total_rows // parts
    many = 4 if width == 128 else 1

    fwd_col, inv_col = column_tables(groups, tail)
    line_fh, line_fl, line_ih, line_il = line_tables()
    twist = np.stack(twist_table())
    twist_line = np.ascontiguousarray(np.broadcast_to(twist[:, :, None], twist.shape[:2] + (8, INNER)))
    twist_col = np.pad(twist, ((0, 0), (0, 64 - twist.shape[1]), (0, 0)))
    twist_col = twist_col.reshape(128, INNER).T.copy()

    u = device // parts
    k0 = jnp.where(u >= RES // 2, u - RES, u)
    place = jnp.stack([k0, (device % parts) * own]).astype(jnp.int32)
    gain_shape = jax.ShapeDtypeStruct((own, RES * 8, 128), jnp.float32)
    gain_spec = pl.BlockSpec((1, RES * 8, 128), lambda g: (g, 0, 0))
    gain_re, gain_im = pl.pallas_call(
        gain_kernel,
        grid=(own,),
        in_specs=[whole(pltpu.SMEM)],
        out_specs=[gain_spec, gain_spec],
        out_shape=[gain_shape, gain_shape],
        compiler_params=params(),
        name="gain",
    )(place)

    pack_rows = min(height, 256)
    tall = (row_total, 2, height // INNER, CHUNK, width)
    place_row = lax.axis_index("row").reshape(1).astype(jnp.int32)
    blocks = height // INNER
    piece = (2, blocks, CHUNK, width)
    piece_shape = jax.ShapeDtypeStruct(piece, jnp.float32)
    anywhere = whole(pl.ANY)
    if width != 128:
        packed = jnp.stack([field_real, field_imag])
        packed = packed.reshape(2, blocks, CHUNKS, CHUNK, row_total, width).transpose(2, 4, 0, 1, 3, 5)
        packed = jnp.take(packed, jnp.arange(row_total) ^ place_row[0], axis=1)
    lines = []
    for chunk in range(CHUNKS):
        if width == 128:
            pieces = pl.pallas_call(
                pack_kernel,
                grid=(blocks,),
                in_specs=[whole(pltpu.SMEM)]
                + [pl.BlockSpec((CHUNK, tile_width), lambda i: (i * CHUNKS + chunk, 0))] * 2,
                out_specs=[pl.BlockSpec((2, 1, CHUNK, width), lambda i: (0, i, 0, 0))] * row_total,
                out_shape=[piece_shape] * row_total,
                compiler_params=params(),
                cost_estimate=cost(4),
                name="pack",
            )(place_row, field_real, field_imag)
        else:
            pieces = [packed[chunk, j] for j in range(row_total)]
        pieces = exchange(pieces, "row")
        rows = slice(chunk * CHUNK, (chunk + 1) * CHUNK)
        slab = pltpu.VMEM((RES // many, 2 * CHUNK, many * width), jnp.bfloat16)
        lines = [
            pl.pallas_call(
                partial(column_forward_kernel, row_total),
                in_specs=[whole(pltpu.SMEM)] + [whole()] * 2 + [anywhere] * (row_total + len(lines)),
                out_specs=whole(),
                out_shape=jax.ShapeDtypeStruct((RES, total_rows, width), jnp.float32),
                scratch_shapes=[
                    pltpu.VMEM((row_total,) + piece, jnp.float32),
                    slab,
                    slab,
                    pltpu.SemaphoreType.DMA((row_total + 1,)),
                ],
                compiler_params=params(),
                cost_estimate=cost(20),
                name="column_forward",
            )(place_row, twist_col[rows], fwd_col[chunk], *pieces, *lines)
        ]
    (lines,) = lines

    lines = lines.reshape(devices, own_rows, width)
    lines = lax.all_to_all(lines, ("row", "col"), split_axis=0, concat_axis=0, tiled=True)
    if width == 128:
        order = tuple((b % row_total) * col_total + b // row_total for b in range(N // 128))
    else:
        order = tuple(range(N // 128))
        lines = lines.reshape(row_total, col_total, own_rows, width).transpose(2, 1, 0, 3)
        lines = lines.reshape(own_rows, N // 128, 128).transpose(1, 0, 2)

    at_once = 2
    line_grain = pl.BlockSpec((N // 128, 16 * at_once, 128), lambda i: (0, i, 0))
    gain_grain = pl.BlockSpec((at_once, RES * 8, 128), lambda i: (i, 0, 0))
    lines = pl.pallas_call(
        partial(line_kernel, order, tail),
        grid=(-(-own // at_once),),
        in_specs=[line_grain, gain_grain, gain_grain] + [whole()] * 5,
        out_specs=line_grain,
        out_shape=jax.ShapeDtypeStruct((N // 128, own_rows, 128), jnp.float32),
        scratch_shapes=[pltpu.VMEM((2 * RES * 8, 2 * INNER), jnp.bfloat16)] * at_once
        + [pltpu.VMEM((RES * 8, 2 * INNER), jnp.float32)] * at_once,
        compiler_params=params(),
        name="line",
    )(lines, gain_re, gain_im, twist_line, line_fh, line_fl, line_ih, line_il)

    if width != 128:
        lines = lines.transpose(1, 0, 2).reshape(own_rows, col_total, row_total, width)
        lines = lines.transpose(2, 1, 0, 3).reshape(devices, own_rows, width)
    lines = lax.all_to_all(lines, ("row", "col"), split_axis=0, concat_axis=0, tiled=True)
    lines = lines.reshape(RES, total_rows, width)

    near, top = pl.pallas_call(
        column_inverse_kernel,
        grid=(CHUNKS + 1,),
        in_specs=[
            whole(),
            pl.BlockSpec((CHUNK, 128), lambda i: (jnp.maximum(i - 1, 0), 0)),
            pl.BlockSpec((1,) + inv_col.shape[1:], lambda i: (jnp.minimum(i, CHUNKS - 1), 0, 0)),
        ],
        out_specs=[
            pl.BlockSpec(tall, lambda i: (0, 0, 0, jnp.maximum(i - 1, 0), 0)),
            whole(),
        ],
        out_shape=[
            jax.ShapeDtypeStruct((row_total, 2, blocks, INNER, width), jnp.float32),
            jax.ShapeDtypeStruct((8, width), jnp.float32),
        ],
        scratch_shapes=[
            pltpu.VMEM((RES // many, inv_col.shape[2], many * width), jnp.bfloat16),
            pltpu.VMEM((2, RES, 2 * CHUNK, width), jnp.float32),
        ],
        compiler_params=params(),
        name="column_inverse",
    )(lines, twist_col, inv_col)

    near = near.reshape(row_total, 2, height, width)
    near = lax.all_to_all(near, "row", split_axis=0, concat_axis=0, tiled=True)
    peak = jnp.max(top)
    shift = 1
    while shift < col_total:
        partner = [(i, i ^ shift) for i in range(col_total)]
        peak = jnp.maximum(peak, lax.ppermute(peak, "col", partner))
        shift *= 2
    for item in exchange([peak] * row_total, "row")[1:]:
        peak = jnp.maximum(peak, item)
    peak = jnp.sqrt(peak)
    if width != 128:
        near = near.transpose(1, 2, 0, 3).reshape(2, height, tile_width)
        even_cell = (jnp.arange(height)[:, None] + jnp.arange(tile_width)[None, :]) % 2 == 0
        return encode(near[0], near[1], peak, even_cell)
    tile_spec = pl.BlockSpec((pack_rows, tile_width), lambda i: (i, 0))
    tile_shape = jax.ShapeDtypeStruct((height, tile_width), jnp.float32)
    return pl.pallas_call(
        encode_kernel,
        grid=(height // pack_rows,),
        in_specs=[
            whole(pltpu.SMEM),
            pl.BlockSpec((row_total, 2, pack_rows, width), lambda i: (0, 0, i, 0)),
        ],
        out_specs=[tile_spec, tile_spec],
        out_shape=[tile_shape, tile_shape],
        compiler_params=params(),
        name="encode",
    )(peak.reshape(1), near)


def solution(mesh):
    in_specs = (P("row", "col"), P("row", "col"))
    out_specs = (P("row", "col"), P("row", "col"))
    return jax.shard_map(body, mesh=mesh, in_specs=in_specs, out_specs=out_specs, check_vma=False)
```

```python
from functools import partial
import math

import jax
import jax.numpy as jnp
import ml_dtypes
import numpy as np
from jax import lax
from jax.experimental import pallas as pl
from jax.experimental.pallas import tpu as pltpu
from jax.sharding import PartitionSpec as P

N = 4096
PAD = 2 * N
wavelength = 5.2e-07
distance = 0.2
INNER = 256
SLABS = N // INNER
RES = PAD // INNER
HALF = 40
CHUNKS = 2
CHUNK = INNER // CHUNKS
STEPS = 4
STEP = INNER // STEPS


def optics(padded_side):
    pitch = 2e-06 * math.sqrt(8192.0 / padded_side)
    extent = padded_side * pitch
    ratio_sq = (wavelength / extent) ** 2
    band_limit = extent / (wavelength * math.sqrt((2.0 * distance / extent) ** 2 + 1.0))
    return (ratio_sq, band_limit)


RATIO_SQ, LIMIT = optics(PAD)
assert RES * HALF - RES // 2 + RES > LIMIT and RES * HALF + RES // 2 > LIMIT


def residue(u):
    return u if u < RES // 2 else u - RES


def split16(table):
    table = np.asarray(table, np.float64)
    high = table.astype(np.float32).astype(ml_dtypes.bfloat16)
    low = (table - high.astype(np.float64)).astype(np.float32).astype(ml_dtypes.bfloat16)
    return high, low


def row_order(groups, tail):
    rows = []
    for group in range(groups):
        size = 4 if tail and group == groups - 1 else 8
        for part in range(2):
            for s in range(size):
                rows.append((part, group * 8 + s - HALF))
    return rows


def column_tables(groups, tail):
    q = np.arange(INNER)
    rows = row_order(groups, tail)
    forward = np.zeros((len(rows), 2, INNER))
    inverse = np.zeros((2, INNER, len(rows)))
    for at, (part, k1) in enumerate(rows):
        if abs(k1) > HALF:
            continue
        angle = 2.0 * np.pi * ((k1 * q) % INNER) / INNER
        c, s = np.cos(angle), np.sin(angle)
        forward[at] = (c, s) if part == 0 else (-s, c)
        inverse[:, :, at] = (c, s) if part == 0 else (-s, c)
    forward = forward.reshape(-1, 2, CHUNKS, CHUNK // 8, 8).transpose(2, 0, 3, 1, 4)
    forward = np.concatenate(split16(forward.reshape(CHUNKS, len(rows), 2 * CHUNK)), axis=1)
    inverse = inverse.reshape(2, STEPS, STEP, -1).transpose(1, 0, 2, 3)
    high, low = split16(inverse.reshape(STEPS, 2 * STEP, len(rows)))
    inverse = np.concatenate([high, high, low], axis=2)
    inverse = np.pad(inverse, ((0, 0), (0, 0), (0, -3 * len(rows) % 16)))
    return forward, inverse


def line_tables():
    q = np.arange(INNER)
    forward = np.zeros((2 * INNER, 256))
    inverse = np.zeros((256, 2 * INNER))
    for lane in range(2 * HALF + 1):
        angle = 2.0 * np.pi * (((lane - HALF) * q) % INNER) / INNER
        c, s = np.cos(angle), np.sin(angle)
        forward[:INNER, lane], forward[INNER:, lane] = c, s
        forward[:INNER, 128 + lane], forward[INNER:, 128 + lane] = -s, c
        inverse[lane, :INNER], inverse[lane, INNER:] = c, s
        inverse[128 + lane, :INNER], inverse[128 + lane, INNER:] = -s, c
    return split16(forward) + split16(inverse)


def twist_table():
    q = np.arange(INNER) + N // 2
    k0 = np.arange(RES // 2 + 1)
    angle = 2.0 * np.pi * ((k0[:, None] * q[None, :]) % PAD) / PAD
    return np.cos(angle).astype(np.float32), (-np.sin(angle)).astype(np.float32)


def turn(value, num, den):
    re, im = value
    num = num % den
    eighth = 8 * num
    if num == 0:
        return re, im
    if 2 * num == den:
        return -re, -im
    if 4 * num == den:
        return -im, re
    if 4 * num == 3 * den:
        return im, -re
    if eighth % den == 0:
        root = np.float32(math.sqrt(0.5))
        kind = eighth // den
        if kind == 1:
            return (re - im) * root, (re + im) * root
        if kind == 3:
            return (re + im) * (-root), (re - im) * root
        if kind == 5:
            return (im - re) * root, (re + im) * (-root)
        return (re + im) * root, (im - re) * root
    c = np.float32(math.cos(2.0 * math.pi * num / den))
    s = np.float32(math.sin(2.0 * math.pi * num / den))
    return re * c - im * s, re * s + im * c


def small_dft(get, ids, sign):
    count = len(ids)
    if count == 1:
        return [get(ids[0])]
    even = small_dft(get, ids[0::2], sign)
    odd = small_dft(get, ids[1::2], sign)
    half = count // 2
    first, second = [], []
    for j in range(half):
        re, im = even[j]
        t_re, t_im = turn(odd[j], sign * j, count)
        first.append((re + t_re, im + t_im))
        second.append((re - t_re, im - t_im))
    return first + second


def forward_slabs(get, put):
    ids = list(range(SLABS))
    for v, value in enumerate(small_dft(get, ids, -1)):
        put(2 * v, value)
    for v, value in enumerate(small_dft(lambda n: turn(get(n), -n, RES), ids, -1)):
        put(2 * v + 1, value)


def inverse_slabs(get, put):
    even = small_dft(get, list(range(0, RES, 2)), 1)
    odd = small_dft(get, list(range(1, RES, 2)), 1)
    for n in range(SLABS):
        t_re, t_im = turn(odd[n], n, RES)
        put(n, (even[n][0] + t_re, even[n][1] + t_im))


def twisted(value, u, sign, read):
    re, im = value
    k0 = residue(u)
    if k0 == 0:
        return value
    c, s = read(abs(k0))
    if (k0 < 0) == (sign > 0):
        return re * c + im * s, im * c - re * s
    return re * c - im * s, re * s + im * c


def high_low(value):
    high = value.astype(jnp.bfloat16)
    low = (value - high.astype(jnp.float32)).astype(jnp.bfloat16)
    return high, low


def dot16(left, right):
    return jnp.dot(left, right, preferred_element_type=jnp.float32)


def three_left(stacked, count, high, low):
    both = dot16(stacked[...], high)
    return both[:count] + both[count:] + dot16(stacked[:count], low)


def three_right(stacked, count, high, low):
    both = dot16(stacked, high)
    return both[:count] + both[count:] + dot16(stacked[:count], low)


def column_twist(twist, q0):
    def read(k):
        rows = pl.ds(q0, 8)
        return twist[rows, k : k + 1], twist[rows, 64 + k : 65 + k]

    return read


def column_forward_kernel(count, place, twist, matrix, *refs):
    pieces, refs = refs[:count], refs[count:]
    before, (out, total, high, low, sems) = refs[:-5], refs[-5:]
    width = pieces[0].shape[-1]
    per_source = pieces[0].shape[1]
    many = high.shape[-1] // width
    products = RES // many
    rows_out = out.shape[1]

    def copy_in(p):
        part = pl.ds(p * many, many)
        return pltpu.make_async_copy(before[0].at[part], total.at[part], sems.at[p])

    def copy_out(p):
        part = pl.ds(p * many, many)
        return pltpu.make_async_copy(total.at[part], out.at[part], sems.at[products + p])

    if before:
        for p in range(products):
            copy_in(p).start()

    for here in range(count):

        @pl.when(place[0] == here)
        def _():
            @pl.loop(0, CHUNK // 8)
            def _(t):
                q0 = pl.multiple_of(t * 8, 8)

                def get(n):
                    source, block = divmod(n, per_source)
                    piece = pieces[source ^ here]
                    rows = pl.ds(q0, 8)
                    return piece[0, block, rows, :], piece[1, block, rows, :]

                def put(u, value):
                    item = jnp.concatenate(twisted(value, u, 1, column_twist(twist, q0)), axis=0)
                    rows = pl.ds(pl.multiple_of(t * 16, 16), 16)
                    at = (u // many, rows, pl.ds((u % many) * width, width))
                    high[at], low[at] = high_low(item)

                forward_slabs(get, put)

    @pl.loop(0, products)
    def _(p):
        done = three_left(matrix, rows_out, high[p], low[p])
        if before:
            copy_in(p).wait()
        for part in range(many):
            item = done[:, part * width : (part + 1) * width]
            at = p * many + part
            total[at] = total[at] + item if before else item
        copy_out(p).start()

    for p in range(products):
        copy_out(p).wait()


def interleave(tiles, products, butterflies, product):
    steps = min(tiles, products)

    @pl.loop(0, steps)
    def _(t):
        if product is not None:
            for part in range(products // steps):
                product(t * (products // steps) + part)
        if butterflies is not None:
            for part in range(tiles // steps):
                butterflies(t * (tiles // steps) + part)


def column_inverse_kernel(source, twist, matrix, out, top, lines, deep, back, sems):
    width = lines.shape[-1]
    rows_in = lines.shape[1]
    per_dest = out.shape[2]
    many = deep.shape[-1] // width
    now = pl.program_id(0)

    def copy_in(p):
        part = pl.ds(p * many, many)
        return pltpu.make_async_copy(source.at[part], lines.at[part], sems.at[p])

    def product(p):
        done = dot16(matrix[0], deep[p])
        slot = now % 2
        for part in range(many):
            back[slot, p * many + part] = done[:, part * width : (part + 1) * width]

    def prepare(p):
        copy_in(p).wait()
        blocks = [lines[p * many + part] for part in range(many)]
        joined = jnp.concatenate(blocks, axis=1) if many > 1 else blocks[0]
        high = joined.astype(jnp.bfloat16).astype(jnp.float32)
        parts = [high, joined - high, high]
        if deep.shape[1] > 3 * rows_in:
            parts.append(jnp.zeros((deep.shape[1] - 3 * rows_in, many * width), jnp.float32))
        deep[p] = jnp.concatenate(parts, axis=0).astype(jnp.bfloat16)
        product(p)

    def butterflies(t):
        q0 = pl.multiple_of(t * 8, 8)
        slot = (now + 1) % 2
        largest = []

        def get(u):
            re = back[slot, u, pl.ds(q0, 8), :]
            im = back[slot, u, pl.ds(STEP + q0, 8), :]
            return twisted((re, im), u, -1, column_twist(twist, q0))

        def put(n, value):
            dest, block = divmod(n, per_dest)
            rows = pl.ds(q0, 8)
            out[dest, 0, block, rows, :], out[dest, 1, block, rows, :] = value
            largest.append(value[0] * value[0] + value[1] * value[1])

        inverse_slabs(get, put)
        while len(largest) > 1:
            largest = [jnp.maximum(a, b) for a, b in zip(largest[0::2], largest[1::2])]
        top[...] = jnp.maximum(top[...], largest[0])

    @pl.when(now == 0)
    def _():
        for p in range(RES // many):
            copy_in(p).start()
        top[...] = jnp.zeros_like(top)
        pl.loop(0, RES // many)(prepare)

    for step in range(1, STEPS + 1):

        @pl.when(now == step)
        def _():
            interleave(
                STEP // 8, RES // many, butterflies, product if step < STEPS else None
            )


def line_kernel(
    order, own, tail, lines, gain_re, gain_im, twist, fwd_high, fwd_low, inv_high, inv_low, out, *scratch
):
    half = RES * 8
    at_end = pl.program_id(0) == pl.num_programs(0) - 1

    def line_twist(side):
        def read(k):
            lanes = pl.ds(side * 128, 128)
            return twist[0, k, :, lanes], twist[1, k, :, lanes]

        return read

    def forward(group, stacked):
        for side in range(2):
            waiting = {}

            def get(m):
                block = order[2 * m + side]
                at = group * 16
                return lines[block, at : at + 8, :], lines[block, at + 8 : at + 16, :]

            def put(u, value):
                waiting[u] = twisted(value, u, 1, line_twist(side))
                v = (u + RES // 2) % RES
                if v in waiting:
                    first = min(u, v)
                    rows = pl.ds(first * 16, 16)
                    rows_low = pl.ds(half + first * 16, 16)
                    for part in range(2):
                        item = jnp.concatenate(
                            [waiting[first][part], waiting[first + RES // 2][part]], axis=0
                        )
                        at = pl.ds(part * INNER + side * 128, 128)
                        stacked[rows, at], stacked[rows_low, at] = high_low(item)

            forward_slabs(get, put)

    def middle(group, stacked, back):
        spec = three_right(stacked[...], half, fwd_high[...], fwd_low[...])
        spec_re, spec_im = spec[:, :128], spec[:, 128:]
        g_re, g_im = gain_re[group], gain_im[group]
        mixed = jnp.concatenate(
            [spec_re * g_re - spec_im * g_im, spec_re * g_im + spec_im * g_re], axis=1
        )
        mixed = jnp.concatenate(high_low(mixed), axis=0)
        back[...] = three_right(mixed, half, inv_high[...], inv_low[...])

    def inverse(group, back):
        for side in range(2):

            def get(u):
                rows = pl.ds((u % (RES // 2)) * 16 + (u // (RES // 2)) * 8, 8)
                re = back[rows, pl.ds(side * 128, 128)]
                im = back[rows, pl.ds(INNER + side * 128, 128)]
                return twisted((re, im), u, -1, line_twist(side))

            def put(m, value):
                block = order[2 * m + side]
                at = group * 16
                out[block, at : at + 8, :], out[block, at + 8 : at + 16, :] = value

            inverse_slabs(get, put)

    if tail:

        @pl.when(at_end)
        def _():
            for block in range(N // 128):
                lines[block, 8:12, :] = lines[block, 4:8, :]

    groups = len(scratch) // 2

    def run(count):
        for group in range(count):
            forward(group, scratch[group])
        for group in range(count):
            middle(group, scratch[group], scratch[groups + group])
        for group in range(count):
            inverse(group, scratch[groups + group])

    rest = own % groups
    if rest:
        pl.when(jnp.logical_not(at_end))(lambda: run(groups))
        pl.when(at_end)(lambda: run(rest))
    else:
        run(groups)

    if tail:

        @pl.when(at_end)
        def _():
            for block in range(N // 128):
                out[block, 4:8, :] = out[block, 8:12, :]


def gain_kernel(place, gain_re, gain_im):
    k0 = place[0]
    group = place[1] + pl.program_id(0)
    down = lax.broadcasted_iota(jnp.int32, (8, 128), 0)
    across = lax.broadcasted_iota(jnp.int32, (8, 128), 1)
    row = (k0 + RES * (group * 8 + down - HALF)).astype(jnp.float32)
    row_sq = row * row
    row_in = jnp.abs(row) < LIMIT
    for u in range(RES):
        col = (residue(u) + RES * (across - HALF)).astype(jnp.float32)
        square = row_sq + col * col
        scaled = RATIO_SQ * square
        phase = -2.0 * math.pi * distance / wavelength * scaled / (1.0 + jnp.sqrt(1.0 - scaled))
        total = jnp.where(
            row_in & (jnp.abs(col) < LIMIT), jnp.exp(square * (-2.0 / (LIMIT * LIMIT))), 0.0
        )
        quarter = jnp.floor(phase * (2.0 / math.pi) + 0.5)
        left = phase - quarter * 1.5703125
        left = left - quarter * 4.837512969970703125e-4
        left = left - quarter * 7.549789954891882e-8
        sq = left * left
        sine = ((-1.9515295891e-4 * sq + 8.3321608736e-3) * sq - 1.6666654611e-1) * sq * left + left
        cosine = (
            (2.443315711809948e-5 * sq - 1.388731625493765e-3) * sq + 4.166664568298827e-2
        ) * sq * sq - 0.5 * sq + 1.0
        which = quarter.astype(jnp.int32) & 3
        swap = (which & 1) == 1
        cos_part = jnp.where(swap, sine, cosine)
        sin_part = jnp.where(swap, cosine, sine)
        cos_part = jnp.where((which == 1) | (which == 2), -cos_part, cos_part)
        sin_part = jnp.where(which >= 2, -sin_part, sin_part)
        at = (u % (RES // 2)) * 16 + (u // (RES // 2)) * 8
        gain_re[0, at : at + 8, :] = total * cos_part
        gain_im[0, at : at + 8, :] = total * sin_part


def inverse_root(value):
    root = lax.rsqrt(value)
    return root * (1.5 - 0.5 * (value * root) * root)


def encode(near_real, near_imag, peak_sq, even_cell):
    square = near_real * near_real + near_imag * near_imag
    root = inverse_root(jnp.maximum(square, 1.2e-38))
    top = inverse_root(peak_sq)
    amp_level = (square * root) * (0.8 * top)
    unit = jnp.minimum(root, 20.0 * top)
    rest = 1.0 - amp_level * amp_level
    lift_part = rest * inverse_root(rest)
    level = unit * amp_level
    lift = jnp.where(even_cell, unit * lift_part, -(unit * lift_part))
    return (near_real * level + near_imag * lift, near_imag * level - near_real * lift)


def encode_kernel(count, *refs):
    tops, (near, slm_real, slm_imag) = refs[:count], refs[count:]
    height, width = slm_real.shape[0], near.shape[-1]
    peak_sq = tops[0][0]
    for top in tops[1:]:
        peak_sq = jnp.maximum(peak_sq, top[0])
    peak_sq = jnp.full((1, width), peak_sq, jnp.float32)
    rows = pl.ds(pl.multiple_of(pl.program_id(0) * height, height), height)
    cell = lax.broadcasted_iota(jnp.int32, (height, width), 0)
    cell = cell + lax.broadcasted_iota(jnp.int32, (height, width), 1)
    for r in range(near.shape[0]):
        lanes = pl.ds(r * width, width)
        slm_real[:, lanes], slm_imag[:, lanes] = encode(
            near[r, 0, rows, :], near[r, 1, rows, :], peak_sq, (cell & 1) == 0
        )


def pack_kernel(chunk, place, field_real, field_imag, *refs):
    pieces, sems = refs[:-1], refs[-1]
    width = pieces[0].shape[-1]
    rows = pl.ds(chunk * CHUNK, CHUNK)
    copies = []
    for j in list(range(1, len(pieces))) + [0]:
        lanes = pl.ds(pl.multiple_of((place[0] ^ j) * width, width), width)
        for part, field in enumerate((field_real, field_imag)):
            copies.append(
                pltpu.make_async_copy(
                    field.at[:, rows, lanes], pieces[j].at[part], sems.at[2 * j + part]
                )
            )
    for copy in copies:
        copy.start()
    for copy in copies:
        copy.wait()


def exchange(pieces, axis):
    total = len(pieces)
    return [pieces[0]] + [
        lax.ppermute(pieces[j], axis, [(i, i ^ j) for i in range(total)]) for j in range(1, total)
    ]


def params(mebibytes):
    return pltpu.CompilerParams(vmem_limit_bytes=mebibytes << 20)


def cost(megabytes):
    return pl.CostEstimate(flops=0, bytes_accessed=megabytes << 20, transcendentals=0)


def whole(memory=pltpu.VMEM):
    return pl.BlockSpec(memory_space=memory)


def body(field_real, field_imag):
    row_total, col_total = lax.axis_size("row"), lax.axis_size("col")
    devices = row_total * col_total
    device = lax.axis_index("row") * col_total + lax.axis_index("col")
    height, tile_width = field_real.shape
    width = tile_width // row_total
    parts = max(1, devices // RES)
    groups = -(-(2 * HALF + 1) // (8 * parts)) * parts
    own = groups // parts
    tail = parts == 1
    total_rows = groups * 16 - (8 if tail else 0)
    own_rows = total_rows // parts
    many = 4 if width == 128 else 1

    fwd_col, inv_col = column_tables(groups, tail)
    line_fh, line_fl, line_ih, line_il = line_tables()
    twist = np.stack(twist_table())
    twist_line = np.ascontiguousarray(np.broadcast_to(twist[:, :, None], twist.shape[:2] + (8, INNER)))
    twist_col = np.pad(twist, ((0, 0), (0, 64 - twist.shape[1]), (0, 0)))
    twist_col = twist_col.reshape(128, INNER).T.copy()

    u = device // parts
    k0 = jnp.where(u >= RES // 2, u - RES, u)
    place = jnp.stack([k0, (device % parts) * own]).astype(jnp.int32)
    gain_shape = jax.ShapeDtypeStruct((own, RES * 8, 128), jnp.float32)
    gain_spec = pl.BlockSpec((1, RES * 8, 128), lambda g: (g, 0, 0))
    gain_re, gain_im = pl.pallas_call(
        gain_kernel,
        grid=(own,),
        in_specs=[whole(pltpu.SMEM)],
        out_specs=[gain_spec, gain_spec],
        out_shape=[gain_shape, gain_shape],
        compiler_params=params(8),
        name="gain",
    )(place)

    place_row = lax.axis_index("row").reshape(1).astype(jnp.int32)
    blocks = height // INNER
    piece = (2, blocks, CHUNK, width)
    piece_shape = jax.ShapeDtypeStruct(piece, jnp.float32)
    anywhere = whole(pl.ANY)
    if width != 128:
        packed = jnp.stack([field_real, field_imag])
        packed = packed.reshape(2, blocks, CHUNKS, CHUNK, row_total, width).transpose(2, 4, 0, 1, 3, 5)
        packed = jnp.take(packed, jnp.arange(row_total) ^ place_row[0], axis=1)
    lines = []
    for chunk in range(CHUNKS):
        if width == 128:
            pieces = pl.pallas_call(
                partial(pack_kernel, chunk),
                in_specs=[whole(pltpu.SMEM), anywhere, anywhere],
                out_specs=[anywhere] * row_total,
                out_shape=[piece_shape] * row_total,
                scratch_shapes=[pltpu.SemaphoreType.DMA((2 * row_total,))],
                compiler_params=params(4),
                cost_estimate=cost(4),
                name="pack",
            )(
                place_row,
                field_real.reshape(blocks, INNER, tile_width),
                field_imag.reshape(blocks, INNER, tile_width),
            )
        else:
            pieces = [packed[chunk, j] for j in range(row_total)]
        pieces = exchange(pieces, "row")
        rows = slice(chunk * CHUNK, (chunk + 1) * CHUNK)
        slab = pltpu.VMEM((RES // many, 2 * CHUNK, many * width), jnp.bfloat16)
        lines = [
            pl.pallas_call(
                partial(column_forward_kernel, row_total),
                in_specs=[whole(pltpu.SMEM)] + [whole()] * (2 + row_total) + [anywhere] * len(lines),
                out_specs=anywhere,
                out_shape=jax.ShapeDtypeStruct((RES, total_rows, width), jnp.float32),
                scratch_shapes=[
                    pltpu.VMEM((RES, total_rows, width), jnp.float32),
                    slab,
                    slab,
                    pltpu.SemaphoreType.DMA((2 * RES // many,)),
                ],
                compiler_params=params(20),
                cost_estimate=cost(20),
                name="column_forward",
            )(place_row, twist_col[rows], fwd_col[chunk], *pieces, *lines)
        ]
    (lines,) = lines

    lines = lines.reshape(devices, own_rows, width)
    lines = lax.all_to_all(lines, ("row", "col"), split_axis=0, concat_axis=0, tiled=True)
    if width == 128:
        order = tuple((b % row_total) * col_total + b // row_total for b in range(N // 128))
    else:
        order = tuple(range(N // 128))
        lines = lines.reshape(row_total, col_total, own_rows, width).transpose(2, 1, 0, 3)
        lines = lines.reshape(own_rows, N // 128, 128).transpose(1, 0, 2)

    at_once = 2
    line_grain = pl.BlockSpec((N // 128, 16 * at_once, 128), lambda i: (0, i, 0))
    gain_grain = pl.BlockSpec((at_once, RES * 8, 128), lambda i: (i, 0, 0))
    lines = pl.pallas_call(
        partial(line_kernel, order, own, tail),
        grid=(-(-own // at_once),),
        in_specs=[line_grain, gain_grain, gain_grain] + [whole()] * 5,
        out_specs=line_grain,
        out_shape=jax.ShapeDtypeStruct((N // 128, own_rows, 128), jnp.float32),
        scratch_shapes=[pltpu.VMEM((2 * RES * 8, 2 * INNER), jnp.bfloat16)] * at_once
        + [pltpu.VMEM((RES * 8, 2 * INNER), jnp.float32)] * at_once,
        compiler_params=params(20),
        name="line",
    )(lines, gain_re, gain_im, twist_line, line_fh, line_fl, line_ih, line_il)

    if width != 128:
        lines = lines.transpose(1, 0, 2).reshape(own_rows, col_total, row_total, width)
        lines = lines.transpose(2, 1, 0, 3).reshape(devices, own_rows, width)
    lines = lax.all_to_all(lines, ("row", "col"), split_axis=0, concat_axis=0, tiled=True)
    lines = lines.reshape(RES, total_rows, width)

    tall = pl.BlockSpec(
        (row_total, 2, blocks, STEP, width), lambda i: (0, 0, 0, jnp.maximum(i - 1, 0), 0)
    )
    near, top = pl.pallas_call(
        column_inverse_kernel,
        grid=(STEPS + 1,),
        in_specs=[
            anywhere,
            pl.BlockSpec((STEP, 128), lambda i: (jnp.maximum(i - 1, 0), 0)),
            pl.BlockSpec((1,) + inv_col.shape[1:], lambda i: (jnp.minimum(i, STEPS - 1), 0, 0)),
        ],
        out_specs=[tall, whole()],
        out_shape=[
            jax.ShapeDtypeStruct((row_total, 2, blocks, INNER, width), jnp.float32),
            jax.ShapeDtypeStruct((8, width), jnp.float32),
        ],
        scratch_shapes=[
            pltpu.VMEM((RES, total_rows, width), jnp.float32),
            pltpu.VMEM((RES // many, inv_col.shape[2], many * width), jnp.bfloat16),
            pltpu.VMEM((2, RES, 2 * STEP, width), jnp.float32),
            pltpu.SemaphoreType.DMA((RES // many,)),
        ],
        compiler_params=params(24),
        name="column_inverse",
    )(lines, twist_col, inv_col)

    near = near.reshape(row_total, 2, height, width)
    near = lax.all_to_all(near, "row", split_axis=0, concat_axis=0, tiled=True)
    peak = jnp.max(top)
    shift = 1
    while shift < col_total:
        partner = [(i, i ^ shift) for i in range(col_total)]
        peak = jnp.maximum(peak, lax.ppermute(peak, "col", partner))
        shift *= 2
    tops = exchange([peak] * row_total, "row")
    if width != 128:
        near = near.transpose(1, 2, 0, 3).reshape(2, height, tile_width)
        even_cell = (jnp.arange(height)[:, None] + jnp.arange(tile_width)[None, :]) % 2 == 0
        return encode(near[0], near[1], jnp.max(jnp.stack(tops)), even_cell)
    tile_rows = min(height, 128)
    tile_spec = pl.BlockSpec((tile_rows, tile_width), lambda i: (i, 0))
    tile_shape = jax.ShapeDtypeStruct((height, tile_width), jnp.float32)
    return pl.pallas_call(
        partial(encode_kernel, row_total),
        grid=(height // tile_rows,),
        in_specs=[whole(pltpu.SMEM)] * row_total + [whole()],
        out_specs=[tile_spec, tile_spec],
        out_shape=[tile_shape, tile_shape],
        compiler_params=params(12),
        name="encode",
    )(*[top.reshape(1) for top in tops], near)


def solution(mesh):
    in_specs = (P("row", "col"), P("row", "col"))
    out_specs = (P("row", "col"), P("row", "col"))
    return jax.shard_map(body, mesh=mesh, in_specs=in_specs, out_specs=out_specs, check_vma=False)
```

```python
from functools import partial
import math

import jax
import jax.numpy as jnp
import ml_dtypes
import numpy as np
from jax import lax
from jax.experimental import pallas as pl
from jax.experimental.pallas import tpu as pltpu
from jax.sharding import PartitionSpec as P

N = 4096
PAD = 2 * N
wavelength = 5.2e-07
distance = 0.2
INNER = 256
SLABS = N // INNER
RES = PAD // INNER
HALF = 40
CHUNKS = 2
CHUNK = INNER // CHUNKS
STEPS = 2
STEP = INNER // STEPS


def optics(padded_side):
    pitch = 2e-06 * math.sqrt(8192.0 / padded_side)
    extent = padded_side * pitch
    ratio_sq = (wavelength / extent) ** 2
    band_limit = extent / (wavelength * math.sqrt((2.0 * distance / extent) ** 2 + 1.0))
    return (ratio_sq, band_limit)


RATIO_SQ, LIMIT = optics(PAD)
assert RES * HALF - RES // 2 + RES > LIMIT and RES * HALF + RES // 2 > LIMIT


def residue(u):
    return u if u < RES // 2 else u - RES


def split16(table):
    table = np.asarray(table, np.float64)
    high = table.astype(np.float32).astype(ml_dtypes.bfloat16)
    low = (table - high.astype(np.float64)).astype(np.float32).astype(ml_dtypes.bfloat16)
    return high, low


def row_order(groups, tail):
    rows = []
    for group in range(groups):
        size = 4 if tail and group == groups - 1 else 8
        for part in range(2):
            for s in range(size):
                rows.append((part, group * 8 + s - HALF))
    return rows


def column_tables(groups, tail):
    q = np.arange(INNER)
    rows = row_order(groups, tail)
    forward = np.zeros((len(rows), 2, INNER))
    inverse = np.zeros((2, INNER, len(rows)))
    for at, (part, k1) in enumerate(rows):
        if abs(k1) > HALF:
            continue
        angle = 2.0 * np.pi * ((k1 * q) % INNER) / INNER
        c, s = np.cos(angle), np.sin(angle)
        forward[at] = (c, s) if part == 0 else (-s, c)
        inverse[:, :, at] = (c, s) if part == 0 else (-s, c)
    forward = forward.reshape(-1, 2, CHUNKS, CHUNK // 8, 8).transpose(2, 0, 3, 1, 4)
    forward = np.concatenate(split16(forward.reshape(CHUNKS, len(rows), 2 * CHUNK)), axis=1)
    inverse = inverse.reshape(2, STEPS, STEP, -1).transpose(1, 0, 2, 3)
    high, low = split16(inverse.reshape(STEPS, 2 * STEP, len(rows)))
    inverse = np.concatenate([high, high, low], axis=2)
    inverse = np.pad(inverse, ((0, 0), (0, 0), (0, -3 * len(rows) % 16)))
    return forward, inverse


def line_tables():
    q = np.arange(INNER)
    forward = np.zeros((2 * INNER, 256))
    inverse = np.zeros((256, 2 * INNER))
    for lane in range(2 * HALF + 1):
        angle = 2.0 * np.pi * (((lane - HALF) * q) % INNER) / INNER
        c, s = np.cos(angle), np.sin(angle)
        forward[:INNER, lane], forward[INNER:, lane] = c, s
        forward[:INNER, 128 + lane], forward[INNER:, 128 + lane] = -s, c
        inverse[lane, :INNER], inverse[lane, INNER:] = c, s
        inverse[128 + lane, :INNER], inverse[128 + lane, INNER:] = -s, c
    return split16(forward) + split16(inverse)


def twist_table():
    q = np.arange(INNER) + N // 2
    k0 = np.arange(RES // 2 + 1)
    angle = 2.0 * np.pi * ((k0[:, None] * q[None, :]) % PAD) / PAD
    return np.cos(angle).astype(np.float32), (-np.sin(angle)).astype(np.float32)


def turn(value, num, den):
    re, im = value
    num = num % den
    eighth = 8 * num
    if num == 0:
        return re, im
    if 2 * num == den:
        return -re, -im
    if 4 * num == den:
        return -im, re
    if 4 * num == 3 * den:
        return im, -re
    if eighth % den == 0:
        root = np.float32(math.sqrt(0.5))
        kind = eighth // den
        if kind == 1:
            return (re - im) * root, (re + im) * root
        if kind == 3:
            return (re + im) * (-root), (re - im) * root
        if kind == 5:
            return (im - re) * root, (re + im) * (-root)
        return (re + im) * root, (im - re) * root
    c = np.float32(math.cos(2.0 * math.pi * num / den))
    s = np.float32(math.sin(2.0 * math.pi * num / den))
    return re * c - im * s, re * s + im * c


def small_dft(get, ids, sign):
    count = len(ids)
    if count == 1:
        return [get(ids[0])]
    even = small_dft(get, ids[0::2], sign)
    odd = small_dft(get, ids[1::2], sign)
    half = count // 2
    first, second = [], []
    for j in range(half):
        re, im = even[j]
        t_re, t_im = turn(odd[j], sign * j, count)
        first.append((re + t_re, im + t_im))
        second.append((re - t_re, im - t_im))
    return first + second


def forward_slabs(get, put):
    ids = list(range(SLABS))
    for v, value in enumerate(small_dft(get, ids, -1)):
        put(2 * v, value)
    for v, value in enumerate(small_dft(lambda n: turn(get(n), -n, RES), ids, -1)):
        put(2 * v + 1, value)


def inverse_slabs(get, put):
    even = small_dft(get, list(range(0, RES, 2)), 1)
    odd = small_dft(get, list(range(1, RES, 2)), 1)
    for n in range(SLABS):
        t_re, t_im = turn(odd[n], n, RES)
        put(n, (even[n][0] + t_re, even[n][1] + t_im))


def twisted(value, u, sign, read):
    re, im = value
    k0 = residue(u)
    if k0 == 0:
        return value
    c, s = read(abs(k0))
    if (k0 < 0) == (sign > 0):
        return re * c + im * s, im * c - re * s
    return re * c - im * s, re * s + im * c


def high_low(value):
    high = value.astype(jnp.bfloat16)
    low = (value - high.astype(jnp.float32)).astype(jnp.bfloat16)
    return high, low


def dot16(left, right):
    return jnp.dot(left, right, preferred_element_type=jnp.float32)


def three_left(stacked, count, high, low):
    both = dot16(stacked[...], high)
    return both[:count] + both[count:] + dot16(stacked[:count], low)


def three_right(stacked, count, high, low):
    both = dot16(stacked, high)
    return both[:count] + both[count:] + dot16(stacked[:count], low)


def column_twist(twist, q0):
    def read(k):
        rows = pl.ds(q0, 8)
        return twist[rows, k : k + 1], twist[rows, 64 + k : 65 + k]

    return read


def column_forward_kernel(count, place, twist, matrix, *refs):
    pieces, refs = refs[:count], refs[count:]
    before, (out, total, high, low, sems) = refs[:-5], refs[-5:]
    width = pieces[0].shape[-1]
    per_source = pieces[0].shape[1]
    many = high.shape[-1] // width
    products = RES // many
    rows_out = out.shape[1]

    def copy_in(p):
        part = pl.ds(p * many, many)
        return pltpu.make_async_copy(before[0].at[part], total.at[part], sems.at[p])

    def copy_out(p):
        part = pl.ds(p * many, many)
        return pltpu.make_async_copy(total.at[part], out.at[part], sems.at[products + p])

    if before:
        for p in range(products):
            copy_in(p).start()

    for here in range(count):

        @pl.when(place[0] == here)
        def _():
            @pl.loop(0, CHUNK // 8)
            def _(t):
                q0 = pl.multiple_of(t * 8, 8)

                def get(n):
                    source, block = divmod(n, per_source)
                    piece = pieces[source ^ here]
                    rows = pl.ds(q0, 8)
                    return piece[0, block, rows, :], piece[1, block, rows, :]

                def put(u, value):
                    item = jnp.concatenate(twisted(value, u, 1, column_twist(twist, q0)), axis=0)
                    rows = pl.ds(pl.multiple_of(t * 16, 16), 16)
                    at = (u // many, rows, pl.ds((u % many) * width, width))
                    high[at], low[at] = high_low(item)

                forward_slabs(get, put)

    @pl.loop(0, products)
    def _(p):
        done = three_left(matrix, rows_out, high[p], low[p])
        if before:
            copy_in(p).wait()
        for part in range(many):
            item = done[:, part * width : (part + 1) * width]
            at = p * many + part
            total[at] = total[at] + item if before else item
        copy_out(p).start()

    for p in range(products):
        copy_out(p).wait()


def column_inverse_kernel(source, twist, matrix, out, top, lines, deep, back, sems):
    width = lines.shape[-1]
    rows_in = lines.shape[1]
    per_dest = out.shape[2]
    many = deep.shape[-1] // width
    now = pl.program_id(0)

    def copy_in(p):
        part = pl.ds(p * many, many)
        return pltpu.make_async_copy(source.at[part], lines.at[part], sems.at[p])

    def product(p, slot):
        done = dot16(matrix[0], deep[p])
        for part in range(many):
            back[slot, p * many + part] = done[:, part * width : (part + 1) * width]

    def prepare(p):
        copy_in(p).wait()
        blocks = [lines[p * many + part] for part in range(many)]
        joined = jnp.concatenate(blocks, axis=1) if many > 1 else blocks[0]
        high = joined.astype(jnp.bfloat16).astype(jnp.float32)
        parts = [high, joined - high, high]
        if deep.shape[1] > 3 * rows_in:
            parts.append(jnp.zeros((deep.shape[1] - 3 * rows_in, many * width), jnp.float32))
        deep[p] = jnp.concatenate(parts, axis=0).astype(jnp.bfloat16)
        product(p, 0)

    def butterflies(t, slot):
        q0 = pl.multiple_of(t * 8, 8)
        largest = []

        def get(u):
            re = back[slot, u, pl.ds(q0, 8), :]
            im = back[slot, u, pl.ds(STEP + q0, 8), :]
            return twisted((re, im), u, -1, column_twist(twist, q0))

        def put(n, value):
            dest, block = divmod(n, per_dest)
            rows = pl.ds(q0, 8)
            out[dest, 0, block, rows, :], out[dest, 1, block, rows, :] = value
            largest.append(value[0] * value[0] + value[1] * value[1])

        inverse_slabs(get, put)
        while len(largest) > 1:
            largest = [jnp.maximum(a, b) for a, b in zip(largest[0::2], largest[1::2])]
        top[...] = jnp.maximum(top[...], largest[0])

    @pl.when(now == 0)
    def _():
        for p in range(RES // many):
            copy_in(p).start()
        top[...] = jnp.zeros_like(top)
        pl.loop(0, RES // many)(prepare)

    for step in range(1, STEPS + 1):

        @pl.when(now == step)
        def _():
            tiles, products = STEP // 8, RES // many
            steps = min(tiles, products)

            @pl.loop(0, steps)
            def _(t):
                for part in range(tiles // steps):
                    butterflies(t * (tiles // steps) + part, (step - 1) % 2)
                if step < STEPS:
                    for part in range(products // steps):
                        product(t * (products // steps) + part, step % 2)


def line_kernel(
    order, own, tail, lines, gain_re, gain_im, twist, fwd_high, fwd_low, inv_high, inv_low, out, *scratch
):
    half = RES * 8
    at_end = pl.program_id(0) == pl.num_programs(0) - 1

    def line_twist(side):
        def read(k):
            lanes = pl.ds(side * 128, 128)
            return twist[0, k, :, lanes], twist[1, k, :, lanes]

        return read

    def forward(group, stacked, sides=(0, 1)):
        for side in sides:
            waiting = {}

            def get(m):
                block = order[2 * m + side]
                at = group * 16
                return lines[block, at : at + 8, :], lines[block, at + 8 : at + 16, :]

            def put(u, value):
                waiting[u] = twisted(value, u, 1, line_twist(side))
                v = (u + RES // 2) % RES
                if v in waiting:
                    first = min(u, v)
                    rows = pl.ds(first * 16, 16)
                    rows_low = pl.ds(half + first * 16, 16)
                    for part in range(2):
                        item = jnp.concatenate(
                            [waiting[first][part], waiting[first + RES // 2][part]], axis=0
                        )
                        at = pl.ds(part * INNER + side * 128, 128)
                        stacked[rows, at], stacked[rows_low, at] = high_low(item)

            forward_slabs(get, put)

    def filtered(group, stacked):
        spec = three_right(stacked[...], half, fwd_high[...], fwd_low[...])
        spec_re, spec_im = spec[:, :128], spec[:, 128:]
        g_re, g_im = gain_re[group], gain_im[group]
        mixed = jnp.concatenate(
            [spec_re * g_re - spec_im * g_im, spec_re * g_im + spec_im * g_re], axis=1
        )
        return jnp.concatenate(high_low(mixed), axis=0)

    def unfold(mixed, back):
        back[...] = three_right(mixed, half, inv_high[...], inv_low[...])

    def inverse(group, back, sides=(0, 1)):
        for side in sides:

            def get(u):
                rows = pl.ds((u % (RES // 2)) * 16 + (u // (RES // 2)) * 8, 8)
                re = back[rows, pl.ds(side * 128, 128)]
                im = back[rows, pl.ds(INNER + side * 128, 128)]
                return twisted((re, im), u, -1, line_twist(side))

            def put(m, value):
                block = order[2 * m + side]
                at = group * 16
                out[block, at : at + 8, :], out[block, at + 8 : at + 16, :] = value

            inverse_slabs(get, put)

    if tail:

        @pl.when(at_end)
        def _():
            for block in range(N // 128):
                lines[block, 8:12, :] = lines[block, 4:8, :]

    groups = len(scratch) // 2

    stacked, back = scratch[:groups], scratch[groups:]

    def run(count):
        forward(0, stacked[0])
        for group in range(count):
            mixed = filtered(group, stacked[group])
            if group + 1 < count:
                forward(group + 1, stacked[group + 1], (0,))
            if group > 0:
                inverse(group - 1, back[group - 1], (0,))
            unfold(mixed, back[group])
            if group + 1 < count:
                forward(group + 1, stacked[group + 1], (1,))
            if group > 0:
                inverse(group - 1, back[group - 1], (1,))
        inverse(count - 1, back[count - 1])

    rest = own % groups
    if rest:
        pl.when(jnp.logical_not(at_end))(lambda: run(groups))
        pl.when(at_end)(lambda: run(rest))
    else:
        run(groups)

    if tail:

        @pl.when(at_end)
        def _():
            for block in range(N // 128):
                out[block, 4:8, :] = out[block, 8:12, :]


def gain_kernel(place, gain_re, gain_im):
    k0 = place[0]
    group = place[1] + pl.program_id(0)
    down = lax.broadcasted_iota(jnp.int32, (8, 128), 0)
    across = lax.broadcasted_iota(jnp.int32, (8, 128), 1)
    row = (k0 + RES * (group * 8 + down - HALF)).astype(jnp.float32)
    row_sq = row * row
    row_in = jnp.abs(row) < LIMIT
    for u in range(RES):
        col = (residue(u) + RES * (across - HALF)).astype(jnp.float32)
        square = row_sq + col * col
        scaled = RATIO_SQ * square
        phase = -2.0 * math.pi * distance / wavelength * scaled / (1.0 + jnp.sqrt(1.0 - scaled))
        total = jnp.where(
            row_in & (jnp.abs(col) < LIMIT), jnp.exp(square * (-2.0 / (LIMIT * LIMIT))), 0.0
        )
        quarter = jnp.floor(phase * (2.0 / math.pi) + 0.5)
        left = phase - quarter * 1.5703125
        left = left - quarter * 4.837512969970703125e-4
        left = left - quarter * 7.549789954891882e-8
        sq = left * left
        sine = ((-1.9515295891e-4 * sq + 8.3321608736e-3) * sq - 1.6666654611e-1) * sq * left + left
        cosine = (
            (2.443315711809948e-5 * sq - 1.388731625493765e-3) * sq + 4.166664568298827e-2
        ) * sq * sq - 0.5 * sq + 1.0
        which = quarter.astype(jnp.int32) & 3
        swap = (which & 1) == 1
        cos_part = jnp.where(swap, sine, cosine)
        sin_part = jnp.where(swap, cosine, sine)
        cos_part = jnp.where((which == 1) | (which == 2), -cos_part, cos_part)
        sin_part = jnp.where(which >= 2, -sin_part, sin_part)
        at = (u % (RES // 2)) * 16 + (u // (RES // 2)) * 8
        gain_re[0, at : at + 8, :] = total * cos_part
        gain_im[0, at : at + 8, :] = total * sin_part


def encode(near_real, near_imag, peak_sq, cell_sign):
    square = near_real * near_real + near_imag * near_imag
    root = lax.rsqrt(jnp.maximum(square, 1.2e-38))
    top = lax.rsqrt(peak_sq)
    amp_level = (square * root) * (0.8 * top)
    unit = jnp.minimum(root, 20.0 * top)
    rest = 1.0 - amp_level * amp_level
    level = unit * amp_level
    lift = (rest * lax.rsqrt(rest)) * (unit * cell_sign)
    return (near_real * level + near_imag * lift, near_imag * level - near_real * lift)


def encode_kernel(count, *refs):
    tops, (near, slm_real, slm_imag) = refs[:count], refs[count:]
    height, width = slm_real.shape[0], near.shape[-1]
    peak_sq = tops[0][0]
    for top in tops[1:]:
        peak_sq = jnp.maximum(peak_sq, top[0])
    peak_sq = jnp.full((1, width), peak_sq, jnp.float32)
    cell = lax.broadcasted_iota(jnp.int32, (height, width), 0)
    cell = cell + lax.broadcasted_iota(jnp.int32, (height, width), 1)
    cell_sign = (1 - 2 * (cell & 1)).astype(jnp.float32)
    for r in range(near.shape[0]):
        lanes = pl.ds(r * width, width)
        slm_real[:, lanes], slm_imag[:, lanes] = encode(near[r, 0], near[r, 1], peak_sq, cell_sign)


def pack_kernel(chunk, place, field_real, field_imag, *refs):
    pieces, sems = refs[:-1], refs[-1]
    width = pieces[0].shape[-1]
    rows = pl.ds(chunk * CHUNK, CHUNK)
    copies = []
    for j in list(range(1, len(pieces))) + [0]:
        lanes = pl.ds(pl.multiple_of((place[0] ^ j) * width, width), width)
        for part, field in enumerate((field_real, field_imag)):
            copies.append(
                pltpu.make_async_copy(
                    field.at[:, rows, lanes], pieces[j].at[part], sems.at[2 * j + part]
                )
            )
    for copy in copies:
        copy.start()
    for copy in copies:
        copy.wait()


def exchange(pieces, axis):
    total = len(pieces)
    return [pieces[0]] + [
        lax.ppermute(pieces[j], axis, [(i, i ^ j) for i in range(total)]) for j in range(1, total)
    ]


def params(mebibytes):
    return pltpu.CompilerParams(vmem_limit_bytes=mebibytes << 20)


def cost(megabytes):
    return pl.CostEstimate(flops=0, bytes_accessed=megabytes << 20, transcendentals=0)


def whole(memory=pltpu.VMEM):
    return pl.BlockSpec(memory_space=memory)


def body(field_real, field_imag):
    row_total, col_total = lax.axis_size("row"), lax.axis_size("col")
    devices = row_total * col_total
    device = lax.axis_index("row") * col_total + lax.axis_index("col")
    height, tile_width = field_real.shape
    width = tile_width // row_total
    parts = max(1, devices // RES)
    groups = -(-(2 * HALF + 1) // (8 * parts)) * parts
    own = groups // parts
    tail = parts == 1
    total_rows = groups * 16 - (8 if tail else 0)
    own_rows = total_rows // parts
    many = 4 if width == 128 else 1

    fwd_col, inv_col = column_tables(groups, tail)
    line_fh, line_fl, line_ih, line_il = line_tables()
    twist = np.stack(twist_table())
    twist_line = np.ascontiguousarray(np.broadcast_to(twist[:, :, None], twist.shape[:2] + (8, INNER)))
    twist_col = np.pad(twist, ((0, 0), (0, 64 - twist.shape[1]), (0, 0)))
    twist_col = twist_col.reshape(128, INNER).T.copy()

    u = device // parts
    k0 = jnp.where(u >= RES // 2, u - RES, u)
    place = jnp.stack([k0, (device % parts) * own]).astype(jnp.int32)
    gain_shape = jax.ShapeDtypeStruct((own, RES * 8, 128), jnp.float32)
    gain_spec = pl.BlockSpec((1, RES * 8, 128), lambda g: (g, 0, 0))
    gain_re, gain_im = pl.pallas_call(
        gain_kernel,
        grid=(own,),
        in_specs=[whole(pltpu.SMEM)],
        out_specs=[gain_spec, gain_spec],
        out_shape=[gain_shape, gain_shape],
        compiler_params=params(56),
        name="gain",
    )(place)

    place_row = lax.axis_index("row").reshape(1).astype(jnp.int32)
    blocks = height // INNER
    piece = (2, blocks, CHUNK, width)
    piece_shape = jax.ShapeDtypeStruct(piece, jnp.float32)
    anywhere = whole(pl.ANY)
    if width != 128:
        packed = jnp.stack([field_real, field_imag])
        packed = packed.reshape(2, blocks, CHUNKS, CHUNK, row_total, width).transpose(2, 4, 0, 1, 3, 5)
        packed = jnp.take(packed, jnp.arange(row_total) ^ place_row[0], axis=1)
    lines = []
    for chunk in range(CHUNKS):
        if width == 128:
            pieces = pl.pallas_call(
                partial(pack_kernel, chunk),
                in_specs=[whole(pltpu.SMEM), anywhere, anywhere],
                out_specs=[anywhere] * row_total,
                out_shape=[piece_shape] * row_total,
                scratch_shapes=[pltpu.SemaphoreType.DMA((2 * row_total,))],
                compiler_params=params(56),
                cost_estimate=cost(4),
                name="pack",
            )(
                place_row,
                field_real.reshape(blocks, INNER, tile_width),
                field_imag.reshape(blocks, INNER, tile_width),
            )
        else:
            pieces = [packed[chunk, j] for j in range(row_total)]
        pieces = exchange(pieces, "row")
        rows = slice(chunk * CHUNK, (chunk + 1) * CHUNK)
        slab = pltpu.VMEM((RES // many, 2 * CHUNK, many * width), jnp.bfloat16)
        lines = [
            pl.pallas_call(
                partial(column_forward_kernel, row_total),
                in_specs=[whole(pltpu.SMEM)] + [whole()] * (2 + row_total) + [anywhere] * len(lines),
                out_specs=anywhere,
                out_shape=jax.ShapeDtypeStruct((RES, total_rows, width), jnp.float32),
                scratch_shapes=[
                    pltpu.VMEM((RES, total_rows, width), jnp.float32),
                    slab,
                    slab,
                    pltpu.SemaphoreType.DMA((2 * RES // many,)),
                ],
                compiler_params=params(20),
                cost_estimate=cost(20),
                name="column_forward",
            )(place_row, twist_col[rows], fwd_col[chunk], *pieces, *lines)
        ]
    (lines,) = lines

    lines = lines.reshape(devices, own_rows, width)
    lines = lax.all_to_all(lines, ("row", "col"), split_axis=0, concat_axis=0, tiled=True)
    if width == 128:
        order = tuple((b % row_total) * col_total + b // row_total for b in range(N // 128))
    else:
        order = tuple(range(N // 128))
        lines = lines.reshape(row_total, col_total, own_rows, width).transpose(2, 1, 0, 3)
        lines = lines.reshape(own_rows, N // 128, 128).transpose(1, 0, 2)

    at_once = 2
    line_grain = pl.BlockSpec((N // 128, 16 * at_once, 128), lambda i: (0, i, 0))
    gain_grain = pl.BlockSpec((at_once, RES * 8, 128), lambda i: (i, 0, 0))
    lines = pl.pallas_call(
        partial(line_kernel, order, own, tail),
        grid=(-(-own // at_once),),
        in_specs=[line_grain, gain_grain, gain_grain] + [whole()] * 5,
        out_specs=line_grain,
        out_shape=jax.ShapeDtypeStruct((N // 128, own_rows, 128), jnp.float32),
        scratch_shapes=[pltpu.VMEM((2 * RES * 8, 2 * INNER), jnp.bfloat16)] * at_once
        + [pltpu.VMEM((RES * 8, 2 * INNER), jnp.float32)] * at_once,
        compiler_params=params(52),
        name="line",
    )(lines, gain_re, gain_im, twist_line, line_fh, line_fl, line_ih, line_il)

    if width != 128:
        lines = lines.transpose(1, 0, 2).reshape(own_rows, col_total, row_total, width)
        lines = lines.transpose(2, 1, 0, 3).reshape(devices, own_rows, width)
    lines = lax.all_to_all(lines, ("row", "col"), split_axis=0, concat_axis=0, tiled=True)
    lines = lines.reshape(RES, total_rows, width)

    tall = pl.BlockSpec(
        (row_total, 2, blocks, STEP, width), lambda i: (0, 0, 0, jnp.maximum(i - 1, 0), 0)
    )
    near, top = pl.pallas_call(
        column_inverse_kernel,
        grid=(STEPS + 1,),
        in_specs=[
            anywhere,
            pl.BlockSpec((STEP, 128), lambda i: (jnp.maximum(i - 1, 0), 0)),
            pl.BlockSpec((1,) + inv_col.shape[1:], lambda i: (jnp.minimum(i, STEPS - 1), 0, 0)),
        ],
        out_specs=[tall, whole()],
        out_shape=[
            jax.ShapeDtypeStruct((row_total, 2, blocks, INNER, width), jnp.float32),
            jax.ShapeDtypeStruct((8, width), jnp.float32),
        ],
        scratch_shapes=[
            pltpu.VMEM((RES, total_rows, width), jnp.float32),
            pltpu.VMEM((RES // many, inv_col.shape[2], many * width), jnp.bfloat16),
            pltpu.VMEM((2, RES, 2 * STEP, width), jnp.float32),
            pltpu.SemaphoreType.DMA((RES // many,)),
        ],
        compiler_params=params(56),
        name="column_inverse",
    )(lines, twist_col, inv_col)

    near = near.reshape(row_total, 2, height, width)
    near = lax.all_to_all(near, "row", split_axis=0, concat_axis=0, tiled=True)
    peak = jnp.max(top)
    shift = 1
    while shift < col_total:
        partner = [(i, i ^ shift) for i in range(col_total)]
        peak = jnp.maximum(peak, lax.ppermute(peak, "col", partner))
        shift *= 2
    tops = exchange([peak] * row_total, "row")
    if width != 128:
        near = near.transpose(1, 2, 0, 3).reshape(2, height, tile_width)
        odd_cell = (jnp.arange(height)[:, None] + jnp.arange(tile_width)[None, :]) % 2
        cell_sign = (1 - 2 * odd_cell).astype(jnp.float32)
        return encode(near[0], near[1], jnp.max(jnp.stack(tops)), cell_sign)
    tile_rows = min(height, 128)
    tile_spec = pl.BlockSpec((tile_rows, tile_width), lambda i: (i, 0))
    tile_shape = jax.ShapeDtypeStruct((height, tile_width), jnp.float32)
    return pl.pallas_call(
        partial(encode_kernel, row_total),
        grid=(height // tile_rows,),
        in_specs=[whole(pltpu.SMEM)] * row_total
        + [pl.BlockSpec((row_total, 2, tile_rows, width), lambda i: (0, 0, i, 0))],
        out_specs=[tile_spec, tile_spec],
        out_shape=[tile_shape, tile_shape],
        compiler_params=params(56),
        name="encode",
    )(*[top.reshape(1) for top in tops], near)


def solution(mesh):
    in_specs = (P("row", "col"), P("row", "col"))
    out_specs = (P("row", "col"), P("row", "col"))
    return jax.shard_map(body, mesh=mesh, in_specs=in_specs, out_specs=out_specs, check_vma=False)
```

```python
from functools import partial
import math

import jax
import jax.numpy as jnp
import ml_dtypes
import numpy as np
from jax import lax
from jax.experimental import pallas as pl
from jax.experimental.pallas import tpu as pltpu
from jax.sharding import PartitionSpec as P

N = 4096
PAD = 2 * N
wavelength = 5.2e-07
distance = 0.2
INNER = 256
SLABS = N // INNER
RES = PAD // INNER
HALF = 40
CHUNKS = 2
CHUNK = INNER // CHUNKS
STEPS = 2
STEP = INNER // STEPS


def optics(padded_side):
    pitch = 2e-06 * math.sqrt(8192.0 / padded_side)
    extent = padded_side * pitch
    ratio_sq = (wavelength / extent) ** 2
    band_limit = extent / (wavelength * math.sqrt((2.0 * distance / extent) ** 2 + 1.0))
    return (ratio_sq, band_limit)


RATIO_SQ, LIMIT = optics(PAD)
assert RES * HALF - RES // 2 + RES > LIMIT and RES * HALF + RES // 2 > LIMIT


def residue(u):
    return u if u < RES // 2 else u - RES


def split16(table):
    table = np.asarray(table, np.float64)
    high = table.astype(np.float32).astype(ml_dtypes.bfloat16)
    low = (table - high.astype(np.float64)).astype(np.float32).astype(ml_dtypes.bfloat16)
    return high, low


def row_order(groups, tail):
    rows = []
    for group in range(groups):
        size = 4 if tail and group == groups - 1 else 8
        for part in range(2):
            for s in range(size):
                rows.append((part, group * 8 + s - HALF))
    return rows


def column_tables(groups, tail):
    q = np.arange(INNER)
    rows = row_order(groups, tail)
    forward = np.zeros((len(rows), 2, INNER))
    inverse = np.zeros((2, INNER, len(rows)))
    for at, (part, k1) in enumerate(rows):
        if abs(k1) > HALF:
            continue
        angle = 2.0 * np.pi * ((k1 * q) % INNER) / INNER
        c, s = np.cos(angle), np.sin(angle)
        forward[at] = (c, s) if part == 0 else (-s, c)
        inverse[:, :, at] = (c, s) if part == 0 else (-s, c)
    forward = forward.reshape(-1, 2, CHUNKS, CHUNK // 8, 8).transpose(2, 0, 3, 1, 4)
    forward = np.concatenate(split16(forward.reshape(CHUNKS, len(rows), 2 * CHUNK)), axis=1)
    inverse = inverse.reshape(2, STEPS, STEP, -1).transpose(1, 0, 2, 3)
    high, low = split16(inverse.reshape(STEPS, 2 * STEP, len(rows)))
    inverse = np.concatenate([high, high, low], axis=2)
    inverse = np.pad(inverse, ((0, 0), (0, 0), (0, -3 * len(rows) % 16)))
    return forward, inverse


def line_tables():
    q = np.arange(INNER)
    forward = np.zeros((2 * INNER, 256))
    inverse = np.zeros((256, 2 * INNER))
    for lane in range(2 * HALF + 1):
        angle = 2.0 * np.pi * (((lane - HALF) * q) % INNER) / INNER
        c, s = np.cos(angle), np.sin(angle)
        forward[:INNER, lane], forward[INNER:, lane] = c, s
        forward[:INNER, 128 + lane], forward[INNER:, 128 + lane] = -s, c
        inverse[lane, :INNER], inverse[lane, INNER:] = c, s
        inverse[128 + lane, :INNER], inverse[128 + lane, INNER:] = -s, c
    return split16(forward) + split16(inverse)


def twist_table():
    q = np.arange(INNER) + N // 2
    k0 = np.arange(RES // 2 + 1)
    angle = 2.0 * np.pi * ((k0[:, None] * q[None, :]) % PAD) / PAD
    return np.cos(angle).astype(np.float32), (-np.sin(angle)).astype(np.float32)


def turn(value, num, den):
    re, im = value
    num = num % den
    eighth = 8 * num
    if num == 0:
        return re, im
    if 2 * num == den:
        return -re, -im
    if 4 * num == den:
        return -im, re
    if 4 * num == 3 * den:
        return im, -re
    if eighth % den == 0:
        root = np.float32(math.sqrt(0.5))
        kind = eighth // den
        if kind == 1:
            return (re - im) * root, (re + im) * root
        if kind == 3:
            return (re + im) * (-root), (re - im) * root
        if kind == 5:
            return (im - re) * root, (re + im) * (-root)
        return (re + im) * root, (im - re) * root
    c = np.float32(math.cos(2.0 * math.pi * num / den))
    s = np.float32(math.sin(2.0 * math.pi * num / den))
    return re * c - im * s, re * s + im * c


def small_dft(get, ids, sign):
    count = len(ids)
    if count == 1:
        return [get(ids[0])]
    even = small_dft(get, ids[0::2], sign)
    odd = small_dft(get, ids[1::2], sign)
    half = count // 2
    first, second = [], []
    for j in range(half):
        re, im = even[j]
        t_re, t_im = turn(odd[j], sign * j, count)
        first.append((re + t_re, im + t_im))
        second.append((re - t_re, im - t_im))
    return first + second


def forward_slabs(get, put):
    ids = list(range(SLABS))
    for v, value in enumerate(small_dft(get, ids, -1)):
        put(2 * v, value)
    for v, value in enumerate(small_dft(lambda n: turn(get(n), -n, RES), ids, -1)):
        put(2 * v + 1, value)


def inverse_slabs(get, put):
    even = small_dft(get, list(range(0, RES, 2)), 1)
    odd = small_dft(get, list(range(1, RES, 2)), 1)
    for n in range(SLABS):
        t_re, t_im = turn(odd[n], n, RES)
        put(n, (even[n][0] + t_re, even[n][1] + t_im))


def twisted(value, u, sign, read):
    re, im = value
    k0 = residue(u)
    if k0 == 0:
        return value
    c, s = read(abs(k0))
    if (k0 < 0) == (sign > 0):
        return re * c + im * s, im * c - re * s
    return re * c - im * s, re * s + im * c


def high_low(value):
    high = value.astype(jnp.bfloat16)
    low = (value - high.astype(jnp.float32)).astype(jnp.bfloat16)
    return high, low


def dot16(left, right):
    return jnp.dot(left, right, preferred_element_type=jnp.float32)


def three_left(stacked, count, high, low):
    both = dot16(stacked[...], high)
    return both[:count] + both[count:] + dot16(stacked[:count], low)


def three_right(stacked, count, high, low):
    both = dot16(stacked, high)
    return both[:count] + both[count:] + dot16(stacked[:count], low)


def column_twist(twist, q0):
    def read(k):
        rows = pl.ds(q0, 8)
        return twist[rows, k : k + 1], twist[rows, 64 + k : 65 + k]

    return read


def column_forward_kernel(count, place, twist, matrix, *refs):
    pieces, refs = refs[:count], refs[count:]
    before, (out, total, high, low, sems) = refs[:-5], refs[-5:]
    width = pieces[0].shape[-1]
    per_source = pieces[0].shape[1]
    many = high.shape[-1] // width
    products = RES // many
    rows_out = out.shape[1]

    def copy_in(p):
        part = pl.ds(p * many, many)
        return pltpu.make_async_copy(before[0].at[part], total.at[part], sems.at[p])

    def copy_out(p):
        part = pl.ds(p * many, many)
        return pltpu.make_async_copy(total.at[part], out.at[part], sems.at[products + p])

    if before:
        for p in range(products):
            copy_in(p).start()

    for here in range(count):

        @pl.when(place[0] == here)
        def _():
            @pl.loop(0, CHUNK // 8)
            def _(t):
                q0 = pl.multiple_of(t * 8, 8)

                def get(n):
                    source, block = divmod(n, per_source)
                    piece = pieces[source ^ here]
                    rows = pl.ds(q0, 8)
                    return piece[0, block, rows, :], piece[1, block, rows, :]

                def put(u, value):
                    item = jnp.concatenate(twisted(value, u, 1, column_twist(twist, q0)), axis=0)
                    rows = pl.ds(pl.multiple_of(t * 16, 16), 16)
                    at = (u // many, rows, pl.ds((u % many) * width, width))
                    high[at], low[at] = high_low(item)

                forward_slabs(get, put)

    @pl.loop(0, products)
    def _(p):
        done = three_left(matrix, rows_out, high[p], low[p])
        if before:
            copy_in(p).wait()
        for part in range(many):
            item = done[:, part * width : (part + 1) * width]
            at = p * many + part
            total[at] = total[at] + item if before else item
        copy_out(p).start()

    for p in range(products):
        copy_out(p).wait()


def column_inverse_kernel(count, place, source, twist, matrix, *refs):
    pieces, (top, near, lines, deep, back, sems, out_sems) = refs[:count], refs[count:]
    width = lines.shape[-1]
    rows_in = lines.shape[1]
    per_dest = near.shape[3]
    many = deep.shape[-1] // width
    now = pl.program_id(0)

    def copy_in(p):
        part = pl.ds(p * many, many)
        return pltpu.make_async_copy(source.at[part], lines.at[part], sems.at[p])

    def product(p, slot):
        done = dot16(matrix[0], deep[p])
        for part in range(many):
            back[slot, p * many + part] = done[:, part * width : (part + 1) * width]

    def prepare(p):
        copy_in(p).wait()
        blocks = [lines[p * many + part] for part in range(many)]
        joined = jnp.concatenate(blocks, axis=1) if many > 1 else blocks[0]
        high = joined.astype(jnp.bfloat16).astype(jnp.float32)
        parts = [high, joined - high, high]
        if deep.shape[1] > 3 * rows_in:
            parts.append(jnp.zeros((deep.shape[1] - 3 * rows_in, many * width), jnp.float32))
        deep[p] = jnp.concatenate(parts, axis=0).astype(jnp.bfloat16)
        product(p, 0)

    def butterflies(t, slot):
        q0 = pl.multiple_of(t * 8, 8)
        largest = []

        def get(u):
            re = back[slot, u, pl.ds(q0, 8), :]
            im = back[slot, u, pl.ds(STEP + q0, 8), :]
            return twisted((re, im), u, -1, column_twist(twist, q0))

        def put(n, value):
            dest, block = divmod(n, per_dest)
            rows = pl.ds(q0, 8)
            near[slot, dest, 0, block, rows, :], near[slot, dest, 1, block, rows, :] = value
            largest.append(value[0] * value[0] + value[1] * value[1])

        inverse_slabs(get, put)
        while len(largest) > 1:
            largest = [jnp.maximum(a, b) for a, b in zip(largest[0::2], largest[1::2])]
        top[...] = jnp.maximum(top[...], largest[0])

    def copies_out(slot, part):
        size = STEP // 2
        here = pl.ds(part * size, size)
        there = pl.ds(slot * STEP + part * size, size)
        return [
            pltpu.make_async_copy(
                near.at[slot, place[0] ^ j, :, :, here],
                piece.at[:, :, there],
                out_sems.at[(slot * 2 + part) * count + j],
            )
            for j, piece in enumerate(pieces)
        ]

    @pl.when(now == 0)
    def _():
        for p in range(RES // many):
            copy_in(p).start()
        top[...] = jnp.zeros_like(top)
        pl.loop(0, RES // many)(prepare)

    for step in range(1, STEPS + 1):

        @pl.when(now == step)
        def _():
            tiles, products = STEP // 16, RES // many // 2
            steps = min(tiles, products)

            for part in range(2):

                @pl.loop(part * steps, (part + 1) * steps)
                def _(t):
                    for item in range(tiles // steps):
                        butterflies(t * (tiles // steps) + item, step - 1)
                    if step < STEPS:
                        for item in range(products // steps):
                            product(t * (products // steps) + item, step)

                for copy in copies_out(step - 1, part):
                    copy.start()

            if step == STEPS:
                for slot in range(STEPS):
                    for part in range(2):
                        for copy in copies_out(slot, part):
                            copy.wait()


def line_kernel(
    order, own, tail, lines, gain_re, gain_im, twist, fwd_high, fwd_low, inv_high, inv_low, out, *scratch
):
    half = RES * 8
    at_end = pl.program_id(0) == pl.num_programs(0) - 1

    def line_twist(side):
        def read(k):
            lanes = pl.ds(side * 128, 128)
            return twist[0, k, :, lanes], twist[1, k, :, lanes]

        return read

    def forward(group, stacked, sides=(0, 1)):
        for side in sides:
            waiting = {}

            def get(m):
                block = order[2 * m + side]
                at = group * 16
                return lines[block, at : at + 8, :], lines[block, at + 8 : at + 16, :]

            def put(u, value):
                waiting[u] = twisted(value, u, 1, line_twist(side))
                v = (u + RES // 2) % RES
                if v in waiting:
                    first = min(u, v)
                    rows = pl.ds(first * 16, 16)
                    rows_low = pl.ds(half + first * 16, 16)
                    for part in range(2):
                        item = jnp.concatenate(
                            [waiting[first][part], waiting[first + RES // 2][part]], axis=0
                        )
                        at = pl.ds(part * INNER + side * 128, 128)
                        stacked[rows, at], stacked[rows_low, at] = high_low(item)

            forward_slabs(get, put)

    def filtered(group, stacked):
        spec = three_right(stacked[...], half, fwd_high[...], fwd_low[...])
        spec_re, spec_im = spec[:, :128], spec[:, 128:]
        g_re, g_im = gain_re[group], gain_im[group]
        mixed = jnp.concatenate(
            [spec_re * g_re - spec_im * g_im, spec_re * g_im + spec_im * g_re], axis=1
        )
        return jnp.concatenate(high_low(mixed), axis=0)

    def unfold(mixed, back):
        back[...] = three_right(mixed, half, inv_high[...], inv_low[...])

    def inverse(group, back, sides=(0, 1)):
        for side in sides:

            def get(u):
                rows = pl.ds((u % (RES // 2)) * 16 + (u // (RES // 2)) * 8, 8)
                re = back[rows, pl.ds(side * 128, 128)]
                im = back[rows, pl.ds(INNER + side * 128, 128)]
                return twisted((re, im), u, -1, line_twist(side))

            def put(m, value):
                block = order[2 * m + side]
                at = group * 16
                out[block, at : at + 8, :], out[block, at + 8 : at + 16, :] = value

            inverse_slabs(get, put)

    if tail:

        @pl.when(at_end)
        def _():
            for block in range(N // 128):
                lines[block, 8:12, :] = lines[block, 4:8, :]

    groups = len(scratch) // 2

    stacked, back = scratch[:groups], scratch[groups:]

    def run(count):
        forward(0, stacked[0])
        for group in range(count):
            mixed = filtered(group, stacked[group])
            if group + 1 < count:
                forward(group + 1, stacked[group + 1], (0,))
            if group > 0:
                inverse(group - 1, back[group - 1], (0,))
            unfold(mixed, back[group])
            if group + 1 < count:
                forward(group + 1, stacked[group + 1], (1,))
            if group > 0:
                inverse(group - 1, back[group - 1], (1,))
        inverse(count - 1, back[count - 1])

    rest = own % groups
    if rest:
        pl.when(jnp.logical_not(at_end))(lambda: run(groups))
        pl.when(at_end)(lambda: run(rest))
    else:
        run(groups)

    if tail:

        @pl.when(at_end)
        def _():
            for block in range(N // 128):
                out[block, 4:8, :] = out[block, 8:12, :]


def gain_kernel(place, gain_re, gain_im):
    k0 = place[0]
    group = place[1] + pl.program_id(0)
    down = lax.broadcasted_iota(jnp.int32, (8, 128), 0)
    across = lax.broadcasted_iota(jnp.int32, (8, 128), 1)
    row = (k0 + RES * (group * 8 + down - HALF)).astype(jnp.float32)
    row_sq = row * row
    row_in = jnp.abs(row) < LIMIT
    for u in range(RES):
        col = (residue(u) + RES * (across - HALF)).astype(jnp.float32)
        square = row_sq + col * col
        scaled = RATIO_SQ * square
        phase = -2.0 * math.pi * distance / wavelength * scaled / (1.0 + jnp.sqrt(1.0 - scaled))
        total = jnp.where(
            row_in & (jnp.abs(col) < LIMIT), jnp.exp(square * (-2.0 / (LIMIT * LIMIT))), 0.0
        )
        quarter = jnp.floor(phase * (2.0 / math.pi) + 0.5)
        left = phase - quarter * 1.5703125
        left = left - quarter * 4.837512969970703125e-4
        left = left - quarter * 7.549789954891882e-8
        sq = left * left
        sine = ((-1.9515295891e-4 * sq + 8.3321608736e-3) * sq - 1.6666654611e-1) * sq * left + left
        cosine = (
            (2.443315711809948e-5 * sq - 1.388731625493765e-3) * sq + 4.166664568298827e-2
        ) * sq * sq - 0.5 * sq + 1.0
        which = quarter.astype(jnp.int32) & 3
        swap = (which & 1) == 1
        cos_part = jnp.where(swap, sine, cosine)
        sin_part = jnp.where(swap, cosine, sine)
        cos_part = jnp.where((which == 1) | (which == 2), -cos_part, cos_part)
        sin_part = jnp.where(which >= 2, -sin_part, sin_part)
        at = (u % (RES // 2)) * 16 + (u // (RES // 2)) * 8
        gain_re[0, at : at + 8, :] = total * cos_part
        gain_im[0, at : at + 8, :] = total * sin_part


def encode(near_real, near_imag, peak_sq, cell_sign):
    square = near_real * near_real + near_imag * near_imag
    root = lax.rsqrt(jnp.maximum(square, 1.2e-38))
    top = lax.rsqrt(peak_sq)
    amp_level = (square * root) * (0.8 * top)
    unit = jnp.minimum(root, 20.0 * top)
    rest = 1.0 - amp_level * amp_level
    level = unit * amp_level
    lift = (rest * lax.rsqrt(rest)) * (unit * cell_sign)
    return (near_real * level + near_imag * lift, near_imag * level - near_real * lift)


def encode_kernel(count, place, top, *refs):
    pieces, (slm_real, slm_imag, tile_real, tile_imag, sems) = refs[:count], refs[count:]
    blocks, height, width = pieces[0].shape[1:]
    peak_sq = jnp.full((1, width), top[0], jnp.float32)
    cell = lax.broadcasted_iota(jnp.int32, (height, width), 0)
    cell = cell + lax.broadcasted_iota(jnp.int32, (height, width), 1)
    cell_sign = (1 - 2 * (cell & 1)).astype(jnp.float32)

    def copies_out(block):
        rows = pl.ds(block * height, height)
        return [
            pltpu.make_async_copy(tile.at[block], slm.at[rows], sems.at[2 * block + part])
            for part, (tile, slm) in enumerate(((tile_real, slm_real), (tile_imag, slm_imag)))
        ]

    @pl.loop(0, blocks)
    def _(block):
        for j, piece in enumerate(pieces):
            lanes = pl.ds(pl.multiple_of((place[0] ^ j) * width, width), width)
            tile_real[block, :, lanes], tile_imag[block, :, lanes] = encode(
                piece[0, block], piece[1, block], peak_sq, cell_sign
            )
        for copy in copies_out(block):
            copy.start()

    for block in range(blocks):
        for copy in copies_out(block):
            copy.wait()


def pack_kernel(place, field_real, field_imag, *refs):
    pieces, sems = refs[:-1], refs[-1]
    width = pieces[0].shape[-1]
    copies = []
    for j in list(range(1, len(pieces))) + [0]:
        lanes = pl.ds(pl.multiple_of((place[0] ^ j) * width, width), width)
        for part, field in enumerate((field_real, field_imag)):
            copies.append(
                pltpu.make_async_copy(
                    field.at[:, :, lanes], pieces[j].at[part], sems.at[2 * j + part]
                )
            )
    for copy in copies:
        copy.start()
    for copy in copies:
        copy.wait()


def exchange(pieces, axis):
    total = len(pieces)
    return [pieces[0]] + [
        lax.ppermute(pieces[j], axis, [(i, i ^ j) for i in range(total)]) for j in range(1, total)
    ]


def params(mebibytes):
    return pltpu.CompilerParams(vmem_limit_bytes=mebibytes << 20)


def cost(megabytes):
    return pl.CostEstimate(flops=0, bytes_accessed=megabytes << 20, transcendentals=0)


def whole(memory=pltpu.VMEM):
    return pl.BlockSpec(memory_space=memory)


def body(field_real, field_imag):
    row_total, col_total = lax.axis_size("row"), lax.axis_size("col")
    devices = row_total * col_total
    device = lax.axis_index("row") * col_total + lax.axis_index("col")
    height, tile_width = field_real.shape
    width = tile_width // row_total
    parts = max(1, devices // RES)
    groups = -(-(2 * HALF + 1) // (8 * parts)) * parts
    own = groups // parts
    tail = parts == 1
    total_rows = groups * 16 - (8 if tail else 0)
    own_rows = total_rows // parts
    many = 4 if width == 128 else 1

    fwd_col, inv_col = column_tables(groups, tail)
    line_fh, line_fl, line_ih, line_il = line_tables()
    twist = np.stack(twist_table())
    twist_line = np.ascontiguousarray(np.broadcast_to(twist[:, :, None], twist.shape[:2] + (8, INNER)))
    twist_col = np.pad(twist, ((0, 0), (0, 64 - twist.shape[1]), (0, 0)))
    twist_col = twist_col.reshape(128, INNER).T.copy()

    u = device // parts
    k0 = jnp.where(u >= RES // 2, u - RES, u)
    place = jnp.stack([k0, (device % parts) * own]).astype(jnp.int32)
    gain_shape = jax.ShapeDtypeStruct((own, RES * 8, 128), jnp.float32)
    gain_spec = pl.BlockSpec((1, RES * 8, 128), lambda g: (g, 0, 0))
    gain_re, gain_im = pl.pallas_call(
        gain_kernel,
        grid=(own,),
        in_specs=[whole(pltpu.SMEM)],
        out_specs=[gain_spec, gain_spec],
        out_shape=[gain_shape, gain_shape],
        compiler_params=params(56),
        name="gain",
    )(place)

    place_row = lax.axis_index("row").reshape(1).astype(jnp.int32)
    blocks = height // INNER
    piece = (2, blocks, CHUNK, width)
    piece_shape = jax.ShapeDtypeStruct(piece, jnp.float32)
    anywhere = whole(pl.ANY)
    if width != 128:
        packed = jnp.stack([field_real, field_imag])
        packed = packed.reshape(2, blocks, CHUNKS, CHUNK, row_total, width).transpose(2, 4, 0, 1, 3, 5)
        packed = jnp.take(packed, jnp.arange(row_total) ^ place_row[0], axis=1)
    lines = []
    for chunk in range(CHUNKS):
        if width == 128:
            pieces = pl.pallas_call(
                pack_kernel,
                grid=(1,),
                in_specs=[whole(pltpu.SMEM)]
                + [pl.BlockSpec((blocks, CHUNK, tile_width), lambda i: (0, chunk, 0))] * 2,
                out_specs=[anywhere] * row_total,
                out_shape=[piece_shape] * row_total,
                scratch_shapes=[pltpu.SemaphoreType.DMA((2 * row_total,))],
                compiler_params=params(56),
                cost_estimate=cost(4),
                name="pack",
            )(
                place_row,
                field_real.reshape(blocks, INNER, tile_width),
                field_imag.reshape(blocks, INNER, tile_width),
            )
        else:
            pieces = [packed[chunk, j] for j in range(row_total)]
        pieces = exchange(pieces, "row")
        rows = slice(chunk * CHUNK, (chunk + 1) * CHUNK)
        slab = pltpu.VMEM((RES // many, 2 * CHUNK, many * width), jnp.bfloat16)
        lines = [
            pl.pallas_call(
                partial(column_forward_kernel, row_total),
                in_specs=[whole(pltpu.SMEM)] + [whole()] * (2 + row_total) + [anywhere] * len(lines),
                out_specs=anywhere,
                out_shape=jax.ShapeDtypeStruct((RES, total_rows, width), jnp.float32),
                scratch_shapes=[
                    pltpu.VMEM((RES, total_rows, width), jnp.float32),
                    slab,
                    slab,
                    pltpu.SemaphoreType.DMA((2 * RES // many,)),
                ],
                compiler_params=params(20),
                cost_estimate=cost(20),
                name="column_forward",
            )(place_row, twist_col[rows], fwd_col[chunk], *pieces, *lines)
        ]
    (lines,) = lines

    lines = lines.reshape(devices, own_rows, width)
    lines = lax.all_to_all(lines, ("row", "col"), split_axis=0, concat_axis=0, tiled=True)
    if width == 128:
        order = tuple((b % row_total) * col_total + b // row_total for b in range(N // 128))
    else:
        order = tuple(range(N // 128))
        lines = lines.reshape(row_total, col_total, own_rows, width).transpose(2, 1, 0, 3)
        lines = lines.reshape(own_rows, N // 128, 128).transpose(1, 0, 2)

    at_once = 2
    line_grain = pl.BlockSpec((N // 128, 16 * at_once, 128), lambda i: (0, i, 0))
    gain_grain = pl.BlockSpec((at_once, RES * 8, 128), lambda i: (i, 0, 0))
    lines = pl.pallas_call(
        partial(line_kernel, order, own, tail),
        grid=(-(-own // at_once),),
        in_specs=[line_grain, gain_grain, gain_grain] + [whole()] * 5,
        out_specs=line_grain,
        out_shape=jax.ShapeDtypeStruct((N // 128, own_rows, 128), jnp.float32),
        scratch_shapes=[pltpu.VMEM((2 * RES * 8, 2 * INNER), jnp.bfloat16)] * at_once
        + [pltpu.VMEM((RES * 8, 2 * INNER), jnp.float32)] * at_once,
        compiler_params=params(52),
        name="line",
    )(lines, gain_re, gain_im, twist_line, line_fh, line_fl, line_ih, line_il)

    if width != 128:
        lines = lines.transpose(1, 0, 2).reshape(own_rows, col_total, row_total, width)
        lines = lines.transpose(2, 1, 0, 3).reshape(devices, own_rows, width)
    lines = lax.all_to_all(lines, ("row", "col"), split_axis=0, concat_axis=0, tiled=True)
    lines = lines.reshape(RES, total_rows, width)

    piece = (2, blocks, INNER, width)
    piece_shape = jax.ShapeDtypeStruct(piece, jnp.float32)
    *near, top = pl.pallas_call(
        partial(column_inverse_kernel, row_total),
        grid=(STEPS + 1,),
        in_specs=[
            whole(pltpu.SMEM),
            anywhere,
            pl.BlockSpec((STEP, 128), lambda i: (jnp.maximum(i - 1, 0), 0)),
            pl.BlockSpec((1,) + inv_col.shape[1:], lambda i: (jnp.minimum(i, STEPS - 1), 0, 0)),
        ],
        out_specs=[anywhere] * row_total + [whole()],
        out_shape=[piece_shape] * row_total + [jax.ShapeDtypeStruct((8, width), jnp.float32)],
        scratch_shapes=[
            pltpu.VMEM((STEPS, row_total, 2, blocks, STEP, width), jnp.float32),
            pltpu.VMEM((RES, total_rows, width), jnp.float32),
            pltpu.VMEM((RES // many, inv_col.shape[2], many * width), jnp.bfloat16),
            pltpu.VMEM((STEPS, RES, 2 * STEP, width), jnp.float32),
            pltpu.SemaphoreType.DMA((RES // many,)),
            pltpu.SemaphoreType.DMA((2 * STEPS * row_total,)),
        ],
        compiler_params=params(56),
        name="column_inverse",
    )(place_row, lines, twist_col, inv_col)

    near = exchange(near, "row")
    peak_sq = jnp.max(top)
    for axis, total in (("col", col_total), ("row", row_total)):
        shift = 1
        while shift < total:
            partner = [(i, i ^ shift) for i in range(total)]
            peak_sq = jnp.maximum(peak_sq, lax.ppermute(peak_sq, axis, partner))
            shift *= 2
    if width != 128:
        near = jnp.take(jnp.stack(near), jnp.arange(row_total) ^ place_row[0], axis=0)
        near = near.transpose(1, 2, 3, 0, 4).reshape(2, height, tile_width)
        odd_cell = (jnp.arange(height)[:, None] + jnp.arange(tile_width)[None, :]) % 2
        cell_sign = (1 - 2 * odd_cell).astype(jnp.float32)
        return encode(near[0], near[1], peak_sq, cell_sign)
    tile_shape = jax.ShapeDtypeStruct((height, tile_width), jnp.float32)
    tile = pltpu.VMEM((blocks, INNER, tile_width), jnp.float32)
    return pl.pallas_call(
        partial(encode_kernel, row_total),
        in_specs=[whole(pltpu.SMEM)] * 2 + [whole()] * row_total,
        out_specs=[anywhere] * 2,
        out_shape=[tile_shape, tile_shape],
        scratch_shapes=[tile, tile, pltpu.SemaphoreType.DMA((2 * blocks,))],
        compiler_params=params(16),
        name="encode",
    )(place_row, peak_sq.reshape(1), *near)


def solution(mesh):
    in_specs = (P("row", "col"), P("row", "col"))
    out_specs = (P("row", "col"), P("row", "col"))
    return jax.shard_map(body, mesh=mesh, in_specs=in_specs, out_specs=out_specs, check_vma=False)
```

```python
from functools import partial
import math

import jax
import jax.numpy as jnp
import ml_dtypes
import numpy as np
from jax import lax
from jax.experimental import pallas as pl
from jax.experimental.pallas import tpu as pltpu
from jax.sharding import PartitionSpec as P

N = 4096
PAD = 2 * N
wavelength = 5.2e-07
distance = 0.2
INNER = 256
SLABS = N // INNER
RES = PAD // INNER
HALF = 40
CHUNKS = 2
CHUNK = INNER // CHUNKS
STEPS = 2
STEP = CHUNK // STEPS
SPARE = 8


def optics(padded_side):
    pitch = 2e-06 * math.sqrt(8192.0 / padded_side)
    extent = padded_side * pitch
    ratio_sq = (wavelength / extent) ** 2
    band_limit = extent / (wavelength * math.sqrt((2.0 * distance / extent) ** 2 + 1.0))
    return (ratio_sq, band_limit)


RATIO_SQ, LIMIT = optics(PAD)
assert RES * HALF - RES // 2 + RES > LIMIT and RES * HALF + RES // 2 > LIMIT


def residue(u):
    return u if u < RES // 2 else u - RES


def split16(table):
    table = np.asarray(table, np.float64)
    high = table.astype(np.float32).astype(ml_dtypes.bfloat16)
    low = (table - high.astype(np.float64)).astype(np.float32).astype(ml_dtypes.bfloat16)
    return high, low


def row_order(groups, tail):
    rows = []
    for group in range(groups):
        size = 4 if tail and group == groups - 1 else 8
        for part in range(2):
            for s in range(size):
                rows.append((part, group * 8 + s - HALF))
    return rows


def column_tables(groups, tail):
    q = np.arange(INNER)
    rows = row_order(groups, tail)
    forward = np.zeros((len(rows), 2, INNER))
    inverse = np.zeros((2, INNER, len(rows)))
    for at, (part, k1) in enumerate(rows):
        if abs(k1) > HALF:
            continue
        angle = 2.0 * np.pi * ((k1 * q) % INNER) / INNER
        c, s = np.cos(angle), np.sin(angle)
        forward[at] = (c, s) if part == 0 else (-s, c)
        inverse[:, :, at] = (c, s) if part == 0 else (-s, c)
    forward = forward.reshape(-1, 2, CHUNKS, CHUNK // 8, 8).transpose(2, 0, 3, 1, 4)
    forward = np.concatenate(split16(forward.reshape(CHUNKS, len(rows), 2 * CHUNK)), axis=1)
    inverse = inverse.reshape(2, CHUNKS * STEPS, STEP, -1).transpose(1, 0, 2, 3)
    high, low = split16(inverse.reshape(CHUNKS * STEPS, 2 * STEP, len(rows)))
    inverse = np.concatenate([high, high, low], axis=2)
    inverse = np.pad(inverse, ((0, 0), (0, 0), (0, -3 * len(rows) % 16)))
    return forward, inverse


def line_tables():
    q = np.arange(INNER)
    forward = np.zeros((2 * INNER, 256))
    inverse = np.zeros((256, 2 * INNER))
    for lane in range(2 * HALF + 1):
        angle = 2.0 * np.pi * (((lane - HALF) * q) % INNER) / INNER
        c, s = np.cos(angle), np.sin(angle)
        forward[:INNER, lane], forward[INNER:, lane] = c, s
        forward[:INNER, 128 + lane], forward[INNER:, 128 + lane] = -s, c
        inverse[lane, :INNER], inverse[lane, INNER:] = c, s
        inverse[128 + lane, :INNER], inverse[128 + lane, INNER:] = -s, c
    return split16(forward) + split16(inverse)


def twist_table():
    q = np.arange(INNER) + N // 2
    k0 = np.arange(RES // 2 + 1)
    angle = 2.0 * np.pi * ((k0[:, None] * q[None, :]) % PAD) / PAD
    return np.cos(angle).astype(np.float32), (-np.sin(angle)).astype(np.float32)


def turn(value, num, den):
    re, im = value
    num = num % den
    eighth = 8 * num
    if num == 0:
        return re, im
    if 2 * num == den:
        return -re, -im
    if 4 * num == den:
        return -im, re
    if 4 * num == 3 * den:
        return im, -re
    if eighth % den == 0:
        root = np.float32(math.sqrt(0.5))
        kind = eighth // den
        if kind == 1:
            return (re - im) * root, (re + im) * root
        if kind == 3:
            return (re + im) * (-root), (re - im) * root
        if kind == 5:
            return (im - re) * root, (re + im) * (-root)
        return (re + im) * root, (im - re) * root
    c = np.float32(math.cos(2.0 * math.pi * num / den))
    s = np.float32(math.sin(2.0 * math.pi * num / den))
    return re * c - im * s, re * s + im * c


def small_dft(get, ids, sign):
    count = len(ids)
    if count == 1:
        return [get(ids[0])]
    even = small_dft(get, ids[0::2], sign)
    odd = small_dft(get, ids[1::2], sign)
    half = count // 2
    first, second = [], []
    for j in range(half):
        re, im = even[j]
        t_re, t_im = turn(odd[j], sign * j, count)
        first.append((re + t_re, im + t_im))
        second.append((re - t_re, im - t_im))
    return first + second


def forward_slabs(get, put):
    ids = list(range(SLABS))
    for v, value in enumerate(small_dft(get, ids, -1)):
        put(2 * v, value)
    for v, value in enumerate(small_dft(lambda n: turn(get(n), -n, RES), ids, -1)):
        put(2 * v + 1, value)


def inverse_slabs(get, put):
    even = small_dft(get, list(range(0, RES, 2)), 1)
    odd = small_dft(get, list(range(1, RES, 2)), 1)
    for n in range(SLABS):
        t_re, t_im = turn(odd[n], n, RES)
        put(n, (even[n][0] + t_re, even[n][1] + t_im))


def twisted(value, u, sign, read):
    re, im = value
    k0 = residue(u)
    if k0 == 0:
        return value
    c, s = read(abs(k0))
    if (k0 < 0) == (sign > 0):
        return re * c + im * s, im * c - re * s
    return re * c - im * s, re * s + im * c


def high_low(value):
    high = value.astype(jnp.bfloat16)
    low = (value - high.astype(jnp.float32)).astype(jnp.bfloat16)
    return high, low


def dot16(left, right):
    return jnp.dot(left, right, preferred_element_type=jnp.float32)


def three_left(stacked, count, high, low):
    both = dot16(stacked[...], high)
    return both[:count] + both[count:] + dot16(stacked[:count], low)


def three_right(stacked, count, high, low):
    both = dot16(stacked, high)
    return both[:count] + both[count:] + dot16(stacked[:count], low)


def column_twist(twist, q0):
    def read(k):
        rows = pl.ds(q0, 8)
        return twist[rows, k : k + 1], twist[rows, 64 + k : 65 + k]

    return read


def column_forward_kernel(count, place, twist, matrix, *refs):
    pieces, refs = refs[:count], refs[count:]
    before, (out, total, high, low, sems) = refs[:-5], refs[-5:]
    width = pieces[0].shape[-1]
    per_source = pieces[0].shape[1]
    many = high.shape[-1] // width
    products = RES // many
    rows_out = out.shape[1]

    def copy_in(p):
        part = pl.ds(p * many, many)
        return pltpu.make_async_copy(before[0].at[part], total.at[part], sems.at[p])

    def copy_out(p):
        part = pl.ds(p * many, many)
        return pltpu.make_async_copy(total.at[part], out.at[part], sems.at[products + p])

    if before:
        for p in range(products):
            copy_in(p).start()

    for here in range(count):

        @pl.when(place[0] == here)
        def _():
            @pl.loop(0, CHUNK // 8)
            def _(t):
                q0 = pl.multiple_of(t * 8, 8)

                def get(n):
                    source, block = divmod(n, per_source)
                    piece = pieces[source ^ here]
                    rows = pl.ds(q0, 8)
                    return piece[0, block, rows, :], piece[1, block, rows, :]

                def put(u, value):
                    item = jnp.concatenate(twisted(value, u, 1, column_twist(twist, q0)), axis=0)
                    rows = pl.ds(pl.multiple_of(t * 16, 16), 16)
                    at = (u // many, rows, pl.ds((u % many) * width, width))
                    high[at], low[at] = high_low(item)

                forward_slabs(get, put)

    @pl.loop(0, products)
    def _(p):
        done = three_left(matrix, rows_out, high[p], low[p])
        if before:
            copy_in(p).wait()
        for part in range(many):
            item = done[:, part * width : (part + 1) * width]
            at = p * many + part
            total[at] = total[at] + item if before else item
        copy_out(p).start()

    for p in range(products):
        copy_out(p).wait()


def column_inverse_kernel(count, place, source, twist, matrix, *refs):
    pieces, (top, near, lines, deep, back, sems, out_sems) = refs[:count], refs[count:]
    width = lines.shape[-1]
    rows_in = lines.shape[1]
    per_dest = near.shape[3]
    many = deep.shape[-1] // width
    now = pl.program_id(0)

    def copy_in(p):
        part = pl.ds(p * many, many)
        return pltpu.make_async_copy(source.at[part], lines.at[part], sems.at[p])

    def product(p, slot):
        done = dot16(matrix[0], deep[p])
        for part in range(many):
            back[slot, p * many + part] = done[:, part * width : (part + 1) * width]

    def prepare(p):
        copy_in(p).wait()
        blocks = [lines[p * many + part] for part in range(many)]
        joined = jnp.concatenate(blocks, axis=1) if many > 1 else blocks[0]
        high = joined.astype(jnp.bfloat16).astype(jnp.float32)
        parts = [high, joined - high, high]
        if deep.shape[1] > 3 * rows_in:
            parts.append(jnp.zeros((deep.shape[1] - 3 * rows_in, many * width), jnp.float32))
        deep[p] = jnp.concatenate(parts, axis=0).astype(jnp.bfloat16)
        product(p, 0)

    def butterflies(t, slot):
        q0 = pl.multiple_of(t * 8, 8)
        largest = []

        def get(u):
            re = back[slot, u, pl.ds(q0, 8), :]
            im = back[slot, u, pl.ds(STEP + q0, 8), :]
            return twisted((re, im), u, -1, column_twist(twist, q0))

        def put(n, value):
            dest, block = divmod(n, per_dest)
            rows = pl.ds(q0, 8)
            near[slot, dest, 0, block, rows, :], near[slot, dest, 1, block, rows, :] = value
            largest.append(value[0] * value[0] + value[1] * value[1])

        inverse_slabs(get, put)
        while len(largest) > 1:
            largest = [jnp.maximum(a, b) for a, b in zip(largest[0::2], largest[1::2])]
        top[...] = jnp.maximum(top[...], largest[0])

    def copies_out(slot):
        copies = []
        for j, piece in enumerate(pieces):
            for part in range(2):
                for block in range(per_dest):
                    at = part * per_dest + block
                    rows = pl.ds(at * CHUNK + slot * STEP, STEP)
                    sem = out_sems.at[(slot * count + j) * 2 * per_dest + at]
                    source_rows = near.at[slot, place[0] ^ j, part, block]
                    copies.append(pltpu.make_async_copy(source_rows, piece.at[rows], sem))
        return copies

    @pl.when(now == 0)
    def _():
        for p in range(RES // many):
            copy_in(p).start()
        top[...] = jnp.zeros_like(top)
        pl.loop(0, RES // many)(prepare)

    for step in range(1, STEPS + 1):

        @pl.when(now == step)
        def _():
            tiles, products = STEP // 8, RES // many
            steps = min(tiles, products)

            @pl.loop(0, steps)
            def _(t):
                for item in range(tiles // steps):
                    butterflies(t * (tiles // steps) + item, step - 1)
                if step < STEPS:
                    for item in range(products // steps):
                        product(t * (products // steps) + item, step)

            for copy in copies_out(step - 1):
                copy.start()
            if step == STEPS:
                for slot in range(STEPS):
                    for copy in copies_out(slot):
                        copy.wait()


def line_kernel(
    order, own, tail, lines, gain_re, gain_im, twist, fwd_high, fwd_low, inv_high, inv_low, out, *scratch
):
    half = RES * 8
    at_end = pl.program_id(0) == pl.num_programs(0) - 1

    def line_twist(side):
        def read(k):
            lanes = pl.ds(side * 128, 128)
            return twist[0, k, :, lanes], twist[1, k, :, lanes]

        return read

    def forward(group, stacked, sides=(0, 1)):
        for side in sides:
            waiting = {}

            def get(m):
                block = order[2 * m + side]
                at = group * 16
                return lines[block, at : at + 8, :], lines[block, at + 8 : at + 16, :]

            def put(u, value):
                waiting[u] = twisted(value, u, 1, line_twist(side))
                v = (u + RES // 2) % RES
                if v in waiting:
                    first = min(u, v)
                    rows = pl.ds(first * 16, 16)
                    rows_low = pl.ds(half + first * 16, 16)
                    for part in range(2):
                        item = jnp.concatenate(
                            [waiting[first][part], waiting[first + RES // 2][part]], axis=0
                        )
                        at = pl.ds(part * INNER + side * 128, 128)
                        stacked[rows, at], stacked[rows_low, at] = high_low(item)

            forward_slabs(get, put)

    def filtered(group, stacked):
        spec = three_right(stacked[...], half, fwd_high[...], fwd_low[...])
        spec_re, spec_im = spec[:, :128], spec[:, 128:]
        g_re, g_im = gain_re[group], gain_im[group]
        mixed = jnp.concatenate(
            [spec_re * g_re - spec_im * g_im, spec_re * g_im + spec_im * g_re], axis=1
        )
        return jnp.concatenate(high_low(mixed), axis=0)

    def unfold(mixed, back):
        back[...] = three_right(mixed, half, inv_high[...], inv_low[...])

    def inverse(group, back, sides=(0, 1)):
        for side in sides:

            def get(u):
                rows = pl.ds((u % (RES // 2)) * 16 + (u // (RES // 2)) * 8, 8)
                re = back[rows, pl.ds(side * 128, 128)]
                im = back[rows, pl.ds(INNER + side * 128, 128)]
                return twisted((re, im), u, -1, line_twist(side))

            def put(m, value):
                block = order[2 * m + side]
                at = group * 16
                out[block, at : at + 8, :], out[block, at + 8 : at + 16, :] = value

            inverse_slabs(get, put)

    if tail:

        @pl.when(at_end)
        def _():
            for block in range(N // 128):
                lines[block, 8:12, :] = lines[block, 4:8, :]

    groups = len(scratch) // 2

    stacked, back = scratch[:groups], scratch[groups:]

    def run(count):
        forward(0, stacked[0])
        for group in range(count):
            mixed = filtered(group, stacked[group])
            if group + 1 < count:
                forward(group + 1, stacked[group + 1], (0,))
            if group > 0:
                inverse(group - 1, back[group - 1], (0,))
            unfold(mixed, back[group])
            if group + 1 < count:
                forward(group + 1, stacked[group + 1], (1,))
            if group > 0:
                inverse(group - 1, back[group - 1], (1,))
        inverse(count - 1, back[count - 1])

    rest = own % groups
    if rest:
        pl.when(jnp.logical_not(at_end))(lambda: run(groups))
        pl.when(at_end)(lambda: run(rest))
    else:
        run(groups)

    if tail:

        @pl.when(at_end)
        def _():
            for block in range(N // 128):
                out[block, 4:8, :] = out[block, 8:12, :]


def gain_kernel(place, gain_re, gain_im):
    k0 = place[0]
    group = place[1] + pl.program_id(0)
    down = lax.broadcasted_iota(jnp.int32, (8, 128), 0)
    across = lax.broadcasted_iota(jnp.int32, (8, 128), 1)
    row = (k0 + RES * (group * 8 + down - HALF)).astype(jnp.float32)
    row_sq = row * row
    row_in = jnp.abs(row) < LIMIT
    for u in range(RES):
        col = (residue(u) + RES * (across - HALF)).astype(jnp.float32)
        square = row_sq + col * col
        scaled = RATIO_SQ * square
        phase = -2.0 * math.pi * distance / wavelength * scaled / (1.0 + jnp.sqrt(1.0 - scaled))
        total = jnp.where(
            row_in & (jnp.abs(col) < LIMIT), jnp.exp(square * (-2.0 / (LIMIT * LIMIT))), 0.0
        )
        quarter = jnp.floor(phase * (2.0 / math.pi) + 0.5)
        left = phase - quarter * 1.5703125
        left = left - quarter * 4.837512969970703125e-4
        left = left - quarter * 7.549789954891882e-8
        sq = left * left
        sine = ((-1.9515295891e-4 * sq + 8.3321608736e-3) * sq - 1.6666654611e-1) * sq * left + left
        cosine = (
            (2.443315711809948e-5 * sq - 1.388731625493765e-3) * sq + 4.166664568298827e-2
        ) * sq * sq - 0.5 * sq + 1.0
        which = quarter.astype(jnp.int32) & 3
        swap = (which & 1) == 1
        cos_part = jnp.where(swap, sine, cosine)
        sin_part = jnp.where(swap, cosine, sine)
        cos_part = jnp.where((which == 1) | (which == 2), -cos_part, cos_part)
        sin_part = jnp.where(which >= 2, -sin_part, sin_part)
        at = (u % (RES // 2)) * 16 + (u // (RES // 2)) * 8
        gain_re[0, at : at + 8, :] = total * cos_part
        gain_im[0, at : at + 8, :] = total * sin_part


def encode(near_real, near_imag, peak_sq, cell_sign):
    square = near_real * near_real + near_imag * near_imag
    root = lax.rsqrt(jnp.maximum(square, 1.2e-38))
    top = lax.rsqrt(peak_sq)
    amp_level = (square * root) * (0.8 * top)
    unit = jnp.minimum(root, 20.0 * top)
    rest = 1.0 - amp_level * amp_level
    level = unit * amp_level
    lift = (rest * lax.rsqrt(rest)) * (unit * cell_sign)
    return (near_real * level + near_imag * lift, near_imag * level - near_real * lift)


def stamp_kernel(peak_sq, *refs):
    count = (len(refs) - 2) // 2
    pieces, tile, sems = refs[count : 2 * count], refs[-2], refs[-1]
    tile[...] = jnp.full(tile.shape, peak_sq[0], jnp.float32)
    copies = []
    for j, piece in enumerate(pieces):
        rows = pl.ds(piece.shape[0] - SPARE, SPARE)
        copies.append(pltpu.make_async_copy(tile, piece.at[rows], sems.at[j]))
    for copy in copies:
        copy.start()
    for copy in copies:
        copy.wait()


def encode_kernel(count, place, peak_sq, *refs):
    pieces, (slm_real, slm_imag, *refs) = refs[: CHUNKS * count], refs[CHUNKS * count :]
    own, (tile_real, tile_imag, own_sems, sems) = refs[:CHUNKS], refs[CHUNKS:]
    blocks, width = tile_real.shape[0], pieces[0].shape[-1]
    fetches = [
        pltpu.make_async_copy(pieces[chunk * count], own[chunk], own_sems.at[chunk])
        for chunk in range(CHUNKS)
    ]
    for fetch in fetches:
        fetch.start()
    top = jnp.full((1, width), peak_sq[0], jnp.float32)
    for piece in pieces[(CHUNKS - 1) * count + 1 :]:
        top = jnp.maximum(top, piece[pl.ds(piece.shape[0] - SPARE, 1), :])
    cell = lax.broadcasted_iota(jnp.int32, (CHUNK, width), 0)
    cell = cell + lax.broadcasted_iota(jnp.int32, (CHUNK, width), 1)
    cell_sign = (1 - 2 * (cell & 1)).astype(jnp.float32)
    for fetch in fetches:
        fetch.wait()

    def copies_out(block):
        rows = pl.ds(block * INNER, INNER)
        return [
            pltpu.make_async_copy(tile.at[block], slm.at[rows], sems.at[2 * block + part])
            for part, (tile, slm) in enumerate(((tile_real, slm_real), (tile_imag, slm_imag)))
        ]

    @pl.loop(0, blocks)
    def _(block):
        for at in range(CHUNKS * count):
            chunk, j = divmod(at, count)
            piece = pieces[at] if j else own[chunk]
            lanes = pl.ds(pl.multiple_of((place[0] ^ j) * width, width), width)
            rows = pl.ds(chunk * CHUNK, CHUNK)
            real = pl.ds(pl.multiple_of(block * CHUNK, CHUNK), CHUNK)
            imag = pl.ds(pl.multiple_of((blocks + block) * CHUNK, CHUNK), CHUNK)
            tile_real[block, rows, lanes], tile_imag[block, rows, lanes] = encode(
                piece[real, :], piece[imag, :], top, cell_sign
            )
        for copy in copies_out(block):
            copy.start()

    for block in range(blocks):
        for copy in copies_out(block):
            copy.wait()


def pack_kernel(place, field_real, field_imag, *refs):
    pieces, sems = refs[:-1], refs[-1]
    width = pieces[0].shape[-1]
    copies = []
    for j in list(range(1, len(pieces))) + [0]:
        lanes = pl.ds(pl.multiple_of((place[0] ^ j) * width, width), width)
        for part, field in enumerate((field_real, field_imag)):
            copies.append(
                pltpu.make_async_copy(
                    field.at[:, :, lanes], pieces[j].at[part], sems.at[2 * j + part]
                )
            )
    for copy in copies:
        copy.start()
    for copy in copies:
        copy.wait()


def exchange(pieces, axis):
    total = len(pieces)
    return [pieces[0]] + [
        lax.ppermute(pieces[j], axis, [(i, i ^ j) for i in range(total)]) for j in range(1, total)
    ]


def params(mebibytes):
    return pltpu.CompilerParams(vmem_limit_bytes=mebibytes << 20)


def cost(megabytes):
    return pl.CostEstimate(flops=0, bytes_accessed=megabytes << 20, transcendentals=0)


def whole(memory=pltpu.VMEM):
    return pl.BlockSpec(memory_space=memory)


def body(field_real, field_imag):
    row_total, col_total = lax.axis_size("row"), lax.axis_size("col")
    devices = row_total * col_total
    device = lax.axis_index("row") * col_total + lax.axis_index("col")
    height, tile_width = field_real.shape
    width = tile_width // row_total
    parts = max(1, devices // RES)
    groups = -(-(2 * HALF + 1) // (8 * parts)) * parts
    own = groups // parts
    tail = parts == 1
    total_rows = groups * 16 - (8 if tail else 0)
    own_rows = total_rows // parts
    many = 4 if width == 128 else 1

    fwd_col, inv_col = column_tables(groups, tail)
    line_fh, line_fl, line_ih, line_il = line_tables()
    twist = np.stack(twist_table())
    twist_line = np.ascontiguousarray(np.broadcast_to(twist[:, :, None], twist.shape[:2] + (8, INNER)))
    twist_col = np.pad(twist, ((0, 0), (0, 64 - twist.shape[1]), (0, 0)))
    twist_col = twist_col.reshape(128, INNER).T.copy()

    u = device // parts
    k0 = jnp.where(u >= RES // 2, u - RES, u)
    place = jnp.stack([k0, (device % parts) * own]).astype(jnp.int32)
    gain_shape = jax.ShapeDtypeStruct((own, RES * 8, 128), jnp.float32)
    gain_spec = pl.BlockSpec((1, RES * 8, 128), lambda g: (g, 0, 0))
    gain_re, gain_im = pl.pallas_call(
        gain_kernel,
        grid=(own,),
        in_specs=[whole(pltpu.SMEM)],
        out_specs=[gain_spec, gain_spec],
        out_shape=[gain_shape, gain_shape],
        compiler_params=params(56),
        name="gain",
    )(place)

    place_row = lax.axis_index("row").reshape(1).astype(jnp.int32)
    blocks = height // INNER
    piece = (2, blocks, CHUNK, width)
    piece_shape = jax.ShapeDtypeStruct(piece, jnp.float32)
    anywhere = whole(pl.ANY)
    if width != 128:
        packed = jnp.stack([field_real, field_imag])
        packed = packed.reshape(2, blocks, CHUNKS, CHUNK, row_total, width).transpose(2, 4, 0, 1, 3, 5)
        packed = jnp.take(packed, jnp.arange(row_total) ^ place_row[0], axis=1)
    lines = []
    for chunk in range(CHUNKS):
        if width == 128:
            pieces = pl.pallas_call(
                pack_kernel,
                grid=(1,),
                in_specs=[whole(pltpu.SMEM)]
                + [pl.BlockSpec((blocks, CHUNK, tile_width), lambda i: (0, chunk, 0))] * 2,
                out_specs=[anywhere] * row_total,
                out_shape=[piece_shape] * row_total,
                scratch_shapes=[pltpu.SemaphoreType.DMA((2 * row_total,))],
                compiler_params=params(56),
                cost_estimate=cost(4),
                name="pack",
            )(
                place_row,
                field_real.reshape(blocks, INNER, tile_width),
                field_imag.reshape(blocks, INNER, tile_width),
            )
        else:
            pieces = [packed[chunk, j] for j in range(row_total)]
        pieces = exchange(pieces, "row")
        rows = slice(chunk * CHUNK, (chunk + 1) * CHUNK)
        slab = pltpu.VMEM((RES // many, 2 * CHUNK, many * width), jnp.bfloat16)
        lines = [
            pl.pallas_call(
                partial(column_forward_kernel, row_total),
                in_specs=[whole(pltpu.SMEM)] + [whole()] * (2 + row_total) + [anywhere] * len(lines),
                out_specs=anywhere,
                out_shape=jax.ShapeDtypeStruct((RES, total_rows, width), jnp.float32),
                scratch_shapes=[
                    pltpu.VMEM((RES, total_rows, width), jnp.float32),
                    slab,
                    slab,
                    pltpu.SemaphoreType.DMA((2 * RES // many,)),
                ],
                compiler_params=params(20),
                cost_estimate=cost(20),
                name="column_forward",
            )(place_row, twist_col[rows], fwd_col[chunk], *pieces, *lines)
        ]
    (lines,) = lines

    lines = lines.reshape(devices, own_rows, width)
    lines = lax.all_to_all(lines, ("row", "col"), split_axis=0, concat_axis=0, tiled=True)
    if width == 128:
        order = tuple((b % row_total) * col_total + b // row_total for b in range(N // 128))
    else:
        order = tuple(range(N // 128))
        lines = lines.reshape(row_total, col_total, own_rows, width).transpose(2, 1, 0, 3)
        lines = lines.reshape(own_rows, N // 128, 128).transpose(1, 0, 2)

    at_once = 2
    line_grain = pl.BlockSpec((N // 128, 16 * at_once, 128), lambda i: (0, i, 0))
    gain_grain = pl.BlockSpec((at_once, RES * 8, 128), lambda i: (i, 0, 0))
    lines = pl.pallas_call(
        partial(line_kernel, order, own, tail),
        grid=(-(-own // at_once),),
        in_specs=[line_grain, gain_grain, gain_grain] + [whole()] * 5,
        out_specs=line_grain,
        out_shape=jax.ShapeDtypeStruct((N // 128, own_rows, 128), jnp.float32),
        scratch_shapes=[pltpu.VMEM((2 * RES * 8, 2 * INNER), jnp.bfloat16)] * at_once
        + [pltpu.VMEM((RES * 8, 2 * INNER), jnp.float32)] * at_once,
        compiler_params=params(52),
        name="line",
    )(lines, gain_re, gain_im, twist_line, line_fh, line_fl, line_ih, line_il)

    if width != 128:
        lines = lines.transpose(1, 0, 2).reshape(own_rows, col_total, row_total, width)
        lines = lines.transpose(2, 1, 0, 3).reshape(devices, own_rows, width)
    lines = lax.all_to_all(lines, ("row", "col"), split_axis=0, concat_axis=0, tiled=True)
    lines = lines.reshape(RES, total_rows, width)

    near, tops = [], []
    for chunk in range(CHUNKS):
        spare = SPARE if chunk == CHUNKS - 1 else 0
        piece_shape = jax.ShapeDtypeStruct((2 * blocks * CHUNK + spare, width), jnp.float32)
        steps = slice(chunk * STEPS, (chunk + 1) * STEPS)
        *pieces, top = pl.pallas_call(
            partial(column_inverse_kernel, row_total),
            grid=(STEPS + 1,),
            in_specs=[
                whole(pltpu.SMEM),
                anywhere,
                pl.BlockSpec((STEP, 128), lambda i: (chunk * STEPS + jnp.maximum(i - 1, 0), 0)),
                pl.BlockSpec((1,) + inv_col.shape[1:], lambda i: (jnp.minimum(i, STEPS - 1), 0, 0)),
            ],
            out_specs=[anywhere] * row_total + [whole()],
            out_shape=[piece_shape] * row_total + [jax.ShapeDtypeStruct((8, width), jnp.float32)],
            scratch_shapes=[
                pltpu.VMEM((STEPS, row_total, 2, blocks, STEP, width), jnp.float32),
                pltpu.VMEM((RES, total_rows, width), jnp.float32),
                pltpu.VMEM((RES // many, inv_col.shape[2], many * width), jnp.bfloat16),
                pltpu.VMEM((STEPS, RES, 2 * STEP, width), jnp.float32),
                pltpu.SemaphoreType.DMA((RES // many,)),
                pltpu.SemaphoreType.DMA((STEPS * row_total * 2 * blocks,)),
            ],
            compiler_params=params(56),
            cost_estimate=cost(60),
            name="column_inverse",
        )(place_row, lines, twist_col, inv_col[steps])
        near.append(pieces)
        tops.append(top)
    near[0] = exchange(near[0], "row")
    peak_sq = jnp.max(jnp.maximum(*tops))
    shift = 1
    while shift < col_total:
        partner = [(i, i ^ shift) for i in range(col_total)]
        peak_sq = jnp.maximum(peak_sq, lax.ppermute(peak_sq, "col", partner))
        shift *= 2
    near = lax.optimization_barrier(near)
    peak_own = peak_sq.reshape(1)
    others = row_total - 1
    near[1][1:] = pl.pallas_call(
        stamp_kernel,
        in_specs=[whole(pltpu.SMEM)] + [anywhere] * others,
        out_specs=[anywhere] * others,
        out_shape=[piece_shape] * others,
        scratch_shapes=[
            pltpu.VMEM((SPARE, width), jnp.float32),
            pltpu.SemaphoreType.DMA((others,)),
        ],
        input_output_aliases={1 + j: j for j in range(others)},
        compiler_params=params(56),
        name="stamp",
    )(peak_own, *near[1][1:])
    near[1] = exchange(near[1], "row")
    if width != 128:
        for piece in near[1][1:]:
            peak_sq = jnp.maximum(peak_sq, piece[-1, 0])
        near = jnp.stack([jnp.stack([piece[: 2 * blocks * CHUNK] for piece in pieces]) for pieces in near])
        near = jnp.take(near, jnp.arange(row_total) ^ place_row[0], axis=1)
        near = near.reshape(CHUNKS, row_total, 2, blocks, CHUNK, width)
        near = near.transpose(2, 3, 0, 4, 1, 5).reshape(2, height, tile_width)
        odd_cell = (jnp.arange(height)[:, None] + jnp.arange(tile_width)[None, :]) % 2
        cell_sign = (1 - 2 * odd_cell).astype(jnp.float32)
        return encode(near[0], near[1], peak_sq, cell_sign)
    tile_shape = jax.ShapeDtypeStruct((height, tile_width), jnp.float32)
    tile = pltpu.VMEM((blocks, INNER, tile_width), jnp.float32)
    return pl.pallas_call(
        partial(encode_kernel, row_total),
        in_specs=[whole(pltpu.SMEM)] * 2 + ([anywhere] + [whole()] * others) * CHUNKS,
        out_specs=[anywhere] * 2,
        out_shape=[tile_shape, tile_shape],
        scratch_shapes=[pltpu.VMEM(pieces[0].shape, jnp.float32) for pieces in near]
        + [tile, tile, pltpu.SemaphoreType.DMA((CHUNKS,)), pltpu.SemaphoreType.DMA((2 * blocks,))],
        compiler_params=params(16),
        name="encode",
    )(place_row, peak_own, *near[0], *near[1])


def solution(mesh):
    in_specs = (P("row", "col"), P("row", "col"))
    out_specs = (P("row", "col"), P("row", "col"))
    return jax.shard_map(body, mesh=mesh, in_specs=in_specs, out_specs=out_specs, check_vma=False)
```

```python
from functools import partial
import math

import jax
import jax.numpy as jnp
import ml_dtypes
import numpy as np
from jax import lax
from jax.experimental import pallas as pl
from jax.experimental.pallas import tpu as pltpu
from jax.sharding import PartitionSpec as P

N = 4096
PAD = 2 * N
wavelength = 5.2e-07
distance = 0.2
INNER = 256
SLABS = N // INNER
RES = PAD // INNER
HALF = 40
CHUNKS = 2
CHUNK = INNER // CHUNKS
SPARE = 8


def optics(padded_side):
    pitch = 2e-06 * math.sqrt(8192.0 / padded_side)
    extent = padded_side * pitch
    ratio_sq = (wavelength / extent) ** 2
    band_limit = extent / (wavelength * math.sqrt((2.0 * distance / extent) ** 2 + 1.0))
    return (ratio_sq, band_limit)


RATIO_SQ, LIMIT = optics(PAD)
assert RES * HALF - RES // 2 + RES > LIMIT and RES * HALF + RES // 2 > LIMIT


def residue(u):
    return u if u < RES // 2 else u - RES


def split16(table):
    table = np.asarray(table, np.float64)
    high = table.astype(np.float32).astype(ml_dtypes.bfloat16)
    low = (table - high.astype(np.float64)).astype(np.float32).astype(ml_dtypes.bfloat16)
    return high, low


def row_order(groups, tail):
    rows = []
    for group in range(groups):
        size = 4 if tail and group == groups - 1 else 8
        for part in range(2):
            for s in range(size):
                rows.append((part, group * 8 + s - HALF))
    return rows


def column_tables(groups, tail):
    q = np.arange(INNER)
    rows = row_order(groups, tail)
    forward = np.zeros((len(rows), 2, INNER))
    inverse = np.zeros((2, INNER, len(rows)))
    for at, (part, k1) in enumerate(rows):
        if abs(k1) > HALF:
            continue
        angle = 2.0 * np.pi * ((k1 * q) % INNER) / INNER
        c, s = np.cos(angle), np.sin(angle)
        forward[at] = (c, s) if part == 0 else (-s, c)
        inverse[:, :, at] = (c, s) if part == 0 else (-s, c)
    forward = forward.reshape(-1, 2, CHUNKS, CHUNK // 8, 8).transpose(2, 0, 3, 1, 4)
    forward = np.concatenate(split16(forward.reshape(CHUNKS, len(rows), 2 * CHUNK)), axis=1)
    inverse = inverse.reshape(2, CHUNKS, CHUNK, -1).transpose(1, 0, 2, 3)
    high, low = split16(inverse.reshape(CHUNKS, 2 * CHUNK, len(rows)))
    inverse = np.concatenate([high, high, low], axis=2)
    inverse = np.pad(inverse, ((0, 0), (0, 0), (0, -3 * len(rows) % 16)))
    return forward, inverse


def line_tables():
    q = np.arange(INNER)
    forward = np.zeros((2 * INNER, 256))
    inverse = np.zeros((256, 2 * INNER))
    for lane in range(2 * HALF + 1):
        angle = 2.0 * np.pi * (((lane - HALF) * q) % INNER) / INNER
        c, s = np.cos(angle), np.sin(angle)
        forward[:INNER, lane], forward[INNER:, lane] = c, s
        forward[:INNER, 128 + lane], forward[INNER:, 128 + lane] = -s, c
        inverse[lane, :INNER], inverse[lane, INNER:] = c, s
        inverse[128 + lane, :INNER], inverse[128 + lane, INNER:] = -s, c
    return split16(forward) + split16(inverse)


def twist_table():
    q = np.arange(INNER) + N // 2
    k0 = np.arange(RES // 2 + 1)
    angle = 2.0 * np.pi * ((k0[:, None] * q[None, :]) % PAD) / PAD
    return np.cos(angle).astype(np.float32), (-np.sin(angle)).astype(np.float32)


def turn(value, num, den):
    re, im = value
    num = num % den
    eighth = 8 * num
    if num == 0:
        return re, im
    if 2 * num == den:
        return -re, -im
    if 4 * num == den:
        return -im, re
    if 4 * num == 3 * den:
        return im, -re
    if eighth % den == 0:
        root = np.float32(math.sqrt(0.5))
        kind = eighth // den
        if kind == 1:
            return (re - im) * root, (re + im) * root
        if kind == 3:
            return (re + im) * (-root), (re - im) * root
        if kind == 5:
            return (im - re) * root, (re + im) * (-root)
        return (re + im) * root, (im - re) * root
    c = np.float32(math.cos(2.0 * math.pi * num / den))
    s = np.float32(math.sin(2.0 * math.pi * num / den))
    return re * c - im * s, re * s + im * c


def small_dft(get, ids, sign):
    count = len(ids)
    if count == 1:
        return [get(ids[0])]
    even = small_dft(get, ids[0::2], sign)
    odd = small_dft(get, ids[1::2], sign)
    half = count // 2
    first, second = [], []
    for j in range(half):
        re, im = even[j]
        t_re, t_im = turn(odd[j], sign * j, count)
        first.append((re + t_re, im + t_im))
        second.append((re - t_re, im - t_im))
    return first + second


def forward_slabs(get, put):
    ids = list(range(SLABS))
    for v, value in enumerate(small_dft(get, ids, -1)):
        put(2 * v, value)
    for v, value in enumerate(small_dft(lambda n: turn(get(n), -n, RES), ids, -1)):
        put(2 * v + 1, value)


def inverse_slabs(get, put):
    even = small_dft(get, list(range(0, RES, 2)), 1)
    odd = small_dft(get, list(range(1, RES, 2)), 1)
    for n in range(SLABS):
        t_re, t_im = turn(odd[n], n, RES)
        put(n, (even[n][0] + t_re, even[n][1] + t_im))


def twisted(value, u, sign, read):
    re, im = value
    k0 = residue(u)
    if k0 == 0:
        return value
    c, s = read(abs(k0))
    if (k0 < 0) == (sign > 0):
        return re * c + im * s, im * c - re * s
    return re * c - im * s, re * s + im * c


def high_low(value):
    high = value.astype(jnp.bfloat16)
    low = (value - high.astype(jnp.float32)).astype(jnp.bfloat16)
    return high, low


def dot16(left, right):
    return jnp.dot(left, right, preferred_element_type=jnp.float32)


def three_left(stacked, count, high, low):
    both = dot16(stacked[...], high)
    return both[:count] + both[count:] + dot16(stacked[:count], low)


def three_right(stacked, count, high, low):
    both = dot16(stacked, high)
    return both[:count] + both[count:] + dot16(stacked[:count], low)


def column_twist(twist, q0):
    def read(k):
        rows = pl.ds(q0, 8)
        return twist[rows, k : k + 1], twist[rows, 64 + k : 65 + k]

    return read


def column_forward_kernel(count, place, twist, matrix, *refs):
    pieces, refs = refs[:count], refs[count:]
    before, (out, total, high, low, sems) = refs[:-5], refs[-5:]
    width = pieces[0].shape[-1]
    per_source = pieces[0].shape[1]
    many = high.shape[-1] // width
    products = RES // many
    rows_out = out.shape[1]

    def copy_in(p):
        part = pl.ds(p * many, many)
        return pltpu.make_async_copy(before[0].at[part], total.at[part], sems.at[p])

    def copy_out(p):
        part = pl.ds(p * many, many)
        return pltpu.make_async_copy(total.at[part], out.at[part], sems.at[products + p])

    if before:
        for p in range(products):
            copy_in(p).start()

    for here in range(count):

        @pl.when(place[0] == here)
        def _():
            @pl.loop(0, CHUNK // 8)
            def _(t):
                q0 = pl.multiple_of(t * 8, 8)

                def get(n):
                    source, block = divmod(n, per_source)
                    piece = pieces[source ^ here]
                    rows = pl.ds(q0, 8)
                    return piece[0, block, rows, :], piece[1, block, rows, :]

                def put(u, value):
                    item = jnp.concatenate(twisted(value, u, 1, column_twist(twist, q0)), axis=0)
                    rows = pl.ds(pl.multiple_of(t * 16, 16), 16)
                    at = (u // many, rows, pl.ds((u % many) * width, width))
                    high[at], low[at] = high_low(item)

                forward_slabs(get, put)

    @pl.loop(0, products)
    def _(p):
        done = three_left(matrix, rows_out, high[p], low[p])
        if before:
            copy_in(p).wait()
        for part in range(many):
            item = done[:, part * width : (part + 1) * width]
            at = p * many + part
            total[at] = total[at] + item if before else item
        copy_out(p).start()

    for p in range(products):
        copy_out(p).wait()


def column_inverse_kernel(count, place, source, twist, matrix, *refs):
    pieces, (top, near, lines, deep, back, sems, out_sems) = refs[:count], refs[count:]
    width = lines.shape[-1]
    rows_in = lines.shape[1]
    per_dest = near.shape[2]
    many = deep.shape[-1] // width

    def copy_in(p):
        part = pl.ds(p * many, many)
        return pltpu.make_async_copy(source.at[part], lines.at[part], sems.at[p])

    def copies_out(part):
        size = CHUNK // 2
        copies = []
        for j, piece in enumerate(pieces):
            for at in range(2 * per_dest):
                here = near.at[place[0] ^ j, at // per_dest, at % per_dest, pl.ds(part * size, size)]
                there = piece.at[pl.ds(at * CHUNK + part * size, size)]
                sem = out_sems.at[(part * count + j) * 2 * per_dest + at]
                copies.append(pltpu.make_async_copy(here, there, sem))
        return copies

    for p in range(RES // many):
        copy_in(p).start()
    top[...] = jnp.zeros_like(top)

    @pl.loop(0, RES // many)
    def _(p):
        copy_in(p).wait()
        blocks = [lines[p * many + part] for part in range(many)]
        joined = jnp.concatenate(blocks, axis=1) if many > 1 else blocks[0]
        high = joined.astype(jnp.bfloat16).astype(jnp.float32)
        parts = [high, joined - high, high]
        if deep.shape[1] > 3 * rows_in:
            parts.append(jnp.zeros((deep.shape[1] - 3 * rows_in, many * width), jnp.float32))
        deep[p] = jnp.concatenate(parts, axis=0).astype(jnp.bfloat16)
        done = dot16(matrix[...], deep[p])
        for part in range(many):
            back[p * many + part] = done[:, part * width : (part + 1) * width]

    def butterflies(t):
        q0 = pl.multiple_of(t * 8, 8)
        largest = []

        def get(u):
            re = back[u, pl.ds(q0, 8), :]
            im = back[u, pl.ds(CHUNK + q0, 8), :]
            return twisted((re, im), u, -1, column_twist(twist, q0))

        def put(n, value):
            dest, block = divmod(n, per_dest)
            rows = pl.ds(q0, 8)
            near[dest, 0, block, rows, :], near[dest, 1, block, rows, :] = value
            largest.append(value[0] * value[0] + value[1] * value[1])

        inverse_slabs(get, put)
        while len(largest) > 1:
            largest = [jnp.maximum(a, b) for a, b in zip(largest[0::2], largest[1::2])]
        top[...] = jnp.maximum(top[...], largest[0])

    for part in range(2):
        tiles = CHUNK // 16
        pl.loop(part * tiles, (part + 1) * tiles)(butterflies)
        for copy in copies_out(part):
            copy.start()
    for part in range(2):
        for copy in copies_out(part):
            copy.wait()


def line_kernel(
    order, own, tail, lines, gain_re, gain_im, twist, fwd_high, fwd_low, inv_high, inv_low, out, stacked, back
):
    half = RES * 8
    at_end = pl.program_id(0) == pl.num_programs(0) - 1
    tail_at = (own - 1) % gain_re.shape[0] * 16

    def line_twist(side):
        def read(k):
            lanes = pl.ds(side * 128, 128)
            return twist[0, k, :, lanes], twist[1, k, :, lanes]

        return read

    def forward(group, count):
        for side in range(2):
            waiting = {}

            def get(m):
                block = order[2 * m + side]
                at = group * 16
                return lines[block, at : at + 8, :], lines[block, at + 8 : at + 16, :]

            def put(u, value):
                waiting[u] = twisted(value, u, 1, line_twist(side))
                v = (u + RES // 2) % RES
                if v in waiting:
                    first = min(u, v)
                    rows = pl.ds(group * half + first * 16, 16)
                    rows_low = pl.ds((count + group) * half + first * 16, 16)
                    for part in range(2):
                        item = jnp.concatenate(
                            [waiting[first][part], waiting[first + RES // 2][part]], axis=0
                        )
                        at = pl.ds(part * INNER + side * 128, 128)
                        stacked[rows, at], stacked[rows_low, at] = high_low(item)

            forward_slabs(get, put)

    def middle(count):
        rows = count * half
        spec = three_right(stacked[: 2 * rows], rows, fwd_high[...], fwd_low[...])
        spec_re, spec_im = spec[:, :128], spec[:, 128:]
        g_re = gain_re[:count].reshape(rows, 128)
        g_im = gain_im[:count].reshape(rows, 128)
        mixed = jnp.concatenate(
            [spec_re * g_re - spec_im * g_im, spec_re * g_im + spec_im * g_re], axis=1
        )
        mixed = jnp.concatenate(high_low(mixed), axis=0)
        back[:rows] = three_right(mixed, rows, inv_high[...], inv_low[...])

    def inverse(group):
        for side in range(2):

            def get(u):
                rows = pl.ds(group * half + (u % (RES // 2)) * 16 + (u // (RES // 2)) * 8, 8)
                re = back[rows, pl.ds(side * 128, 128)]
                im = back[rows, pl.ds(INNER + side * 128, 128)]
                return twisted((re, im), u, -1, line_twist(side))

            def put(m, value):
                block = order[2 * m + side]
                at = group * 16
                out[block, at : at + 8, :], out[block, at + 8 : at + 16, :] = value

            inverse_slabs(get, put)

    def run(count):
        for group in range(count):
            forward(group, count)
        middle(count)
        for group in range(count):
            inverse(group)

    if tail:

        @pl.when(at_end)
        def _():
            for block in range(N // 128):
                lines[block, tail_at + 8 : tail_at + 12, :] = lines[block, tail_at + 4 : tail_at + 8, :]

    groups = gain_re.shape[0]
    rest = own % groups
    if rest:
        pl.when(jnp.logical_not(at_end))(lambda: run(groups))
        pl.when(at_end)(lambda: run(rest))
    else:
        run(groups)

    if tail:

        @pl.when(at_end)
        def _():
            for block in range(N // 128):
                out[block, tail_at + 4 : tail_at + 8, :] = out[block, tail_at + 8 : tail_at + 12, :]


def gain_kernel(place, gain_re, gain_im):
    k0 = place[0]
    group = place[1] + pl.program_id(0)
    down = lax.broadcasted_iota(jnp.int32, (8, 128), 0)
    across = lax.broadcasted_iota(jnp.int32, (8, 128), 1)
    row = (k0 + RES * (group * 8 + down - HALF)).astype(jnp.float32)
    row_sq = row * row
    row_in = jnp.abs(row) < LIMIT
    for u in range(RES):
        col = (residue(u) + RES * (across - HALF)).astype(jnp.float32)
        square = row_sq + col * col
        scaled = RATIO_SQ * square
        phase = -2.0 * math.pi * distance / wavelength * scaled / (1.0 + jnp.sqrt(1.0 - scaled))
        total = jnp.where(
            row_in & (jnp.abs(col) < LIMIT), jnp.exp(square * (-2.0 / (LIMIT * LIMIT))), 0.0
        )
        quarter = jnp.floor(phase * (2.0 / math.pi) + 0.5)
        left = phase - quarter * 1.5703125
        left = left - quarter * 4.837512969970703125e-4
        left = left - quarter * 7.549789954891882e-8
        sq = left * left
        sine = ((-1.9515295891e-4 * sq + 8.3321608736e-3) * sq - 1.6666654611e-1) * sq * left + left
        cosine = (
            (2.443315711809948e-5 * sq - 1.388731625493765e-3) * sq + 4.166664568298827e-2
        ) * sq * sq - 0.5 * sq + 1.0
        which = quarter.astype(jnp.int32) & 3
        swap = (which & 1) == 1
        cos_part = jnp.where(swap, sine, cosine)
        sin_part = jnp.where(swap, cosine, sine)
        cos_part = jnp.where((which == 1) | (which == 2), -cos_part, cos_part)
        sin_part = jnp.where(which >= 2, -sin_part, sin_part)
        at = (u % (RES // 2)) * 16 + (u // (RES // 2)) * 8
        gain_re[0, at : at + 8, :] = total * cos_part
        gain_im[0, at : at + 8, :] = total * sin_part


def encode(near_real, near_imag, peak_sq, cell_sign):
    square = near_real * near_real + near_imag * near_imag
    root = lax.rsqrt(jnp.maximum(square, 1.2e-38))
    top = lax.rsqrt(peak_sq)
    amp_level = (square * root) * (0.8 * top)
    unit = jnp.minimum(root, 20.0 * top)
    rest = 1.0 - amp_level * amp_level
    level = unit * amp_level
    lift = (rest * lax.rsqrt(rest)) * (unit * cell_sign)
    return (near_real * level + near_imag * lift, near_imag * level - near_real * lift)


def stamp_kernel(peak_sq, *refs):
    count = (len(refs) - 2) // 2
    pieces, tile, sems = refs[count : 2 * count], refs[-2], refs[-1]
    tile[...] = jnp.full(tile.shape, peak_sq[0], jnp.float32)
    copies = []
    for j, piece in enumerate(pieces):
        rows = pl.ds(piece.shape[0] - SPARE, SPARE)
        copies.append(pltpu.make_async_copy(tile, piece.at[rows], sems.at[j]))
    for copy in copies:
        copy.start()
    for copy in copies:
        copy.wait()


def encode_kernel(count, place, peak_sq, *refs):
    pieces, (slm_real, slm_imag, *refs) = refs[: CHUNKS * count], refs[CHUNKS * count :]
    own, (tile_real, tile_imag, own_sems, sems) = refs[:CHUNKS], refs[CHUNKS:]
    blocks, width = tile_real.shape[0], pieces[0].shape[-1]
    fetches = [
        pltpu.make_async_copy(pieces[chunk * count], own[chunk], own_sems.at[chunk])
        for chunk in range(CHUNKS)
    ]
    for fetch in fetches:
        fetch.start()
    top = jnp.full((1, width), peak_sq[0], jnp.float32)
    for piece in pieces[(CHUNKS - 1) * count + 1 :]:
        top = jnp.maximum(top, piece[pl.ds(piece.shape[0] - SPARE, 1), :])
    cell = lax.broadcasted_iota(jnp.int32, (CHUNK, width), 0)
    cell = cell + lax.broadcasted_iota(jnp.int32, (CHUNK, width), 1)
    cell_sign = (1 - 2 * (cell & 1)).astype(jnp.float32)
    for fetch in fetches:
        fetch.wait()

    def copies_out(block):
        rows = pl.ds(block * INNER, INNER)
        return [
            pltpu.make_async_copy(tile.at[block], slm.at[rows], sems.at[2 * block + part])
            for part, (tile, slm) in enumerate(((tile_real, slm_real), (tile_imag, slm_imag)))
        ]

    @pl.loop(0, blocks)
    def _(block):
        for at in range(CHUNKS * count):
            chunk, j = divmod(at, count)
            piece = pieces[at] if j else own[chunk]
            lanes = pl.ds(pl.multiple_of((place[0] ^ j) * width, width), width)
            rows = pl.ds(chunk * CHUNK, CHUNK)
            real = pl.ds(pl.multiple_of(block * CHUNK, CHUNK), CHUNK)
            imag = pl.ds(pl.multiple_of((blocks + block) * CHUNK, CHUNK), CHUNK)
            tile_real[block, rows, lanes], tile_imag[block, rows, lanes] = encode(
                piece[real, :], piece[imag, :], top, cell_sign
            )
        for copy in copies_out(block):
            copy.start()

    for block in range(blocks):
        for copy in copies_out(block):
            copy.wait()


def pack_kernel(place, field_real, field_imag, *refs):
    pieces, sems = refs[:-1], refs[-1]
    width = pieces[0].shape[-1]
    copies = []
    for j in list(range(1, len(pieces))) + [0]:
        lanes = pl.ds(pl.multiple_of((place[0] ^ j) * width, width), width)
        for part, field in enumerate((field_real, field_imag)):
            copies.append(
                pltpu.make_async_copy(
                    field.at[:, :, lanes], pieces[j].at[part], sems.at[2 * j + part]
                )
            )
    for copy in copies:
        copy.start()
    for copy in copies:
        copy.wait()


def exchange(pieces, axis):
    total = len(pieces)
    return [pieces[0]] + [
        lax.ppermute(pieces[j], axis, [(i, i ^ j) for i in range(total)]) for j in range(1, total)
    ]


def params(mebibytes):
    return pltpu.CompilerParams(vmem_limit_bytes=mebibytes << 20)


def cost(megabytes):
    return pl.CostEstimate(flops=0, bytes_accessed=megabytes << 20, transcendentals=0)


def whole(memory=pltpu.VMEM):
    return pl.BlockSpec(memory_space=memory)


def body(field_real, field_imag):
    row_total, col_total = lax.axis_size("row"), lax.axis_size("col")
    devices = row_total * col_total
    device = lax.axis_index("row") * col_total + lax.axis_index("col")
    height, tile_width = field_real.shape
    width = tile_width // row_total
    parts = max(1, devices // RES)
    groups = -(-(2 * HALF + 1) // (8 * parts)) * parts
    own = groups // parts
    tail = parts == 1
    total_rows = groups * 16 - (8 if tail else 0)
    own_rows = total_rows // parts
    many = 4 if width == 128 else 1

    fwd_col, inv_col = column_tables(groups, tail)
    line_fh, line_fl, line_ih, line_il = line_tables()
    twist = np.stack(twist_table())
    twist_line = np.ascontiguousarray(np.broadcast_to(twist[:, :, None], twist.shape[:2] + (8, INNER)))
    twist_col = np.pad(twist, ((0, 0), (0, 64 - twist.shape[1]), (0, 0)))
    twist_col = twist_col.reshape(128, INNER).T.copy()

    u = device // parts
    k0 = jnp.where(u >= RES // 2, u - RES, u)
    place = jnp.stack([k0, (device % parts) * own]).astype(jnp.int32)
    gain_shape = jax.ShapeDtypeStruct((own, RES * 8, 128), jnp.float32)
    gain_spec = pl.BlockSpec((1, RES * 8, 128), lambda g: (g, 0, 0))
    gain_re, gain_im = pl.pallas_call(
        gain_kernel,
        grid=(own,),
        in_specs=[whole(pltpu.SMEM)],
        out_specs=[gain_spec, gain_spec],
        out_shape=[gain_shape, gain_shape],
        compiler_params=params(56),
        name="gain",
    )(place)

    place_row = lax.axis_index("row").reshape(1).astype(jnp.int32)
    blocks = height // INNER
    piece = (2, blocks, CHUNK, width)
    piece_shape = jax.ShapeDtypeStruct(piece, jnp.float32)
    anywhere = whole(pl.ANY)
    if width != 128:
        packed = jnp.stack([field_real, field_imag])
        packed = packed.reshape(2, blocks, CHUNKS, CHUNK, row_total, width).transpose(2, 4, 0, 1, 3, 5)
        packed = jnp.take(packed, jnp.arange(row_total) ^ place_row[0], axis=1)
    lines = []
    for chunk in range(CHUNKS):
        if width == 128:
            pieces = pl.pallas_call(
                pack_kernel,
                grid=(1,),
                in_specs=[whole(pltpu.SMEM)]
                + [pl.BlockSpec((blocks, CHUNK, tile_width), lambda i: (0, chunk, 0))] * 2,
                out_specs=[anywhere] * row_total,
                out_shape=[piece_shape] * row_total,
                scratch_shapes=[pltpu.SemaphoreType.DMA((2 * row_total,))],
                compiler_params=params(56),
                cost_estimate=cost(4),
                name="pack",
            )(
                place_row,
                field_real.reshape(blocks, INNER, tile_width),
                field_imag.reshape(blocks, INNER, tile_width),
            )
        else:
            pieces = [packed[chunk, j] for j in range(row_total)]
        pieces = exchange(pieces, "row")
        if chunk == 0:
            pieces, gain_re, gain_im = lax.optimization_barrier((pieces, gain_re, gain_im))
        rows = slice(chunk * CHUNK, (chunk + 1) * CHUNK)
        slab = pltpu.VMEM((RES // many, 2 * CHUNK, many * width), jnp.bfloat16)
        lines = [
            pl.pallas_call(
                partial(column_forward_kernel, row_total),
                in_specs=[whole(pltpu.SMEM)] + [whole()] * (2 + row_total) + [anywhere] * len(lines),
                out_specs=anywhere,
                out_shape=jax.ShapeDtypeStruct((RES, total_rows, width), jnp.float32),
                scratch_shapes=[
                    pltpu.VMEM((RES, total_rows, width), jnp.float32),
                    slab,
                    slab,
                    pltpu.SemaphoreType.DMA((2 * RES // many,)),
                ],
                compiler_params=params(20),
                cost_estimate=cost(20),
                name="column_forward",
            )(place_row, twist_col[rows], fwd_col[chunk], *pieces, *lines)
        ]
    (lines,) = lines

    lines = lines.reshape(devices, own_rows, width)
    lines = lax.all_to_all(lines, ("row", "col"), split_axis=0, concat_axis=0, tiled=True)
    if width == 128:
        order = tuple((b % row_total) * col_total + b // row_total for b in range(N // 128))
    else:
        order = tuple(range(N // 128))
        lines = lines.reshape(row_total, col_total, own_rows, width).transpose(2, 1, 0, 3)
        lines = lines.reshape(own_rows, N // 128, 128).transpose(1, 0, 2)

    at_once = 4 if tail else 1
    line_grain = pl.BlockSpec((N // 128, 16 * at_once, 128), lambda i: (0, i, 0))
    gain_grain = pl.BlockSpec((at_once, RES * 8, 128), lambda i: (i, 0, 0))
    lines = pl.pallas_call(
        partial(line_kernel, order, own, tail),
        grid=(-(-own // at_once),),
        in_specs=[line_grain, gain_grain, gain_grain] + [whole()] * 5,
        out_specs=line_grain,
        out_shape=jax.ShapeDtypeStruct((N // 128, own_rows, 128), jnp.float32),
        scratch_shapes=[
            pltpu.VMEM((at_once * 2 * RES * 8, 2 * INNER), jnp.bfloat16),
            pltpu.VMEM((at_once * RES * 8, 2 * INNER), jnp.float32),
        ],
        compiler_params=params(52),
        name="line",
    )(lines, gain_re, gain_im, twist_line, line_fh, line_fl, line_ih, line_il)

    if width != 128:
        lines = lines.transpose(1, 0, 2).reshape(own_rows, col_total, row_total, width)
        lines = lines.transpose(2, 1, 0, 3).reshape(devices, own_rows, width)
    lines = lax.all_to_all(lines, ("row", "col"), split_axis=0, concat_axis=0, tiled=True)
    lines = lines.reshape(RES, total_rows, width)

    near, tops = [], []
    for chunk in range(CHUNKS):
        spare = SPARE if chunk == CHUNKS - 1 else 0
        piece_shape = jax.ShapeDtypeStruct((2 * blocks * CHUNK + spare, width), jnp.float32)
        rows = slice(chunk * CHUNK, (chunk + 1) * CHUNK)
        *pieces, top = pl.pallas_call(
            partial(column_inverse_kernel, row_total),
            in_specs=[whole(pltpu.SMEM), anywhere, whole(), whole()],
            out_specs=[anywhere] * row_total + [whole()],
            out_shape=[piece_shape] * row_total + [jax.ShapeDtypeStruct((8, width), jnp.float32)],
            scratch_shapes=[
                pltpu.VMEM((row_total, 2, blocks, CHUNK, width), jnp.float32),
                pltpu.VMEM((RES, total_rows, width), jnp.float32),
                pltpu.VMEM((RES // many, inv_col.shape[2], many * width), jnp.bfloat16),
                pltpu.VMEM((RES, 2 * CHUNK, width), jnp.float32),
                pltpu.SemaphoreType.DMA((RES // many,)),
                pltpu.SemaphoreType.DMA((2 * row_total * 2 * blocks,)),
            ],
            compiler_params=params(56),
            cost_estimate=cost(60),
            name="column_inverse",
        )(place_row, lines, twist_col[rows], inv_col[chunk])
        near.append(pieces)
        tops.append(top)
    near[0] = exchange(near[0], "row")
    peak_sq = jnp.max(jnp.maximum(*tops))
    shift = 1
    while shift < col_total:
        partner = [(i, i ^ shift) for i in range(col_total)]
        peak_sq = jnp.maximum(peak_sq, lax.ppermute(peak_sq, "col", partner))
        shift *= 2
    near = lax.optimization_barrier(near)
    peak_own = peak_sq.reshape(1)
    others = row_total - 1
    near[1][1:] = pl.pallas_call(
        stamp_kernel,
        in_specs=[whole(pltpu.SMEM)] + [anywhere] * others,
        out_specs=[anywhere] * others,
        out_shape=[piece_shape] * others,
        scratch_shapes=[
            pltpu.VMEM((SPARE, width), jnp.float32),
            pltpu.SemaphoreType.DMA((others,)),
        ],
        input_output_aliases={1 + j: j for j in range(others)},
        compiler_params=params(56),
        name="stamp",
    )(peak_own, *near[1][1:])
    near[1] = exchange(near[1], "row")
    if width != 128:
        for piece in near[1][1:]:
            peak_sq = jnp.maximum(peak_sq, piece[-1, 0])
        near = jnp.stack([jnp.stack([piece[: 2 * blocks * CHUNK] for piece in pieces]) for pieces in near])
        near = jnp.take(near, jnp.arange(row_total) ^ place_row[0], axis=1)
        near = near.reshape(CHUNKS, row_total, 2, blocks, CHUNK, width)
        near = near.transpose(2, 3, 0, 4, 1, 5).reshape(2, height, tile_width)
        odd_cell = (jnp.arange(height)[:, None] + jnp.arange(tile_width)[None, :]) % 2
        cell_sign = (1 - 2 * odd_cell).astype(jnp.float32)
        return encode(near[0], near[1], peak_sq, cell_sign)
    tile_shape = jax.ShapeDtypeStruct((height, tile_width), jnp.float32)
    tile = pltpu.VMEM((blocks, INNER, tile_width), jnp.float32)
    return pl.pallas_call(
        partial(encode_kernel, row_total),
        in_specs=[whole(pltpu.SMEM)] * 2 + ([whole(pltpu.HBM)] + [whole()] * others) * CHUNKS,
        out_specs=[anywhere] * 2,
        out_shape=[tile_shape, tile_shape],
        scratch_shapes=[pltpu.VMEM(pieces[0].shape, jnp.float32) for pieces in near]
        + [tile, tile, pltpu.SemaphoreType.DMA((CHUNKS,)), pltpu.SemaphoreType.DMA((2 * blocks,))],
        compiler_params=params(16),
        name="encode",
    )(place_row, peak_own, *near[0], *near[1])


def solution(mesh):
    in_specs = (P("row", "col"), P("row", "col"))
    out_specs = (P("row", "col"), P("row", "col"))
    return jax.shard_map(body, mesh=mesh, in_specs=in_specs, out_specs=out_specs, check_vma=False)
```

```python
from functools import partial
import math

import jax
import jax.numpy as jnp
import ml_dtypes
import numpy as np
from jax import lax
from jax.experimental import pallas as pl
from jax.experimental.pallas import tpu as pltpu
from jax.sharding import PartitionSpec as P

N = 4096
PAD = 2 * N
wavelength = 5.2e-07
distance = 0.2
INNER = 256
SLABS = N // INNER
RES = PAD // INNER
HALF = 40
CHUNKS = 2
CHUNK = INNER // CHUNKS
SPARE = 8


def optics(padded_side):
    pitch = 2e-06 * math.sqrt(8192.0 / padded_side)
    extent = padded_side * pitch
    ratio_sq = (wavelength / extent) ** 2
    band_limit = extent / (wavelength * math.sqrt((2.0 * distance / extent) ** 2 + 1.0))
    return (ratio_sq, band_limit)


RATIO_SQ, LIMIT = optics(PAD)
assert RES * HALF - RES // 2 + RES > LIMIT and RES * HALF + RES // 2 > LIMIT


def residue(u):
    return u if u < RES // 2 else u - RES


def split16(table):
    table = np.asarray(table, np.float64)
    high = table.astype(np.float32).astype(ml_dtypes.bfloat16)
    low = (table - high.astype(np.float64)).astype(np.float32).astype(ml_dtypes.bfloat16)
    return high, low


def row_order(groups, tail):
    rows = []
    for group in range(groups):
        size = 4 if tail and group == groups - 1 else 8
        for part in range(2):
            for s in range(size):
                rows.append((part, group * 8 + s - HALF))
    return rows


def column_tables(groups, tail):
    q = np.arange(INNER)
    rows = row_order(groups, tail)
    forward = np.zeros((len(rows), 2, INNER))
    inverse = np.zeros((2, INNER, len(rows)))
    for at, (part, k1) in enumerate(rows):
        if abs(k1) > HALF:
            continue
        angle = 2.0 * np.pi * ((k1 * q) % INNER) / INNER
        c, s = np.cos(angle), np.sin(angle)
        forward[at] = (c, s) if part == 0 else (-s, c)
        inverse[:, :, at] = (c, s) if part == 0 else (-s, c)
    forward = forward.reshape(-1, 2, CHUNKS, CHUNK // 8, 8).transpose(2, 0, 3, 1, 4)
    forward = np.concatenate(split16(forward.reshape(CHUNKS, len(rows), 2 * CHUNK)), axis=1)
    inverse = inverse.reshape(2, CHUNKS, CHUNK, -1).transpose(1, 0, 2, 3)
    high, low = split16(inverse.reshape(CHUNKS, 2 * CHUNK, len(rows)))
    inverse = np.concatenate([high, high, low], axis=2)
    inverse = np.pad(inverse, ((0, 0), (0, 0), (0, -3 * len(rows) % 16)))
    return forward, inverse


def line_tables():
    q = np.arange(INNER)
    forward = np.zeros((2 * INNER, 256))
    inverse = np.zeros((256, 2 * INNER))
    for lane in range(2 * HALF + 1):
        angle = 2.0 * np.pi * (((lane - HALF) * q) % INNER) / INNER
        c, s = np.cos(angle), np.sin(angle)
        forward[:INNER, lane], forward[INNER:, lane] = c, s
        forward[:INNER, 128 + lane], forward[INNER:, 128 + lane] = -s, c
        inverse[lane, :INNER], inverse[lane, INNER:] = c, s
        inverse[128 + lane, :INNER], inverse[128 + lane, INNER:] = -s, c
    return split16(forward) + split16(inverse)


def twist_table():
    q = np.arange(INNER) + N // 2
    k0 = np.arange(RES // 2 + 1)
    angle = 2.0 * np.pi * ((k0[:, None] * q[None, :]) % PAD) / PAD
    return np.cos(angle).astype(np.float32), (-np.sin(angle)).astype(np.float32)


def turn(value, num, den):
    re, im = value
    num = num % den
    eighth = 8 * num
    if num == 0:
        return re, im
    if 2 * num == den:
        return -re, -im
    if 4 * num == den:
        return -im, re
    if 4 * num == 3 * den:
        return im, -re
    if eighth % den == 0:
        root = np.float32(math.sqrt(0.5))
        kind = eighth // den
        if kind == 1:
            return (re - im) * root, (re + im) * root
        if kind == 3:
            return (re + im) * (-root), (re - im) * root
        if kind == 5:
            return (im - re) * root, (re + im) * (-root)
        return (re + im) * root, (im - re) * root
    c = np.float32(math.cos(2.0 * math.pi * num / den))
    s = np.float32(math.sin(2.0 * math.pi * num / den))
    return re * c - im * s, re * s + im * c


def small_dft(get, ids, sign):
    count = len(ids)
    if count == 1:
        return [get(ids[0])]
    even = small_dft(get, ids[0::2], sign)
    odd = small_dft(get, ids[1::2], sign)
    half = count // 2
    first, second = [], []
    for j in range(half):
        re, im = even[j]
        t_re, t_im = turn(odd[j], sign * j, count)
        first.append((re + t_re, im + t_im))
        second.append((re - t_re, im - t_im))
    return first + second


def forward_slabs(get, put):
    ids = list(range(SLABS))
    for v, value in enumerate(small_dft(get, ids, -1)):
        put(2 * v, value)
    for v, value in enumerate(small_dft(lambda n: turn(get(n), -n, RES), ids, -1)):
        put(2 * v + 1, value)


def inverse_slabs(get, put):
    even = small_dft(get, list(range(0, RES, 2)), 1)
    odd = small_dft(get, list(range(1, RES, 2)), 1)
    for n in range(SLABS):
        t_re, t_im = turn(odd[n], n, RES)
        put(n, (even[n][0] + t_re, even[n][1] + t_im))


def twisted(value, u, sign, read):
    re, im = value
    k0 = residue(u)
    if k0 == 0:
        return value
    c, s = read(abs(k0))
    if (k0 < 0) == (sign > 0):
        return re * c + im * s, im * c - re * s
    return re * c - im * s, re * s + im * c


def high_low(value):
    high = value.astype(jnp.bfloat16)
    low = (value - high.astype(jnp.float32)).astype(jnp.bfloat16)
    return high, low


def dot16(left, right):
    return jnp.dot(left, right, preferred_element_type=jnp.float32)


def three_left(stacked, count, high, low):
    both = dot16(stacked[...], high)
    return both[:count] + both[count:] + dot16(stacked[:count], low)


def three_right(stacked, count, high, low):
    both = dot16(stacked, high)
    return both[:count] + both[count:] + dot16(stacked[:count], low)


def column_twist(twist, q0):
    seen = {}

    def read(k):
        if k not in seen:
            rows = pl.ds(q0, 8)
            seen[k] = twist[rows, k : k + 1], twist[rows, 64 + k : 65 + k]
        return seen[k]

    return read


def column_forward_kernel(count, place, twist, matrix, *refs):
    pieces, refs = refs[:count], refs[count:]
    before, (out, total, high, low, sems) = refs[:-5], refs[-5:]
    width = pieces[0].shape[-1]
    per_source = pieces[0].shape[1]
    many = high.shape[-1] // width
    products = RES // many
    rows_out = out.shape[1]

    def copy_in(p):
        part = pl.ds(p * many, many)
        return pltpu.make_async_copy(before[0].at[part], total.at[part], sems.at[p])

    def copy_out(p):
        part = pl.ds(p * many, many)
        return pltpu.make_async_copy(total.at[part], out.at[part], sems.at[products + p])

    if before:
        for p in range(products):
            copy_in(p).start()

    for here in range(count):

        @pl.when(place[0] == here)
        def _():
            @pl.loop(0, CHUNK // 8)
            def _(t):
                q0 = pl.multiple_of(t * 8, 8)
                read = column_twist(twist, q0)

                def get(n):
                    source, block = divmod(n, per_source)
                    piece = pieces[source ^ here]
                    rows = pl.ds(q0, 8)
                    return piece[0, block, rows, :], piece[1, block, rows, :]

                def put(u, value):
                    item = jnp.concatenate(twisted(value, u, 1, read), axis=0)
                    rows = pl.ds(pl.multiple_of(t * 16, 16), 16)
                    at = (u // many, rows, pl.ds((u % many) * width, width))
                    high[at], low[at] = high_low(item)

                forward_slabs(get, put)

    @pl.loop(0, products)
    def _(p):
        done = three_left(matrix, rows_out, high[p], low[p])
        if before:
            copy_in(p).wait()
        for part in range(many):
            item = done[:, part * width : (part + 1) * width]
            at = p * many + part
            total[at] = total[at] + item if before else item
        copy_out(p).start()

    for p in range(products):
        copy_out(p).wait()


def column_inverse_kernel(count, place, before, source, twist, matrix, *refs):
    pieces, (peak_sq, near, lines, deep, back, top, sems, out_sems) = refs[:count], refs[count:]
    width = lines.shape[-1]
    rows_in = lines.shape[1]
    per_dest = near.shape[2]
    many = deep.shape[-1] // width

    def copy_in(p):
        part = pl.ds(p * many, many)
        return pltpu.make_async_copy(source.at[part], lines.at[part], sems.at[p])

    def copies_out(part):
        size = CHUNK // 2
        copies = []
        for j, piece in enumerate(pieces):
            for at in range(2 * per_dest):
                here = near.at[place[0] ^ j, at // per_dest, at % per_dest, pl.ds(part * size, size)]
                there = piece.at[pl.ds(at * CHUNK + part * size, size)]
                sem = out_sems.at[(part * count + j) * 2 * per_dest + at]
                copies.append(pltpu.make_async_copy(here, there, sem))
        return copies

    for p in range(RES // many):
        copy_in(p).start()
    top[...] = jnp.zeros_like(top)

    def prepare(p):
        copy_in(p).wait()
        blocks = [lines[p * many + part] for part in range(many)]
        joined = jnp.concatenate(blocks, axis=1) if many > 1 else blocks[0]
        high = joined.astype(jnp.bfloat16).astype(jnp.float32)
        parts = [high, joined - high, high]
        if deep.shape[1] > 3 * rows_in:
            parts.append(jnp.zeros((deep.shape[1] - 3 * rows_in, many * width), jnp.float32))
        deep[p] = jnp.concatenate(parts, axis=0).astype(jnp.bfloat16)

    def product(p):
        done = dot16(matrix[...], deep[p])
        for part in range(many):
            back[p * many + part] = done[:, part * width : (part + 1) * width]

    prepare(0)

    @pl.loop(1, RES // many)
    def _(p):
        product(p - 1)
        prepare(p)

    product(RES // many - 1)

    def butterflies(t):
        q0 = pl.multiple_of(t * 8, 8)
        read = column_twist(twist, q0)
        largest = []

        def get(u):
            re = back[u, pl.ds(q0, 8), :]
            im = back[u, pl.ds(CHUNK + q0, 8), :]
            return twisted((re, im), u, -1, read)

        def put(n, value):
            dest, block = divmod(n, per_dest)
            rows = pl.ds(q0, 8)
            near[dest, 0, block, rows, :], near[dest, 1, block, rows, :] = value
            largest.append(value[0] * value[0] + value[1] * value[1])

        inverse_slabs(get, put)
        while len(largest) > 1:
            largest = [jnp.maximum(a, b) for a, b in zip(largest[0::2], largest[1::2])]
        top[...] = jnp.maximum(top[...], largest[0])

    for part in range(2):
        tiles = CHUNK // 16
        pl.loop(part * tiles, (part + 1) * tiles)(butterflies)
        for copy in copies_out(part):
            copy.start()
    peak_sq[0] = jnp.maximum(before[0], jnp.max(top[...]))
    for part in range(2):
        for copy in copies_out(part):
            copy.wait()


def line_kernel(
    order, own, tail, lines, gain_re, gain_im, twist, fwd_high, fwd_low, inv_high, inv_low, out, *scratch
):
    half = RES * 8
    at_end = pl.program_id(0) == pl.num_programs(0) - 1

    def line_twist(side):
        def read(k):
            lanes = pl.ds(side * 128, 128)
            return twist[0, k, :, lanes], twist[1, k, :, lanes]

        return read

    def forward(group, stacked, sides=(0, 1)):
        for side in sides:
            waiting = {}

            def get(m):
                block = order[2 * m + side]
                at = group * 16
                return lines[block, at : at + 8, :], lines[block, at + 8 : at + 16, :]

            def put(u, value):
                waiting[u] = twisted(value, u, 1, line_twist(side))
                v = (u + RES // 2) % RES
                if v in waiting:
                    first = min(u, v)
                    rows = pl.ds(first * 16, 16)
                    rows_low = pl.ds(half + first * 16, 16)
                    for part in range(2):
                        item = jnp.concatenate(
                            [waiting[first][part], waiting[first + RES // 2][part]], axis=0
                        )
                        at = pl.ds(part * INNER + side * 128, 128)
                        stacked[rows, at], stacked[rows_low, at] = high_low(item)

            forward_slabs(get, put)

    def filtered(group, stacked):
        spec = three_right(stacked[...], half, fwd_high[...], fwd_low[...])
        spec_re, spec_im = spec[:, :128], spec[:, 128:]
        g_re, g_im = gain_re[group], gain_im[group]
        mixed = jnp.concatenate(
            [spec_re * g_re - spec_im * g_im, spec_re * g_im + spec_im * g_re], axis=1
        )
        return jnp.concatenate(high_low(mixed), axis=0)

    def unfold(mixed, back):
        back[...] = three_right(mixed, half, inv_high[...], inv_low[...])

    def inverse(group, back, sides=(0, 1)):
        for side in sides:

            def get(u):
                rows = pl.ds((u % (RES // 2)) * 16 + (u // (RES // 2)) * 8, 8)
                re = back[rows, pl.ds(side * 128, 128)]
                im = back[rows, pl.ds(INNER + side * 128, 128)]
                return twisted((re, im), u, -1, line_twist(side))

            def put(m, value):
                block = order[2 * m + side]
                at = group * 16
                out[block, at : at + 8, :], out[block, at + 8 : at + 16, :] = value

            inverse_slabs(get, put)

    if tail:

        @pl.when(at_end)
        def _():
            for block in range(N // 128):
                lines[block, 8:12, :] = lines[block, 4:8, :]

    groups = len(scratch) // 2

    stacked, back = scratch[:groups], scratch[groups:]

    def run(count):
        forward(0, stacked[0])
        for group in range(count):
            mixed = filtered(group, stacked[group])
            if group + 1 < count:
                forward(group + 1, stacked[group + 1], (0,))
            if group > 0:
                inverse(group - 1, back[group - 1], (0,))
            unfold(mixed, back[group])
            if group + 1 < count:
                forward(group + 1, stacked[group + 1], (1,))
            if group > 0:
                inverse(group - 1, back[group - 1], (1,))
        inverse(count - 1, back[count - 1])

    rest = own % groups
    if rest:
        pl.when(jnp.logical_not(at_end))(lambda: run(groups))
        pl.when(at_end)(lambda: run(rest))
    else:
        run(groups)

    if tail:

        @pl.when(at_end)
        def _():
            for block in range(N // 128):
                out[block, 4:8, :] = out[block, 8:12, :]


def gain_kernel(place, gain_re, gain_im):
    k0 = place[0]
    group = place[1] + pl.program_id(0)
    down = lax.broadcasted_iota(jnp.int32, (8, 128), 0)
    across = lax.broadcasted_iota(jnp.int32, (8, 128), 1)
    row = (k0 + RES * (group * 8 + down - HALF)).astype(jnp.float32)
    row_sq = row * row
    row_in = jnp.abs(row) < LIMIT
    for u in range(RES):
        col = (residue(u) + RES * (across - HALF)).astype(jnp.float32)
        square = row_sq + col * col
        scaled = RATIO_SQ * square
        phase = -2.0 * math.pi * distance / wavelength * scaled / (1.0 + jnp.sqrt(1.0 - scaled))
        total = jnp.where(
            row_in & (jnp.abs(col) < LIMIT), jnp.exp(square * (-2.0 / (LIMIT * LIMIT))), 0.0
        )
        quarter = jnp.floor(phase * (2.0 / math.pi) + 0.5)
        left = phase - quarter * 1.5703125
        left = left - quarter * 4.837512969970703125e-4
        left = left - quarter * 7.549789954891882e-8
        sq = left * left
        sine = ((-1.9515295891e-4 * sq + 8.3321608736e-3) * sq - 1.6666654611e-1) * sq * left + left
        cosine = (
            (2.443315711809948e-5 * sq - 1.388731625493765e-3) * sq + 4.166664568298827e-2
        ) * sq * sq - 0.5 * sq + 1.0
        which = quarter.astype(jnp.int32) & 3
        swap = (which & 1) == 1
        cos_part = jnp.where(swap, sine, cosine)
        sin_part = jnp.where(swap, cosine, sine)
        cos_part = jnp.where((which == 1) | (which == 2), -cos_part, cos_part)
        sin_part = jnp.where(which >= 2, -sin_part, sin_part)
        at = (u % (RES // 2)) * 16 + (u // (RES // 2)) * 8
        gain_re[0, at : at + 8, :] = total * cos_part
        gain_im[0, at : at + 8, :] = total * sin_part


def encode(near_real, near_imag, peak_sq, cell_sign):
    square = near_real * near_real + near_imag * near_imag
    root = lax.rsqrt(jnp.maximum(square, 1.2e-38))
    top = lax.rsqrt(peak_sq)
    amp_level = (square * root) * (0.8 * top)
    unit = jnp.minimum(root, 20.0 * top)
    rest = 1.0 - amp_level * amp_level
    level = unit * amp_level
    lift = (rest * lax.rsqrt(rest)) * (unit * cell_sign)
    return (near_real * level + near_imag * lift, near_imag * level - near_real * lift)


def stamp_kernel(peak_one, peak_two, *refs):
    count = (len(refs) - 2) // 2
    pieces, tile, sems = refs[count : 2 * count], refs[-2], refs[-1]
    tile[...] = jnp.full(tile.shape, jnp.maximum(peak_one[0], peak_two[0]), jnp.float32)
    copies = []
    for j, piece in enumerate(pieces):
        rows = pl.ds(piece.shape[0] - SPARE, SPARE)
        copies.append(pltpu.make_async_copy(tile, piece.at[rows], sems.at[j]))
    for copy in copies:
        copy.start()
    for copy in copies:
        copy.wait()


def encode_kernel(count, place, peak_one, peak_two, *refs):
    pieces, (slm_real, slm_imag, *refs) = refs[: CHUNKS * count], refs[CHUNKS * count :]
    own, (tile_real, tile_imag, own_sems, sems) = refs[:CHUNKS], refs[CHUNKS:]
    blocks, width = tile_real.shape[0], pieces[0].shape[-1]
    fetches = [
        pltpu.make_async_copy(pieces[chunk * count], own[chunk], own_sems.at[chunk])
        for chunk in range(CHUNKS)
    ]
    for fetch in fetches:
        fetch.start()
    top = jnp.full((1, width), jnp.maximum(peak_one[0], peak_two[0]), jnp.float32)
    for piece in pieces[(CHUNKS - 1) * count + 1 :]:
        top = jnp.maximum(top, piece[pl.ds(piece.shape[0] - SPARE, 1), :])
    cell = lax.broadcasted_iota(jnp.int32, (CHUNK, width), 0)
    cell = cell + lax.broadcasted_iota(jnp.int32, (CHUNK, width), 1)
    cell_sign = (1 - 2 * (cell & 1)).astype(jnp.float32)
    for fetch in fetches:
        fetch.wait()

    def copies_out(block):
        rows = pl.ds(block * INNER, INNER)
        return [
            pltpu.make_async_copy(tile.at[block], slm.at[rows], sems.at[2 * block + part])
            for part, (tile, slm) in enumerate(((tile_real, slm_real), (tile_imag, slm_imag)))
        ]

    @pl.loop(0, blocks)
    def _(block):
        for at in range(CHUNKS * count):
            chunk, j = divmod(at, count)
            piece = pieces[at] if j else own[chunk]
            lanes = pl.ds(pl.multiple_of((place[0] ^ j) * width, width), width)
            rows = pl.ds(chunk * CHUNK, CHUNK)
            real = pl.ds(pl.multiple_of(block * CHUNK, CHUNK), CHUNK)
            imag = pl.ds(pl.multiple_of((blocks + block) * CHUNK, CHUNK), CHUNK)
            tile_real[block, rows, lanes], tile_imag[block, rows, lanes] = encode(
                piece[real, :], piece[imag, :], top, cell_sign
            )
        for copy in copies_out(block):
            copy.start()

    for block in range(blocks):
        for copy in copies_out(block):
            copy.wait()


def pack_kernel(place, field_real, field_imag, *refs):
    pieces, sems = refs[:-1], refs[-1]
    width = pieces[0].shape[-1]
    copies = []
    for j in list(range(1, len(pieces))) + [0]:
        lanes = pl.ds(pl.multiple_of((place[0] ^ j) * width, width), width)
        for part, field in enumerate((field_real, field_imag)):
            copies.append(
                pltpu.make_async_copy(
                    field.at[:, :, lanes], pieces[j].at[part], sems.at[2 * j + part]
                )
            )
    for copy in copies:
        copy.start()
    for copy in copies:
        copy.wait()


def exchange(pieces, axis):
    total = len(pieces)
    return [pieces[0]] + [
        lax.ppermute(pieces[j], axis, [(i, i ^ j) for i in range(total)]) for j in range(1, total)
    ]


def params(mebibytes):
    return pltpu.CompilerParams(vmem_limit_bytes=mebibytes << 20)


def cost(megabytes):
    return pl.CostEstimate(flops=0, bytes_accessed=megabytes << 20, transcendentals=0)


def whole(memory=pltpu.VMEM):
    return pl.BlockSpec(memory_space=memory)


def body(field_real, field_imag):
    row_total, col_total = lax.axis_size("row"), lax.axis_size("col")
    devices = row_total * col_total
    device = lax.axis_index("row") * col_total + lax.axis_index("col")
    height, tile_width = field_real.shape
    width = tile_width // row_total
    parts = max(1, devices // RES)
    groups = -(-(2 * HALF + 1) // (8 * parts)) * parts
    own = groups // parts
    tail = parts == 1
    total_rows = groups * 16 - (8 if tail else 0)
    own_rows = total_rows // parts
    many = 4 if width == 128 else 1

    fwd_col, inv_col = column_tables(groups, tail)
    line_fh, line_fl, line_ih, line_il = line_tables()
    twist = np.stack(twist_table())
    twist_line = np.ascontiguousarray(np.broadcast_to(twist[:, :, None], twist.shape[:2] + (8, INNER)))
    twist_col = np.pad(twist, ((0, 0), (0, 64 - twist.shape[1]), (0, 0)))
    twist_col = twist_col.reshape(128, INNER).T.copy()

    u = device // parts
    k0 = jnp.where(u >= RES // 2, u - RES, u)
    place = jnp.stack([k0, (device % parts) * own]).astype(jnp.int32)
    gain_shape = jax.ShapeDtypeStruct((own, RES * 8, 128), jnp.float32)
    gain_spec = pl.BlockSpec((1, RES * 8, 128), lambda g: (g, 0, 0))
    gain_re, gain_im = pl.pallas_call(
        gain_kernel,
        grid=(own,),
        in_specs=[whole(pltpu.SMEM)],
        out_specs=[gain_spec, gain_spec],
        out_shape=[gain_shape, gain_shape],
        compiler_params=params(56),
        name="gain",
    )(place)

    place_row = lax.axis_index("row").reshape(1).astype(jnp.int32)
    blocks = height // INNER
    piece = (2, blocks, CHUNK, width)
    piece_shape = jax.ShapeDtypeStruct(piece, jnp.float32)
    anywhere = whole(pl.ANY)
    if width != 128:
        packed = jnp.stack([field_real, field_imag])
        packed = packed.reshape(2, blocks, CHUNKS, CHUNK, row_total, width).transpose(2, 4, 0, 1, 3, 5)
        packed = jnp.take(packed, jnp.arange(row_total) ^ place_row[0], axis=1)
    lines = []
    for chunk in range(CHUNKS):
        if width == 128:
            pieces = pl.pallas_call(
                pack_kernel,
                grid=(1,),
                in_specs=[whole(pltpu.SMEM)]
                + [pl.BlockSpec((blocks, CHUNK, tile_width), lambda i: (0, chunk, 0))] * 2,
                out_specs=[anywhere] * row_total,
                out_shape=[piece_shape] * row_total,
                scratch_shapes=[pltpu.SemaphoreType.DMA((2 * row_total,))],
                compiler_params=params(56),
                cost_estimate=cost(4),
                name="pack",
            )(
                place_row,
                field_real.reshape(blocks, INNER, tile_width),
                field_imag.reshape(blocks, INNER, tile_width),
            )
        else:
            pieces = [packed[chunk, j] for j in range(row_total)]
        pieces = exchange(pieces, "row")
        rows = slice(chunk * CHUNK, (chunk + 1) * CHUNK)
        slab = pltpu.VMEM((RES // many, 2 * CHUNK, many * width), jnp.bfloat16)
        lines = [
            pl.pallas_call(
                partial(column_forward_kernel, row_total),
                in_specs=[whole(pltpu.SMEM)] + [whole()] * (2 + row_total) + [anywhere] * len(lines),
                out_specs=anywhere,
                out_shape=jax.ShapeDtypeStruct((RES, total_rows, width), jnp.float32),
                scratch_shapes=[
                    pltpu.VMEM((RES, total_rows, width), jnp.float32),
                    slab,
                    slab,
                    pltpu.SemaphoreType.DMA((2 * RES // many,)),
                ],
                compiler_params=params(20),
                cost_estimate=cost(20),
                name="column_forward",
            )(place_row, twist_col[rows], fwd_col[chunk], *pieces, *lines)
        ]
    (lines,) = lines

    lines = lines.reshape(devices, own_rows, width)
    lines = lax.all_to_all(lines, ("row", "col"), split_axis=0, concat_axis=0, tiled=True)
    if width == 128:
        order = tuple((b % row_total) * col_total + b // row_total for b in range(N // 128))
    else:
        order = tuple(range(N // 128))
        lines = lines.reshape(row_total, col_total, own_rows, width).transpose(2, 1, 0, 3)
        lines = lines.reshape(own_rows, N // 128, 128).transpose(1, 0, 2)

    at_once = 2
    line_grain = pl.BlockSpec((N // 128, 16 * at_once, 128), lambda i: (0, i, 0))
    gain_grain = pl.BlockSpec((at_once, RES * 8, 128), lambda i: (i, 0, 0))
    lines = pl.pallas_call(
        partial(line_kernel, order, own, tail),
        grid=(-(-own // at_once),),
        in_specs=[line_grain, gain_grain, gain_grain] + [whole()] * 5,
        out_specs=line_grain,
        out_shape=jax.ShapeDtypeStruct((N // 128, own_rows, 128), jnp.float32),
        scratch_shapes=[pltpu.VMEM((2 * RES * 8, 2 * INNER), jnp.bfloat16)] * at_once
        + [pltpu.VMEM((RES * 8, 2 * INNER), jnp.float32)] * at_once,
        compiler_params=params(52),
        name="line",
    )(lines, gain_re, gain_im, twist_line, line_fh, line_fl, line_ih, line_il)

    if width != 128:
        lines = lines.transpose(1, 0, 2).reshape(own_rows, col_total, row_total, width)
        lines = lines.transpose(2, 1, 0, 3).reshape(devices, own_rows, width)
    lines = lax.all_to_all(lines, ("row", "col"), split_axis=0, concat_axis=0, tiled=True)
    lines = lines.reshape(RES, total_rows, width)

    near, peak_sq = [], jnp.zeros((1,), jnp.float32)
    for chunk in range(CHUNKS):
        spare = SPARE if chunk == CHUNKS - 1 else 0
        piece_shape = jax.ShapeDtypeStruct((2 * blocks * CHUNK + spare, width), jnp.float32)
        rows = slice(chunk * CHUNK, (chunk + 1) * CHUNK)
        *pieces, peak_sq = pl.pallas_call(
            partial(column_inverse_kernel, row_total),
            in_specs=[whole(pltpu.SMEM), whole(pltpu.SMEM), anywhere, whole(), whole()],
            out_specs=[anywhere] * row_total + [whole(pltpu.SMEM)],
            out_shape=[piece_shape] * row_total + [jax.ShapeDtypeStruct((1,), jnp.float32)],
            scratch_shapes=[
                pltpu.VMEM((row_total, 2, blocks, CHUNK, width), jnp.float32),
                pltpu.VMEM((RES, total_rows, width), jnp.float32),
                pltpu.VMEM((RES // many, inv_col.shape[2], many * width), jnp.bfloat16),
                pltpu.VMEM((RES, 2 * CHUNK, width), jnp.float32),
                pltpu.VMEM((8, width), jnp.float32),
                pltpu.SemaphoreType.DMA((RES // many,)),
                pltpu.SemaphoreType.DMA((2 * row_total * 2 * blocks,)),
            ],
            compiler_params=params(56),
            cost_estimate=cost(60),
            name="column_inverse",
        )(place_row, peak_sq, lines, twist_col[rows], inv_col[chunk])
        near.append(pieces)
    near[0] = exchange(near[0], "row")
    shift = 1
    while shift < col_total:
        partner = [(i, i ^ shift) for i in range(col_total)]
        peaks = [peak_sq, lax.ppermute(peak_sq, "col", partner)]
        shift *= 2
        if shift < col_total:
            peak_sq = jnp.maximum(*peaks)
    near = lax.optimization_barrier(near)
    others = row_total - 1
    near[1][1:] = pl.pallas_call(
        stamp_kernel,
        in_specs=[whole(pltpu.SMEM)] * 2 + [anywhere] * others,
        out_specs=[anywhere] * others,
        out_shape=[piece_shape] * others,
        scratch_shapes=[
            pltpu.VMEM((SPARE, width), jnp.float32),
            pltpu.SemaphoreType.DMA((others,)),
        ],
        input_output_aliases={2 + j: j for j in range(others)},
        compiler_params=params(56),
        name="stamp",
    )(*peaks, *near[1][1:])
    near[1] = exchange(near[1], "row")
    if width != 128:
        peak_sq = jnp.maximum(*peaks)[0]
        for piece in near[1][1:]:
            peak_sq = jnp.maximum(peak_sq, piece[-1, 0])
        near = jnp.stack([jnp.stack([piece[: 2 * blocks * CHUNK] for piece in pieces]) for pieces in near])
        near = jnp.take(near, jnp.arange(row_total) ^ place_row[0], axis=1)
        near = near.reshape(CHUNKS, row_total, 2, blocks, CHUNK, width)
        near = near.transpose(2, 3, 0, 4, 1, 5).reshape(2, height, tile_width)
        odd_cell = (jnp.arange(height)[:, None] + jnp.arange(tile_width)[None, :]) % 2
        cell_sign = (1 - 2 * odd_cell).astype(jnp.float32)
        return encode(near[0], near[1], peak_sq, cell_sign)
    tile_shape = jax.ShapeDtypeStruct((height, tile_width), jnp.float32)
    tile = pltpu.VMEM((blocks, INNER, tile_width), jnp.float32)
    return pl.pallas_call(
        partial(encode_kernel, row_total),
        in_specs=[whole(pltpu.SMEM)] * 3 + ([anywhere] + [whole()] * others) * CHUNKS,
        out_specs=[anywhere] * 2,
        out_shape=[tile_shape, tile_shape],
        scratch_shapes=[pltpu.VMEM(pieces[0].shape, jnp.float32) for pieces in near]
        + [tile, tile, pltpu.SemaphoreType.DMA((CHUNKS,)), pltpu.SemaphoreType.DMA((2 * blocks,))],
        compiler_params=params(16),
        name="encode",
    )(place_row, *peaks, *near[0], *near[1])


def solution(mesh):
    in_specs = (P("row", "col"), P("row", "col"))
    out_specs = (P("row", "col"), P("row", "col"))
    return jax.shard_map(body, mesh=mesh, in_specs=in_specs, out_specs=out_specs, check_vma=False)
```

```python
from functools import partial
import math

import jax
import jax.numpy as jnp
import ml_dtypes
import numpy as np
from jax import lax
from jax.experimental import pallas as pl
from jax.experimental.pallas import tpu as pltpu
from jax.sharding import PartitionSpec as P

N = 4096
PAD = 2 * N
wavelength = 5.2e-07
distance = 0.2
INNER = 256
SLABS = N // INNER
RES = PAD // INNER
HALF = 40
CHUNKS = 2
CHUNK = INNER // CHUNKS
SPARE = 8


def optics(padded_side):
    pitch = 2e-06 * math.sqrt(8192.0 / padded_side)
    extent = padded_side * pitch
    ratio_sq = (wavelength / extent) ** 2
    band_limit = extent / (wavelength * math.sqrt((2.0 * distance / extent) ** 2 + 1.0))
    return (ratio_sq, band_limit)


RATIO_SQ, LIMIT = optics(PAD)
assert RES * HALF - RES // 2 + RES > LIMIT and RES * HALF + RES // 2 > LIMIT


def residue(u):
    return u if u < RES // 2 else u - RES


def split16(table):
    table = np.asarray(table, np.float64)
    high = table.astype(np.float32).astype(ml_dtypes.bfloat16)
    low = (table - high.astype(np.float64)).astype(np.float32).astype(ml_dtypes.bfloat16)
    return high, low


def row_order(groups, tail):
    rows = []
    for group in range(groups):
        size = 4 if tail and group == groups - 1 else 8
        for part in range(2):
            for s in range(size):
                rows.append((part, group * 8 + s - HALF))
    return rows


def column_tables(groups, tail):
    q = np.arange(INNER)
    rows = row_order(groups, tail)
    forward = np.zeros((len(rows), 2, INNER))
    inverse = np.zeros((2, INNER, len(rows)))
    for at, (part, k1) in enumerate(rows):
        if abs(k1) > HALF:
            continue
        angle = 2.0 * np.pi * ((k1 * q) % INNER) / INNER
        c, s = np.cos(angle), np.sin(angle)
        forward[at] = (c, s) if part == 0 else (-s, c)
        inverse[:, :, at] = (c, s) if part == 0 else (-s, c)
    forward = forward.reshape(-1, 2, CHUNKS, CHUNK // 8, 8).transpose(2, 0, 3, 1, 4)
    forward = np.concatenate(split16(forward.reshape(CHUNKS, len(rows), 2 * CHUNK)), axis=1)
    inverse = inverse.reshape(2, CHUNKS, CHUNK, -1).transpose(1, 0, 2, 3)
    high, low = split16(inverse.reshape(CHUNKS, 2 * CHUNK, len(rows)))
    inverse = np.concatenate([high, high, low], axis=2)
    inverse = np.pad(inverse, ((0, 0), (0, 0), (0, -3 * len(rows) % 16)))
    return forward, inverse


def line_tables():
    q = np.arange(INNER)
    forward = np.zeros((2 * INNER, 256))
    inverse = np.zeros((256, 2 * INNER))
    for lane in range(2 * HALF + 1):
        angle = 2.0 * np.pi * (((lane - HALF) * q) % INNER) / INNER
        c, s = np.cos(angle), np.sin(angle)
        forward[:INNER, lane], forward[INNER:, lane] = c, s
        forward[:INNER, 128 + lane], forward[INNER:, 128 + lane] = -s, c
        inverse[lane, :INNER], inverse[lane, INNER:] = c, s
        inverse[128 + lane, :INNER], inverse[128 + lane, INNER:] = -s, c
    return split16(forward) + split16(inverse)


def twist_table():
    q = np.arange(INNER) + N // 2
    k0 = np.arange(RES // 2 + 1)
    angle = 2.0 * np.pi * ((k0[:, None] * q[None, :]) % PAD) / PAD
    return np.cos(angle).astype(np.float32), (-np.sin(angle)).astype(np.float32)


def turn(value, num, den):
    re, im = value
    num = num % den
    eighth = 8 * num
    if num == 0:
        return re, im
    if 2 * num == den:
        return -re, -im
    if 4 * num == den:
        return -im, re
    if 4 * num == 3 * den:
        return im, -re
    if eighth % den == 0:
        root = np.float32(math.sqrt(0.5))
        kind = eighth // den
        if kind == 1:
            return (re - im) * root, (re + im) * root
        if kind == 3:
            return (re + im) * (-root), (re - im) * root
        if kind == 5:
            return (im - re) * root, (re + im) * (-root)
        return (re + im) * root, (im - re) * root
    c = np.float32(math.cos(2.0 * math.pi * num / den))
    s = np.float32(math.sin(2.0 * math.pi * num / den))
    return re * c - im * s, re * s + im * c


def small_dft(get, ids, sign):
    count = len(ids)
    if count == 1:
        return [get(ids[0])]
    even = small_dft(get, ids[0::2], sign)
    odd = small_dft(get, ids[1::2], sign)
    half = count // 2
    first, second = [], []
    for j in range(half):
        re, im = even[j]
        t_re, t_im = turn(odd[j], sign * j, count)
        first.append((re + t_re, im + t_im))
        second.append((re - t_re, im - t_im))
    return first + second


def forward_slabs(get, put):
    ids = list(range(SLABS))
    for v, value in enumerate(small_dft(get, ids, -1)):
        put(2 * v, value)
    for v, value in enumerate(small_dft(lambda n: turn(get(n), -n, RES), ids, -1)):
        put(2 * v + 1, value)


def inverse_slabs(get, put):
    even = small_dft(get, list(range(0, RES, 2)), 1)
    odd = small_dft(get, list(range(1, RES, 2)), 1)
    for n in range(SLABS):
        t_re, t_im = turn(odd[n], n, RES)
        put(n, (even[n][0] + t_re, even[n][1] + t_im))


def twisted(value, u, sign, read):
    re, im = value
    k0 = residue(u)
    if k0 == 0:
        return value
    c, s = read(abs(k0))
    if (k0 < 0) == (sign > 0):
        return re * c + im * s, im * c - re * s
    return re * c - im * s, re * s + im * c


def high_low(value):
    high = value.astype(jnp.bfloat16)
    low = (value - high.astype(jnp.float32)).astype(jnp.bfloat16)
    return high, low


def dot16(left, right):
    return jnp.dot(left, right, preferred_element_type=jnp.float32)


def three_left(stacked, count, high, low):
    both = dot16(stacked[...], high)
    return both[:count] + both[count:] + dot16(stacked[:count], low)


def three_right(stacked, count, high, low):
    both = dot16(stacked, high)
    return both[:count] + both[count:] + dot16(stacked[:count], low)


def column_twist(twist, q0):
    seen = {}

    def read(k):
        if k not in seen:
            rows = pl.ds(q0, 8)
            seen[k] = twist[rows, k : k + 1], twist[rows, 64 + k : 65 + k]
        return seen[k]

    return read


def column_forward_kernel(count, place, twist, matrix, *refs):
    pieces, refs = refs[:count], refs[count:]
    before, (out, total, high, low, sems) = refs[:-5], refs[-5:]
    width = pieces[0].shape[-1]
    per_source = pieces[0].shape[1]
    many = high.shape[-1] // width
    products = RES // many
    rows_out = out.shape[1]

    def copy_in(p):
        part = pl.ds(p * many, many)
        return pltpu.make_async_copy(before[0].at[part], total.at[part], sems.at[p])

    def copy_out(p):
        part = pl.ds(p * many, many)
        return pltpu.make_async_copy(total.at[part], out.at[part], sems.at[products + p])

    if before:
        for p in range(products):
            copy_in(p).start()

    for here in range(count):

        @pl.when(place[0] == here)
        def _():
            @pl.loop(0, CHUNK // 8)
            def _(t):
                q0 = pl.multiple_of(t * 8, 8)
                read = column_twist(twist, q0)

                def get(n):
                    source, block = divmod(n, per_source)
                    piece = pieces[source ^ here]
                    rows = pl.ds(q0, 8)
                    return piece[0, block, rows, :], piece[1, block, rows, :]

                def put(u, value):
                    item = jnp.concatenate(twisted(value, u, 1, read), axis=0)
                    rows = pl.ds(pl.multiple_of(t * 16, 16), 16)
                    at = (u // many, rows, pl.ds((u % many) * width, width))
                    high[at], low[at] = high_low(item)

                forward_slabs(get, put)

    @pl.loop(0, products)
    def _(p):
        done = three_left(matrix, rows_out, high[p], low[p])
        if before:
            copy_in(p).wait()
        for part in range(many):
            item = done[:, part * width : (part + 1) * width]
            at = p * many + part
            total[at] = total[at] + item if before else item
        copy_out(p).start()

    for p in range(products):
        copy_out(p).wait()


def column_inverse_kernel(count, place, source, twist, matrix, *refs):
    pieces, (peak_sq, near, lines, deep, back, top, sems, out_sems) = refs[:-8], refs[-8:]
    width = lines.shape[-1]
    rows_in = lines.shape[1]
    per_dest = near.shape[3]
    many = deep.shape[-1] // width
    products = RES // many

    def copy_in(p):
        part = pl.ds(p * many, many)
        return pltpu.make_async_copy(source.at[part], lines.at[part], sems.at[p])

    def copies_out(chunk, part):
        size = CHUNK // 2
        copies = []
        for j in range(count):
            for at in range(2 * per_dest):
                rows = pl.ds(part * size, size)
                here = near.at[chunk, place[0] ^ j, at // per_dest, at % per_dest, rows]
                there = pieces[chunk * count + j].at[pl.ds(at * CHUNK + part * size, size)]
                sem = out_sems.at[((chunk * 2 + part) * count + j) * 2 * per_dest + at]
                copies.append(pltpu.make_async_copy(here, there, sem))
        return copies

    def prepare(p):
        copy_in(p).wait()
        blocks = [lines[p * many + part] for part in range(many)]
        joined = jnp.concatenate(blocks, axis=1) if many > 1 else blocks[0]
        high = joined.astype(jnp.bfloat16).astype(jnp.float32)
        parts = [high, joined - high, high]
        if deep.shape[1] > 3 * rows_in:
            parts.append(jnp.zeros((deep.shape[1] - 3 * rows_in, many * width), jnp.float32))
        deep[p] = jnp.concatenate(parts, axis=0).astype(jnp.bfloat16)

    def product(p, chunk):
        done = dot16(matrix[chunk], deep[p])
        for part in range(many):
            back[chunk, p * many + part] = done[:, part * width : (part + 1) * width]

    def butterflies(t, chunk):
        q0 = pl.multiple_of(t * 8, 8)
        largest = []
        read = column_twist(twist, pl.multiple_of(chunk * CHUNK + q0, 8))

        def get(u):
            re = back[chunk, u, pl.ds(q0, 8), :]
            im = back[chunk, u, pl.ds(CHUNK + q0, 8), :]
            return twisted((re, im), u, -1, read)

        def put(n, value):
            dest, block = divmod(n, per_dest)
            rows = pl.ds(q0, 8)
            near[chunk, dest, 0, block, rows, :], near[chunk, dest, 1, block, rows, :] = value
            largest.append(value[0] * value[0] + value[1] * value[1])

        inverse_slabs(get, put)
        while len(largest) > 1:
            largest = [jnp.maximum(a, b) for a, b in zip(largest[0::2], largest[1::2])]
        top[...] = jnp.maximum(top[...], largest[0])

    for p in range(products):
        copy_in(p).start()
    top[...] = jnp.zeros_like(top)

    @pl.loop(0, products)
    def _(p):
        prepare(p)
        product(p, 0)

    tiles = CHUNK // 16
    steps = min(tiles, products // 2)
    for chunk in range(CHUNKS):
        for part in range(2):

            @pl.loop(part * steps, (part + 1) * steps)
            def _(t):
                for item in range(tiles // steps):
                    butterflies(t * (tiles // steps) + item, chunk)
                if chunk + 1 < CHUNKS:
                    for item in range(products // 2 // steps):
                        product(t * (products // 2 // steps) + item, chunk + 1)

            for copy in copies_out(chunk, part):
                copy.start()
    peak_sq[0] = jnp.max(top[...])
    for chunk in range(CHUNKS):
        for part in range(2):
            for copy in copies_out(chunk, part):
                copy.wait()


def line_kernel(
    order, own, tail, lines, gain_re, gain_im, twist, fwd_high, fwd_low, inv_high, inv_low, out, *scratch
):
    half = RES * 8
    at_end = pl.program_id(0) == pl.num_programs(0) - 1

    def line_twist(side):
        def read(k):
            lanes = pl.ds(side * 128, 128)
            return twist[0, k, :, lanes], twist[1, k, :, lanes]

        return read

    def forward(group, stacked, sides=(0, 1)):
        for side in sides:
            waiting = {}

            def get(m):
                block = order[2 * m + side]
                at = group * 16
                return lines[block, at : at + 8, :], lines[block, at + 8 : at + 16, :]

            def put(u, value):
                waiting[u] = twisted(value, u, 1, line_twist(side))
                v = (u + RES // 2) % RES
                if v in waiting:
                    first = min(u, v)
                    rows = pl.ds(first * 16, 16)
                    rows_low = pl.ds(half + first * 16, 16)
                    for part in range(2):
                        item = jnp.concatenate(
                            [waiting[first][part], waiting[first + RES // 2][part]], axis=0
                        )
                        at = pl.ds(part * INNER + side * 128, 128)
                        stacked[rows, at], stacked[rows_low, at] = high_low(item)

            forward_slabs(get, put)

    def filtered(group, stacked):
        spec = three_right(stacked[...], half, fwd_high[...], fwd_low[...])
        spec_re, spec_im = spec[:, :128], spec[:, 128:]
        g_re, g_im = gain_re[group], gain_im[group]
        mixed = jnp.concatenate(
            [spec_re * g_re - spec_im * g_im, spec_re * g_im + spec_im * g_re], axis=1
        )
        return jnp.concatenate(high_low(mixed), axis=0)

    def unfold(mixed, back):
        back[...] = three_right(mixed, half, inv_high[...], inv_low[...])

    def inverse(group, back, sides=(0, 1)):
        for side in sides:

            def get(u):
                rows = pl.ds((u % (RES // 2)) * 16 + (u // (RES // 2)) * 8, 8)
                re = back[rows, pl.ds(side * 128, 128)]
                im = back[rows, pl.ds(INNER + side * 128, 128)]
                return twisted((re, im), u, -1, line_twist(side))

            def put(m, value):
                block = order[2 * m + side]
                at = group * 16
                out[block, at : at + 8, :], out[block, at + 8 : at + 16, :] = value

            inverse_slabs(get, put)

    if tail:

        @pl.when(at_end)
        def _():
            for block in range(N // 128):
                lines[block, 8:12, :] = lines[block, 4:8, :]

    groups = len(scratch) // 2

    stacked, back = scratch[:groups], scratch[groups:]

    def run(count):
        forward(0, stacked[0])
        for group in range(count):
            mixed = filtered(group, stacked[group])
            if group + 1 < count:
                forward(group + 1, stacked[group + 1], (0,))
            if group > 0:
                inverse(group - 1, back[group - 1], (0,))
            unfold(mixed, back[group])
            if group + 1 < count:
                forward(group + 1, stacked[group + 1], (1,))
            if group > 0:
                inverse(group - 1, back[group - 1], (1,))
        inverse(count - 1, back[count - 1])

    rest = own % groups
    if rest:
        pl.when(jnp.logical_not(at_end))(lambda: run(groups))
        pl.when(at_end)(lambda: run(rest))
    else:
        run(groups)

    if tail:

        @pl.when(at_end)
        def _():
            for block in range(N // 128):
                out[block, 4:8, :] = out[block, 8:12, :]


def gain_kernel(place, gain_re, gain_im):
    k0 = place[0]
    group = place[1] + pl.program_id(0)
    down = lax.broadcasted_iota(jnp.int32, (8, 128), 0)
    across = lax.broadcasted_iota(jnp.int32, (8, 128), 1)
    row = (k0 + RES * (group * 8 + down - HALF)).astype(jnp.float32)
    row_sq = row * row
    row_in = jnp.abs(row) < LIMIT
    for u in range(RES):
        col = (residue(u) + RES * (across - HALF)).astype(jnp.float32)
        square = row_sq + col * col
        scaled = RATIO_SQ * square
        phase = -2.0 * math.pi * distance / wavelength * scaled / (1.0 + jnp.sqrt(1.0 - scaled))
        total = jnp.where(
            row_in & (jnp.abs(col) < LIMIT), jnp.exp(square * (-2.0 / (LIMIT * LIMIT))), 0.0
        )
        quarter = jnp.floor(phase * (2.0 / math.pi) + 0.5)
        left = phase - quarter * 1.5703125
        left = left - quarter * 4.837512969970703125e-4
        left = left - quarter * 7.549789954891882e-8
        sq = left * left
        sine = ((-1.9515295891e-4 * sq + 8.3321608736e-3) * sq - 1.6666654611e-1) * sq * left + left
        cosine = (
            (2.443315711809948e-5 * sq - 1.388731625493765e-3) * sq + 4.166664568298827e-2
        ) * sq * sq - 0.5 * sq + 1.0
        which = quarter.astype(jnp.int32) & 3
        swap = (which & 1) == 1
        cos_part = jnp.where(swap, sine, cosine)
        sin_part = jnp.where(swap, cosine, sine)
        cos_part = jnp.where((which == 1) | (which == 2), -cos_part, cos_part)
        sin_part = jnp.where(which >= 2, -sin_part, sin_part)
        at = (u % (RES // 2)) * 16 + (u // (RES // 2)) * 8
        gain_re[0, at : at + 8, :] = total * cos_part
        gain_im[0, at : at + 8, :] = total * sin_part


def encode(near_real, near_imag, peak_sq, cell_sign):
    square = near_real * near_real + near_imag * near_imag
    root = lax.rsqrt(jnp.maximum(square, 1.2e-38))
    top = lax.rsqrt(peak_sq)
    amp_level = (square * root) * (0.8 * top)
    unit = jnp.minimum(root, 20.0 * top)
    rest = 1.0 - amp_level * amp_level
    level = unit * amp_level
    lift = (rest * lax.rsqrt(rest)) * (unit * cell_sign)
    return (near_real * level + near_imag * lift, near_imag * level - near_real * lift)


def stamp_kernel(peak_one, peak_two, *refs):
    count = (len(refs) - 2) // 2
    pieces, tile, sems = refs[count : 2 * count], refs[-2], refs[-1]
    tile[...] = jnp.full(tile.shape, jnp.maximum(peak_one[0], peak_two[0]), jnp.float32)
    copies = []
    for j, piece in enumerate(pieces):
        rows = pl.ds(piece.shape[0] - SPARE, SPARE)
        copies.append(pltpu.make_async_copy(tile, piece.at[rows], sems.at[j]))
    for copy in copies:
        copy.start()
    for copy in copies:
        copy.wait()


def encode_kernel(count, place, peak_one, peak_two, *refs):
    pieces, (slm_real, slm_imag, *refs) = refs[: CHUNKS * count], refs[CHUNKS * count :]
    own, (tile_real, tile_imag, own_sems, sems) = refs[:CHUNKS], refs[CHUNKS:]
    blocks, width = tile_real.shape[0], pieces[0].shape[-1]
    fetches = [
        pltpu.make_async_copy(pieces[chunk * count], own[chunk], own_sems.at[chunk])
        for chunk in range(CHUNKS)
    ]
    for fetch in fetches:
        fetch.start()
    top = jnp.full((1, width), jnp.maximum(peak_one[0], peak_two[0]), jnp.float32)
    for piece in pieces[(CHUNKS - 1) * count + 1 :]:
        top = jnp.maximum(top, piece[pl.ds(piece.shape[0] - SPARE, 1), :])
    cell = lax.broadcasted_iota(jnp.int32, (CHUNK, width), 0)
    cell = cell + lax.broadcasted_iota(jnp.int32, (CHUNK, width), 1)
    cell_sign = (1 - 2 * (cell & 1)).astype(jnp.float32)
    for fetch in fetches:
        fetch.wait()

    def copies_out(block):
        rows = pl.ds(block * INNER, INNER)
        return [
            pltpu.make_async_copy(tile.at[block], slm.at[rows], sems.at[2 * block + part])
            for part, (tile, slm) in enumerate(((tile_real, slm_real), (tile_imag, slm_imag)))
        ]

    @pl.loop(0, blocks)
    def _(block):
        for at in range(CHUNKS * count):
            chunk, j = divmod(at, count)
            piece = pieces[at] if j else own[chunk]
            lanes = pl.ds(pl.multiple_of((place[0] ^ j) * width, width), width)
            rows = pl.ds(chunk * CHUNK, CHUNK)
            real = pl.ds(pl.multiple_of(block * CHUNK, CHUNK), CHUNK)
            imag = pl.ds(pl.multiple_of((blocks + block) * CHUNK, CHUNK), CHUNK)
            tile_real[block, rows, lanes], tile_imag[block, rows, lanes] = encode(
                piece[real, :], piece[imag, :], top, cell_sign
            )
        for copy in copies_out(block):
            copy.start()

    for block in range(blocks):
        for copy in copies_out(block):
            copy.wait()


def pack_kernel(place, field_real, field_imag, *refs):
    pieces, sems = refs[:-1], refs[-1]
    width = pieces[0].shape[-1]
    copies = []
    for j in list(range(1, len(pieces))) + [0]:
        lanes = pl.ds(pl.multiple_of((place[0] ^ j) * width, width), width)
        for part, field in enumerate((field_real, field_imag)):
            copies.append(
                pltpu.make_async_copy(
                    field.at[:, :, lanes], pieces[j].at[part], sems.at[2 * j + part]
                )
            )
    for copy in copies:
        copy.start()
    for copy in copies:
        copy.wait()


def exchange(pieces, axis):
    total = len(pieces)
    return [pieces[0]] + [
        lax.ppermute(pieces[j], axis, [(i, i ^ j) for i in range(total)]) for j in range(1, total)
    ]


def params(mebibytes):
    return pltpu.CompilerParams(vmem_limit_bytes=mebibytes << 20)


def cost(megabytes):
    return pl.CostEstimate(flops=0, bytes_accessed=megabytes << 20, transcendentals=0)


def whole(memory=pltpu.VMEM):
    return pl.BlockSpec(memory_space=memory)


def body(field_real, field_imag):
    row_total, col_total = lax.axis_size("row"), lax.axis_size("col")
    devices = row_total * col_total
    device = lax.axis_index("row") * col_total + lax.axis_index("col")
    height, tile_width = field_real.shape
    width = tile_width // row_total
    parts = max(1, devices // RES)
    groups = -(-(2 * HALF + 1) // (8 * parts)) * parts
    own = groups // parts
    tail = parts == 1
    total_rows = groups * 16 - (8 if tail else 0)
    own_rows = total_rows // parts
    many = 4 if width == 128 else 1

    fwd_col, inv_col = column_tables(groups, tail)
    line_fh, line_fl, line_ih, line_il = line_tables()
    twist = np.stack(twist_table())
    twist_line = np.ascontiguousarray(np.broadcast_to(twist[:, :, None], twist.shape[:2] + (8, INNER)))
    twist_col = np.pad(twist, ((0, 0), (0, 64 - twist.shape[1]), (0, 0)))
    twist_col = twist_col.reshape(128, INNER).T.copy()

    u = device // parts
    k0 = jnp.where(u >= RES // 2, u - RES, u)
    place = jnp.stack([k0, (device % parts) * own]).astype(jnp.int32)
    gain_shape = jax.ShapeDtypeStruct((own, RES * 8, 128), jnp.float32)
    gain_spec = pl.BlockSpec((1, RES * 8, 128), lambda g: (g, 0, 0))
    gain_re, gain_im = pl.pallas_call(
        gain_kernel,
        grid=(own,),
        in_specs=[whole(pltpu.SMEM)],
        out_specs=[gain_spec, gain_spec],
        out_shape=[gain_shape, gain_shape],
        compiler_params=params(56),
        name="gain",
    )(place)

    place_row = lax.axis_index("row").reshape(1).astype(jnp.int32)
    blocks = height // INNER
    piece = (2, blocks, CHUNK, width)
    piece_shape = jax.ShapeDtypeStruct(piece, jnp.float32)
    anywhere = whole(pl.ANY)
    if width != 128:
        packed = jnp.stack([field_real, field_imag])
        packed = packed.reshape(2, blocks, CHUNKS, CHUNK, row_total, width).transpose(2, 4, 0, 1, 3, 5)
        packed = jnp.take(packed, jnp.arange(row_total) ^ place_row[0], axis=1)
    lines = []
    for chunk in range(CHUNKS):
        if width == 128:
            pieces = pl.pallas_call(
                pack_kernel,
                grid=(1,),
                in_specs=[whole(pltpu.SMEM)]
                + [pl.BlockSpec((blocks, CHUNK, tile_width), lambda i: (0, chunk, 0))] * 2,
                out_specs=[anywhere] * row_total,
                out_shape=[piece_shape] * row_total,
                scratch_shapes=[pltpu.SemaphoreType.DMA((2 * row_total,))],
                compiler_params=params(56),
                cost_estimate=cost(4),
                name="pack",
            )(
                place_row,
                field_real.reshape(blocks, INNER, tile_width),
                field_imag.reshape(blocks, INNER, tile_width),
            )
        else:
            pieces = [packed[chunk, j] for j in range(row_total)]
        pieces = exchange(pieces, "row")
        rows = slice(chunk * CHUNK, (chunk + 1) * CHUNK)
        slab = pltpu.VMEM((RES // many, 2 * CHUNK, many * width), jnp.bfloat16)
        lines = [
            pl.pallas_call(
                partial(column_forward_kernel, row_total),
                in_specs=[whole(pltpu.SMEM)] + [whole()] * (2 + row_total) + [anywhere] * len(lines),
                out_specs=anywhere,
                out_shape=jax.ShapeDtypeStruct((RES, total_rows, width), jnp.float32),
                scratch_shapes=[
                    pltpu.VMEM((RES, total_rows, width), jnp.float32),
                    slab,
                    slab,
                    pltpu.SemaphoreType.DMA((2 * RES // many,)),
                ],
                compiler_params=params(20),
                cost_estimate=cost(20),
                name="column_forward",
            )(place_row, twist_col[rows], fwd_col[chunk], *pieces, *lines)
        ]
    (lines,) = lines

    lines = lines.reshape(devices, own_rows, width)
    lines = lax.all_to_all(lines, ("row", "col"), split_axis=0, concat_axis=0, tiled=True)
    if width == 128:
        order = tuple((b % row_total) * col_total + b // row_total for b in range(N // 128))
    else:
        order = tuple(range(N // 128))
        lines = lines.reshape(row_total, col_total, own_rows, width).transpose(2, 1, 0, 3)
        lines = lines.reshape(own_rows, N // 128, 128).transpose(1, 0, 2)

    at_once = 2
    line_grain = pl.BlockSpec((N // 128, 16 * at_once, 128), lambda i: (0, i, 0))
    gain_grain = pl.BlockSpec((at_once, RES * 8, 128), lambda i: (i, 0, 0))
    lines = pl.pallas_call(
        partial(line_kernel, order, own, tail),
        grid=(-(-own // at_once),),
        in_specs=[line_grain, gain_grain, gain_grain] + [whole()] * 5,
        out_specs=line_grain,
        out_shape=jax.ShapeDtypeStruct((N // 128, own_rows, 128), jnp.float32),
        scratch_shapes=[pltpu.VMEM((2 * RES * 8, 2 * INNER), jnp.bfloat16)] * at_once
        + [pltpu.VMEM((RES * 8, 2 * INNER), jnp.float32)] * at_once,
        compiler_params=params(52),
        name="line",
    )(lines, gain_re, gain_im, twist_line, line_fh, line_fl, line_ih, line_il)

    if width != 128:
        lines = lines.transpose(1, 0, 2).reshape(own_rows, col_total, row_total, width)
        lines = lines.transpose(2, 1, 0, 3).reshape(devices, own_rows, width)
    lines = lax.all_to_all(lines, ("row", "col"), split_axis=0, concat_axis=0, tiled=True)
    lines = lines.reshape(RES, total_rows, width)

    piece_shapes = [
        jax.ShapeDtypeStruct((2 * blocks * CHUNK + spare, width), jnp.float32)
        for spare in (0,) * (CHUNKS - 1) + (SPARE,)
    ]
    *near, peak_sq = pl.pallas_call(
        partial(column_inverse_kernel, row_total),
        in_specs=[whole(pltpu.SMEM), anywhere, whole(), whole()],
        out_specs=[anywhere] * (CHUNKS * row_total) + [whole(pltpu.SMEM)],
        out_shape=[shape for shape in piece_shapes for _ in range(row_total)]
        + [jax.ShapeDtypeStruct((1,), jnp.float32)],
        scratch_shapes=[
            pltpu.VMEM((CHUNKS, row_total, 2, blocks, CHUNK, width), jnp.float32),
            pltpu.VMEM((RES, total_rows, width), jnp.float32),
            pltpu.VMEM((RES // many, inv_col.shape[2], many * width), jnp.bfloat16),
            pltpu.VMEM((CHUNKS, RES, 2 * CHUNK, width), jnp.float32),
            pltpu.VMEM((8, width), jnp.float32),
            pltpu.SemaphoreType.DMA((RES // many,)),
            pltpu.SemaphoreType.DMA((2 * CHUNKS * row_total * 2 * blocks,)),
        ],
        compiler_params=params(56),
        name="column_inverse",
    )(place_row, lines, twist_col, inv_col)
    near = [near[:row_total], near[row_total:]]
    piece_shape = piece_shapes[-1]
    near[0] = exchange(near[0], "row")
    shift = 1
    while shift < col_total:
        partner = [(i, i ^ shift) for i in range(col_total)]
        peaks = [peak_sq, lax.ppermute(peak_sq, "col", partner)]
        shift *= 2
        if shift < col_total:
            peak_sq = jnp.maximum(*peaks)
    others = row_total - 1
    near[1][1:] = pl.pallas_call(
        stamp_kernel,
        in_specs=[whole(pltpu.SMEM)] * 2 + [anywhere] * others,
        out_specs=[anywhere] * others,
        out_shape=[piece_shape] * others,
        scratch_shapes=[
            pltpu.VMEM((SPARE, width), jnp.float32),
            pltpu.SemaphoreType.DMA((others,)),
        ],
        input_output_aliases={2 + j: j for j in range(others)},
        compiler_params=params(56),
        name="stamp",
    )(*peaks, *near[1][1:])
    near[0][1:], near[1][-1] = lax.optimization_barrier((near[0][1:], near[1][-1]))
    near[1] = exchange(near[1], "row")
    if width != 128:
        peak_sq = jnp.maximum(*peaks)[0]
        for piece in near[1][1:]:
            peak_sq = jnp.maximum(peak_sq, piece[-1, 0])
        near = jnp.stack([jnp.stack([piece[: 2 * blocks * CHUNK] for piece in pieces]) for pieces in near])
        near = jnp.take(near, jnp.arange(row_total) ^ place_row[0], axis=1)
        near = near.reshape(CHUNKS, row_total, 2, blocks, CHUNK, width)
        near = near.transpose(2, 3, 0, 4, 1, 5).reshape(2, height, tile_width)
        odd_cell = (jnp.arange(height)[:, None] + jnp.arange(tile_width)[None, :]) % 2
        cell_sign = (1 - 2 * odd_cell).astype(jnp.float32)
        return encode(near[0], near[1], peak_sq, cell_sign)
    tile_shape = jax.ShapeDtypeStruct((height, tile_width), jnp.float32)
    tile = pltpu.VMEM((blocks, INNER, tile_width), jnp.float32)
    return pl.pallas_call(
        partial(encode_kernel, row_total),
        in_specs=[whole(pltpu.SMEM)] * 3 + ([anywhere] + [whole()] * others) * CHUNKS,
        out_specs=[anywhere] * 2,
        out_shape=[tile_shape, tile_shape],
        scratch_shapes=[pltpu.VMEM(pieces[0].shape, jnp.float32) for pieces in near]
        + [tile, tile, pltpu.SemaphoreType.DMA((CHUNKS,)), pltpu.SemaphoreType.DMA((2 * blocks,))],
        compiler_params=params(16),
        name="encode",
    )(place_row, *peaks, *near[0], *near[1])


def solution(mesh):
    in_specs = (P("row", "col"), P("row", "col"))
    out_specs = (P("row", "col"), P("row", "col"))
    return jax.shard_map(body, mesh=mesh, in_specs=in_specs, out_specs=out_specs, check_vma=False)
```

```python
from functools import partial
import math

import jax
import jax.numpy as jnp
import ml_dtypes
import numpy as np
from jax import lax
from jax.experimental import pallas as pl
from jax.experimental.pallas import tpu as pltpu
from jax.sharding import PartitionSpec as P

N = 4096
PAD = 2 * N
wavelength = 5.2e-07
distance = 0.2
INNER = 256
SLABS = N // INNER
RES = PAD // INNER
HALF = 40
CHUNKS = 2
CHUNK = INNER // CHUNKS
SPARE = 8


def optics(padded_side):
    pitch = 2e-06 * math.sqrt(8192.0 / padded_side)
    extent = padded_side * pitch
    ratio_sq = (wavelength / extent) ** 2
    band_limit = extent / (wavelength * math.sqrt((2.0 * distance / extent) ** 2 + 1.0))
    return (ratio_sq, band_limit)


RATIO_SQ, LIMIT = optics(PAD)
assert RES * HALF - RES // 2 + RES > LIMIT and RES * HALF + RES // 2 > LIMIT


def residue(u):
    return u if u < RES // 2 else u - RES


def split16(table):
    table = np.asarray(table, np.float64)
    high = table.astype(np.float32).astype(ml_dtypes.bfloat16)
    low = (table - high.astype(np.float64)).astype(np.float32).astype(ml_dtypes.bfloat16)
    return high, low


def row_order(groups, tail):
    rows = []
    for group in range(groups):
        size = 4 if tail and group == groups - 1 else 8
        for part in range(2):
            for s in range(size):
                rows.append((part, group * 8 + s - HALF))
    return rows


def column_tables(groups, tail):
    q = np.arange(INNER)
    rows = row_order(groups, tail)
    forward = np.zeros((len(rows), 2, INNER))
    inverse = np.zeros((2, INNER, len(rows)))
    for at, (part, k1) in enumerate(rows):
        if abs(k1) > HALF:
            continue
        angle = 2.0 * np.pi * ((k1 * q) % INNER) / INNER
        c, s = np.cos(angle), np.sin(angle)
        forward[at] = (c, s) if part == 0 else (-s, c)
        inverse[:, :, at] = (c, s) if part == 0 else (-s, c)
    forward = forward.reshape(-1, 2, CHUNKS, CHUNK // 8, 8).transpose(2, 0, 3, 1, 4)
    forward = np.concatenate(split16(forward.reshape(CHUNKS, len(rows), 2 * CHUNK)), axis=1)
    inverse = inverse.reshape(2, CHUNKS, CHUNK, -1).transpose(1, 0, 2, 3)
    high, low = split16(inverse.reshape(CHUNKS, 2 * CHUNK, len(rows)))
    inverse = np.concatenate([high, high, low], axis=2)
    inverse = np.pad(inverse, ((0, 0), (0, 0), (0, -3 * len(rows) % 16)))
    return forward, inverse


def line_tables():
    q = np.arange(INNER)
    forward = np.zeros((2 * INNER, 256))
    inverse = np.zeros((256, 2 * INNER))
    for lane in range(2 * HALF + 1):
        angle = 2.0 * np.pi * (((lane - HALF) * q) % INNER) / INNER
        c, s = np.cos(angle), np.sin(angle)
        forward[:INNER, lane], forward[INNER:, lane] = c, s
        forward[:INNER, 128 + lane], forward[INNER:, 128 + lane] = -s, c
        inverse[lane, :INNER], inverse[lane, INNER:] = c, s
        inverse[128 + lane, :INNER], inverse[128 + lane, INNER:] = -s, c
    return split16(forward) + split16(inverse)


def twist_table():
    q = np.arange(INNER) + N // 2
    k0 = np.arange(RES // 2 + 1)
    angle = 2.0 * np.pi * ((k0[:, None] * q[None, :]) % PAD) / PAD
    return np.cos(angle).astype(np.float32), (-np.sin(angle)).astype(np.float32)


def turn(value, num, den):
    re, im = value
    num = num % den
    eighth = 8 * num
    if num == 0:
        return re, im
    if 2 * num == den:
        return -re, -im
    if 4 * num == den:
        return -im, re
    if 4 * num == 3 * den:
        return im, -re
    if eighth % den == 0:
        root = np.float32(math.sqrt(0.5))
        kind = eighth // den
        if kind == 1:
            return (re - im) * root, (re + im) * root
        if kind == 3:
            return (re + im) * (-root), (re - im) * root
        if kind == 5:
            return (im - re) * root, (re + im) * (-root)
        return (re + im) * root, (im - re) * root
    c = np.float32(math.cos(2.0 * math.pi * num / den))
    s = np.float32(math.sin(2.0 * math.pi * num / den))
    return re * c - im * s, re * s + im * c


def small_dft(get, ids, sign):
    count = len(ids)
    if count == 1:
        return [get(ids[0])]
    even = small_dft(get, ids[0::2], sign)
    odd = small_dft(get, ids[1::2], sign)
    half = count // 2
    first, second = [], []
    for j in range(half):
        re, im = even[j]
        t_re, t_im = turn(odd[j], sign * j, count)
        first.append((re + t_re, im + t_im))
        second.append((re - t_re, im - t_im))
    return first + second


def forward_slabs(get, put):
    ids = list(range(SLABS))
    for v, value in enumerate(small_dft(get, ids, -1)):
        put(2 * v, value)
    for v, value in enumerate(small_dft(lambda n: turn(get(n), -n, RES), ids, -1)):
        put(2 * v + 1, value)


def inverse_slabs(get, put):
    even = small_dft(get, list(range(0, RES, 2)), 1)
    odd = small_dft(get, list(range(1, RES, 2)), 1)
    for n in range(SLABS):
        t_re, t_im = turn(odd[n], n, RES)
        put(n, (even[n][0] + t_re, even[n][1] + t_im))


def twisted(value, u, sign, read):
    re, im = value
    k0 = residue(u)
    if k0 == 0:
        return value
    c, s = read(abs(k0))
    if (k0 < 0) == (sign > 0):
        return re * c + im * s, im * c - re * s
    return re * c - im * s, re * s + im * c


def high_low(value):
    high = value.astype(jnp.bfloat16)
    low = (value - high.astype(jnp.float32)).astype(jnp.bfloat16)
    return high, low


def dot16(left, right):
    return jnp.dot(left, right, preferred_element_type=jnp.float32)


def three_left(stacked, count, high, low):
    both = dot16(stacked[...], high)
    return both[:count] + both[count:] + dot16(stacked[:count], low)


def three_right(stacked, count, high, low):
    both = dot16(stacked, high)
    return both[:count] + both[count:] + dot16(stacked[:count], low)


def column_twist(twist, q0):
    seen = {}

    def read(k):
        if k not in seen:
            rows = pl.ds(q0, 8)
            seen[k] = twist[rows, k : k + 1], twist[rows, 64 + k : 65 + k]
        return seen[k]

    return read


def column_forward_kernel(count, place, twist, matrix, *refs):
    pieces, refs = refs[:count], refs[count:]
    before, (out, total, high, low, sems) = refs[:-5], refs[-5:]
    width = pieces[0].shape[-1]
    per_source = pieces[0].shape[1]
    many = high.shape[-1] // width
    products = RES // many
    rows_out = out.shape[1]

    def copy_in(p):
        part = pl.ds(p * many, many)
        return pltpu.make_async_copy(before[0].at[part], total.at[part], sems.at[p])

    def copy_out(p):
        part = pl.ds(p * many, many)
        return pltpu.make_async_copy(total.at[part], out.at[part], sems.at[products + p])

    if before:
        for p in range(products):
            copy_in(p).start()

    for here in range(count):

        @pl.when(place[0] == here)
        def _():
            @pl.loop(0, CHUNK // 8)
            def _(t):
                q0 = pl.multiple_of(t * 8, 8)
                read = column_twist(twist, q0)

                def get(n):
                    source, block = divmod(n, per_source)
                    piece = pieces[source ^ here]
                    rows = pl.ds(q0, 8)
                    return piece[0, block, rows, :], piece[1, block, rows, :]

                def put(u, value):
                    item = jnp.concatenate(twisted(value, u, 1, read), axis=0)
                    rows = pl.ds(pl.multiple_of(t * 16, 16), 16)
                    at = (u // many, rows, pl.ds((u % many) * width, width))
                    high[at], low[at] = high_low(item)

                forward_slabs(get, put)

    @pl.loop(0, products)
    def _(p):
        done = three_left(matrix, rows_out, high[p], low[p])
        if before:
            copy_in(p).wait()
        for part in range(many):
            item = done[:, part * width : (part + 1) * width]
            at = p * many + part
            total[at] = total[at] + item if before else item
        copy_out(p).start()

    for p in range(products):
        copy_out(p).wait()


def column_inverse_kernel(count, place, source, twist, matrix, *refs):
    pieces, (peak_sq, near, lines, deep, back, top, sems, out_sems) = refs[:-8], refs[-8:]
    width = lines.shape[-1]
    rows_in = lines.shape[1]
    per_dest = near.shape[3]
    many = deep.shape[-1] // width
    products = RES // many

    def copy_in(p):
        part = pl.ds(p * many, many)
        return pltpu.make_async_copy(source.at[part], lines.at[part], sems.at[p])

    def copies_out(chunk, part):
        size = CHUNK // 2
        copies = []
        for j in range(count):
            for at in range(2 * per_dest):
                rows = pl.ds(part * size, size)
                here = near.at[chunk, place[0] ^ j, at // per_dest, at % per_dest, rows]
                there = pieces[chunk * count + j].at[pl.ds(at * CHUNK + part * size, size)]
                sem = out_sems.at[((chunk * 2 + part) * count + j) * 2 * per_dest + at]
                copies.append(pltpu.make_async_copy(here, there, sem))
        return copies

    def prepare(p):
        copy_in(p).wait()
        blocks = [lines[p * many + part] for part in range(many)]
        joined = jnp.concatenate(blocks, axis=1) if many > 1 else blocks[0]
        high = joined.astype(jnp.bfloat16).astype(jnp.float32)
        parts = [high, joined - high, high]
        if deep.shape[1] > 3 * rows_in:
            parts.append(jnp.zeros((deep.shape[1] - 3 * rows_in, many * width), jnp.float32))
        deep[p] = jnp.concatenate(parts, axis=0).astype(jnp.bfloat16)

    def product(p, chunk):
        done = dot16(matrix[chunk], deep[p])
        for part in range(many):
            back[chunk, p * many + part] = done[:, part * width : (part + 1) * width]

    def butterflies(t, chunk):
        q0 = pl.multiple_of(t * 8, 8)
        largest = []
        read = column_twist(twist, pl.multiple_of(chunk * CHUNK + q0, 8))

        def get(u):
            re = back[chunk, u, pl.ds(q0, 8), :]
            im = back[chunk, u, pl.ds(CHUNK + q0, 8), :]
            return twisted((re, im), u, -1, read)

        def put(n, value):
            dest, block = divmod(n, per_dest)
            rows = pl.ds(q0, 8)
            near[chunk, dest, 0, block, rows, :], near[chunk, dest, 1, block, rows, :] = value
            largest.append(value[0] * value[0] + value[1] * value[1])

        inverse_slabs(get, put)
        while len(largest) > 1:
            largest = [jnp.maximum(a, b) for a, b in zip(largest[0::2], largest[1::2])]
        top[...] = jnp.maximum(top[...], largest[0])

    for p in range(products):
        copy_in(p).start()
    top[...] = jnp.zeros_like(top)

    @pl.loop(0, products)
    def _(p):
        prepare(p)
        product(p, 0)

    tiles = CHUNK // 16
    steps = min(tiles, products // 2)
    for chunk in range(CHUNKS):
        for part in range(2):

            @pl.loop(part * steps, (part + 1) * steps)
            def _(t):
                for item in range(tiles // steps):
                    butterflies(t * (tiles // steps) + item, chunk)
                if chunk + 1 < CHUNKS:
                    for item in range(products // 2 // steps):
                        product(t * (products // 2 // steps) + item, chunk + 1)

            for copy in copies_out(chunk, part):
                copy.start()
    peak_sq[0] = jnp.max(top[...])
    for chunk in range(CHUNKS):
        for part in range(2):
            for copy in copies_out(chunk, part):
                copy.wait()


def line_kernel(
    order, own, tail, lines, gain, twist, fwd_high, fwd_low, inv_high, inv_low, out, *scratch
):
    half = RES * 8
    at_end = pl.program_id(0) == pl.num_programs(0) - 1

    def line_twist(side):
        def read(k):
            lanes = pl.ds(side * 128, 128)
            return twist[0, k, :, lanes], twist[1, k, :, lanes]

        return read

    def forward(group, stacked, sides=(0, 1)):
        for side in sides:
            waiting = {}

            def get(m):
                block = order[2 * m + side]
                at = group * 16
                return lines[block, at : at + 8, :], lines[block, at + 8 : at + 16, :]

            def put(u, value):
                waiting[u] = twisted(value, u, 1, line_twist(side))
                v = (u + RES // 2) % RES
                if v in waiting:
                    first = min(u, v)
                    rows = pl.ds(first * 16, 16)
                    rows_low = pl.ds(half + first * 16, 16)
                    for part in range(2):
                        item = jnp.concatenate(
                            [waiting[first][part], waiting[first + RES // 2][part]], axis=0
                        )
                        at = pl.ds(part * INNER + side * 128, 128)
                        stacked[rows, at], stacked[rows_low, at] = high_low(item)

            forward_slabs(get, put)

    def filtered(group, stacked):
        spec = three_right(stacked[...], half, fwd_high[...], fwd_low[...])
        spec_re, spec_im = spec[:, :128], spec[:, 128:]
        g_re, g_im = gain[0, group], gain[1, group]
        mixed = jnp.concatenate(
            [spec_re * g_re - spec_im * g_im, spec_re * g_im + spec_im * g_re], axis=1
        )
        return jnp.concatenate(high_low(mixed), axis=0)

    def unfold(mixed, back):
        back[...] = three_right(mixed, half, inv_high[...], inv_low[...])

    def inverse(group, back, sides=(0, 1)):
        for side in sides:

            def get(u):
                rows = pl.ds((u % (RES // 2)) * 16 + (u // (RES // 2)) * 8, 8)
                re = back[rows, pl.ds(side * 128, 128)]
                im = back[rows, pl.ds(INNER + side * 128, 128)]
                return twisted((re, im), u, -1, line_twist(side))

            def put(m, value):
                block = order[2 * m + side]
                at = group * 16
                out[block, at : at + 8, :], out[block, at + 8 : at + 16, :] = value

            inverse_slabs(get, put)

    if tail:

        @pl.when(at_end)
        def _():
            for block in range(N // 128):
                lines[block, 8:12, :] = lines[block, 4:8, :]

    groups = len(scratch) // 2

    stacked, back = scratch[:groups], scratch[groups:]

    def run(count):
        forward(0, stacked[0])
        for group in range(count):
            mixed = filtered(group, stacked[group])
            if group + 1 < count:
                forward(group + 1, stacked[group + 1], (0,))
            if group > 0:
                inverse(group - 1, back[group - 1], (0,))
            unfold(mixed, back[group])
            if group + 1 < count:
                forward(group + 1, stacked[group + 1], (1,))
            if group > 0:
                inverse(group - 1, back[group - 1], (1,))
        inverse(count - 1, back[count - 1])

    rest = own % groups
    if rest:
        pl.when(jnp.logical_not(at_end))(lambda: run(groups))
        pl.when(at_end)(lambda: run(rest))
    else:
        run(groups)

    if tail:

        @pl.when(at_end)
        def _():
            for block in range(N // 128):
                out[block, 4:8, :] = out[block, 8:12, :]


def gain_kernel(place, gain):
    k0 = place[0]
    group = place[1] + pl.program_id(0)
    down = lax.broadcasted_iota(jnp.int32, (8, 128), 0)
    across = lax.broadcasted_iota(jnp.int32, (8, 128), 1)
    row = (k0 + RES * (group * 8 + down - HALF)).astype(jnp.float32)
    row_sq = row * row
    row_in = jnp.abs(row) < LIMIT
    for u in range(RES):
        col = (residue(u) + RES * (across - HALF)).astype(jnp.float32)
        square = row_sq + col * col
        scaled = RATIO_SQ * square
        phase = -2.0 * math.pi * distance / wavelength * scaled / (1.0 + jnp.sqrt(1.0 - scaled))
        total = jnp.where(
            row_in & (jnp.abs(col) < LIMIT), jnp.exp(square * (-2.0 / (LIMIT * LIMIT))), 0.0
        )
        quarter = jnp.floor(phase * (2.0 / math.pi) + 0.5)
        left = phase - quarter * 1.5703125
        left = left - quarter * 4.837512969970703125e-4
        left = left - quarter * 7.549789954891882e-8
        sq = left * left
        sine = ((-1.9515295891e-4 * sq + 8.3321608736e-3) * sq - 1.6666654611e-1) * sq * left + left
        cosine = (
            (2.443315711809948e-5 * sq - 1.388731625493765e-3) * sq + 4.166664568298827e-2
        ) * sq * sq - 0.5 * sq + 1.0
        which = quarter.astype(jnp.int32) & 3
        swap = (which & 1) == 1
        cos_part = jnp.where(swap, sine, cosine)
        sin_part = jnp.where(swap, cosine, sine)
        cos_part = jnp.where((which == 1) | (which == 2), -cos_part, cos_part)
        sin_part = jnp.where(which >= 2, -sin_part, sin_part)
        at = (u % (RES // 2)) * 16 + (u // (RES // 2)) * 8
        gain[0, 0, at : at + 8, :] = total * cos_part
        gain[1, 0, at : at + 8, :] = total * sin_part


def encode(near_real, near_imag, peak_sq, cell_sign):
    square = near_real * near_real + near_imag * near_imag
    root = lax.rsqrt(jnp.maximum(square, 1.2e-38))
    top = lax.rsqrt(peak_sq)
    amp_level = (square * root) * (0.8 * top)
    unit = jnp.minimum(root, 20.0 * top)
    rest = 1.0 - amp_level * amp_level
    level = unit * amp_level
    lift = (rest * lax.rsqrt(rest)) * (unit * cell_sign)
    return (near_real * level + near_imag * lift, near_imag * level - near_real * lift)


def stamp_kernel(others, peak_one, peak_two, *refs):
    refs = refs[others:]
    stay, pieces, refs = refs[:CHUNKS], refs[CHUNKS : CHUNKS + others], refs[CHUNKS + others :]
    fetched, (tile, sems) = refs[:CHUNKS], refs[CHUNKS:]
    tile[...] = jnp.full(tile.shape, jnp.maximum(peak_one[0], peak_two[0]), jnp.float32)
    copies = []
    for j, piece in enumerate(pieces):
        rows = pl.ds(piece.shape[0] - SPARE, SPARE)
        copies.append(pltpu.make_async_copy(tile, piece.at[rows], sems.at[j]))
    for chunk in range(CHUNKS):
        copies.append(pltpu.make_async_copy(stay[chunk], fetched[chunk], sems.at[others + chunk]))
    for copy in copies:
        copy.start()
    for copy in copies:
        copy.wait()


def encode_kernel(count, place, peak_one, peak_two, *refs):
    pieces, refs = refs[: CHUNKS * count], refs[CHUNKS * count :]
    slm_real, slm_imag, tile_real, tile_imag, sems = refs
    blocks, width = tile_real.shape[0], pieces[0].shape[-1]
    top = jnp.full((1, width), jnp.maximum(peak_one[0], peak_two[0]), jnp.float32)
    for piece in pieces[(CHUNKS - 1) * count + 1 :]:
        top = jnp.maximum(top, piece[pl.ds(piece.shape[0] - SPARE, 1), :])
    cell = lax.broadcasted_iota(jnp.int32, (CHUNK, width), 0)
    cell = cell + lax.broadcasted_iota(jnp.int32, (CHUNK, width), 1)
    cell_sign = (1 - 2 * (cell & 1)).astype(jnp.float32)

    def copies_out(block):
        rows = pl.ds(block * INNER, INNER)
        return [
            pltpu.make_async_copy(tile.at[block], slm.at[rows], sems.at[2 * block + part])
            for part, (tile, slm) in enumerate(((tile_real, slm_real), (tile_imag, slm_imag)))
        ]

    @pl.loop(0, blocks)
    def _(block):
        for at in range(CHUNKS * count):
            chunk, j = divmod(at, count)
            piece = pieces[at]
            lanes = pl.ds(pl.multiple_of((place[0] ^ j) * width, width), width)
            rows = pl.ds(chunk * CHUNK, CHUNK)
            real = pl.ds(pl.multiple_of(block * CHUNK, CHUNK), CHUNK)
            imag = pl.ds(pl.multiple_of((blocks + block) * CHUNK, CHUNK), CHUNK)
            tile_real[block, rows, lanes], tile_imag[block, rows, lanes] = encode(
                piece[real, :], piece[imag, :], top, cell_sign
            )
        for copy in copies_out(block):
            copy.start()

    for block in range(blocks):
        for copy in copies_out(block):
            copy.wait()


def pack_kernel(place, field_real, field_imag, *refs):
    pieces, sems = refs[:-1], refs[-1]
    width = pieces[0].shape[-1]
    copies = []
    for j in list(range(1, len(pieces))) + [0]:
        lanes = pl.ds(pl.multiple_of((place[0] ^ j) * width, width), width)
        for part, field in enumerate((field_real, field_imag)):
            copies.append(
                pltpu.make_async_copy(
                    field.at[:, :, lanes], pieces[j].at[part], sems.at[2 * j + part]
                )
            )
    for copy in copies:
        copy.start()
    for copy in copies:
        copy.wait()


def exchange(pieces, axis):
    total = len(pieces)
    return [pieces[0]] + [
        lax.ppermute(pieces[j], axis, [(i, i ^ j) for i in range(total)]) for j in range(1, total)
    ]


def params(mebibytes):
    return pltpu.CompilerParams(vmem_limit_bytes=mebibytes << 20)


def cost(megabytes):
    return pl.CostEstimate(flops=0, bytes_accessed=megabytes << 20, transcendentals=0)


def whole(memory=pltpu.VMEM):
    return pl.BlockSpec(memory_space=memory)


def body(field_real, field_imag):
    row_total, col_total = lax.axis_size("row"), lax.axis_size("col")
    devices = row_total * col_total
    device = lax.axis_index("row") * col_total + lax.axis_index("col")
    height, tile_width = field_real.shape
    width = tile_width // row_total
    parts = max(1, devices // RES)
    groups = -(-(2 * HALF + 1) // (8 * parts)) * parts
    own = groups // parts
    tail = parts == 1
    total_rows = groups * 16 - (8 if tail else 0)
    own_rows = total_rows // parts
    many = 4 if width == 128 else 1

    fwd_col, inv_col = column_tables(groups, tail)
    line_fh, line_fl, line_ih, line_il = line_tables()
    twist = np.stack(twist_table())
    twist_line = np.ascontiguousarray(np.broadcast_to(twist[:, :, None], twist.shape[:2] + (8, INNER)))
    twist_col = np.pad(twist, ((0, 0), (0, 64 - twist.shape[1]), (0, 0)))
    twist_col = twist_col.reshape(128, INNER).T.copy()

    u = device // parts
    k0 = jnp.where(u >= RES // 2, u - RES, u)
    place = jnp.stack([k0, (device % parts) * own]).astype(jnp.int32)
    gain = pl.pallas_call(
        gain_kernel,
        grid=(own,),
        in_specs=[whole(pltpu.SMEM)],
        out_specs=pl.BlockSpec((2, 1, RES * 8, 128), lambda g: (0, g, 0, 0)),
        out_shape=jax.ShapeDtypeStruct((2, own, RES * 8, 128), jnp.float32),
        compiler_params=params(56),
        name="gain",
    )(place)

    place_row = lax.axis_index("row").reshape(1).astype(jnp.int32)
    blocks = height // INNER
    piece = (2, blocks, CHUNK, width)
    piece_shape = jax.ShapeDtypeStruct(piece, jnp.float32)
    anywhere = whole(pl.ANY)
    if width != 128:
        packed = jnp.stack([field_real, field_imag])
        packed = packed.reshape(2, blocks, CHUNKS, CHUNK, row_total, width).transpose(2, 4, 0, 1, 3, 5)
        packed = jnp.take(packed, jnp.arange(row_total) ^ place_row[0], axis=1)
    lines = []
    for chunk in range(CHUNKS):
        if width == 128:
            pieces = pl.pallas_call(
                pack_kernel,
                grid=(1,),
                in_specs=[whole(pltpu.SMEM)]
                + [pl.BlockSpec((blocks, CHUNK, tile_width), lambda i: (0, chunk, 0))] * 2,
                out_specs=[anywhere] * row_total,
                out_shape=[piece_shape] * row_total,
                scratch_shapes=[pltpu.SemaphoreType.DMA((2 * row_total,))],
                compiler_params=params(56),
                cost_estimate=cost(4),
                name="pack",
            )(
                place_row,
                field_real.reshape(blocks, INNER, tile_width),
                field_imag.reshape(blocks, INNER, tile_width),
            )
        else:
            pieces = [packed[chunk, j] for j in range(row_total)]
        pieces = exchange(pieces, "row")
        rows = slice(chunk * CHUNK, (chunk + 1) * CHUNK)
        slab = pltpu.VMEM((RES // many, 2 * CHUNK, many * width), jnp.bfloat16)
        lines = [
            pl.pallas_call(
                partial(column_forward_kernel, row_total),
                in_specs=[whole(pltpu.SMEM)] + [whole()] * (2 + row_total) + [anywhere] * len(lines),
                out_specs=anywhere,
                out_shape=jax.ShapeDtypeStruct((RES, total_rows, width), jnp.float32),
                scratch_shapes=[
                    pltpu.VMEM((RES, total_rows, width), jnp.float32),
                    slab,
                    slab,
                    pltpu.SemaphoreType.DMA((2 * RES // many,)),
                ],
                compiler_params=params(20),
                cost_estimate=cost(20),
                name="column_forward",
            )(place_row, twist_col[rows], fwd_col[chunk], *pieces, *lines)
        ]
    (lines,) = lines

    lines = lines.reshape(devices, own_rows, width)
    lines = lax.all_to_all(lines, ("row", "col"), split_axis=0, concat_axis=0, tiled=True)
    if width == 128:
        order = tuple((b % row_total) * col_total + b // row_total for b in range(N // 128))
    else:
        order = tuple(range(N // 128))
        lines = lines.reshape(row_total, col_total, own_rows, width).transpose(2, 1, 0, 3)
        lines = lines.reshape(own_rows, N // 128, 128).transpose(1, 0, 2)

    at_once = 2
    line_grain = pl.BlockSpec((N // 128, 16 * at_once, 128), lambda i: (0, i, 0))
    gain_grain = pl.BlockSpec((2, at_once, RES * 8, 128), lambda i: (0, i, 0, 0))
    lines = pl.pallas_call(
        partial(line_kernel, order, own, tail),
        grid=(-(-own // at_once),),
        in_specs=[line_grain, gain_grain] + [whole()] * 5,
        out_specs=line_grain,
        out_shape=jax.ShapeDtypeStruct((N // 128, own_rows, 128), jnp.float32),
        scratch_shapes=[pltpu.VMEM((2 * RES * 8, 2 * INNER), jnp.bfloat16)] * at_once
        + [pltpu.VMEM((RES * 8, 2 * INNER), jnp.float32)] * at_once,
        compiler_params=params(48),
        name="line",
    )(lines, gain, twist_line, line_fh, line_fl, line_ih, line_il)

    if width != 128:
        lines = lines.transpose(1, 0, 2).reshape(own_rows, col_total, row_total, width)
        lines = lines.transpose(2, 1, 0, 3).reshape(devices, own_rows, width)
    lines = lax.all_to_all(lines, ("row", "col"), split_axis=0, concat_axis=0, tiled=True)
    lines = lines.reshape(RES, total_rows, width)

    piece_shapes = [
        jax.ShapeDtypeStruct((2 * blocks * CHUNK + spare, width), jnp.float32)
        for spare in (0,) * (CHUNKS - 1) + (SPARE,)
    ]
    *near, peak_sq = pl.pallas_call(
        partial(column_inverse_kernel, row_total),
        in_specs=[whole(pltpu.SMEM), anywhere, whole(), whole()],
        out_specs=[anywhere] * (CHUNKS * row_total) + [whole(pltpu.SMEM)],
        out_shape=[shape for shape in piece_shapes for _ in range(row_total)]
        + [jax.ShapeDtypeStruct((1,), jnp.float32)],
        scratch_shapes=[
            pltpu.VMEM((CHUNKS, row_total, 2, blocks, CHUNK, width), jnp.float32),
            pltpu.VMEM((RES, total_rows, width), jnp.float32),
            pltpu.VMEM((RES // many, inv_col.shape[2], many * width), jnp.bfloat16),
            pltpu.VMEM((CHUNKS, RES, 2 * CHUNK, width), jnp.float32),
            pltpu.VMEM((8, width), jnp.float32),
            pltpu.SemaphoreType.DMA((RES // many,)),
            pltpu.SemaphoreType.DMA((2 * CHUNKS * row_total * 2 * blocks,)),
        ],
        compiler_params=params(56),
        name="column_inverse",
    )(place_row, lines, twist_col, inv_col)
    near = [near[:row_total], near[row_total:]]
    piece_shape = piece_shapes[-1]
    near[0] = exchange(near[0], "row")
    shift = 1
    while shift < col_total:
        partner = [(i, i ^ shift) for i in range(col_total)]
        peaks = [peak_sq, lax.ppermute(peak_sq, "col", partner)]
        shift *= 2
        if shift < col_total:
            peak_sq = jnp.maximum(*peaks)
    others = row_total - 1
    stamped = pl.pallas_call(
        partial(stamp_kernel, others),
        in_specs=[whole(pltpu.SMEM)] * 2 + [anywhere] * (others + CHUNKS),
        out_specs=[anywhere] * others + [whole()] * CHUNKS,
        out_shape=[piece_shape] * others + piece_shapes,
        scratch_shapes=[
            pltpu.VMEM((SPARE, width), jnp.float32),
            pltpu.SemaphoreType.DMA((others + CHUNKS,)),
        ],
        input_output_aliases={2 + j: j for j in range(others)},
        compiler_params=params(16),
        name="stamp",
    )(*peaks, *near[1][1:], near[0][0], near[1][0])
    near[1][1:] = stamped[:others]
    near[0][0], near[1][0] = stamped[others:]
    near[0][1:], near[1][-1] = lax.optimization_barrier((near[0][1:], near[1][-1]))
    near[1] = exchange(near[1], "row")
    if width != 128:
        peak_sq = jnp.maximum(*peaks)[0]
        for piece in near[1][1:]:
            peak_sq = jnp.maximum(peak_sq, piece[-1, 0])
        near = jnp.stack([jnp.stack([piece[: 2 * blocks * CHUNK] for piece in pieces]) for pieces in near])
        near = jnp.take(near, jnp.arange(row_total) ^ place_row[0], axis=1)
        near = near.reshape(CHUNKS, row_total, 2, blocks, CHUNK, width)
        near = near.transpose(2, 3, 0, 4, 1, 5).reshape(2, height, tile_width)
        odd_cell = (jnp.arange(height)[:, None] + jnp.arange(tile_width)[None, :]) % 2
        cell_sign = (1 - 2 * odd_cell).astype(jnp.float32)
        return encode(near[0], near[1], peak_sq, cell_sign)
    tile_shape = jax.ShapeDtypeStruct((height, tile_width), jnp.float32)
    tile = pltpu.VMEM((blocks, INNER, tile_width), jnp.float32)
    return pl.pallas_call(
        partial(encode_kernel, row_total),
        in_specs=[whole(pltpu.SMEM)] * 3 + [whole()] * (CHUNKS * row_total),
        out_specs=[anywhere] * 2,
        out_shape=[tile_shape, tile_shape],
        scratch_shapes=[tile, tile, pltpu.SemaphoreType.DMA((2 * blocks,))],
        compiler_params=params(16),
        name="encode",
    )(place_row, *peaks, *near[0], *near[1])


def solution(mesh):
    in_specs = (P("row", "col"), P("row", "col"))
    out_specs = (P("row", "col"), P("row", "col"))
    return jax.shard_map(body, mesh=mesh, in_specs=in_specs, out_specs=out_specs, check_vma=False)
```

```python
from functools import partial
import math

import jax
import jax.numpy as jnp
import ml_dtypes
import numpy as np
from jax import lax
from jax.experimental import pallas as pl
from jax.experimental.pallas import tpu as pltpu
from jax.sharding import PartitionSpec as P

N = 4096
PAD = 2 * N
wavelength = 5.2e-07
distance = 0.2
INNER = 256
SLABS = N // INNER
RES = PAD // INNER
HALF = 40
CHUNKS = 2
CHUNK = INNER // CHUNKS
FRONT = ((0, 64), (128, 128), (64, 64))
SPARE = 8


def optics(padded_side):
    pitch = 2e-06 * math.sqrt(8192.0 / padded_side)
    extent = padded_side * pitch
    ratio_sq = (wavelength / extent) ** 2
    band_limit = extent / (wavelength * math.sqrt((2.0 * distance / extent) ** 2 + 1.0))
    return (ratio_sq, band_limit)


RATIO_SQ, LIMIT = optics(PAD)
assert RES * HALF - RES // 2 + RES > LIMIT and RES * HALF + RES // 2 > LIMIT


def residue(u):
    return u if u < RES // 2 else u - RES


def split16(table):
    table = np.asarray(table, np.float64)
    high = table.astype(np.float32).astype(ml_dtypes.bfloat16)
    low = (table - high.astype(np.float64)).astype(np.float32).astype(ml_dtypes.bfloat16)
    return high, low


def row_order(groups, tail):
    rows = []
    for group in range(groups):
        size = 4 if tail and group == groups - 1 else 8
        for part in range(2):
            for s in range(size):
                rows.append((part, group * 8 + s - HALF))
    return rows


def column_tables(groups, tail):
    q = np.arange(INNER)
    rows = row_order(groups, tail)
    forward = np.zeros((len(rows), 2, INNER))
    inverse = np.zeros((2, INNER, len(rows)))
    for at, (part, k1) in enumerate(rows):
        if abs(k1) > HALF:
            continue
        angle = 2.0 * np.pi * ((k1 * q) % INNER) / INNER
        c, s = np.cos(angle), np.sin(angle)
        forward[at] = (c, s) if part == 0 else (-s, c)
        inverse[:, :, at] = (c, s) if part == 0 else (-s, c)
    tables = []
    for start, size in FRONT:
        part = forward[:, :, start : start + size].reshape(-1, 2, size // 8, 8)
        part = part.transpose(0, 2, 1, 3).reshape(-1, 2 * size)
        tables.append(np.concatenate(split16(part), axis=0))
    inverse = inverse.reshape(2, CHUNKS, CHUNK, -1).transpose(1, 0, 2, 3)
    high, low = split16(inverse.reshape(CHUNKS, 2 * CHUNK, len(rows)))
    inverse = np.concatenate([high, high, low], axis=2)
    inverse = np.pad(inverse, ((0, 0), (0, 0), (0, -3 * len(rows) % 16)))
    return tables, inverse


def line_tables():
    q = np.arange(INNER)
    forward = np.zeros((2 * INNER, 256))
    inverse = np.zeros((256, 2 * INNER))
    for lane in range(2 * HALF + 1):
        angle = 2.0 * np.pi * (((lane - HALF) * q) % INNER) / INNER
        c, s = np.cos(angle), np.sin(angle)
        forward[:INNER, lane], forward[INNER:, lane] = c, s
        forward[:INNER, 128 + lane], forward[INNER:, 128 + lane] = -s, c
        inverse[lane, :INNER], inverse[lane, INNER:] = c, s
        inverse[128 + lane, :INNER], inverse[128 + lane, INNER:] = -s, c
    return split16(forward) + split16(inverse)


def twist_table():
    q = np.arange(INNER) + N // 2
    k0 = np.arange(RES // 2 + 1)
    angle = 2.0 * np.pi * ((k0[:, None] * q[None, :]) % PAD) / PAD
    return np.cos(angle).astype(np.float32), (-np.sin(angle)).astype(np.float32)


def turn(value, num, den):
    re, im = value
    num = num % den
    eighth = 8 * num
    if num == 0:
        return re, im
    if 2 * num == den:
        return -re, -im
    if 4 * num == den:
        return -im, re
    if 4 * num == 3 * den:
        return im, -re
    if eighth % den == 0:
        root = np.float32(math.sqrt(0.5))
        kind = eighth // den
        if kind == 1:
            return (re - im) * root, (re + im) * root
        if kind == 3:
            return (re + im) * (-root), (re - im) * root
        if kind == 5:
            return (im - re) * root, (re + im) * (-root)
        return (re + im) * root, (im - re) * root
    c = np.float32(math.cos(2.0 * math.pi * num / den))
    s = np.float32(math.sin(2.0 * math.pi * num / den))
    return re * c - im * s, re * s + im * c


def small_dft(get, ids, sign):
    count = len(ids)
    if count == 1:
        return [get(ids[0])]
    even = small_dft(get, ids[0::2], sign)
    odd = small_dft(get, ids[1::2], sign)
    half = count // 2
    first, second = [], []
    for j in range(half):
        re, im = even[j]
        t_re, t_im = turn(odd[j], sign * j, count)
        first.append((re + t_re, im + t_im))
        second.append((re - t_re, im - t_im))
    return first + second


def forward_slabs(get, put):
    ids = list(range(SLABS))
    for v, value in enumerate(small_dft(get, ids, -1)):
        put(2 * v, value)
    for v, value in enumerate(small_dft(lambda n: turn(get(n), -n, RES), ids, -1)):
        put(2 * v + 1, value)


def inverse_slabs(get, put):
    even = small_dft(get, list(range(0, RES, 2)), 1)
    odd = small_dft(get, list(range(1, RES, 2)), 1)
    for n in range(SLABS):
        t_re, t_im = turn(odd[n], n, RES)
        put(n, (even[n][0] + t_re, even[n][1] + t_im))


def twisted(value, u, sign, read):
    re, im = value
    k0 = residue(u)
    if k0 == 0:
        return value
    c, s = read(abs(k0))
    if (k0 < 0) == (sign > 0):
        return re * c + im * s, im * c - re * s
    return re * c - im * s, re * s + im * c


def high_low(value):
    high = value.astype(jnp.bfloat16)
    low = (value - high.astype(jnp.float32)).astype(jnp.bfloat16)
    return high, low


def dot16(left, right):
    return jnp.dot(left, right, preferred_element_type=jnp.float32)


def three_left(stacked, count, high, low):
    both = dot16(stacked[...], high)
    return both[:count] + both[count:] + dot16(stacked[:count], low)


def three_right(stacked, count, high, low):
    both = dot16(stacked, high)
    return both[:count] + both[count:] + dot16(stacked[:count], low)


def column_twist(twist, q0):
    seen = {}

    def read(k):
        if k not in seen:
            rows = pl.ds(q0, 8)
            seen[k] = twist[rows, k : k + 1], twist[rows, 64 + k : 65 + k]
        return seen[k]

    return read


def column_forward_kernel(count, place, twist, matrix, *refs):
    pieces, refs = refs[:count], refs[count:]
    before, (out, total, high, low, sems) = refs[:-5], refs[-5:]
    width = pieces[0].shape[-1]
    per_source, size = pieces[0].shape[1:3]
    many = high.shape[-1] // width
    products = RES // many
    rows_out = out.shape[1]

    def copy_in(p):
        part = pl.ds(p * many, many)
        return pltpu.make_async_copy(before[0].at[part], total.at[part], sems.at[p])

    def copy_out(p):
        part = pl.ds(p * many, many)
        return pltpu.make_async_copy(total.at[part], out.at[part], sems.at[products + p])

    if before:
        for p in range(products):
            copy_in(p).start()

    for here in range(count):

        @pl.when(place[0] == here)
        def _():
            @pl.loop(0, size // 8)
            def _(t):
                q0 = pl.multiple_of(t * 8, 8)
                read = column_twist(twist, q0)

                def get(n):
                    source, block = divmod(n, per_source)
                    piece = pieces[source ^ here]
                    rows = pl.ds(q0, 8)
                    return piece[0, block, rows, :], piece[1, block, rows, :]

                def put(u, value):
                    item = jnp.concatenate(twisted(value, u, 1, read), axis=0)
                    rows = pl.ds(pl.multiple_of(t * 16, 16), 16)
                    at = (u // many, rows, pl.ds((u % many) * width, width))
                    high[at], low[at] = high_low(item)

                forward_slabs(get, put)

    @pl.loop(0, products)
    def _(p):
        done = three_left(matrix, rows_out, high[p], low[p])
        if before:
            copy_in(p).wait()
        for part in range(many):
            item = done[:, part * width : (part + 1) * width]
            at = p * many + part
            total[at] = total[at] + item if before else item
        copy_out(p).start()

    for p in range(products):
        copy_out(p).wait()


def column_inverse_kernel(count, place, source, twist, matrix, *refs):
    pieces, (peak_sq, near, lines, deep, back, top, sems, out_sems) = refs[:-8], refs[-8:]
    width = lines.shape[-1]
    rows_in = lines.shape[1]
    per_dest = near.shape[3]
    many = deep.shape[-1] // width
    products = RES // many

    def copy_in(p):
        part = pl.ds(p * many, many)
        return pltpu.make_async_copy(source.at[part], lines.at[part], sems.at[p])

    def copies_out(chunk, part):
        parts = 1 if chunk + 1 < CHUNKS else 2
        if part >= parts:
            return []
        rows = pl.ds(part * CHUNK // parts, CHUNK // parts)
        copies = []
        for j in range(count):
            piece = pieces[chunk * count + j].at[pl.ds(0, 2 * per_dest * CHUNK)]
            there = piece.reshape(2, per_dest, CHUNK, width).at[:, :, rows]
            here = near.at[chunk, place[0] ^ j, :, :, rows]
            copies.append(pltpu.make_async_copy(here, there, out_sems.at[(chunk * 2 + part) * count + j]))
        return copies

    def prepare(p):
        copy_in(p).wait()
        blocks = [lines[p * many + part] for part in range(many)]
        joined = jnp.concatenate(blocks, axis=1) if many > 1 else blocks[0]
        high = joined.astype(jnp.bfloat16).astype(jnp.float32)
        parts = [high, joined - high, high]
        if deep.shape[1] > 3 * rows_in:
            parts.append(jnp.zeros((deep.shape[1] - 3 * rows_in, many * width), jnp.float32))
        deep[p] = jnp.concatenate(parts, axis=0).astype(jnp.bfloat16)

    def product(p, chunk):
        done = dot16(matrix[chunk], deep[p])
        for part in range(many):
            back[chunk, p * many + part] = done[:, part * width : (part + 1) * width]

    def butterflies(t, chunk):
        q0 = pl.multiple_of(t * 8, 8)
        largest = []
        read = column_twist(twist, pl.multiple_of(chunk * CHUNK + q0, 8))

        def get(u):
            re = back[chunk, u, pl.ds(q0, 8), :]
            im = back[chunk, u, pl.ds(CHUNK + q0, 8), :]
            return twisted((re, im), u, -1, read)

        def put(n, value):
            dest, block = divmod(n, per_dest)
            rows = pl.ds(q0, 8)
            near[chunk, dest, 0, block, rows, :], near[chunk, dest, 1, block, rows, :] = value
            largest.append(value[0] * value[0] + value[1] * value[1])

        inverse_slabs(get, put)
        while len(largest) > 1:
            largest = [jnp.maximum(a, b) for a, b in zip(largest[0::2], largest[1::2])]
        top[...] = jnp.maximum(top[...], largest[0])

    for p in range(products):
        copy_in(p).start()
    top[...] = jnp.zeros_like(top)

    @pl.loop(0, products)
    def _(p):
        prepare(p)
        product(p, 0)

    tiles = CHUNK // 16
    steps = min(tiles, products // 2)
    for chunk in range(CHUNKS):
        for part in range(2):

            @pl.loop(part * steps, (part + 1) * steps)
            def _(t):
                for item in range(tiles // steps):
                    butterflies(t * (tiles // steps) + item, chunk)
                if chunk + 1 < CHUNKS:
                    for item in range(products // 2 // steps):
                        product(t * (products // 2 // steps) + item, chunk + 1)

            for copy in copies_out(chunk, part if chunk + 1 == CHUNKS else 1 - part):
                copy.start()
    peak_sq[0] = jnp.max(top[...])
    for chunk in range(CHUNKS):
        for part in range(2):
            for copy in copies_out(chunk, part):
                copy.wait()


def line_kernel(
    order, own, tail, lines, gain, twist, fwd_high, fwd_low, inv_high, inv_low, out, *scratch
):
    half = RES * 8
    at_end = pl.program_id(0) == pl.num_programs(0) - 1

    def line_twist(side):
        def read(k):
            lanes = pl.ds(side * 128, 128)
            return twist[0, k, :, lanes], twist[1, k, :, lanes]

        return read

    def forward(group, stacked, sides=(0, 1)):
        for side in sides:
            waiting = {}

            def get(m):
                block = order[2 * m + side]
                at = group * 16
                return lines[block, at : at + 8, :], lines[block, at + 8 : at + 16, :]

            def put(u, value):
                waiting[u] = twisted(value, u, 1, line_twist(side))
                v = (u + RES // 2) % RES
                if v in waiting:
                    first = min(u, v)
                    rows = pl.ds(first * 16, 16)
                    rows_low = pl.ds(half + first * 16, 16)
                    for part in range(2):
                        item = jnp.concatenate(
                            [waiting[first][part], waiting[first + RES // 2][part]], axis=0
                        )
                        at = pl.ds(part * INNER + side * 128, 128)
                        stacked[rows, at], stacked[rows_low, at] = high_low(item)

            forward_slabs(get, put)

    def filtered(group, stacked):
        spec = three_right(stacked[...], half, fwd_high[...], fwd_low[...])
        spec_re, spec_im = spec[:, :128], spec[:, 128:]
        g_re, g_im = gain[0, group], gain[1, group]
        mixed = jnp.concatenate(
            [spec_re * g_re - spec_im * g_im, spec_re * g_im + spec_im * g_re], axis=1
        )
        return jnp.concatenate(high_low(mixed), axis=0)

    def unfold(mixed, back):
        back[...] = three_right(mixed, half, inv_high[...], inv_low[...])

    def inverse(group, back, sides=(0, 1)):
        for side in sides:

            def get(u):
                rows = pl.ds((u % (RES // 2)) * 16 + (u // (RES // 2)) * 8, 8)
                re = back[rows, pl.ds(side * 128, 128)]
                im = back[rows, pl.ds(INNER + side * 128, 128)]
                return twisted((re, im), u, -1, line_twist(side))

            def put(m, value):
                block = order[2 * m + side]
                at = group * 16
                out[block, at : at + 8, :], out[block, at + 8 : at + 16, :] = value

            inverse_slabs(get, put)

    if tail:

        @pl.when(at_end)
        def _():
            for block in range(N // 128):
                lines[block, 8:12, :] = lines[block, 4:8, :]

    groups = len(scratch) // 2

    stacked, back = scratch[:groups], scratch[groups:]

    def run(count):
        forward(0, stacked[0])
        for group in range(count):
            mixed = filtered(group, stacked[group])
            if group + 1 < count:
                forward(group + 1, stacked[group + 1], (0,))
            if group > 0:
                inverse(group - 1, back[group - 1], (0,))
            unfold(mixed, back[group])
            if group + 1 < count:
                forward(group + 1, stacked[group + 1], (1,))
            if group > 0:
                inverse(group - 1, back[group - 1], (1,))
        inverse(count - 1, back[count - 1])

    rest = own % groups
    if rest:
        pl.when(jnp.logical_not(at_end))(lambda: run(groups))
        pl.when(at_end)(lambda: run(rest))
    else:
        run(groups)

    if tail:

        @pl.when(at_end)
        def _():
            for block in range(N // 128):
                out[block, 4:8, :] = out[block, 8:12, :]


def gain_kernel(place, gain):
    k0 = place[0]
    group = place[1] + pl.program_id(0)
    down = lax.broadcasted_iota(jnp.int32, (8, 128), 0)
    across = lax.broadcasted_iota(jnp.int32, (8, 128), 1)
    row = (k0 + RES * (group * 8 + down - HALF)).astype(jnp.float32)
    row_sq = row * row
    row_in = jnp.abs(row) < LIMIT
    for u in range(RES):
        col = (residue(u) + RES * (across - HALF)).astype(jnp.float32)
        square = row_sq + col * col
        scaled = RATIO_SQ * square
        phase = -2.0 * math.pi * distance / wavelength * scaled / (1.0 + jnp.sqrt(1.0 - scaled))
        total = jnp.where(
            row_in & (jnp.abs(col) < LIMIT), jnp.exp(square * (-2.0 / (LIMIT * LIMIT))), 0.0
        )
        quarter = jnp.floor(phase * (2.0 / math.pi) + 0.5)
        left = phase - quarter * 1.5703125
        left = left - quarter * 4.837512969970703125e-4
        left = left - quarter * 7.549789954891882e-8
        sq = left * left
        sine = ((-1.9515295891e-4 * sq + 8.3321608736e-3) * sq - 1.6666654611e-1) * sq * left + left
        cosine = (
            (2.443315711809948e-5 * sq - 1.388731625493765e-3) * sq + 4.166664568298827e-2
        ) * sq * sq - 0.5 * sq + 1.0
        which = quarter.astype(jnp.int32) & 3
        swap = (which & 1) == 1
        cos_part = jnp.where(swap, sine, cosine)
        sin_part = jnp.where(swap, cosine, sine)
        cos_part = jnp.where((which == 1) | (which == 2), -cos_part, cos_part)
        sin_part = jnp.where(which >= 2, -sin_part, sin_part)
        at = (u % (RES // 2)) * 16 + (u // (RES // 2)) * 8
        gain[0, 0, at : at + 8, :] = total * cos_part
        gain[1, 0, at : at + 8, :] = total * sin_part


def encode(near_real, near_imag, peak_sq, cell_sign):
    square = near_real * near_real + near_imag * near_imag
    root = lax.rsqrt(jnp.maximum(square, 1.2e-38))
    top = lax.rsqrt(peak_sq)
    amp_level = (square * root) * (0.8 * top)
    unit = jnp.minimum(root, 20.0 * top)
    rest = 1.0 - amp_level * amp_level
    level = unit * amp_level
    lift = (rest * lax.rsqrt(rest)) * (unit * cell_sign)
    return (near_real * level + near_imag * lift, near_imag * level - near_real * lift)


def stamp_kernel(others, peak_one, peak_two, *refs):
    refs = refs[others:]
    stay, pieces, refs = refs[:CHUNKS], refs[CHUNKS : CHUNKS + others], refs[CHUNKS + others :]
    fetched, (tile, sems) = refs[:CHUNKS], refs[CHUNKS:]
    tile[...] = jnp.full(tile.shape, jnp.maximum(peak_one[0], peak_two[0]), jnp.float32)
    copies = []
    for j, piece in enumerate(pieces):
        rows = pl.ds(piece.shape[0] - SPARE, SPARE)
        copies.append(pltpu.make_async_copy(tile, piece.at[rows], sems.at[j]))
    for chunk in range(CHUNKS):
        copies.append(pltpu.make_async_copy(stay[chunk], fetched[chunk], sems.at[others + chunk]))
    for copy in copies:
        copy.start()
    for copy in copies:
        copy.wait()


def encode_kernel(count, place, peak_one, peak_two, *refs):
    pieces, refs = refs[: CHUNKS * count], refs[CHUNKS * count :]
    slm_real, slm_imag, tile_real, tile_imag, sems = refs
    blocks, width = tile_real.shape[0], pieces[0].shape[-1]
    top = jnp.full((1, width), jnp.maximum(peak_one[0], peak_two[0]), jnp.float32)
    for piece in pieces[(CHUNKS - 1) * count + 1 :]:
        top = jnp.maximum(top, piece[pl.ds(piece.shape[0] - SPARE, 1), :])
    cell = lax.broadcasted_iota(jnp.int32, (CHUNK, width), 0)
    cell = cell + lax.broadcasted_iota(jnp.int32, (CHUNK, width), 1)
    cell_sign = (1 - 2 * (cell & 1)).astype(jnp.float32)

    def copies_out(block):
        rows = pl.ds(block * INNER, INNER)
        return [
            pltpu.make_async_copy(tile.at[block], slm.at[rows], sems.at[2 * block + part])
            for part, (tile, slm) in enumerate(((tile_real, slm_real), (tile_imag, slm_imag)))
        ]

    @pl.loop(0, blocks)
    def _(block):
        for at in range(CHUNKS * count):
            chunk, j = divmod(at, count)
            piece = pieces[at]
            lanes = pl.ds(pl.multiple_of((place[0] ^ j) * width, width), width)
            rows = pl.ds(chunk * CHUNK, CHUNK)
            real = pl.ds(pl.multiple_of(block * CHUNK, CHUNK), CHUNK)
            imag = pl.ds(pl.multiple_of((blocks + block) * CHUNK, CHUNK), CHUNK)
            tile_real[block, rows, lanes], tile_imag[block, rows, lanes] = encode(
                piece[real, :], piece[imag, :], top, cell_sign
            )
        for copy in copies_out(block):
            copy.start()

    for block in range(blocks):
        for copy in copies_out(block):
            copy.wait()


def pack_kernel(place, field_real, field_imag, *refs):
    pieces, sems = refs[:-1], refs[-1]
    width = pieces[0].shape[-1]
    copies = []
    for j in list(range(1, len(pieces))) + [0]:
        lanes = pl.ds(pl.multiple_of((place[0] ^ j) * width, width), width)
        for part, field in enumerate((field_real, field_imag)):
            copies.append(
                pltpu.make_async_copy(
                    field.at[:, :, lanes], pieces[j].at[part], sems.at[2 * j + part]
                )
            )
    for copy in copies:
        copy.start()
    for copy in copies:
        copy.wait()


def exchange(pieces, axis):
    total = len(pieces)
    return [pieces[0]] + [
        lax.ppermute(pieces[j], axis, [(i, i ^ j) for i in range(total)]) for j in range(1, total)
    ]


def params(mebibytes):
    return pltpu.CompilerParams(vmem_limit_bytes=mebibytes << 20)


def cost(megabytes):
    return pl.CostEstimate(flops=0, bytes_accessed=megabytes << 20, transcendentals=0)


def whole(memory=pltpu.VMEM):
    return pl.BlockSpec(memory_space=memory)


def body(field_real, field_imag):
    row_total, col_total = lax.axis_size("row"), lax.axis_size("col")
    devices = row_total * col_total
    device = lax.axis_index("row") * col_total + lax.axis_index("col")
    height, tile_width = field_real.shape
    width = tile_width // row_total
    parts = max(1, devices // RES)
    groups = -(-(2 * HALF + 1) // (8 * parts)) * parts
    own = groups // parts
    tail = parts == 1
    total_rows = groups * 16 - (8 if tail else 0)
    own_rows = total_rows // parts
    many = 4 if width == 128 else 1

    fwd_col, inv_col = column_tables(groups, tail)
    line_fh, line_fl, line_ih, line_il = line_tables()
    twist = np.stack(twist_table())
    twist_line = np.ascontiguousarray(np.broadcast_to(twist[:, :, None], twist.shape[:2] + (8, INNER)))
    twist_col = np.pad(twist, ((0, 0), (0, 64 - twist.shape[1]), (0, 0)))
    twist_col = twist_col.reshape(128, INNER).T.copy()

    u = device // parts
    k0 = jnp.where(u >= RES // 2, u - RES, u)
    place = jnp.stack([k0, (device % parts) * own]).astype(jnp.int32)
    gain = pl.pallas_call(
        gain_kernel,
        grid=(own,),
        in_specs=[whole(pltpu.SMEM)],
        out_specs=pl.BlockSpec((2, 1, RES * 8, 128), lambda g: (0, g, 0, 0)),
        out_shape=jax.ShapeDtypeStruct((2, own, RES * 8, 128), jnp.float32),
        compiler_params=params(56),
        name="gain",
    )(place)

    place_row = lax.axis_index("row").reshape(1).astype(jnp.int32)
    blocks = height // INNER
    anywhere = whole(pl.ANY)
    if width != 128:
        packed = jnp.stack([field_real, field_imag]).reshape(2, blocks, INNER, row_total, width)
        packed = jnp.take(packed, jnp.arange(row_total) ^ place_row[0], axis=3)
    lines = []
    for chunk, (start, size) in enumerate(FRONT):
        piece_shape = jax.ShapeDtypeStruct((2, blocks, size, width), jnp.float32)
        at = start // size
        if width == 128:
            pieces = pl.pallas_call(
                pack_kernel,
                grid=(1,),
                in_specs=[whole(pltpu.SMEM)]
                + [pl.BlockSpec((blocks, size, tile_width), lambda i: (0, at, 0))] * 2,
                out_specs=[anywhere] * row_total,
                out_shape=[piece_shape] * row_total,
                scratch_shapes=[pltpu.SemaphoreType.DMA((2 * row_total,))],
                compiler_params=params(56),
                cost_estimate=cost(4),
                name="pack",
            )(
                place_row,
                field_real.reshape(blocks, INNER, tile_width),
                field_imag.reshape(blocks, INNER, tile_width),
            )
        else:
            pieces = [packed[:, :, start : start + size, j] for j in range(row_total)]
        pieces = exchange(pieces, "row")
        rows = slice(start, start + size)
        slab = pltpu.VMEM((RES // many, 2 * size, many * width), jnp.bfloat16)
        lines = [
            pl.pallas_call(
                partial(column_forward_kernel, row_total),
                in_specs=[whole(pltpu.SMEM)] + [whole()] * (2 + row_total) + [anywhere] * len(lines),
                out_specs=anywhere,
                out_shape=jax.ShapeDtypeStruct((RES, total_rows, width), jnp.float32),
                scratch_shapes=[
                    pltpu.VMEM((RES, total_rows, width), jnp.float32),
                    slab,
                    slab,
                    pltpu.SemaphoreType.DMA((2 * RES // many,)),
                ],
                compiler_params=params(20),
                cost_estimate=cost(20),
                name="column_forward",
            )(place_row, twist_col[rows], fwd_col[chunk], *pieces, *lines)
        ]
    (lines,) = lines

    lines = lines.reshape(devices, own_rows, width)
    lines = lax.all_to_all(lines, ("row", "col"), split_axis=0, concat_axis=0, tiled=True)
    if width == 128:
        order = tuple((b % row_total) * col_total + b // row_total for b in range(N // 128))
    else:
        order = tuple(range(N // 128))
        lines = lines.reshape(row_total, col_total, own_rows, width).transpose(2, 1, 0, 3)
        lines = lines.reshape(own_rows, N // 128, 128).transpose(1, 0, 2)

    at_once = 2
    line_grain = pl.BlockSpec((N // 128, 16 * at_once, 128), lambda i: (0, i, 0))
    gain_grain = pl.BlockSpec((2, at_once, RES * 8, 128), lambda i: (0, i, 0, 0))
    lines = pl.pallas_call(
        partial(line_kernel, order, own, tail),
        grid=(-(-own // at_once),),
        in_specs=[line_grain, gain_grain] + [whole()] * 5,
        out_specs=line_grain,
        out_shape=jax.ShapeDtypeStruct((N // 128, own_rows, 128), jnp.float32),
        scratch_shapes=[pltpu.VMEM((2 * RES * 8, 2 * INNER), jnp.bfloat16)] * at_once
        + [pltpu.VMEM((RES * 8, 2 * INNER), jnp.float32)] * at_once,
        compiler_params=params(48),
        name="line",
    )(lines, gain, twist_line, line_fh, line_fl, line_ih, line_il)

    if width != 128:
        lines = lines.transpose(1, 0, 2).reshape(own_rows, col_total, row_total, width)
        lines = lines.transpose(2, 1, 0, 3).reshape(devices, own_rows, width)
    lines = lax.all_to_all(lines, ("row", "col"), split_axis=0, concat_axis=0, tiled=True)
    lines = lines.reshape(RES, total_rows, width)

    piece_shapes = [
        jax.ShapeDtypeStruct((2 * blocks * CHUNK + spare, width), jnp.float32)
        for spare in (0,) * (CHUNKS - 1) + (SPARE,)
    ]
    *near, peak_sq = pl.pallas_call(
        partial(column_inverse_kernel, row_total),
        in_specs=[whole(pltpu.SMEM), anywhere, whole(), whole()],
        out_specs=[anywhere] * (CHUNKS * row_total) + [whole(pltpu.SMEM)],
        out_shape=[shape for shape in piece_shapes for _ in range(row_total)]
        + [jax.ShapeDtypeStruct((1,), jnp.float32)],
        scratch_shapes=[
            pltpu.VMEM((CHUNKS, row_total, 2, blocks, CHUNK, width), jnp.float32),
            pltpu.VMEM((RES, total_rows, width), jnp.float32),
            pltpu.VMEM((RES // many, inv_col.shape[2], many * width), jnp.bfloat16),
            pltpu.VMEM((CHUNKS, RES, 2 * CHUNK, width), jnp.float32),
            pltpu.VMEM((8, width), jnp.float32),
            pltpu.SemaphoreType.DMA((RES // many,)),
            pltpu.SemaphoreType.DMA((2 * CHUNKS * row_total,)),
        ],
        compiler_params=params(56),
        name="column_inverse",
    )(place_row, lines, twist_col, inv_col)
    near = [near[:row_total], near[row_total:]]
    piece_shape = piece_shapes[-1]
    near[0] = exchange(near[0], "row")
    shift = 1
    while shift < col_total:
        partner = [(i, i ^ shift) for i in range(col_total)]
        peaks = [peak_sq, lax.ppermute(peak_sq, "col", partner)]
        shift *= 2
        if shift < col_total:
            peak_sq = jnp.maximum(*peaks)
    others = row_total - 1
    stamped = pl.pallas_call(
        partial(stamp_kernel, others),
        in_specs=[whole(pltpu.SMEM)] * 2 + [anywhere] * (others + CHUNKS),
        out_specs=[anywhere] * others + [whole()] * CHUNKS,
        out_shape=[piece_shape] * others + piece_shapes,
        scratch_shapes=[
            pltpu.VMEM((SPARE, width), jnp.float32),
            pltpu.SemaphoreType.DMA((others + CHUNKS,)),
        ],
        input_output_aliases={2 + j: j for j in range(others)},
        compiler_params=params(16),
        name="stamp",
    )(*peaks, *near[1][1:], near[0][0], near[1][0])
    near[1][1:] = stamped[:others]
    near[0][0], near[1][0] = stamped[others:]
    near[0][1:], near[1][-1] = lax.optimization_barrier((near[0][1:], near[1][-1]))
    near[1] = exchange(near[1], "row")
    if width != 128:
        peak_sq = jnp.maximum(*peaks)[0]
        for piece in near[1][1:]:
            peak_sq = jnp.maximum(peak_sq, piece[-1, 0])
        near = jnp.stack([jnp.stack([piece[: 2 * blocks * CHUNK] for piece in pieces]) for pieces in near])
        near = jnp.take(near, jnp.arange(row_total) ^ place_row[0], axis=1)
        near = near.reshape(CHUNKS, row_total, 2, blocks, CHUNK, width)
        near = near.transpose(2, 3, 0, 4, 1, 5).reshape(2, height, tile_width)
        odd_cell = (jnp.arange(height)[:, None] + jnp.arange(tile_width)[None, :]) % 2
        cell_sign = (1 - 2 * odd_cell).astype(jnp.float32)
        return encode(near[0], near[1], peak_sq, cell_sign)
    tile_shape = jax.ShapeDtypeStruct((height, tile_width), jnp.float32)
    tile = pltpu.VMEM((blocks, INNER, tile_width), jnp.float32)
    return pl.pallas_call(
        partial(encode_kernel, row_total),
        in_specs=[whole(pltpu.SMEM)] * 3 + [whole()] * (CHUNKS * row_total),
        out_specs=[anywhere] * 2,
        out_shape=[tile_shape, tile_shape],
        scratch_shapes=[tile, tile, pltpu.SemaphoreType.DMA((2 * blocks,))],
        compiler_params=params(16),
        name="encode",
    )(place_row, *peaks, *near[0], *near[1])


def solution(mesh):
    in_specs = (P("row", "col"), P("row", "col"))
    out_specs = (P("row", "col"), P("row", "col"))
    return jax.shard_map(body, mesh=mesh, in_specs=in_specs, out_specs=out_specs, check_vma=False)
```

```python
from functools import partial
import math

import jax
import jax.numpy as jnp
import ml_dtypes
import numpy as np
from jax import lax
from jax.experimental import pallas as pl
from jax.experimental.pallas import tpu as pltpu
from jax.sharding import PartitionSpec as P

N = 4096
PAD = 2 * N
wavelength = 5.2e-07
distance = 0.2
INNER = 256
SLABS = N // INNER
RES = PAD // INNER
HALF = 40
CHUNKS = 2
CHUNK = INNER // CHUNKS
FRONT = ((0, 128), (128, 128))
SPARE = 8


def optics(padded_side):
    pitch = 2e-06 * math.sqrt(8192.0 / padded_side)
    extent = padded_side * pitch
    ratio_sq = (wavelength / extent) ** 2
    band_limit = extent / (wavelength * math.sqrt((2.0 * distance / extent) ** 2 + 1.0))
    return (ratio_sq, band_limit)


RATIO_SQ, LIMIT = optics(PAD)
assert RES * HALF - RES // 2 + RES > LIMIT and RES * HALF + RES // 2 > LIMIT


def residue(u):
    return u if u < RES // 2 else u - RES


def split16(table):
    table = np.asarray(table, np.float64)
    high = table.astype(np.float32).astype(ml_dtypes.bfloat16)
    low = (table - high.astype(np.float64)).astype(np.float32).astype(ml_dtypes.bfloat16)
    return high, low


def row_order(groups, tail):
    rows = []
    for group in range(groups):
        size = 4 if tail and group == groups - 1 else 8
        for part in range(2):
            for s in range(size):
                rows.append((part, group * 8 + s - HALF))
    return rows


def column_tables(groups, tail):
    q = np.arange(INNER)
    rows = row_order(groups, tail)
    forward = np.zeros((len(rows), 2, INNER))
    inverse = np.zeros((2, INNER, len(rows)))
    for at, (part, k1) in enumerate(rows):
        if abs(k1) > HALF:
            continue
        angle = 2.0 * np.pi * ((k1 * q) % INNER) / INNER
        c, s = np.cos(angle), np.sin(angle)
        forward[at] = (c, s) if part == 0 else (-s, c)
        inverse[:, :, at] = (c, s) if part == 0 else (-s, c)
    tables = []
    for start, size in FRONT:
        part = forward[:, :, start : start + size].reshape(-1, 2, size // 8, 8)
        part = part.transpose(0, 2, 1, 3).reshape(-1, 2 * size)
        tables.append(np.concatenate(split16(part), axis=0))
    inverse = inverse.reshape(2, CHUNKS, CHUNK, -1).transpose(1, 0, 2, 3)
    high, low = split16(inverse.reshape(CHUNKS, 2 * CHUNK, len(rows)))
    inverse = np.concatenate([high, high, low], axis=2)
    inverse = np.pad(inverse, ((0, 0), (0, 0), (0, -3 * len(rows) % 16)))
    return tables, inverse


def line_tables():
    q = np.arange(INNER)
    forward = np.zeros((2 * INNER, 256))
    inverse = np.zeros((256, 2 * INNER))
    for lane in range(2 * HALF + 1):
        angle = 2.0 * np.pi * (((lane - HALF) * q) % INNER) / INNER
        c, s = np.cos(angle), np.sin(angle)
        forward[:INNER, lane], forward[INNER:, lane] = c, s
        forward[:INNER, 128 + lane], forward[INNER:, 128 + lane] = -s, c
        inverse[lane, :INNER], inverse[lane, INNER:] = c, s
        inverse[128 + lane, :INNER], inverse[128 + lane, INNER:] = -s, c
    return split16(forward) + split16(inverse)


def twist_table():
    q = np.arange(INNER) + N // 2
    k0 = np.arange(RES // 2 + 1)
    angle = 2.0 * np.pi * ((k0[:, None] * q[None, :]) % PAD) / PAD
    return np.cos(angle).astype(np.float32), (-np.sin(angle)).astype(np.float32)


def turn(value, num, den):
    re, im = value
    num = num % den
    eighth = 8 * num
    if num == 0:
        return re, im
    if 2 * num == den:
        return -re, -im
    if 4 * num == den:
        return -im, re
    if 4 * num == 3 * den:
        return im, -re
    if eighth % den == 0:
        root = np.float32(math.sqrt(0.5))
        kind = eighth // den
        if kind == 1:
            return (re - im) * root, (re + im) * root
        if kind == 3:
            return (re + im) * (-root), (re - im) * root
        if kind == 5:
            return (im - re) * root, (re + im) * (-root)
        return (re + im) * root, (im - re) * root
    c = np.float32(math.cos(2.0 * math.pi * num / den))
    s = np.float32(math.sin(2.0 * math.pi * num / den))
    return re * c - im * s, re * s + im * c


def small_dft(get, ids, sign):
    count = len(ids)
    if count == 1:
        return [get(ids[0])]
    even = small_dft(get, ids[0::2], sign)
    odd = small_dft(get, ids[1::2], sign)
    half = count // 2
    first, second = [], []
    for j in range(half):
        re, im = even[j]
        t_re, t_im = turn(odd[j], sign * j, count)
        first.append((re + t_re, im + t_im))
        second.append((re - t_re, im - t_im))
    return first + second


def forward_slabs(get, put):
    ids = list(range(SLABS))
    for v, value in enumerate(small_dft(get, ids, -1)):
        put(2 * v, value)
    for v, value in enumerate(small_dft(lambda n: turn(get(n), -n, RES), ids, -1)):
        put(2 * v + 1, value)


def inverse_slabs(get, put):
    even = small_dft(get, list(range(0, RES, 2)), 1)
    odd = small_dft(get, list(range(1, RES, 2)), 1)
    for n in range(SLABS):
        t_re, t_im = turn(odd[n], n, RES)
        put(n, (even[n][0] + t_re, even[n][1] + t_im))


def twisted(value, u, sign, read):
    re, im = value
    k0 = residue(u)
    if k0 == 0:
        return value
    c, s = read(abs(k0))
    if (k0 < 0) == (sign > 0):
        return re * c + im * s, im * c - re * s
    return re * c - im * s, re * s + im * c


def high_low(value):
    high = value.astype(jnp.bfloat16)
    low = (value - high.astype(jnp.float32)).astype(jnp.bfloat16)
    return high, low


def dot16(left, right):
    return jnp.dot(left, right, preferred_element_type=jnp.float32)


def three_left(stacked, count, high, low):
    both = dot16(stacked[...], high)
    return both[:count] + both[count:] + dot16(stacked[:count], low)


def three_right(stacked, count, high, low):
    both = dot16(stacked, high)
    return both[:count] + both[count:] + dot16(stacked[:count], low)


def column_twist(twist, q0):
    seen = {}

    def read(k):
        if k not in seen:
            rows = pl.ds(q0, 8)
            seen[k] = twist[rows, k : k + 1], twist[rows, 64 + k : 65 + k]
        return seen[k]

    return read


def column_forward_kernel(count, place, twist, matrix, *refs):
    pieces, refs = refs[:count], refs[count:]
    before, (out, total, high, low, sems) = refs[:-5], refs[-5:]
    width = pieces[0].shape[-1]
    per_source, size = pieces[0].shape[1:3]
    many = high.shape[-1] // width
    products = RES // many
    rows_out = out.shape[1]

    def copy_in(p):
        part = pl.ds(p * many, many)
        return pltpu.make_async_copy(before[0].at[part], total.at[part], sems.at[p])

    def copy_out(p):
        part = pl.ds(p * many, many)
        return pltpu.make_async_copy(total.at[part], out.at[part], sems.at[products + p])

    if before:
        for p in range(products):
            copy_in(p).start()

    for here in range(count):

        @pl.when(place[0] == here)
        def _():
            @pl.loop(0, size // 8)
            def _(t):
                q0 = pl.multiple_of(t * 8, 8)
                read = column_twist(twist, q0)

                def get(n):
                    source, block = divmod(n, per_source)
                    piece = pieces[source ^ here]
                    rows = pl.ds(q0, 8)
                    return piece[0, block, rows, :], piece[1, block, rows, :]

                def put(u, value):
                    item = jnp.concatenate(twisted(value, u, 1, read), axis=0)
                    rows = pl.ds(pl.multiple_of(t * 16, 16), 16)
                    at = (u // many, rows, pl.ds((u % many) * width, width))
                    high[at], low[at] = high_low(item)

                forward_slabs(get, put)

    @pl.loop(0, products)
    def _(p):
        done = three_left(matrix, rows_out, high[p], low[p])
        if before:
            copy_in(p).wait()
        for part in range(many):
            item = done[:, part * width : (part + 1) * width]
            at = p * many + part
            total[at] = total[at] + item if before else item
        copy_out(p).start()

    for p in range(products):
        copy_out(p).wait()


def column_inverse_kernel(count, place, source, twist, matrix, *refs):
    pieces, (peak_sq, near, lines, deep, back, top, sems, out_sems) = refs[:-8], refs[-8:]
    width = lines.shape[-1]
    rows_in = lines.shape[1]
    per_dest = near.shape[3]
    many = deep.shape[-1] // width
    products = RES // many

    def copy_in(p):
        part = pl.ds(p * many, many)
        return pltpu.make_async_copy(source.at[part], lines.at[part], sems.at[p])

    def copies_out(chunk, part):
        parts = 1 if chunk + 1 < CHUNKS else 2
        if part >= parts:
            return []
        rows = pl.ds(part * CHUNK // parts, CHUNK // parts)
        copies = []
        for j in range(count):
            piece = pieces[chunk * count + j].at[pl.ds(0, 2 * per_dest * CHUNK)]
            there = piece.reshape(2, per_dest, CHUNK, width).at[:, :, rows]
            here = near.at[chunk, place[0] ^ j, :, :, rows]
            copies.append(pltpu.make_async_copy(here, there, out_sems.at[(chunk * 2 + part) * count + j]))
        return copies

    def prepare(p):
        copy_in(p).wait()
        blocks = [lines[p * many + part] for part in range(many)]
        joined = jnp.concatenate(blocks, axis=1) if many > 1 else blocks[0]
        high = joined.astype(jnp.bfloat16).astype(jnp.float32)
        parts = [high, joined - high, high]
        if deep.shape[1] > 3 * rows_in:
            parts.append(jnp.zeros((deep.shape[1] - 3 * rows_in, many * width), jnp.float32))
        deep[p] = jnp.concatenate(parts, axis=0).astype(jnp.bfloat16)

    def product(p, chunk):
        done = dot16(matrix[chunk], deep[p])
        for part in range(many):
            back[chunk, p * many + part] = done[:, part * width : (part + 1) * width]

    def butterflies(t, chunk):
        q0 = pl.multiple_of(t * 8, 8)
        largest = []
        read = column_twist(twist, pl.multiple_of(chunk * CHUNK + q0, 8))

        def get(u):
            re = back[chunk, u, pl.ds(q0, 8), :]
            im = back[chunk, u, pl.ds(CHUNK + q0, 8), :]
            return twisted((re, im), u, -1, read)

        def put(n, value):
            dest, block = divmod(n, per_dest)
            rows = pl.ds(q0, 8)
            near[chunk, dest, 0, block, rows, :], near[chunk, dest, 1, block, rows, :] = value
            largest.append(value[0] * value[0] + value[1] * value[1])

        inverse_slabs(get, put)
        while len(largest) > 1:
            largest = [jnp.maximum(a, b) for a, b in zip(largest[0::2], largest[1::2])]
        top[...] = jnp.maximum(top[...], largest[0])

    for p in range(products):
        copy_in(p).start()
    top[...] = jnp.zeros_like(top)

    @pl.loop(0, products)
    def _(p):
        prepare(p)
        product(p, 0)

    tiles = CHUNK // 16
    steps = min(tiles, products // 2)
    for chunk in range(CHUNKS):
        for part in range(2):

            @pl.loop(part * steps, (part + 1) * steps)
            def _(t):
                for item in range(tiles // steps):
                    butterflies(t * (tiles // steps) + item, chunk)
                if chunk + 1 < CHUNKS:
                    for item in range(products // 2 // steps):
                        product(t * (products // 2 // steps) + item, chunk + 1)

            for copy in copies_out(chunk, part if chunk + 1 == CHUNKS else 1 - part):
                copy.start()
    peak_sq[0] = jnp.max(top[...])
    for chunk in range(CHUNKS):
        for part in range(2):
            for copy in copies_out(chunk, part):
                copy.wait()


def line_kernel(
    order, own, tail, lines, gain, twist, fwd_high, fwd_low, inv_high, inv_low, out, *scratch
):
    half = RES * 8
    at_end = pl.program_id(0) == pl.num_programs(0) - 1

    def line_twist(side):
        def read(k):
            lanes = pl.ds(side * 128, 128)
            return twist[0, k, :, lanes], twist[1, k, :, lanes]

        return read

    def forward(group, stacked, sides=(0, 1)):
        for side in sides:
            waiting = {}

            def get(m):
                block = order[2 * m + side]
                at = group * 16
                return lines[block, at : at + 8, :], lines[block, at + 8 : at + 16, :]

            def put(u, value):
                waiting[u] = twisted(value, u, 1, line_twist(side))
                v = (u + RES // 2) % RES
                if v in waiting:
                    first = min(u, v)
                    rows = pl.ds(first * 16, 16)
                    rows_low = pl.ds(half + first * 16, 16)
                    for part in range(2):
                        item = jnp.concatenate(
                            [waiting[first][part], waiting[first + RES // 2][part]], axis=0
                        )
                        at = pl.ds(part * INNER + side * 128, 128)
                        stacked[rows, at], stacked[rows_low, at] = high_low(item)

            forward_slabs(get, put)

    def filtered(group, stacked):
        spec = three_right(stacked[...], half, fwd_high[...], fwd_low[...])
        spec_re, spec_im = spec[:, :128], spec[:, 128:]
        g_re, g_im = gain[0, group], gain[1, group]
        mixed = jnp.concatenate(
            [spec_re * g_re - spec_im * g_im, spec_re * g_im + spec_im * g_re], axis=1
        )
        return jnp.concatenate(high_low(mixed), axis=0)

    def unfold(mixed, back):
        back[...] = three_right(mixed, half, inv_high[...], inv_low[...])

    def inverse(group, back, sides=(0, 1)):
        for side in sides:

            def get(u):
                rows = pl.ds((u % (RES // 2)) * 16 + (u // (RES // 2)) * 8, 8)
                re = back[rows, pl.ds(side * 128, 128)]
                im = back[rows, pl.ds(INNER + side * 128, 128)]
                return twisted((re, im), u, -1, line_twist(side))

            def put(m, value):
                block = order[2 * m + side]
                at = group * 16
                out[block, at : at + 8, :], out[block, at + 8 : at + 16, :] = value

            inverse_slabs(get, put)

    if tail:

        @pl.when(at_end)
        def _():
            for block in range(N // 128):
                lines[block, 8:12, :] = lines[block, 4:8, :]

    groups = len(scratch) // 2

    stacked, back = scratch[:groups], scratch[groups:]

    def run(count):
        forward(0, stacked[0])
        for group in range(count):
            mixed = filtered(group, stacked[group])
            if group + 1 < count:
                forward(group + 1, stacked[group + 1], (0,))
            if group > 0:
                inverse(group - 1, back[group - 1], (0,))
            unfold(mixed, back[group])
            if group + 1 < count:
                forward(group + 1, stacked[group + 1], (1,))
            if group > 0:
                inverse(group - 1, back[group - 1], (1,))
        inverse(count - 1, back[count - 1])

    rest = own % groups
    if rest:
        pl.when(jnp.logical_not(at_end))(lambda: run(groups))
        pl.when(at_end)(lambda: run(rest))
    else:
        run(groups)

    if tail:

        @pl.when(at_end)
        def _():
            for block in range(N // 128):
                out[block, 4:8, :] = out[block, 8:12, :]


def gain_kernel(place, gain):
    k0 = place[0]
    group = place[1] + pl.program_id(0)
    down = lax.broadcasted_iota(jnp.int32, (8, 128), 0)
    across = lax.broadcasted_iota(jnp.int32, (8, 128), 1)
    row = (k0 + RES * (group * 8 + down - HALF)).astype(jnp.float32)
    row_sq = row * row
    row_in = jnp.abs(row) < LIMIT
    for u in range(RES):
        col = (residue(u) + RES * (across - HALF)).astype(jnp.float32)
        square = row_sq + col * col
        scaled = RATIO_SQ * square
        phase = -2.0 * math.pi * distance / wavelength * scaled / (1.0 + jnp.sqrt(1.0 - scaled))
        total = jnp.where(
            row_in & (jnp.abs(col) < LIMIT), jnp.exp(square * (-2.0 / (LIMIT * LIMIT))), 0.0
        )
        quarter = jnp.floor(phase * (2.0 / math.pi) + 0.5)
        left = phase - quarter * 1.5703125
        left = left - quarter * 4.837512969970703125e-4
        left = left - quarter * 7.549789954891882e-8
        sq = left * left
        sine = ((-1.9515295891e-4 * sq + 8.3321608736e-3) * sq - 1.6666654611e-1) * sq * left + left
        cosine = (
            (2.443315711809948e-5 * sq - 1.388731625493765e-3) * sq + 4.166664568298827e-2
        ) * sq * sq - 0.5 * sq + 1.0
        which = quarter.astype(jnp.int32) & 3
        swap = (which & 1) == 1
        cos_part = jnp.where(swap, sine, cosine)
        sin_part = jnp.where(swap, cosine, sine)
        cos_part = jnp.where((which == 1) | (which == 2), -cos_part, cos_part)
        sin_part = jnp.where(which >= 2, -sin_part, sin_part)
        at = (u % (RES // 2)) * 16 + (u // (RES // 2)) * 8
        gain[0, 0, at : at + 8, :] = total * cos_part
        gain[1, 0, at : at + 8, :] = total * sin_part


def encode(near_real, near_imag, peak_sq, cell_sign):
    square = near_real * near_real + near_imag * near_imag
    root = lax.rsqrt(jnp.maximum(square, 1.2e-38))
    top = lax.rsqrt(peak_sq)
    amp_level = (square * root) * (0.8 * top)
    unit = jnp.minimum(root, 20.0 * top)
    rest = 1.0 - amp_level * amp_level
    level = unit * amp_level
    lift = (rest * lax.rsqrt(rest)) * (unit * cell_sign)
    return (near_real * level + near_imag * lift, near_imag * level - near_real * lift)


def stamp_kernel(others, peak_one, peak_two, *refs):
    refs = refs[others:]
    stay, pieces, refs = refs[:CHUNKS], refs[CHUNKS : CHUNKS + others], refs[CHUNKS + others :]
    fetched, (tile, sems) = refs[:CHUNKS], refs[CHUNKS:]
    tile[...] = jnp.full(tile.shape, jnp.maximum(peak_one[0], peak_two[0]), jnp.float32)
    copies = []
    for j, piece in enumerate(pieces):
        rows = pl.ds(piece.shape[0] - SPARE, SPARE)
        copies.append(pltpu.make_async_copy(tile, piece.at[rows], sems.at[j]))
    for chunk in range(CHUNKS):
        copies.append(pltpu.make_async_copy(stay[chunk], fetched[chunk], sems.at[others + chunk]))
    for copy in copies:
        copy.start()
    for copy in copies:
        copy.wait()


def encode_kernel(count, place, peak_one, peak_two, *refs):
    pieces, refs = refs[: CHUNKS * count], refs[CHUNKS * count :]
    slm_real, slm_imag, tile_real, tile_imag, sems = refs
    blocks, width = tile_real.shape[0], pieces[0].shape[-1]
    top = jnp.full((1, width), jnp.maximum(peak_one[0], peak_two[0]), jnp.float32)
    for piece in pieces[(CHUNKS - 1) * count + 1 :]:
        top = jnp.maximum(top, piece[pl.ds(piece.shape[0] - SPARE, 1), :])
    cell = lax.broadcasted_iota(jnp.int32, (CHUNK, width), 0)
    cell = cell + lax.broadcasted_iota(jnp.int32, (CHUNK, width), 1)
    cell_sign = (1 - 2 * (cell & 1)).astype(jnp.float32)

    def copies_out(block):
        rows = pl.ds(block * INNER, INNER)
        return [
            pltpu.make_async_copy(tile.at[block], slm.at[rows], sems.at[2 * block + part])
            for part, (tile, slm) in enumerate(((tile_real, slm_real), (tile_imag, slm_imag)))
        ]

    @pl.loop(0, blocks)
    def _(block):
        for at in range(CHUNKS * count):
            chunk, j = divmod(at, count)
            piece = pieces[at]
            lanes = pl.ds(pl.multiple_of((place[0] ^ j) * width, width), width)
            rows = pl.ds(chunk * CHUNK, CHUNK)
            real = pl.ds(pl.multiple_of(block * CHUNK, CHUNK), CHUNK)
            imag = pl.ds(pl.multiple_of((blocks + block) * CHUNK, CHUNK), CHUNK)
            tile_real[block, rows, lanes], tile_imag[block, rows, lanes] = encode(
                piece[real, :], piece[imag, :], top, cell_sign
            )
        for copy in copies_out(block):
            copy.start()

    for block in range(blocks):
        for copy in copies_out(block):
            copy.wait()


def pack_kernel(place, field_real, field_imag, *refs):
    pieces, sems = refs[:-1], refs[-1]
    width = pieces[0].shape[-1]
    copies = []
    for j in list(range(1, len(pieces))) + [0]:
        lanes = pl.ds(pl.multiple_of((place[0] ^ j) * width, width), width)
        for part, field in enumerate((field_real, field_imag)):
            copies.append(
                pltpu.make_async_copy(
                    field.at[:, :, lanes], pieces[j].at[part], sems.at[2 * j + part]
                )
            )
    for copy in copies:
        copy.start()
    for copy in copies:
        copy.wait()


def exchange(pieces, axis):
    total = len(pieces)
    return [pieces[0]] + [
        lax.ppermute(pieces[j], axis, [(i, i ^ j) for i in range(total)]) for j in range(1, total)
    ]


def params(mebibytes):
    return pltpu.CompilerParams(vmem_limit_bytes=mebibytes << 20)


def cost(megabytes):
    return pl.CostEstimate(flops=0, bytes_accessed=megabytes << 20, transcendentals=0)


def whole(memory=pltpu.VMEM):
    return pl.BlockSpec(memory_space=memory)


def body(field_real, field_imag):
    row_total, col_total = lax.axis_size("row"), lax.axis_size("col")
    devices = row_total * col_total
    device = lax.axis_index("row") * col_total + lax.axis_index("col")
    height, tile_width = field_real.shape
    width = tile_width // row_total
    parts = max(1, devices // RES)
    groups = -(-(2 * HALF + 1) // (8 * parts)) * parts
    own = groups // parts
    tail = parts == 1
    total_rows = groups * 16 - (8 if tail else 0)
    own_rows = total_rows // parts
    many = 4 if width == 128 else 1

    fwd_col, inv_col = column_tables(groups, tail)
    line_fh, line_fl, line_ih, line_il = line_tables()
    twist = np.stack(twist_table())
    twist_line = np.ascontiguousarray(np.broadcast_to(twist[:, :, None], twist.shape[:2] + (8, INNER)))
    twist_col = np.pad(twist, ((0, 0), (0, 64 - twist.shape[1]), (0, 0)))
    twist_col = twist_col.reshape(128, INNER).T.copy()

    u = device // parts
    k0 = jnp.where(u >= RES // 2, u - RES, u)
    place = jnp.stack([k0, (device % parts) * own]).astype(jnp.int32)
    gain = pl.pallas_call(
        gain_kernel,
        grid=(own,),
        in_specs=[whole(pltpu.SMEM)],
        out_specs=pl.BlockSpec((2, 1, RES * 8, 128), lambda g: (0, g, 0, 0)),
        out_shape=jax.ShapeDtypeStruct((2, own, RES * 8, 128), jnp.float32),
        compiler_params=params(56),
        name="gain",
    )(place)

    place_row = lax.axis_index("row").reshape(1).astype(jnp.int32)
    blocks = height // INNER
    anywhere = whole(pl.ANY)
    if width != 128:
        packed = jnp.stack([field_real, field_imag]).reshape(2, blocks, INNER, row_total, width)
        packed = jnp.take(packed, jnp.arange(row_total) ^ place_row[0], axis=3)
    lines = []
    for chunk, (start, size) in enumerate(FRONT):
        piece_shape = jax.ShapeDtypeStruct((2, blocks, size, width), jnp.float32)
        at = start // size
        if width == 128:
            pieces = pl.pallas_call(
                pack_kernel,
                grid=(1,),
                in_specs=[whole(pltpu.SMEM)]
                + [pl.BlockSpec((blocks, size, tile_width), lambda i: (0, at, 0))] * 2,
                out_specs=[anywhere] * row_total,
                out_shape=[piece_shape] * row_total,
                scratch_shapes=[pltpu.SemaphoreType.DMA((2 * row_total,))],
                compiler_params=params(56),
                cost_estimate=cost(4),
                name="pack",
            )(
                place_row,
                field_real.reshape(blocks, INNER, tile_width),
                field_imag.reshape(blocks, INNER, tile_width),
            )
        else:
            pieces = [packed[:, :, start : start + size, j] for j in range(row_total)]
        pieces = exchange(pieces, "row")
        rows = slice(start, start + size)
        slab = pltpu.VMEM((RES // many, 2 * size, many * width), jnp.bfloat16)
        lines = [
            pl.pallas_call(
                partial(column_forward_kernel, row_total),
                in_specs=[whole(pltpu.SMEM)] + [whole()] * (2 + row_total) + [anywhere] * len(lines),
                out_specs=anywhere,
                out_shape=jax.ShapeDtypeStruct((RES, total_rows, width), jnp.float32),
                scratch_shapes=[
                    pltpu.VMEM((RES, total_rows, width), jnp.float32),
                    slab,
                    slab,
                    pltpu.SemaphoreType.DMA((2 * RES // many,)),
                ],
                compiler_params=params(20),
                cost_estimate=cost(20),
                name="column_forward",
            )(place_row, twist_col[rows], fwd_col[chunk], *pieces, *lines)
        ]
    (lines,) = lines

    lines = lines.reshape(devices, own_rows, width)
    lines = lax.all_to_all(lines, ("row", "col"), split_axis=0, concat_axis=0, tiled=True)
    if width == 128:
        order = tuple((b % row_total) * col_total + b // row_total for b in range(N // 128))
    else:
        order = tuple(range(N // 128))
        lines = lines.reshape(row_total, col_total, own_rows, width).transpose(2, 1, 0, 3)
        lines = lines.reshape(own_rows, N // 128, 128).transpose(1, 0, 2)

    at_once = 2
    line_grain = pl.BlockSpec((N // 128, 16 * at_once, 128), lambda i: (0, i, 0))
    gain_grain = pl.BlockSpec((2, at_once, RES * 8, 128), lambda i: (0, i, 0, 0))
    lines = pl.pallas_call(
        partial(line_kernel, order, own, tail),
        grid=(-(-own // at_once),),
        in_specs=[line_grain, gain_grain] + [whole()] * 5,
        out_specs=line_grain,
        out_shape=jax.ShapeDtypeStruct((N // 128, own_rows, 128), jnp.float32),
        scratch_shapes=[pltpu.VMEM((2 * RES * 8, 2 * INNER), jnp.bfloat16)] * at_once
        + [pltpu.VMEM((RES * 8, 2 * INNER), jnp.float32)] * at_once,
        compiler_params=params(48),
        name="line",
    )(lines, gain, twist_line, line_fh, line_fl, line_ih, line_il)

    if width != 128:
        lines = lines.transpose(1, 0, 2).reshape(own_rows, col_total, row_total, width)
        lines = lines.transpose(2, 1, 0, 3).reshape(devices, own_rows, width)
    lines = lax.all_to_all(lines, ("row", "col"), split_axis=0, concat_axis=0, tiled=True)
    lines = lines.reshape(RES, total_rows, width)

    piece_shapes = [
        jax.ShapeDtypeStruct((2 * blocks * CHUNK + spare, width), jnp.float32)
        for spare in (0,) * (CHUNKS - 1) + (SPARE,)
    ]
    *near, peak_sq = pl.pallas_call(
        partial(column_inverse_kernel, row_total),
        in_specs=[whole(pltpu.SMEM), anywhere, whole(), whole()],
        out_specs=[anywhere] * (CHUNKS * row_total) + [whole(pltpu.SMEM)],
        out_shape=[shape for shape in piece_shapes for _ in range(row_total)]
        + [jax.ShapeDtypeStruct((1,), jnp.float32)],
        scratch_shapes=[
            pltpu.VMEM((CHUNKS, row_total, 2, blocks, CHUNK, width), jnp.float32),
            pltpu.VMEM((RES, total_rows, width), jnp.float32),
            pltpu.VMEM((RES // many, inv_col.shape[2], many * width), jnp.bfloat16),
            pltpu.VMEM((CHUNKS, RES, 2 * CHUNK, width), jnp.float32),
            pltpu.VMEM((8, width), jnp.float32),
            pltpu.SemaphoreType.DMA((RES // many,)),
            pltpu.SemaphoreType.DMA((2 * CHUNKS * row_total,)),
        ],
        compiler_params=params(56),
        name="column_inverse",
    )(place_row, lines, twist_col, inv_col)
    near = [near[:row_total], near[row_total:]]
    piece_shape = piece_shapes[-1]
    near[0] = exchange(near[0], "row")
    shift = 1
    while shift < col_total:
        partner = [(i, i ^ shift) for i in range(col_total)]
        peaks = [peak_sq, lax.ppermute(peak_sq, "col", partner)]
        shift *= 2
        if shift < col_total:
            peak_sq = jnp.maximum(*peaks)
    others = row_total - 1
    stamped = pl.pallas_call(
        partial(stamp_kernel, others),
        in_specs=[whole(pltpu.SMEM)] * 2 + [anywhere] * (others + CHUNKS),
        out_specs=[anywhere] * others + [whole()] * CHUNKS,
        out_shape=[piece_shape] * others + piece_shapes,
        scratch_shapes=[
            pltpu.VMEM((SPARE, width), jnp.float32),
            pltpu.SemaphoreType.DMA((others + CHUNKS,)),
        ],
        input_output_aliases={2 + j: j for j in range(others)},
        compiler_params=params(16),
        name="stamp",
    )(*peaks, *near[1][1:], near[0][0], near[1][0])
    near[1][1:] = stamped[:others]
    near[0][0], near[1][0] = stamped[others:]
    near[0][1:], near[1][1] = lax.optimization_barrier((near[0][1:], near[1][1]))
    near[1] = exchange(near[1], "row")
    if width != 128:
        peak_sq = jnp.maximum(*peaks)[0]
        for piece in near[1][1:]:
            peak_sq = jnp.maximum(peak_sq, piece[-1, 0])
        near = jnp.stack([jnp.stack([piece[: 2 * blocks * CHUNK] for piece in pieces]) for pieces in near])
        near = jnp.take(near, jnp.arange(row_total) ^ place_row[0], axis=1)
        near = near.reshape(CHUNKS, row_total, 2, blocks, CHUNK, width)
        near = near.transpose(2, 3, 0, 4, 1, 5).reshape(2, height, tile_width)
        odd_cell = (jnp.arange(height)[:, None] + jnp.arange(tile_width)[None, :]) % 2
        cell_sign = (1 - 2 * odd_cell).astype(jnp.float32)
        return encode(near[0], near[1], peak_sq, cell_sign)
    tile_shape = jax.ShapeDtypeStruct((height, tile_width), jnp.float32)
    tile = pltpu.VMEM((blocks, INNER, tile_width), jnp.float32)
    return pl.pallas_call(
        partial(encode_kernel, row_total),
        in_specs=[whole(pltpu.SMEM)] * 3 + [whole()] * (CHUNKS * row_total),
        out_specs=[anywhere] * 2,
        out_shape=[tile_shape, tile_shape],
        scratch_shapes=[tile, tile, pltpu.SemaphoreType.DMA((2 * blocks,))],
        compiler_params=params(16),
        name="encode",
    )(place_row, *peaks, *near[0], *near[1])


def solution(mesh):
    in_specs = (P("row", "col"), P("row", "col"))
    out_specs = (P("row", "col"), P("row", "col"))
    return jax.shard_map(body, mesh=mesh, in_specs=in_specs, out_specs=out_specs, check_vma=False)
```

```python
from functools import partial
import math

import jax
import jax.numpy as jnp
import ml_dtypes
import numpy as np
from jax import lax
from jax.experimental import pallas as pl
from jax.experimental.pallas import tpu as pltpu
from jax.sharding import PartitionSpec as P

N = 4096
PAD = 2 * N
wavelength = 5.2e-07
distance = 0.2
INNER = 256
SLABS = N // INNER
RES = PAD // INNER
HALF = 40
CHUNKS = 2
CHUNK = INNER // CHUNKS
FRONT = ((0, 128), (128, 128))
SPARE = 8


def optics(padded_side):
    pitch = 2e-06 * math.sqrt(8192.0 / padded_side)
    extent = padded_side * pitch
    ratio_sq = (wavelength / extent) ** 2
    band_limit = extent / (wavelength * math.sqrt((2.0 * distance / extent) ** 2 + 1.0))
    return (ratio_sq, band_limit)


RATIO_SQ, LIMIT = optics(PAD)
assert RES * HALF - RES // 2 + RES > LIMIT and RES * HALF + RES // 2 > LIMIT


def residue(u):
    return u if u < RES // 2 else u - RES


def split16(table):
    table = np.asarray(table, np.float64)
    high = table.astype(np.float32).astype(ml_dtypes.bfloat16)
    low = (table - high.astype(np.float64)).astype(np.float32).astype(ml_dtypes.bfloat16)
    return high, low


def row_order(groups, tail):
    rows = []
    for group in range(groups):
        size = 4 if tail and group == groups - 1 else 8
        for part in range(2):
            for s in range(size):
                rows.append((part, group * 8 + s - HALF))
    return rows


def column_tables(groups, tail):
    q = np.arange(INNER)
    rows = row_order(groups, tail)
    forward = np.zeros((len(rows), 2, INNER))
    inverse = np.zeros((2, INNER, len(rows)))
    for at, (part, k1) in enumerate(rows):
        if abs(k1) > HALF:
            continue
        angle = 2.0 * np.pi * ((k1 * q) % INNER) / INNER
        c, s = np.cos(angle), np.sin(angle)
        forward[at] = (c, s) if part == 0 else (-s, c)
        inverse[:, :, at] = (c, s) if part == 0 else (-s, c)
    tables = []
    for start, size in FRONT:
        part = forward[:, :, start : start + size].reshape(-1, 2, size // 8, 8)
        part = part.transpose(0, 2, 1, 3).reshape(-1, 2 * size)
        tables.append(np.concatenate(split16(part), axis=0))
    inverse = inverse.reshape(2, CHUNKS, CHUNK, -1).transpose(1, 0, 2, 3)
    high, low = split16(inverse.reshape(CHUNKS, 2 * CHUNK, len(rows)))
    inverse = np.concatenate([high, high, low], axis=2)
    inverse = np.pad(inverse, ((0, 0), (0, 0), (0, -3 * len(rows) % 16)))
    return tables, inverse


def line_tables():
    q = np.arange(INNER)
    forward = np.zeros((2 * INNER, 256))
    inverse = np.zeros((256, 2 * INNER))
    for lane in range(2 * HALF + 1):
        angle = 2.0 * np.pi * (((lane - HALF) * q) % INNER) / INNER
        c, s = np.cos(angle), np.sin(angle)
        forward[:INNER, lane], forward[INNER:, lane] = c, s
        forward[:INNER, 128 + lane], forward[INNER:, 128 + lane] = -s, c
        inverse[lane, :INNER], inverse[lane, INNER:] = c, s
        inverse[128 + lane, :INNER], inverse[128 + lane, INNER:] = -s, c
    return split16(forward) + split16(inverse)


def twist_table():
    q = np.arange(INNER) + N // 2
    k0 = np.arange(RES // 2 + 1)
    angle = 2.0 * np.pi * ((k0[:, None] * q[None, :]) % PAD) / PAD
    return np.cos(angle).astype(np.float32), (-np.sin(angle)).astype(np.float32)


def turn(value, num, den):
    re, im = value
    num = num % den
    eighth = 8 * num
    if num == 0:
        return re, im
    if 2 * num == den:
        return -re, -im
    if 4 * num == den:
        return -im, re
    if 4 * num == 3 * den:
        return im, -re
    if eighth % den == 0:
        root = np.float32(math.sqrt(0.5))
        kind = eighth // den
        if kind == 1:
            return (re - im) * root, (re + im) * root
        if kind == 3:
            return (re + im) * (-root), (re - im) * root
        if kind == 5:
            return (im - re) * root, (re + im) * (-root)
        return (re + im) * root, (im - re) * root
    c = np.float32(math.cos(2.0 * math.pi * num / den))
    s = np.float32(math.sin(2.0 * math.pi * num / den))
    return re * c - im * s, re * s + im * c


def small_dft(get, ids, sign):
    count = len(ids)
    if count == 1:
        return [get(ids[0])]
    even = small_dft(get, ids[0::2], sign)
    odd = small_dft(get, ids[1::2], sign)
    half = count // 2
    first, second = [], []
    for j in range(half):
        re, im = even[j]
        t_re, t_im = turn(odd[j], sign * j, count)
        first.append((re + t_re, im + t_im))
        second.append((re - t_re, im - t_im))
    return first + second


def forward_slabs(get, put):
    ids = list(range(SLABS))
    for v, value in enumerate(small_dft(get, ids, -1)):
        put(2 * v, value)
    for v, value in enumerate(small_dft(lambda n: turn(get(n), -n, RES), ids, -1)):
        put(2 * v + 1, value)


def inverse_slabs(get, put):
    even = small_dft(get, list(range(0, RES, 2)), 1)
    odd = small_dft(get, list(range(1, RES, 2)), 1)
    for n in range(SLABS):
        t_re, t_im = turn(odd[n], n, RES)
        put(n, (even[n][0] + t_re, even[n][1] + t_im))


def twisted(value, u, sign, read):
    re, im = value
    k0 = residue(u)
    if k0 == 0:
        return value
    c, s = read(abs(k0))
    if (k0 < 0) == (sign > 0):
        return re * c + im * s, im * c - re * s
    return re * c - im * s, re * s + im * c


def high_low(value):
    high = value.astype(jnp.bfloat16)
    low = (value - high.astype(jnp.float32)).astype(jnp.bfloat16)
    return high, low


def dot16(left, right):
    return jnp.dot(left, right, preferred_element_type=jnp.float32)


def three_left(stacked, count, high, low):
    both = dot16(stacked[...], high)
    return both[:count] + both[count:] + dot16(stacked[:count], low)


def three_right(stacked, count, high, low):
    both = dot16(stacked, high)
    return both[:count] + both[count:] + dot16(stacked[:count], low)


def column_twist(twist, q0):
    seen = {}

    def read(k):
        if k not in seen:
            rows = pl.ds(q0, 8)
            seen[k] = twist[rows, k : k + 1], twist[rows, 64 + k : 65 + k]
        return seen[k]

    return read


def column_forward_kernel(count, place, twist, matrix, *refs):
    pieces, refs = refs[:count], refs[count:]
    before, (out, total, high, low, sems) = refs[:-5], refs[-5:]
    width = pieces[0].shape[-1]
    per_source, size = pieces[0].shape[1:3]
    many = high.shape[-1] // width
    products = RES // many
    rows_out = out.shape[1]

    def copy_in(p):
        part = pl.ds(p * many, many)
        return pltpu.make_async_copy(before[0].at[part], total.at[part], sems.at[p])

    def copy_out(p):
        part = pl.ds(p * many, many)
        return pltpu.make_async_copy(total.at[part], out.at[part], sems.at[products + p])

    if before:
        for p in range(products):
            copy_in(p).start()

    for here in range(count):

        @pl.when(place[0] == here)
        def _():
            @pl.loop(0, size // 8)
            def _(t):
                q0 = pl.multiple_of(t * 8, 8)
                read = column_twist(twist, q0)

                def get(n):
                    source, block = divmod(n, per_source)
                    piece = pieces[source ^ here]
                    rows = pl.ds(q0, 8)
                    return piece[0, block, rows, :], piece[1, block, rows, :]

                def put(u, value):
                    item = jnp.concatenate(twisted(value, u, 1, read), axis=0)
                    rows = pl.ds(pl.multiple_of(t * 16, 16), 16)
                    at = (u // many, rows, pl.ds((u % many) * width, width))
                    high[at], low[at] = high_low(item)

                forward_slabs(get, put)

    @pl.loop(0, products)
    def _(p):
        done = three_left(matrix, rows_out, high[p], low[p])
        if before:
            copy_in(p).wait()
        for part in range(many):
            item = done[:, part * width : (part + 1) * width]
            at = p * many + part
            total[at] = total[at] + item if before else item
        copy_out(p).start()

    for p in range(products):
        copy_out(p).wait()


def column_inverse_kernel(count, place, source, twist, matrix, *refs):
    pieces, (peak_sq, near, lines, deep, back, top, sems, out_sems) = refs[:-8], refs[-8:]
    width = lines.shape[-1]
    rows_in = lines.shape[1]
    per_dest = near.shape[3]
    many = deep.shape[-1] // width
    products = RES // many

    def copy_in(p):
        part = pl.ds(p * many, many)
        return pltpu.make_async_copy(source.at[part], lines.at[part], sems.at[p])

    def copies_out(chunk, part):
        parts = 1 if chunk + 1 < CHUNKS else 2
        if part >= parts:
            return []
        rows = pl.ds(part * CHUNK // parts, CHUNK // parts)
        copies = []
        for j in range(count):
            piece = pieces[chunk * count + j].at[pl.ds(0, 2 * per_dest * CHUNK)]
            there = piece.reshape(2, per_dest, CHUNK, width).at[:, :, rows]
            here = near.at[chunk, place[0] ^ j, :, :, rows]
            copies.append(pltpu.make_async_copy(here, there, out_sems.at[(chunk * 2 + part) * count + j]))
        return copies

    def prepare(p):
        copy_in(p).wait()
        blocks = [lines[p * many + part] for part in range(many)]
        joined = jnp.concatenate(blocks, axis=1) if many > 1 else blocks[0]
        high = joined.astype(jnp.bfloat16).astype(jnp.float32)
        parts = [high, joined - high, high]
        if deep.shape[1] > 3 * rows_in:
            parts.append(jnp.zeros((deep.shape[1] - 3 * rows_in, many * width), jnp.float32))
        deep[p] = jnp.concatenate(parts, axis=0).astype(jnp.bfloat16)

    def product(p, chunk):
        done = dot16(matrix[chunk], deep[p])
        for part in range(many):
            back[chunk, p * many + part] = done[:, part * width : (part + 1) * width]

    def butterflies(t, chunk):
        q0 = pl.multiple_of(t * 8, 8)
        largest = []
        read = column_twist(twist, pl.multiple_of(chunk * CHUNK + q0, 8))

        def get(u):
            re = back[chunk, u, pl.ds(q0, 8), :]
            im = back[chunk, u, pl.ds(CHUNK + q0, 8), :]
            return twisted((re, im), u, -1, read)

        def put(n, value):
            dest, block = divmod(n, per_dest)
            rows = pl.ds(q0, 8)
            near[chunk, dest, 0, block, rows, :], near[chunk, dest, 1, block, rows, :] = value
            largest.append(value[0] * value[0] + value[1] * value[1])

        inverse_slabs(get, put)
        while len(largest) > 1:
            largest = [jnp.maximum(a, b) for a, b in zip(largest[0::2], largest[1::2])]
        top[...] = jnp.maximum(top[...], largest[0])

    for p in range(products):
        copy_in(p).start()
    top[...] = jnp.zeros_like(top)

    @pl.loop(0, products)
    def _(p):
        prepare(p)
        product(p, 0)

    tiles = CHUNK // 16
    steps = min(tiles, products // 2)
    for chunk in range(CHUNKS):
        for part in range(2):

            @pl.loop(part * steps, (part + 1) * steps)
            def _(t):
                for item in range(tiles // steps):
                    butterflies(t * (tiles // steps) + item, chunk)
                if chunk + 1 < CHUNKS:
                    for item in range(products // 2 // steps):
                        product(t * (products // 2 // steps) + item, chunk + 1)

            for copy in copies_out(chunk, part if chunk + 1 == CHUNKS else 1 - part):
                copy.start()
    peak_sq[0] = jnp.max(top[...])
    for chunk in range(CHUNKS):
        for part in range(2):
            for copy in copies_out(chunk, part):
                copy.wait()


def line_kernel(
    order, own, tail, lines, gain, twist, fwd_high, fwd_low, inv_high, inv_low, out, *scratch
):
    half = RES * 8
    at_end = pl.program_id(0) == pl.num_programs(0) - 1

    def line_twist(side):
        def read(k):
            lanes = pl.ds(side * 128, 128)
            return twist[0, k, :, lanes], twist[1, k, :, lanes]

        return read

    def forward(group, stacked, sides=(0, 1)):
        for side in sides:
            waiting = {}

            def get(m):
                block = order[2 * m + side]
                at = group * 16
                return lines[block, at : at + 8, :], lines[block, at + 8 : at + 16, :]

            def put(u, value):
                waiting[u] = twisted(value, u, 1, line_twist(side))
                v = (u + RES // 2) % RES
                if v in waiting:
                    first = min(u, v)
                    rows = pl.ds(first * 16, 16)
                    rows_low = pl.ds(half + first * 16, 16)
                    for part in range(2):
                        item = jnp.concatenate(
                            [waiting[first][part], waiting[first + RES // 2][part]], axis=0
                        )
                        at = pl.ds(part * INNER + side * 128, 128)
                        stacked[rows, at], stacked[rows_low, at] = high_low(item)

            forward_slabs(get, put)

    def filtered(group, stacked):
        spec = three_right(stacked[...], half, fwd_high[...], fwd_low[...])
        spec_re, spec_im = spec[:, :128], spec[:, 128:]
        g_re, g_im = gain[0, group], gain[1, group]
        mixed = jnp.concatenate(
            [spec_re * g_re - spec_im * g_im, spec_re * g_im + spec_im * g_re], axis=1
        )
        return jnp.concatenate(high_low(mixed), axis=0)

    def unfold(mixed, back):
        back[...] = three_right(mixed, half, inv_high[...], inv_low[...])

    def inverse(group, back, sides=(0, 1)):
        for side in sides:

            def get(u):
                rows = pl.ds((u % (RES // 2)) * 16 + (u // (RES // 2)) * 8, 8)
                re = back[rows, pl.ds(side * 128, 128)]
                im = back[rows, pl.ds(INNER + side * 128, 128)]
                return twisted((re, im), u, -1, line_twist(side))

            def put(m, value):
                block = order[2 * m + side]
                at = group * 16
                out[block, at : at + 8, :], out[block, at + 8 : at + 16, :] = value

            inverse_slabs(get, put)

    if tail:

        @pl.when(at_end)
        def _():
            for block in range(N // 128):
                lines[block, 8:12, :] = lines[block, 4:8, :]

    groups = len(scratch) // 2

    stacked, back = scratch[:groups], scratch[groups:]

    def run(count):
        forward(0, stacked[0])
        for group in range(count):
            mixed = filtered(group, stacked[group])
            if group + 1 < count:
                forward(group + 1, stacked[group + 1], (0,))
            if group > 0:
                inverse(group - 1, back[group - 1], (0,))
            unfold(mixed, back[group])
            if group + 1 < count:
                forward(group + 1, stacked[group + 1], (1,))
            if group > 0:
                inverse(group - 1, back[group - 1], (1,))
        inverse(count - 1, back[count - 1])

    rest = own % groups
    if rest:
        pl.when(jnp.logical_not(at_end))(lambda: run(groups))
        pl.when(at_end)(lambda: run(rest))
    else:
        run(groups)

    if tail:

        @pl.when(at_end)
        def _():
            for block in range(N // 128):
                out[block, 4:8, :] = out[block, 8:12, :]


def gain_kernel(place, gain):
    k0 = place[0]
    group = place[1] + pl.program_id(0)
    down = lax.broadcasted_iota(jnp.int32, (8, 128), 0)
    across = lax.broadcasted_iota(jnp.int32, (8, 128), 1)
    row = (k0 + RES * (group * 8 + down - HALF)).astype(jnp.float32)
    row_sq = row * row
    row_in = jnp.abs(row) < LIMIT
    for u in range(RES):
        col = (residue(u) + RES * (across - HALF)).astype(jnp.float32)
        square = row_sq + col * col
        scaled = RATIO_SQ * square
        phase = -2.0 * math.pi * distance / wavelength * scaled / (1.0 + jnp.sqrt(1.0 - scaled))
        total = jnp.where(
            row_in & (jnp.abs(col) < LIMIT), jnp.exp(square * (-2.0 / (LIMIT * LIMIT))), 0.0
        )
        quarter = jnp.floor(phase * (2.0 / math.pi) + 0.5)
        left = phase - quarter * 1.5703125
        left = left - quarter * 4.837512969970703125e-4
        left = left - quarter * 7.549789954891882e-8
        sq = left * left
        sine = ((-1.9515295891e-4 * sq + 8.3321608736e-3) * sq - 1.6666654611e-1) * sq * left + left
        cosine = (
            (2.443315711809948e-5 * sq - 1.388731625493765e-3) * sq + 4.166664568298827e-2
        ) * sq * sq - 0.5 * sq + 1.0
        which = quarter.astype(jnp.int32) & 3
        swap = (which & 1) == 1
        cos_part = jnp.where(swap, sine, cosine)
        sin_part = jnp.where(swap, cosine, sine)
        cos_part = jnp.where((which == 1) | (which == 2), -cos_part, cos_part)
        sin_part = jnp.where(which >= 2, -sin_part, sin_part)
        at = (u % (RES // 2)) * 16 + (u // (RES // 2)) * 8
        gain[0, 0, at : at + 8, :] = total * cos_part
        gain[1, 0, at : at + 8, :] = total * sin_part


def encode(near_real, near_imag, peak_sq, cell_sign):
    square = near_real * near_real + near_imag * near_imag
    root = lax.rsqrt(jnp.maximum(square, 1.2e-38))
    top = lax.rsqrt(peak_sq)
    amp_level = (square * root) * (0.8 * top)
    unit = jnp.minimum(root, 20.0 * top)
    rest = 1.0 - amp_level * amp_level
    level = unit * amp_level
    lift = (rest * lax.rsqrt(rest)) * (unit * cell_sign)
    return (near_real * level + near_imag * lift, near_imag * level - near_real * lift)


def stamp_kernel(others, peak_one, peak_two, *refs):
    refs = refs[others:]
    stay, pieces, refs = refs[:CHUNKS], refs[CHUNKS : CHUNKS + others], refs[CHUNKS + others :]
    fetched, (tile, sems) = refs[:CHUNKS], refs[CHUNKS:]
    tile[...] = jnp.full(tile.shape, jnp.maximum(peak_one[0], peak_two[0]), jnp.float32)
    copies = []
    for j, piece in enumerate(pieces):
        rows = pl.ds(piece.shape[0] - SPARE, SPARE)
        copies.append(pltpu.make_async_copy(tile, piece.at[rows], sems.at[j]))
    for chunk in range(CHUNKS):
        copies.append(pltpu.make_async_copy(stay[chunk], fetched[chunk], sems.at[others + chunk]))
    for copy in copies:
        copy.start()
    for copy in copies:
        copy.wait()


def encode_kernel(count, place, peak_one, peak_two, *refs):
    pieces, refs = refs[: CHUNKS * count], refs[CHUNKS * count :]
    slm_real, slm_imag, tile_real, tile_imag, sems = refs
    blocks, width = tile_real.shape[0], pieces[0].shape[-1]
    top = jnp.full((1, width), jnp.maximum(peak_one[0], peak_two[0]), jnp.float32)
    for piece in pieces[(CHUNKS - 1) * count + 1 :]:
        top = jnp.maximum(top, piece[pl.ds(piece.shape[0] - SPARE, 1), :])
    cell = lax.broadcasted_iota(jnp.int32, (CHUNK, width), 0)
    cell = cell + lax.broadcasted_iota(jnp.int32, (CHUNK, width), 1)
    cell_sign = (1 - 2 * (cell & 1)).astype(jnp.float32)

    def copies_out(block):
        rows = pl.ds(block * INNER, INNER)
        return [
            pltpu.make_async_copy(tile.at[block], slm.at[rows], sems.at[2 * block + part])
            for part, (tile, slm) in enumerate(((tile_real, slm_real), (tile_imag, slm_imag)))
        ]

    @pl.loop(0, blocks)
    def _(block):
        for at in range(CHUNKS * count):
            chunk, j = divmod(at, count)
            piece = pieces[at]
            lanes = pl.ds(pl.multiple_of((place[0] ^ j) * width, width), width)
            rows = pl.ds(chunk * CHUNK, CHUNK)
            real = pl.ds(pl.multiple_of(block * CHUNK, CHUNK), CHUNK)
            imag = pl.ds(pl.multiple_of((blocks + block) * CHUNK, CHUNK), CHUNK)
            tile_real[block, rows, lanes], tile_imag[block, rows, lanes] = encode(
                piece[real, :], piece[imag, :], top, cell_sign
            )
        for copy in copies_out(block):
            copy.start()

    for block in range(blocks):
        for copy in copies_out(block):
            copy.wait()


def pack_kernel(place, field_real, field_imag, *refs):
    pieces, sems = refs[:-1], refs[-1]
    width = pieces[0].shape[-1]
    copies = []
    for j in list(range(1, len(pieces))) + [0]:
        lanes = pl.ds(pl.multiple_of((place[0] ^ j) * width, width), width)
        for part, field in enumerate((field_real, field_imag)):
            copies.append(
                pltpu.make_async_copy(
                    field.at[:, :, lanes], pieces[j].at[part], sems.at[2 * j + part]
                )
            )
    for copy in copies:
        copy.start()
    for copy in copies:
        copy.wait()


def exchange(pieces, axis):
    total = len(pieces)
    return [pieces[0]] + [
        lax.ppermute(pieces[j], axis, [(i, i ^ j) for i in range(total)]) for j in range(1, total)
    ]


def params(mebibytes):
    return pltpu.CompilerParams(vmem_limit_bytes=mebibytes << 20)


def cost(megabytes):
    return pl.CostEstimate(flops=0, bytes_accessed=megabytes << 20, transcendentals=0)


def whole(memory=pltpu.VMEM):
    return pl.BlockSpec(memory_space=memory)


def body(field_real, field_imag):
    row_total, col_total = lax.axis_size("row"), lax.axis_size("col")
    devices = row_total * col_total
    device = lax.axis_index("row") * col_total + lax.axis_index("col")
    height, tile_width = field_real.shape
    width = tile_width // row_total
    parts = max(1, devices // RES)
    groups = -(-(2 * HALF + 1) // (8 * parts)) * parts
    own = groups // parts
    tail = parts == 1
    total_rows = groups * 16 - (8 if tail else 0)
    own_rows = total_rows // parts
    many = 4 if width == 128 else 1

    fwd_col, inv_col = column_tables(groups, tail)
    line_fh, line_fl, line_ih, line_il = line_tables()
    twist = np.stack(twist_table())
    twist_line = np.ascontiguousarray(np.broadcast_to(twist[:, :, None], twist.shape[:2] + (8, INNER)))
    twist_col = np.pad(twist, ((0, 0), (0, 64 - twist.shape[1]), (0, 0)))
    twist_col = twist_col.reshape(128, INNER).T.copy()

    u = device // parts
    k0 = jnp.where(u >= RES // 2, u - RES, u)
    place = jnp.stack([k0, (device % parts) * own]).astype(jnp.int32)
    gain = pl.pallas_call(
        gain_kernel,
        grid=(own,),
        in_specs=[whole(pltpu.SMEM)],
        out_specs=pl.BlockSpec((2, 1, RES * 8, 128), lambda g: (0, g, 0, 0)),
        out_shape=jax.ShapeDtypeStruct((2, own, RES * 8, 128), jnp.float32),
        compiler_params=params(50),
        name="gain",
    )(place)

    place_row = lax.axis_index("row").reshape(1).astype(jnp.int32)
    blocks = height // INNER
    anywhere = whole(pl.ANY)
    if width != 128:
        packed = jnp.stack([field_real, field_imag]).reshape(2, blocks, INNER, row_total, width)
        packed = jnp.take(packed, jnp.arange(row_total) ^ place_row[0], axis=3)
    lines = []
    for chunk, (start, size) in enumerate(FRONT):
        piece_shape = jax.ShapeDtypeStruct((2, blocks, size, width), jnp.float32)
        at = start // size
        if width == 128:
            pieces = pl.pallas_call(
                pack_kernel,
                grid=(1,),
                in_specs=[whole(pltpu.SMEM)]
                + [pl.BlockSpec((blocks, size, tile_width), lambda i: (0, at, 0))] * 2,
                out_specs=[anywhere] * row_total,
                out_shape=[piece_shape] * row_total,
                scratch_shapes=[pltpu.SemaphoreType.DMA((2 * row_total,))],
                compiler_params=params(56),
                cost_estimate=cost(4),
                name="pack",
            )(
                place_row,
                field_real.reshape(blocks, INNER, tile_width),
                field_imag.reshape(blocks, INNER, tile_width),
            )
        else:
            pieces = [packed[:, :, start : start + size, j] for j in range(row_total)]
        pieces = exchange(pieces, "row")
        if chunk == 0:
            pieces, gain = lax.optimization_barrier((pieces, gain))
        rows = slice(start, start + size)
        slab = pltpu.VMEM((RES // many, 2 * size, many * width), jnp.bfloat16)
        lines = [
            pl.pallas_call(
                partial(column_forward_kernel, row_total),
                in_specs=[whole(pltpu.SMEM)] + [whole()] * (2 + row_total) + [anywhere] * len(lines),
                out_specs=anywhere,
                out_shape=jax.ShapeDtypeStruct((RES, total_rows, width), jnp.float32),
                scratch_shapes=[
                    pltpu.VMEM((RES, total_rows, width), jnp.float32),
                    slab,
                    slab,
                    pltpu.SemaphoreType.DMA((2 * RES // many,)),
                ],
                compiler_params=params(20),
                cost_estimate=cost(20),
                name="column_forward",
            )(place_row, twist_col[rows], fwd_col[chunk], *pieces, *lines)
        ]
    (lines,) = lines

    lines = lines.reshape(devices, own_rows, width)
    lines = lax.all_to_all(lines, ("row", "col"), split_axis=0, concat_axis=0, tiled=True)
    if width == 128:
        order = tuple((b % row_total) * col_total + b // row_total for b in range(N // 128))
    else:
        order = tuple(range(N // 128))
        lines = lines.reshape(row_total, col_total, own_rows, width).transpose(2, 1, 0, 3)
        lines = lines.reshape(own_rows, N // 128, 128).transpose(1, 0, 2)

    at_once = 2
    line_grain = pl.BlockSpec((N // 128, 16 * at_once, 128), lambda i: (0, i, 0))
    gain_grain = pl.BlockSpec((2, at_once, RES * 8, 128), lambda i: (0, i, 0, 0))
    lines = pl.pallas_call(
        partial(line_kernel, order, own, tail),
        grid=(-(-own // at_once),),
        in_specs=[line_grain, gain_grain] + [whole()] * 5,
        out_specs=line_grain,
        out_shape=jax.ShapeDtypeStruct((N // 128, own_rows, 128), jnp.float32),
        scratch_shapes=[pltpu.VMEM((2 * RES * 8, 2 * INNER), jnp.bfloat16)] * at_once
        + [pltpu.VMEM((RES * 8, 2 * INNER), jnp.float32)] * at_once,
        compiler_params=params(44),
        name="line",
    )(lines, gain, twist_line, line_fh, line_fl, line_ih, line_il)

    if width != 128:
        lines = lines.transpose(1, 0, 2).reshape(own_rows, col_total, row_total, width)
        lines = lines.transpose(2, 1, 0, 3).reshape(devices, own_rows, width)
    lines = lax.all_to_all(lines, ("row", "col"), split_axis=0, concat_axis=0, tiled=True)
    lines = lines.reshape(RES, total_rows, width)

    piece_shapes = [
        jax.ShapeDtypeStruct((2 * blocks * CHUNK + spare, width), jnp.float32)
        for spare in (0,) * (CHUNKS - 1) + (SPARE,)
    ]
    *near, peak_sq = pl.pallas_call(
        partial(column_inverse_kernel, row_total),
        in_specs=[whole(pltpu.SMEM), anywhere, whole(), whole()],
        out_specs=[anywhere] * (CHUNKS * row_total) + [whole(pltpu.SMEM)],
        out_shape=[shape for shape in piece_shapes for _ in range(row_total)]
        + [jax.ShapeDtypeStruct((1,), jnp.float32)],
        scratch_shapes=[
            pltpu.VMEM((CHUNKS, row_total, 2, blocks, CHUNK, width), jnp.float32),
            pltpu.VMEM((RES, total_rows, width), jnp.float32),
            pltpu.VMEM((RES // many, inv_col.shape[2], many * width), jnp.bfloat16),
            pltpu.VMEM((CHUNKS, RES, 2 * CHUNK, width), jnp.float32),
            pltpu.VMEM((8, width), jnp.float32),
            pltpu.SemaphoreType.DMA((RES // many,)),
            pltpu.SemaphoreType.DMA((2 * CHUNKS * row_total,)),
        ],
        compiler_params=params(56),
        name="column_inverse",
    )(place_row, lines, twist_col, inv_col)
    near = [near[:row_total], near[row_total:]]
    piece_shape = piece_shapes[-1]
    near[0] = exchange(near[0], "row")
    shift = 1
    while shift < col_total:
        partner = [(i, i ^ shift) for i in range(col_total)]
        peaks = [peak_sq, lax.ppermute(peak_sq, "col", partner)]
        shift *= 2
        if shift < col_total:
            peak_sq = jnp.maximum(*peaks)
    others = row_total - 1
    stamped = pl.pallas_call(
        partial(stamp_kernel, others),
        in_specs=[whole(pltpu.SMEM)] * 2 + [anywhere] * (others + CHUNKS),
        out_specs=[anywhere] * others + [whole()] * CHUNKS,
        out_shape=[piece_shape] * others + piece_shapes,
        scratch_shapes=[
            pltpu.VMEM((SPARE, width), jnp.float32),
            pltpu.SemaphoreType.DMA((others + CHUNKS,)),
        ],
        input_output_aliases={2 + j: j for j in range(others)},
        compiler_params=params(16),
        name="stamp",
    )(*peaks, *near[1][1:], near[0][0], near[1][0])
    near[1][1:] = stamped[:others]
    near[0][0], near[1][0] = stamped[others:]
    near[0][1:], near[1][1] = lax.optimization_barrier((near[0][1:], near[1][1]))
    near[1] = exchange(near[1], "row")
    if width != 128:
        peak_sq = jnp.maximum(*peaks)[0]
        for piece in near[1][1:]:
            peak_sq = jnp.maximum(peak_sq, piece[-1, 0])
        near = jnp.stack([jnp.stack([piece[: 2 * blocks * CHUNK] for piece in pieces]) for pieces in near])
        near = jnp.take(near, jnp.arange(row_total) ^ place_row[0], axis=1)
        near = near.reshape(CHUNKS, row_total, 2, blocks, CHUNK, width)
        near = near.transpose(2, 3, 0, 4, 1, 5).reshape(2, height, tile_width)
        odd_cell = (jnp.arange(height)[:, None] + jnp.arange(tile_width)[None, :]) % 2
        cell_sign = (1 - 2 * odd_cell).astype(jnp.float32)
        return encode(near[0], near[1], peak_sq, cell_sign)
    tile_shape = jax.ShapeDtypeStruct((height, tile_width), jnp.float32)
    tile = pltpu.VMEM((blocks, INNER, tile_width), jnp.float32)
    return pl.pallas_call(
        partial(encode_kernel, row_total),
        in_specs=[whole(pltpu.SMEM)] * 3 + [whole()] * (CHUNKS * row_total),
        out_specs=[anywhere] * 2,
        out_shape=[tile_shape, tile_shape],
        scratch_shapes=[tile, tile, pltpu.SemaphoreType.DMA((2 * blocks,))],
        compiler_params=params(16),
        name="encode",
    )(place_row, *peaks, *near[0], *near[1])


def solution(mesh):
    in_specs = (P("row", "col"), P("row", "col"))
    out_specs = (P("row", "col"), P("row", "col"))
    return jax.shard_map(body, mesh=mesh, in_specs=in_specs, out_specs=out_specs, check_vma=False)
```

```python
from functools import partial
import math

import jax
import jax.numpy as jnp
import ml_dtypes
import numpy as np
from jax import lax
from jax.experimental import pallas as pl
from jax.experimental.pallas import tpu as pltpu
from jax.sharding import PartitionSpec as P

N = 4096
PAD = 2 * N
wavelength = 5.2e-07
distance = 0.2
INNER = 256
SLABS = N // INNER
RES = PAD // INNER
HALF = 40
CHUNKS = 2
CHUNK = INNER // CHUNKS
FRONT = ((0, 128), (128, 128))
SPARE = 8


def optics(padded_side):
    pitch = 2e-06 * math.sqrt(8192.0 / padded_side)
    extent = padded_side * pitch
    ratio_sq = (wavelength / extent) ** 2
    band_limit = extent / (wavelength * math.sqrt((2.0 * distance / extent) ** 2 + 1.0))
    return (ratio_sq, band_limit)


RATIO_SQ, LIMIT = optics(PAD)
assert RES * HALF - RES // 2 + RES > LIMIT and RES * HALF + RES // 2 > LIMIT


def residue(u):
    return u if u < RES // 2 else u - RES


def split16(table):
    table = np.asarray(table, np.float64)
    high = table.astype(np.float32).astype(ml_dtypes.bfloat16)
    low = (table - high.astype(np.float64)).astype(np.float32).astype(ml_dtypes.bfloat16)
    return high, low


def row_order(groups, tail):
    rows = []
    for group in range(groups):
        size = 4 if tail and group == groups - 1 else 8
        for part in range(2):
            for s in range(size):
                rows.append((part, group * 8 + s - HALF))
    return rows


def column_tables(groups, tail):
    q = np.arange(INNER)
    rows = row_order(groups, tail)
    forward = np.zeros((len(rows), 2, INNER))
    inverse = np.zeros((2, INNER, len(rows)))
    for at, (part, k1) in enumerate(rows):
        if abs(k1) > HALF:
            continue
        angle = 2.0 * np.pi * ((k1 * q) % INNER) / INNER
        c, s = np.cos(angle), np.sin(angle)
        forward[at] = (c, s) if part == 0 else (-s, c)
        inverse[:, :, at] = (c, s) if part == 0 else (-s, c)
    tables = []
    for start, size in FRONT:
        part = forward[:, :, start : start + size].reshape(-1, 2, size // 8, 8)
        part = part.transpose(0, 2, 1, 3).reshape(-1, 2 * size)
        tables.append(np.concatenate(split16(part), axis=0))
    inverse = inverse.reshape(2, CHUNKS, CHUNK, -1).transpose(1, 0, 2, 3)
    high, low = split16(inverse.reshape(CHUNKS, 2 * CHUNK, len(rows)))
    inverse = np.concatenate([high, high, low], axis=2)
    inverse = np.pad(inverse, ((0, 0), (0, 0), (0, -3 * len(rows) % 16)))
    return tables, inverse


def line_tables():
    q = np.arange(INNER)
    forward = np.zeros((2 * INNER, 256))
    inverse = np.zeros((256, 2 * INNER))
    for lane in range(2 * HALF + 1):
        angle = 2.0 * np.pi * (((lane - HALF) * q) % INNER) / INNER
        c, s = np.cos(angle), np.sin(angle)
        forward[:INNER, lane], forward[INNER:, lane] = c, s
        forward[:INNER, 128 + lane], forward[INNER:, 128 + lane] = -s, c
        inverse[lane, :INNER], inverse[lane, INNER:] = c, s
        inverse[128 + lane, :INNER], inverse[128 + lane, INNER:] = -s, c
    return split16(forward) + split16(inverse)


def twist_table():
    q = np.arange(INNER) + N // 2
    k0 = np.arange(RES // 2 + 1)
    angle = 2.0 * np.pi * ((k0[:, None] * q[None, :]) % PAD) / PAD
    return np.cos(angle).astype(np.float32), (-np.sin(angle)).astype(np.float32)


def turn(value, num, den):
    re, im = value
    num = num % den
    eighth = 8 * num
    if num == 0:
        return re, im
    if 2 * num == den:
        return -re, -im
    if 4 * num == den:
        return -im, re
    if 4 * num == 3 * den:
        return im, -re
    if eighth % den == 0:
        root = np.float32(math.sqrt(0.5))
        kind = eighth // den
        if kind == 1:
            return (re - im) * root, (re + im) * root
        if kind == 3:
            return (re + im) * (-root), (re - im) * root
        if kind == 5:
            return (im - re) * root, (re + im) * (-root)
        return (re + im) * root, (im - re) * root
    c = np.float32(math.cos(2.0 * math.pi * num / den))
    s = np.float32(math.sin(2.0 * math.pi * num / den))
    return re * c - im * s, re * s + im * c


def small_dft(get, ids, sign):
    count = len(ids)
    if count == 1:
        return [get(ids[0])]
    even = small_dft(get, ids[0::2], sign)
    odd = small_dft(get, ids[1::2], sign)
    half = count // 2
    first, second = [], []
    for j in range(half):
        re, im = even[j]
        t_re, t_im = turn(odd[j], sign * j, count)
        first.append((re + t_re, im + t_im))
        second.append((re - t_re, im - t_im))
    return first + second


def forward_slabs(get, put):
    ids = list(range(SLABS))
    for v, value in enumerate(small_dft(get, ids, -1)):
        put(2 * v, value)
    for v, value in enumerate(small_dft(lambda n: turn(get(n), -n, RES), ids, -1)):
        put(2 * v + 1, value)


def inverse_slabs(get, put):
    even = small_dft(get, list(range(0, RES, 2)), 1)
    odd = small_dft(get, list(range(1, RES, 2)), 1)
    for n in range(SLABS):
        t_re, t_im = turn(odd[n], n, RES)
        put(n, (even[n][0] + t_re, even[n][1] + t_im))


def twisted(value, u, sign, read):
    re, im = value
    k0 = residue(u)
    if k0 == 0:
        return value
    c, s = read(abs(k0))
    if (k0 < 0) == (sign > 0):
        return re * c + im * s, im * c - re * s
    return re * c - im * s, re * s + im * c


def high_low(value):
    high = value.astype(jnp.bfloat16)
    low = (value - high.astype(jnp.float32)).astype(jnp.bfloat16)
    return high, low


def dot16(left, right):
    return jnp.dot(left, right, preferred_element_type=jnp.float32)


def three_left(stacked, count, high, low):
    both = dot16(stacked[...], high)
    return both[:count] + both[count:] + dot16(stacked[:count], low)


def three_right(stacked, count, high, low):
    both = dot16(stacked, high)
    return both[:count] + both[count:] + dot16(stacked[:count], low)


def column_twist(twist, q0):
    seen = {}

    def read(k):
        if k not in seen:
            rows = pl.ds(q0, 8)
            seen[k] = twist[rows, k : k + 1], twist[rows, 64 + k : 65 + k]
        return seen[k]

    return read


def column_forward_kernel(count, place, twist, matrix, *refs):
    pieces, refs = refs[:count], refs[count:]
    before, (out, high, low) = refs[:-3], refs[-3:]
    width = pieces[0].shape[-1]
    per_source, size = pieces[0].shape[1:3]
    many = high.shape[-1] // width
    products = RES // many
    rows_out = out.shape[1]

    for here in range(count):

        @pl.when(place[0] == here)
        def _():
            @pl.loop(0, size // 8)
            def _(t):
                q0 = pl.multiple_of(t * 8, 8)
                read = column_twist(twist, q0)

                def get(n):
                    source, block = divmod(n, per_source)
                    piece = pieces[source ^ here]
                    rows = pl.ds(q0, 8)
                    return piece[0, block, rows, :], piece[1, block, rows, :]

                def put(u, value):
                    item = jnp.concatenate(twisted(value, u, 1, read), axis=0)
                    rows = pl.ds(pl.multiple_of(t * 16, 16), 16)
                    at = (u // many, rows, pl.ds((u % many) * width, width))
                    high[at], low[at] = high_low(item)

                forward_slabs(get, put)

    @pl.loop(0, products)
    def _(p):
        done = three_left(matrix, rows_out, high[p], low[p])
        for part in range(many):
            item = done[:, part * width : (part + 1) * width]
            at = p * many + part
            out[at] = before[0][at] + item if before else item


def column_inverse_kernel(count, place, source, twist, matrix, *refs):
    pieces, (peak_sq, near, lines, deep, back, top, sems, out_sems) = refs[:-8], refs[-8:]
    width = lines.shape[-1]
    rows_in = lines.shape[1]
    per_dest = near.shape[3]
    many = deep.shape[-1] // width
    products = RES // many

    def copy_in(p):
        part = pl.ds(p * many, many)
        return pltpu.make_async_copy(source.at[part], lines.at[part], sems.at[p])

    def copies_out(chunk, part):
        parts = 1 if chunk + 1 < CHUNKS else 2
        if part >= parts:
            return []
        rows = pl.ds(part * CHUNK // parts, CHUNK // parts)
        copies = []
        for j in range(count):
            piece = pieces[chunk * count + j].at[pl.ds(0, 2 * per_dest * CHUNK)]
            there = piece.reshape(2, per_dest, CHUNK, width).at[:, :, rows]
            here = near.at[chunk, place[0] ^ j, :, :, rows]
            copies.append(pltpu.make_async_copy(here, there, out_sems.at[(chunk * 2 + part) * count + j]))
        return copies

    def prepare(p):
        copy_in(p).wait()
        blocks = [lines[p * many + part] for part in range(many)]
        joined = jnp.concatenate(blocks, axis=1) if many > 1 else blocks[0]
        high = joined.astype(jnp.bfloat16).astype(jnp.float32)
        parts = [high, joined - high, high]
        if deep.shape[1] > 3 * rows_in:
            parts.append(jnp.zeros((deep.shape[1] - 3 * rows_in, many * width), jnp.float32))
        deep[p] = jnp.concatenate(parts, axis=0).astype(jnp.bfloat16)

    def product(p, chunk):
        done = dot16(matrix[chunk], deep[p])
        for part in range(many):
            back[chunk, p * many + part] = done[:, part * width : (part + 1) * width]

    def butterflies(t, chunk):
        q0 = pl.multiple_of(t * 8, 8)
        largest = []
        read = column_twist(twist, pl.multiple_of(chunk * CHUNK + q0, 8))

        def get(u):
            re = back[chunk, u, pl.ds(q0, 8), :]
            im = back[chunk, u, pl.ds(CHUNK + q0, 8), :]
            return twisted((re, im), u, -1, read)

        def put(n, value):
            dest, block = divmod(n, per_dest)
            rows = pl.ds(q0, 8)
            near[chunk, dest, 0, block, rows, :], near[chunk, dest, 1, block, rows, :] = value
            largest.append(value[0] * value[0] + value[1] * value[1])

        inverse_slabs(get, put)
        while len(largest) > 1:
            largest = [jnp.maximum(a, b) for a, b in zip(largest[0::2], largest[1::2])]
        top[...] = jnp.maximum(top[...], largest[0])

    for p in range(products):
        copy_in(p).start()
    top[...] = jnp.zeros_like(top)

    @pl.loop(0, products)
    def _(p):
        prepare(p)
        product(p, 0)

    tiles = CHUNK // 16
    steps = min(tiles, products // 2)
    for chunk in range(CHUNKS):
        for part in range(2):

            @pl.loop(part * steps, (part + 1) * steps)
            def _(t):
                for item in range(tiles // steps):
                    butterflies(t * (tiles // steps) + item, chunk)
                if chunk + 1 < CHUNKS:
                    for item in range(products // 2 // steps):
                        product(t * (products // 2 // steps) + item, chunk + 1)

            for copy in copies_out(chunk, part if chunk + 1 == CHUNKS else 1 - part):
                copy.start()
    peak_sq[0] = jnp.max(top[...])
    for chunk in range(CHUNKS):
        for part in range(2):
            for copy in copies_out(chunk, part):
                copy.wait()


def line_kernel(
    order, own, tail, lines, gain, twist, fwd_high, fwd_low, inv_high, inv_low, out, *scratch
):
    half = RES * 8
    at_end = pl.program_id(0) == pl.num_programs(0) - 1

    def line_twist(side):
        def read(k):
            lanes = pl.ds(side * 128, 128)
            return twist[0, k, :, lanes], twist[1, k, :, lanes]

        return read

    def forward(group, stacked, sides=(0, 1)):
        for side in sides:
            waiting = {}

            def get(m):
                block = order[2 * m + side]
                at = group * 16
                return lines[block, at : at + 8, :], lines[block, at + 8 : at + 16, :]

            def put(u, value):
                waiting[u] = twisted(value, u, 1, line_twist(side))
                v = (u + RES // 2) % RES
                if v in waiting:
                    first = min(u, v)
                    rows = pl.ds(first * 16, 16)
                    rows_low = pl.ds(half + first * 16, 16)
                    for part in range(2):
                        item = jnp.concatenate(
                            [waiting[first][part], waiting[first + RES // 2][part]], axis=0
                        )
                        at = pl.ds(part * INNER + side * 128, 128)
                        stacked[rows, at], stacked[rows_low, at] = high_low(item)

            forward_slabs(get, put)

    def filtered(group, stacked):
        spec = three_right(stacked[...], half, fwd_high[...], fwd_low[...])
        spec_re, spec_im = spec[:, :128], spec[:, 128:]
        g_re, g_im = gain[0, group], gain[1, group]
        mixed = jnp.concatenate(
            [spec_re * g_re - spec_im * g_im, spec_re * g_im + spec_im * g_re], axis=1
        )
        return jnp.concatenate(high_low(mixed), axis=0)

    def unfold(mixed, back):
        back[...] = three_right(mixed, half, inv_high[...], inv_low[...])

    def inverse(group, back, sides=(0, 1)):
        for side in sides:

            def get(u):
                rows = pl.ds((u % (RES // 2)) * 16 + (u // (RES // 2)) * 8, 8)
                re = back[rows, pl.ds(side * 128, 128)]
                im = back[rows, pl.ds(INNER + side * 128, 128)]
                return twisted((re, im), u, -1, line_twist(side))

            def put(m, value):
                block = order[2 * m + side]
                at = group * 16
                out[block, at : at + 8, :], out[block, at + 8 : at + 16, :] = value

            inverse_slabs(get, put)

    if tail:

        @pl.when(at_end)
        def _():
            for block in range(N // 128):
                lines[block, 8:12, :] = lines[block, 4:8, :]

    groups = len(scratch) // 2

    stacked, back = scratch[:groups], scratch[groups:]

    def run(count):
        forward(0, stacked[0])
        for group in range(count):
            mixed = filtered(group, stacked[group])
            if group + 1 < count:
                forward(group + 1, stacked[group + 1], (0,))
            if group > 0:
                inverse(group - 1, back[group - 1], (0,))
            unfold(mixed, back[group])
            if group + 1 < count:
                forward(group + 1, stacked[group + 1], (1,))
            if group > 0:
                inverse(group - 1, back[group - 1], (1,))
        inverse(count - 1, back[count - 1])

    rest = own % groups
    if rest:
        pl.when(jnp.logical_not(at_end))(lambda: run(groups))
        pl.when(at_end)(lambda: run(rest))
    else:
        run(groups)

    if tail:

        @pl.when(at_end)
        def _():
            for block in range(N // 128):
                out[block, 4:8, :] = out[block, 8:12, :]


def gain_kernel(place, gain):
    k0 = place[0]
    group = place[1] + pl.program_id(0)
    down = lax.broadcasted_iota(jnp.int32, (8, 128), 0)
    across = lax.broadcasted_iota(jnp.int32, (8, 128), 1)
    row = (k0 + RES * (group * 8 + down - HALF)).astype(jnp.float32)
    row_sq = row * row
    row_in = jnp.abs(row) < LIMIT
    for u in range(RES):
        col = (residue(u) + RES * (across - HALF)).astype(jnp.float32)
        square = row_sq + col * col
        scaled = RATIO_SQ * square
        phase = -2.0 * math.pi * distance / wavelength * scaled / (1.0 + jnp.sqrt(1.0 - scaled))
        total = jnp.where(
            row_in & (jnp.abs(col) < LIMIT), jnp.exp(square * (-2.0 / (LIMIT * LIMIT))), 0.0
        )
        quarter = jnp.floor(phase * (2.0 / math.pi) + 0.5)
        left = phase - quarter * 1.5703125
        left = left - quarter * 4.837512969970703125e-4
        left = left - quarter * 7.549789954891882e-8
        sq = left * left
        sine = ((-1.9515295891e-4 * sq + 8.3321608736e-3) * sq - 1.6666654611e-1) * sq * left + left
        cosine = (
            (2.443315711809948e-5 * sq - 1.388731625493765e-3) * sq + 4.166664568298827e-2
        ) * sq * sq - 0.5 * sq + 1.0
        which = quarter.astype(jnp.int32) & 3
        swap = (which & 1) == 1
        cos_part = jnp.where(swap, sine, cosine)
        sin_part = jnp.where(swap, cosine, sine)
        cos_part = jnp.where((which == 1) | (which == 2), -cos_part, cos_part)
        sin_part = jnp.where(which >= 2, -sin_part, sin_part)
        at = (u % (RES // 2)) * 16 + (u // (RES // 2)) * 8
        gain[0, 0, at : at + 8, :] = total * cos_part
        gain[1, 0, at : at + 8, :] = total * sin_part


def encode(near_real, near_imag, peak_sq, cell_sign):
    square = near_real * near_real + near_imag * near_imag
    root = lax.rsqrt(jnp.maximum(square, 1.2e-38))
    top = lax.rsqrt(peak_sq)
    amp_level = (square * root) * (0.8 * top)
    unit = jnp.minimum(root, 20.0 * top)
    rest = 1.0 - amp_level * amp_level
    level = unit * amp_level
    lift = (rest * lax.rsqrt(rest)) * (unit * cell_sign)
    return (near_real * level + near_imag * lift, near_imag * level - near_real * lift)


def stamp_kernel(others, peak_one, peak_two, *refs):
    refs = refs[others:]
    stay, pieces, refs = refs[:CHUNKS], refs[CHUNKS : CHUNKS + others], refs[CHUNKS + others :]
    fetched, (tile, sems) = refs[:CHUNKS], refs[CHUNKS:]
    tile[...] = jnp.full(tile.shape, jnp.maximum(peak_one[0], peak_two[0]), jnp.float32)
    copies = []
    for j, piece in enumerate(pieces):
        rows = pl.ds(piece.shape[0] - SPARE, SPARE)
        copies.append(pltpu.make_async_copy(tile, piece.at[rows], sems.at[j]))
    for chunk in range(CHUNKS):
        copies.append(pltpu.make_async_copy(stay[chunk], fetched[chunk], sems.at[others + chunk]))
    for copy in copies:
        copy.start()
    for copy in copies:
        copy.wait()


def encode_kernel(count, place, peak_one, peak_two, *refs):
    pieces, refs = refs[: CHUNKS * count], refs[CHUNKS * count :]
    slm_real, slm_imag, tile_real, tile_imag, sems = refs
    blocks, width = tile_real.shape[0], pieces[0].shape[-1]
    top = jnp.full((1, width), jnp.maximum(peak_one[0], peak_two[0]), jnp.float32)
    for piece in pieces[(CHUNKS - 1) * count + 1 :]:
        top = jnp.maximum(top, piece[pl.ds(piece.shape[0] - SPARE, 1), :])
    cell = lax.broadcasted_iota(jnp.int32, (CHUNK, width), 0)
    cell = cell + lax.broadcasted_iota(jnp.int32, (CHUNK, width), 1)
    cell_sign = (1 - 2 * (cell & 1)).astype(jnp.float32)

    def copies_out(block):
        rows = pl.ds(block * INNER, INNER)
        return [
            pltpu.make_async_copy(tile.at[block], slm.at[rows], sems.at[2 * block + part])
            for part, (tile, slm) in enumerate(((tile_real, slm_real), (tile_imag, slm_imag)))
        ]

    @pl.loop(0, blocks)
    def _(block):
        for at in range(CHUNKS * count):
            chunk, j = divmod(at, count)
            piece = pieces[at]
            lanes = pl.ds(pl.multiple_of((place[0] ^ j) * width, width), width)
            rows = pl.ds(chunk * CHUNK, CHUNK)
            real = pl.ds(pl.multiple_of(block * CHUNK, CHUNK), CHUNK)
            imag = pl.ds(pl.multiple_of((blocks + block) * CHUNK, CHUNK), CHUNK)
            tile_real[block, rows, lanes], tile_imag[block, rows, lanes] = encode(
                piece[real, :], piece[imag, :], top, cell_sign
            )
        for copy in copies_out(block):
            copy.start()

    for block in range(blocks):
        for copy in copies_out(block):
            copy.wait()


def pack_kernel(place, field_real, field_imag, *refs):
    pieces, sems = refs[:-1], refs[-1]
    width = pieces[0].shape[-1]
    copies = []
    for j in list(range(1, len(pieces))) + [0]:
        lanes = pl.ds(pl.multiple_of((place[0] ^ j) * width, width), width)
        for part, field in enumerate((field_real, field_imag)):
            copies.append(
                pltpu.make_async_copy(
                    field.at[:, :, lanes], pieces[j].at[part], sems.at[2 * j + part]
                )
            )
    for copy in copies:
        copy.start()
    for copy in copies:
        copy.wait()


def exchange(pieces, axis):
    total = len(pieces)
    return [pieces[0]] + [
        lax.ppermute(pieces[j], axis, [(i, i ^ j) for i in range(total)]) for j in range(1, total)
    ]


def params(mebibytes):
    return pltpu.CompilerParams(vmem_limit_bytes=mebibytes << 20)


def cost(megabytes):
    return pl.CostEstimate(flops=0, bytes_accessed=megabytes << 20, transcendentals=0)


def whole(memory=pltpu.VMEM):
    return pl.BlockSpec(memory_space=memory)


def body(field_real, field_imag):
    row_total, col_total = lax.axis_size("row"), lax.axis_size("col")
    devices = row_total * col_total
    device = lax.axis_index("row") * col_total + lax.axis_index("col")
    height, tile_width = field_real.shape
    width = tile_width // row_total
    parts = max(1, devices // RES)
    groups = -(-(2 * HALF + 1) // (8 * parts)) * parts
    own = groups // parts
    tail = parts == 1
    total_rows = groups * 16 - (8 if tail else 0)
    own_rows = total_rows // parts
    many = 4 if width == 128 else 1

    fwd_col, inv_col = column_tables(groups, tail)
    line_fh, line_fl, line_ih, line_il = line_tables()
    twist = np.stack(twist_table())
    twist_line = np.ascontiguousarray(np.broadcast_to(twist[:, :, None], twist.shape[:2] + (8, INNER)))
    twist_col = np.pad(twist, ((0, 0), (0, 64 - twist.shape[1]), (0, 0)))
    twist_col = twist_col.reshape(128, INNER).T.copy()

    u = device // parts
    k0 = jnp.where(u >= RES // 2, u - RES, u)
    place = jnp.stack([k0, (device % parts) * own]).astype(jnp.int32)
    gain = pl.pallas_call(
        gain_kernel,
        grid=(own,),
        in_specs=[whole(pltpu.SMEM)],
        out_specs=pl.BlockSpec((2, 1, RES * 8, 128), lambda g: (0, g, 0, 0)),
        out_shape=jax.ShapeDtypeStruct((2, own, RES * 8, 128), jnp.float32),
        compiler_params=params(50),
        name="gain",
    )(place)

    place_row = lax.axis_index("row").reshape(1).astype(jnp.int32)
    blocks = height // INNER
    anywhere = whole(pl.ANY)
    if width != 128:
        packed = jnp.stack([field_real, field_imag]).reshape(2, blocks, INNER, row_total, width)
        packed = jnp.take(packed, jnp.arange(row_total) ^ place_row[0], axis=3)
    lines = []
    for chunk, (start, size) in enumerate(FRONT):
        piece_shape = jax.ShapeDtypeStruct((2, blocks, size, width), jnp.float32)
        at = start // size
        if width == 128:
            pieces = pl.pallas_call(
                pack_kernel,
                grid=(1,),
                in_specs=[whole(pltpu.SMEM)]
                + [pl.BlockSpec((blocks, size, tile_width), lambda i: (0, at, 0))] * 2,
                out_specs=[anywhere] * row_total,
                out_shape=[piece_shape] * row_total,
                scratch_shapes=[pltpu.SemaphoreType.DMA((2 * row_total,))],
                compiler_params=params(56),
                cost_estimate=cost(4),
                name="pack",
            )(
                place_row,
                field_real.reshape(blocks, INNER, tile_width),
                field_imag.reshape(blocks, INNER, tile_width),
            )
        else:
            pieces = [packed[:, :, start : start + size, j] for j in range(row_total)]
        pieces = exchange(pieces, "row")
        if chunk == 0:
            pieces, gain = lax.optimization_barrier((pieces, gain))
        rows = slice(start, start + size)
        slab = pltpu.VMEM((RES // many, 2 * size, many * width), jnp.bfloat16)
        lines = [
            pl.pallas_call(
                partial(column_forward_kernel, row_total),
                in_specs=[whole(pltpu.SMEM)] + [whole()] * (2 + row_total + len(lines)),
                out_specs=whole(),
                out_shape=jax.ShapeDtypeStruct((RES, total_rows, width), jnp.float32),
                scratch_shapes=[slab, slab],
                compiler_params=params(20),
                cost_estimate=cost(20),
                name="column_forward",
            )(place_row, twist_col[rows], fwd_col[chunk], *pieces, *lines)
        ]
    (lines,) = lines

    lines = lines.reshape(devices, own_rows, width)
    lines = lax.all_to_all(lines, ("row", "col"), split_axis=0, concat_axis=0, tiled=True)
    if width == 128:
        order = tuple((b % row_total) * col_total + b // row_total for b in range(N // 128))
    else:
        order = tuple(range(N // 128))
        lines = lines.reshape(row_total, col_total, own_rows, width).transpose(2, 1, 0, 3)
        lines = lines.reshape(own_rows, N // 128, 128).transpose(1, 0, 2)

    at_once = 2
    line_grain = pl.BlockSpec((N // 128, 16 * at_once, 128), lambda i: (0, i, 0))
    gain_grain = pl.BlockSpec((2, at_once, RES * 8, 128), lambda i: (0, i, 0, 0))
    lines = pl.pallas_call(
        partial(line_kernel, order, own, tail),
        grid=(-(-own // at_once),),
        in_specs=[line_grain, gain_grain] + [whole()] * 5,
        out_specs=line_grain,
        out_shape=jax.ShapeDtypeStruct((N // 128, own_rows, 128), jnp.float32),
        scratch_shapes=[pltpu.VMEM((2 * RES * 8, 2 * INNER), jnp.bfloat16)] * at_once
        + [pltpu.VMEM((RES * 8, 2 * INNER), jnp.float32)] * at_once,
        compiler_params=params(44),
        name="line",
    )(lines, gain, twist_line, line_fh, line_fl, line_ih, line_il)

    if width != 128:
        lines = lines.transpose(1, 0, 2).reshape(own_rows, col_total, row_total, width)
        lines = lines.transpose(2, 1, 0, 3).reshape(devices, own_rows, width)
    lines = lax.all_to_all(lines, ("row", "col"), split_axis=0, concat_axis=0, tiled=True)
    lines = lines.reshape(RES, total_rows, width)

    piece_shapes = [
        jax.ShapeDtypeStruct((2 * blocks * CHUNK + spare, width), jnp.float32)
        for spare in (0,) * (CHUNKS - 1) + (SPARE,)
    ]
    *near, peak_sq = pl.pallas_call(
        partial(column_inverse_kernel, row_total),
        in_specs=[whole(pltpu.SMEM), anywhere, whole(), whole()],
        out_specs=[anywhere] * (CHUNKS * row_total) + [whole(pltpu.SMEM)],
        out_shape=[shape for shape in piece_shapes for _ in range(row_total)]
        + [jax.ShapeDtypeStruct((1,), jnp.float32)],
        scratch_shapes=[
            pltpu.VMEM((CHUNKS, row_total, 2, blocks, CHUNK, width), jnp.float32),
            pltpu.VMEM((RES, total_rows, width), jnp.float32),
            pltpu.VMEM((RES // many, inv_col.shape[2], many * width), jnp.bfloat16),
            pltpu.VMEM((CHUNKS, RES, 2 * CHUNK, width), jnp.float32),
            pltpu.VMEM((8, width), jnp.float32),
            pltpu.SemaphoreType.DMA((RES // many,)),
            pltpu.SemaphoreType.DMA((2 * CHUNKS * row_total,)),
        ],
        compiler_params=params(36),
        name="column_inverse",
    )(place_row, lines, twist_col, inv_col)
    near = [near[:row_total], near[row_total:]]
    piece_shape = piece_shapes[-1]
    near[0] = exchange(near[0], "row")
    shift = 1
    while shift < col_total:
        partner = [(i, i ^ shift) for i in range(col_total)]
        peaks = [peak_sq, lax.ppermute(peak_sq, "col", partner)]
        shift *= 2
        if shift < col_total:
            peak_sq = jnp.maximum(*peaks)
    others = row_total - 1
    stamped = pl.pallas_call(
        partial(stamp_kernel, others),
        in_specs=[whole(pltpu.SMEM)] * 2 + [anywhere] * (others + CHUNKS),
        out_specs=[anywhere] * others + [whole()] * CHUNKS,
        out_shape=[piece_shape] * others + piece_shapes,
        scratch_shapes=[
            pltpu.VMEM((SPARE, width), jnp.float32),
            pltpu.SemaphoreType.DMA((others + CHUNKS,)),
        ],
        input_output_aliases={2 + j: j for j in range(others)},
        compiler_params=params(16),
        name="stamp",
    )(*peaks, *near[1][1:], near[0][0], near[1][0])
    near[1][1:] = stamped[:others]
    near[0][0], near[1][0] = stamped[others:]
    near[0][1:], near[1][1] = lax.optimization_barrier((near[0][1:], near[1][1]))
    near[1] = exchange(near[1], "row")
    if width != 128:
        peak_sq = jnp.maximum(*peaks)[0]
        for piece in near[1][1:]:
            peak_sq = jnp.maximum(peak_sq, piece[-1, 0])
        near = jnp.stack([jnp.stack([piece[: 2 * blocks * CHUNK] for piece in pieces]) for pieces in near])
        near = jnp.take(near, jnp.arange(row_total) ^ place_row[0], axis=1)
        near = near.reshape(CHUNKS, row_total, 2, blocks, CHUNK, width)
        near = near.transpose(2, 3, 0, 4, 1, 5).reshape(2, height, tile_width)
        odd_cell = (jnp.arange(height)[:, None] + jnp.arange(tile_width)[None, :]) % 2
        cell_sign = (1 - 2 * odd_cell).astype(jnp.float32)
        return encode(near[0], near[1], peak_sq, cell_sign)
    tile_shape = jax.ShapeDtypeStruct((height, tile_width), jnp.float32)
    tile = pltpu.VMEM((blocks, INNER, tile_width), jnp.float32)
    return pl.pallas_call(
        partial(encode_kernel, row_total),
        in_specs=[whole(pltpu.SMEM)] * 3 + [whole()] * (CHUNKS * row_total),
        out_specs=[anywhere] * 2,
        out_shape=[tile_shape, tile_shape],
        scratch_shapes=[tile, tile, pltpu.SemaphoreType.DMA((2 * blocks,))],
        compiler_params=params(16),
        name="encode",
    )(place_row, *peaks, *near[0], *near[1])


def solution(mesh):
    in_specs = (P("row", "col"), P("row", "col"))
    out_specs = (P("row", "col"), P("row", "col"))
    return jax.shard_map(body, mesh=mesh, in_specs=in_specs, out_specs=out_specs, check_vma=False)
```

```python
from functools import partial
import math

import jax
import jax.numpy as jnp
import ml_dtypes
import numpy as np
from jax import lax
from jax.experimental import pallas as pl
from jax.experimental.pallas import tpu as pltpu
from jax.sharding import PartitionSpec as P

N = 4096
PAD = 2 * N
wavelength = 5.2e-07
distance = 0.2
INNER = 256
SLABS = N // INNER
RES = PAD // INNER
HALF = 40
CHUNKS = 2
CHUNK = INNER // CHUNKS
FRONT = ((0, 128), (128, 128))
BACK = (192, 64)
SPARE = 8


def optics(padded_side):
    pitch = 2e-06 * math.sqrt(8192.0 / padded_side)
    extent = padded_side * pitch
    ratio_sq = (wavelength / extent) ** 2
    band_limit = extent / (wavelength * math.sqrt((2.0 * distance / extent) ** 2 + 1.0))
    return (ratio_sq, band_limit)


RATIO_SQ, LIMIT = optics(PAD)
assert RES * HALF - RES // 2 + RES > LIMIT and RES * HALF + RES // 2 > LIMIT


def residue(u):
    return u if u < RES // 2 else u - RES


def split16(table):
    table = np.asarray(table, np.float64)
    high = table.astype(np.float32).astype(ml_dtypes.bfloat16)
    low = (table - high.astype(np.float64)).astype(np.float32).astype(ml_dtypes.bfloat16)
    return high, low


def row_order(groups, tail):
    rows = []
    for group in range(groups):
        size = 4 if tail and group == groups - 1 else 8
        for part in range(2):
            for s in range(size):
                rows.append((part, group * 8 + s - HALF))
    return rows


def column_tables(groups, tail):
    q = np.arange(INNER)
    rows = row_order(groups, tail)
    forward = np.zeros((len(rows), 2, INNER))
    inverse = np.zeros((2, INNER, len(rows)))
    for at, (part, k1) in enumerate(rows):
        if abs(k1) > HALF:
            continue
        angle = 2.0 * np.pi * ((k1 * q) % INNER) / INNER
        c, s = np.cos(angle), np.sin(angle)
        forward[at] = (c, s) if part == 0 else (-s, c)
        inverse[:, :, at] = (c, s) if part == 0 else (-s, c)
    tables = []
    for start, size in FRONT:
        part = forward[:, :, start : start + size].reshape(-1, 2, size // 8, 8)
        part = part.transpose(0, 2, 1, 3).reshape(-1, 2 * size)
        tables.append(np.concatenate(split16(part), axis=0))
    inverse = inverse.reshape(2, CHUNKS, CHUNK, -1).transpose(1, 0, 2, 3)
    high, low = split16(inverse.reshape(CHUNKS, 2 * CHUNK, len(rows)))
    inverse = np.concatenate([high, high, low], axis=2)
    inverse = np.pad(inverse, ((0, 0), (0, 0), (0, -3 * len(rows) % 16)))
    return tables, inverse


def line_tables():
    q = np.arange(INNER)
    forward = np.zeros((2 * INNER, 256))
    inverse = np.zeros((256, 2 * INNER))
    for lane in range(2 * HALF + 1):
        angle = 2.0 * np.pi * (((lane - HALF) * q) % INNER) / INNER
        c, s = np.cos(angle), np.sin(angle)
        forward[:INNER, lane], forward[INNER:, lane] = c, s
        forward[:INNER, 128 + lane], forward[INNER:, 128 + lane] = -s, c
        inverse[lane, :INNER], inverse[lane, INNER:] = c, s
        inverse[128 + lane, :INNER], inverse[128 + lane, INNER:] = -s, c
    return split16(forward) + split16(inverse)


def twist_table():
    q = np.arange(INNER) + N // 2
    k0 = np.arange(RES // 2 + 1)
    angle = 2.0 * np.pi * ((k0[:, None] * q[None, :]) % PAD) / PAD
    return np.cos(angle).astype(np.float32), (-np.sin(angle)).astype(np.float32)


def turn(value, num, den):
    re, im = value
    num = num % den
    eighth = 8 * num
    if num == 0:
        return re, im
    if 2 * num == den:
        return -re, -im
    if 4 * num == den:
        return -im, re
    if 4 * num == 3 * den:
        return im, -re
    if eighth % den == 0:
        root = np.float32(math.sqrt(0.5))
        kind = eighth // den
        if kind == 1:
            return (re - im) * root, (re + im) * root
        if kind == 3:
            return (re + im) * (-root), (re - im) * root
        if kind == 5:
            return (im - re) * root, (re + im) * (-root)
        return (re + im) * root, (im - re) * root
    c = np.float32(math.cos(2.0 * math.pi * num / den))
    s = np.float32(math.sin(2.0 * math.pi * num / den))
    return re * c - im * s, re * s + im * c


def small_dft(get, ids, sign):
    count = len(ids)
    if count == 1:
        return [get(ids[0])]
    even = small_dft(get, ids[0::2], sign)
    odd = small_dft(get, ids[1::2], sign)
    half = count // 2
    first, second = [], []
    for j in range(half):
        re, im = even[j]
        t_re, t_im = turn(odd[j], sign * j, count)
        first.append((re + t_re, im + t_im))
        second.append((re - t_re, im - t_im))
    return first + second


def forward_slabs(get, put):
    ids = list(range(SLABS))
    for v, value in enumerate(small_dft(get, ids, -1)):
        put(2 * v, value)
    for v, value in enumerate(small_dft(lambda n: turn(get(n), -n, RES), ids, -1)):
        put(2 * v + 1, value)


def inverse_slabs(get, put):
    even = small_dft(get, list(range(0, RES, 2)), 1)
    odd = small_dft(get, list(range(1, RES, 2)), 1)
    for n in range(SLABS):
        t_re, t_im = turn(odd[n], n, RES)
        put(n, (even[n][0] + t_re, even[n][1] + t_im))


def twisted(value, u, sign, read):
    re, im = value
    k0 = residue(u)
    if k0 == 0:
        return value
    c, s = read(abs(k0))
    if (k0 < 0) == (sign > 0):
        return re * c + im * s, im * c - re * s
    return re * c - im * s, re * s + im * c


def high_low(value):
    high = value.astype(jnp.bfloat16)
    low = (value - high.astype(jnp.float32)).astype(jnp.bfloat16)
    return high, low


def dot16(left, right):
    return jnp.dot(left, right, preferred_element_type=jnp.float32)


def three_left(stacked, count, high, low):
    both = dot16(stacked[...], high)
    return both[:count] + both[count:] + dot16(stacked[:count], low)


def three_right(stacked, count, high, low):
    both = dot16(stacked, high)
    return both[:count] + both[count:] + dot16(stacked[:count], low)


def column_twist(twist, q0):
    seen = {}

    def read(k):
        if k not in seen:
            rows = pl.ds(q0, 8)
            seen[k] = twist[rows, k : k + 1], twist[rows, 64 + k : 65 + k]
        return seen[k]

    return read


def column_forward_kernel(count, place, twist, matrix, *refs):
    pieces, refs = refs[:count], refs[count:]
    before, (out, high, low) = refs[:-3], refs[-3:]
    width = pieces[0].shape[-1]
    per_source, size = pieces[0].shape[1:3]
    many = high.shape[-1] // width
    products = RES // many
    rows_out = out.shape[1]

    for here in range(count):

        @pl.when(place[0] == here)
        def _():
            @pl.loop(0, size // 8)
            def _(t):
                q0 = pl.multiple_of(t * 8, 8)
                read = column_twist(twist, q0)

                def get(n):
                    source, block = divmod(n, per_source)
                    piece = pieces[source ^ here]
                    rows = pl.ds(q0, 8)
                    return piece[0, block, rows, :], piece[1, block, rows, :]

                def put(u, value):
                    item = jnp.concatenate(twisted(value, u, 1, read), axis=0)
                    rows = pl.ds(pl.multiple_of(t * 16, 16), 16)
                    at = (u // many, rows, pl.ds((u % many) * width, width))
                    high[at], low[at] = high_low(item)

                forward_slabs(get, put)

    @pl.loop(0, products)
    def _(p):
        done = three_left(matrix, rows_out, high[p], low[p])
        for part in range(many):
            item = done[:, part * width : (part + 1) * width]
            at = p * many + part
            out[at] = before[0][at] + item if before else item


def column_inverse_kernel(count, place, source, twist, matrix, *refs):
    pieces, (peak_sq, near, lines, deep, back, top, sems, out_sems) = refs[:-8], refs[-8:]
    width = lines.shape[-1]
    rows_in = lines.shape[1]
    per_dest = near.shape[3]
    many = deep.shape[-1] // width
    products = RES // many

    def copy_in(p):
        part = pl.ds(p * many, many)
        return pltpu.make_async_copy(source.at[part], lines.at[part], sems.at[p])

    def copies_out(chunk, part):
        size = CHUNK // 2
        rows = pl.ds(part * size, size)
        first = chunk * CHUNK + part * size
        which = 0 if first < BACK[0] else 1
        there_rows = pl.ds(first - which * BACK[0], size)
        copies = []
        for j in range(count):
            piece = pieces[which * count + j].at[pl.ds(0, 2 * per_dest * BACK[which])]
            there = piece.reshape(2, per_dest, BACK[which], width).at[:, :, there_rows]
            here = near.at[chunk, place[0] ^ j, :, :, rows]
            copies.append(pltpu.make_async_copy(here, there, out_sems.at[(chunk * 2 + part) * count + j]))
        return copies

    def prepare(p):
        copy_in(p).wait()
        blocks = [lines[p * many + part] for part in range(many)]
        joined = jnp.concatenate(blocks, axis=1) if many > 1 else blocks[0]
        high = joined.astype(jnp.bfloat16).astype(jnp.float32)
        parts = [high, joined - high, high]
        if deep.shape[1] > 3 * rows_in:
            parts.append(jnp.zeros((deep.shape[1] - 3 * rows_in, many * width), jnp.float32))
        deep[p] = jnp.concatenate(parts, axis=0).astype(jnp.bfloat16)

    def product(p, chunk):
        done = dot16(matrix[chunk], deep[p])
        for part in range(many):
            back[chunk, p * many + part] = done[:, part * width : (part + 1) * width]

    def butterflies(t, chunk):
        q0 = pl.multiple_of(t * 8, 8)
        largest = []
        read = column_twist(twist, pl.multiple_of(chunk * CHUNK + q0, 8))

        def get(u):
            re = back[chunk, u, pl.ds(q0, 8), :]
            im = back[chunk, u, pl.ds(CHUNK + q0, 8), :]
            return twisted((re, im), u, -1, read)

        def put(n, value):
            dest, block = divmod(n, per_dest)
            rows = pl.ds(q0, 8)
            near[chunk, dest, 0, block, rows, :], near[chunk, dest, 1, block, rows, :] = value
            largest.append(value[0] * value[0] + value[1] * value[1])

        inverse_slabs(get, put)
        while len(largest) > 1:
            largest = [jnp.maximum(a, b) for a, b in zip(largest[0::2], largest[1::2])]
        top[...] = jnp.maximum(top[...], largest[0])

    for p in range(products):
        copy_in(p).start()
    top[...] = jnp.zeros_like(top)

    @pl.loop(0, products)
    def _(p):
        prepare(p)
        product(p, 0)

    tiles = CHUNK // 16
    steps = min(tiles, products // 2)
    for chunk in range(CHUNKS):
        for part in range(2):

            @pl.loop(part * steps, (part + 1) * steps)
            def _(t):
                for item in range(tiles // steps):
                    butterflies(t * (tiles // steps) + item, chunk)
                if chunk + 1 < CHUNKS:
                    for item in range(products // 2 // steps):
                        product(t * (products // 2 // steps) + item, chunk + 1)

            for copy in copies_out(chunk, part):
                copy.start()
    peak_sq[0] = jnp.max(top[...])
    for chunk in range(CHUNKS):
        for part in range(2):
            for copy in copies_out(chunk, part):
                copy.wait()


def line_kernel(
    order, own, tail, lines, gain, twist, fwd_high, fwd_low, inv_high, inv_low, out, *scratch
):
    half = RES * 8
    at_end = pl.program_id(0) == pl.num_programs(0) - 1

    def line_twist(side):
        def read(k):
            lanes = pl.ds(side * 128, 128)
            return twist[0, k, :, lanes], twist[1, k, :, lanes]

        return read

    def forward(group, stacked, sides=(0, 1)):
        for side in sides:
            waiting = {}

            def get(m):
                block = order[2 * m + side]
                at = group * 16
                return lines[block, at : at + 8, :], lines[block, at + 8 : at + 16, :]

            def put(u, value):
                waiting[u] = twisted(value, u, 1, line_twist(side))
                v = (u + RES // 2) % RES
                if v in waiting:
                    first = min(u, v)
                    rows = pl.ds(first * 16, 16)
                    rows_low = pl.ds(half + first * 16, 16)
                    for part in range(2):
                        item = jnp.concatenate(
                            [waiting[first][part], waiting[first + RES // 2][part]], axis=0
                        )
                        at = pl.ds(part * INNER + side * 128, 128)
                        stacked[rows, at], stacked[rows_low, at] = high_low(item)

            forward_slabs(get, put)

    def filtered(group, stacked):
        spec = three_right(stacked[...], half, fwd_high[...], fwd_low[...])
        spec_re, spec_im = spec[:, :128], spec[:, 128:]
        g_re, g_im = gain[0, group], gain[1, group]
        mixed = jnp.concatenate(
            [spec_re * g_re - spec_im * g_im, spec_re * g_im + spec_im * g_re], axis=1
        )
        return jnp.concatenate(high_low(mixed), axis=0)

    def unfold(mixed, back):
        back[...] = three_right(mixed, half, inv_high[...], inv_low[...])

    def inverse(group, back, sides=(0, 1)):
        for side in sides:

            def get(u):
                rows = pl.ds((u % (RES // 2)) * 16 + (u // (RES // 2)) * 8, 8)
                re = back[rows, pl.ds(side * 128, 128)]
                im = back[rows, pl.ds(INNER + side * 128, 128)]
                return twisted((re, im), u, -1, line_twist(side))

            def put(m, value):
                block = order[2 * m + side]
                at = group * 16
                out[block, at : at + 8, :], out[block, at + 8 : at + 16, :] = value

            inverse_slabs(get, put)

    if tail:

        @pl.when(at_end)
        def _():
            for block in range(N // 128):
                lines[block, 8:12, :] = lines[block, 4:8, :]

    groups = len(scratch) // 2

    stacked, back = scratch[:groups], scratch[groups:]

    def run(count):
        forward(0, stacked[0])
        for group in range(count):
            mixed = filtered(group, stacked[group])
            if group + 1 < count:
                forward(group + 1, stacked[group + 1], (0,))
            if group > 0:
                inverse(group - 1, back[group - 1], (0,))
            unfold(mixed, back[group])
            if group + 1 < count:
                forward(group + 1, stacked[group + 1], (1,))
            if group > 0:
                inverse(group - 1, back[group - 1], (1,))
        inverse(count - 1, back[count - 1])

    rest = own % groups
    if rest:
        pl.when(jnp.logical_not(at_end))(lambda: run(groups))
        pl.when(at_end)(lambda: run(rest))
    else:
        run(groups)

    if tail:

        @pl.when(at_end)
        def _():
            for block in range(N // 128):
                out[block, 4:8, :] = out[block, 8:12, :]


def gain_kernel(place, gain):
    k0 = place[0]
    group = place[1] + pl.program_id(0)
    down = lax.broadcasted_iota(jnp.int32, (8, 128), 0)
    across = lax.broadcasted_iota(jnp.int32, (8, 128), 1)
    row = (k0 + RES * (group * 8 + down - HALF)).astype(jnp.float32)
    row_sq = row * row
    row_in = jnp.abs(row) < LIMIT
    for u in range(RES):
        col = (residue(u) + RES * (across - HALF)).astype(jnp.float32)
        square = row_sq + col * col
        scaled = RATIO_SQ * square
        phase = -2.0 * math.pi * distance / wavelength * scaled / (1.0 + jnp.sqrt(1.0 - scaled))
        total = jnp.where(
            row_in & (jnp.abs(col) < LIMIT), jnp.exp(square * (-2.0 / (LIMIT * LIMIT))), 0.0
        )
        quarter = jnp.floor(phase * (2.0 / math.pi) + 0.5)
        left = phase - quarter * 1.5703125
        left = left - quarter * 4.837512969970703125e-4
        left = left - quarter * 7.549789954891882e-8
        sq = left * left
        sine = ((-1.9515295891e-4 * sq + 8.3321608736e-3) * sq - 1.6666654611e-1) * sq * left + left
        cosine = (
            (2.443315711809948e-5 * sq - 1.388731625493765e-3) * sq + 4.166664568298827e-2
        ) * sq * sq - 0.5 * sq + 1.0
        which = quarter.astype(jnp.int32) & 3
        swap = (which & 1) == 1
        cos_part = jnp.where(swap, sine, cosine)
        sin_part = jnp.where(swap, cosine, sine)
        cos_part = jnp.where((which == 1) | (which == 2), -cos_part, cos_part)
        sin_part = jnp.where(which >= 2, -sin_part, sin_part)
        at = (u % (RES // 2)) * 16 + (u // (RES // 2)) * 8
        gain[0, 0, at : at + 8, :] = total * cos_part
        gain[1, 0, at : at + 8, :] = total * sin_part


def encode(near_real, near_imag, peak_sq, cell_sign):
    square = near_real * near_real + near_imag * near_imag
    root = lax.rsqrt(jnp.maximum(square, 1.2e-38))
    top = lax.rsqrt(peak_sq)
    amp_level = (square * root) * (0.8 * top)
    unit = jnp.minimum(root, 20.0 * top)
    rest = 1.0 - amp_level * amp_level
    level = unit * amp_level
    lift = (rest * lax.rsqrt(rest)) * (unit * cell_sign)
    return (near_real * level + near_imag * lift, near_imag * level - near_real * lift)


def stamp_kernel(others, peak_one, peak_two, *refs):
    refs = refs[others:]
    stay, pieces, refs = refs[:CHUNKS], refs[CHUNKS : CHUNKS + others], refs[CHUNKS + others :]
    fetched, (tile, sems) = refs[:CHUNKS], refs[CHUNKS:]
    tile[...] = jnp.full(tile.shape, jnp.maximum(peak_one[0], peak_two[0]), jnp.float32)
    copies = []
    for j, piece in enumerate(pieces):
        rows = pl.ds(piece.shape[0] - SPARE, SPARE)
        copies.append(pltpu.make_async_copy(tile, piece.at[rows], sems.at[j]))
    for chunk in range(CHUNKS):
        copies.append(pltpu.make_async_copy(stay[chunk], fetched[chunk], sems.at[others + chunk]))
    for copy in copies:
        copy.start()
    for copy in copies:
        copy.wait()


def encode_kernel(count, place, peak_one, peak_two, *refs):
    pieces, refs = refs[: 2 * count], refs[2 * count :]
    slm_real, slm_imag, tile_real, tile_imag, sems = refs
    blocks, width = tile_real.shape[0], pieces[0].shape[-1]
    top = jnp.full((1, width), jnp.maximum(peak_one[0], peak_two[0]), jnp.float32)
    for piece in pieces[count + 1 :]:
        top = jnp.maximum(top, piece[pl.ds(piece.shape[0] - SPARE, 1), :])
    cell = lax.broadcasted_iota(jnp.int32, (BACK[0], width), 0)
    cell = cell + lax.broadcasted_iota(jnp.int32, (BACK[0], width), 1)
    cell_sign = (1 - 2 * (cell & 1)).astype(jnp.float32)

    def copies_out(block):
        rows = pl.ds(block * INNER, INNER)
        return [
            pltpu.make_async_copy(tile.at[block], slm.at[rows], sems.at[2 * block + part])
            for part, (tile, slm) in enumerate(((tile_real, slm_real), (tile_imag, slm_imag)))
        ]

    @pl.loop(0, blocks)
    def _(block):
        for at, piece in enumerate(pieces):
            which, j = divmod(at, count)
            cells = BACK[which]
            lanes = pl.ds(pl.multiple_of((place[0] ^ j) * width, width), width)
            rows = pl.ds(which * BACK[0], cells)
            real = pl.ds(pl.multiple_of(block * cells, cells), cells)
            imag = pl.ds(pl.multiple_of((blocks + block) * cells, cells), cells)
            tile_real[block, rows, lanes], tile_imag[block, rows, lanes] = encode(
                piece[real, :], piece[imag, :], top, cell_sign[:cells]
            )
        for copy in copies_out(block):
            copy.start()

    for block in range(blocks):
        for copy in copies_out(block):
            copy.wait()


def pack_kernel(place, field_real, field_imag, *refs):
    pieces, sems = refs[:-1], refs[-1]
    width = pieces[0].shape[-1]
    copies = []
    for j in list(range(1, len(pieces))) + [0]:
        lanes = pl.ds(pl.multiple_of((place[0] ^ j) * width, width), width)
        for part, field in enumerate((field_real, field_imag)):
            copies.append(
                pltpu.make_async_copy(
                    field.at[:, :, lanes], pieces[j].at[part], sems.at[2 * j + part]
                )
            )
    for copy in copies:
        copy.start()
    for copy in copies:
        copy.wait()


def exchange(pieces, axis):
    total = len(pieces)
    return [pieces[0]] + [
        lax.ppermute(pieces[j], axis, [(i, i ^ j) for i in range(total)]) for j in range(1, total)
    ]


def params(mebibytes):
    return pltpu.CompilerParams(vmem_limit_bytes=mebibytes << 20)


def cost(megabytes):
    return pl.CostEstimate(flops=0, bytes_accessed=megabytes << 20, transcendentals=0)


def whole(memory=pltpu.VMEM):
    return pl.BlockSpec(memory_space=memory)


def body(field_real, field_imag):
    row_total, col_total = lax.axis_size("row"), lax.axis_size("col")
    devices = row_total * col_total
    device = lax.axis_index("row") * col_total + lax.axis_index("col")
    height, tile_width = field_real.shape
    width = tile_width // row_total
    parts = max(1, devices // RES)
    groups = -(-(2 * HALF + 1) // (8 * parts)) * parts
    own = groups // parts
    tail = parts == 1
    total_rows = groups * 16 - (8 if tail else 0)
    own_rows = total_rows // parts
    many = 4 if width == 128 else 1

    fwd_col, inv_col = column_tables(groups, tail)
    line_fh, line_fl, line_ih, line_il = line_tables()
    twist = np.stack(twist_table())
    twist_line = np.ascontiguousarray(np.broadcast_to(twist[:, :, None], twist.shape[:2] + (8, INNER)))
    twist_col = np.pad(twist, ((0, 0), (0, 64 - twist.shape[1]), (0, 0)))
    twist_col = twist_col.reshape(128, INNER).T.copy()

    u = device // parts
    k0 = jnp.where(u >= RES // 2, u - RES, u)
    place = jnp.stack([k0, (device % parts) * own]).astype(jnp.int32)
    gain = pl.pallas_call(
        gain_kernel,
        grid=(own,),
        in_specs=[whole(pltpu.SMEM)],
        out_specs=pl.BlockSpec((2, 1, RES * 8, 128), lambda g: (0, g, 0, 0)),
        out_shape=jax.ShapeDtypeStruct((2, own, RES * 8, 128), jnp.float32),
        compiler_params=params(50),
        name="gain",
    )(place)

    place_row = lax.axis_index("row").reshape(1).astype(jnp.int32)
    blocks = height // INNER
    anywhere = whole(pl.ANY)
    if width != 128:
        packed = jnp.stack([field_real, field_imag]).reshape(2, blocks, INNER, row_total, width)
        packed = jnp.take(packed, jnp.arange(row_total) ^ place_row[0], axis=3)
    lines = []
    for chunk, (start, size) in enumerate(FRONT):
        piece_shape = jax.ShapeDtypeStruct((2, blocks, size, width), jnp.float32)
        at = start // size
        if width == 128:
            pieces = pl.pallas_call(
                pack_kernel,
                grid=(1,),
                in_specs=[whole(pltpu.SMEM)]
                + [pl.BlockSpec((blocks, size, tile_width), lambda i: (0, at, 0))] * 2,
                out_specs=[anywhere] * row_total,
                out_shape=[piece_shape] * row_total,
                scratch_shapes=[pltpu.SemaphoreType.DMA((2 * row_total,))],
                compiler_params=params(56),
                cost_estimate=cost(4),
                name="pack",
            )(
                place_row,
                field_real.reshape(blocks, INNER, tile_width),
                field_imag.reshape(blocks, INNER, tile_width),
            )
        else:
            pieces = [packed[:, :, start : start + size, j] for j in range(row_total)]
        pieces = exchange(pieces, "row")
        if chunk == 0:
            pieces, gain = lax.optimization_barrier((pieces, gain))
        rows = slice(start, start + size)
        slab = pltpu.VMEM((RES // many, 2 * size, many * width), jnp.bfloat16)
        lines = [
            pl.pallas_call(
                partial(column_forward_kernel, row_total),
                in_specs=[whole(pltpu.SMEM)] + [whole()] * (2 + row_total + len(lines)),
                out_specs=whole(),
                out_shape=jax.ShapeDtypeStruct((RES, total_rows, width), jnp.float32),
                scratch_shapes=[slab, slab],
                compiler_params=params(20),
                cost_estimate=cost(20),
                name="column_forward",
            )(place_row, twist_col[rows], fwd_col[chunk], *pieces, *lines)
        ]
    (lines,) = lines

    lines = lines.reshape(devices, own_rows, width)
    lines = lax.all_to_all(lines, ("row", "col"), split_axis=0, concat_axis=0, tiled=True)
    if width == 128:
        order = tuple((b % row_total) * col_total + b // row_total for b in range(N // 128))
    else:
        order = tuple(range(N // 128))
        lines = lines.reshape(row_total, col_total, own_rows, width).transpose(2, 1, 0, 3)
        lines = lines.reshape(own_rows, N // 128, 128).transpose(1, 0, 2)

    at_once = 2
    line_grain = pl.BlockSpec((N // 128, 16 * at_once, 128), lambda i: (0, i, 0))
    gain_grain = pl.BlockSpec((2, at_once, RES * 8, 128), lambda i: (0, i, 0, 0))
    lines = pl.pallas_call(
        partial(line_kernel, order, own, tail),
        grid=(-(-own // at_once),),
        in_specs=[line_grain, gain_grain] + [whole()] * 5,
        out_specs=line_grain,
        out_shape=jax.ShapeDtypeStruct((N // 128, own_rows, 128), jnp.float32),
        scratch_shapes=[pltpu.VMEM((2 * RES * 8, 2 * INNER), jnp.bfloat16)] * at_once
        + [pltpu.VMEM((RES * 8, 2 * INNER), jnp.float32)] * at_once,
        compiler_params=params(44),
        name="line",
    )(lines, gain, twist_line, line_fh, line_fl, line_ih, line_il)

    if width != 128:
        lines = lines.transpose(1, 0, 2).reshape(own_rows, col_total, row_total, width)
        lines = lines.transpose(2, 1, 0, 3).reshape(devices, own_rows, width)
    lines = lax.all_to_all(lines, ("row", "col"), split_axis=0, concat_axis=0, tiled=True)
    lines = lines.reshape(RES, total_rows, width)

    piece_shapes = [
        jax.ShapeDtypeStruct((2 * blocks * cells + spare, width), jnp.float32)
        for cells, spare in zip(BACK, (0, SPARE))
    ]
    *near, peak_sq = pl.pallas_call(
        partial(column_inverse_kernel, row_total),
        in_specs=[whole(pltpu.SMEM), anywhere, whole(), whole()],
        out_specs=[anywhere] * (2 * row_total) + [whole(pltpu.SMEM)],
        out_shape=[shape for shape in piece_shapes for _ in range(row_total)]
        + [jax.ShapeDtypeStruct((1,), jnp.float32)],
        scratch_shapes=[
            pltpu.VMEM((CHUNKS, row_total, 2, blocks, CHUNK, width), jnp.float32),
            pltpu.VMEM((RES, total_rows, width), jnp.float32),
            pltpu.VMEM((RES // many, inv_col.shape[2], many * width), jnp.bfloat16),
            pltpu.VMEM((CHUNKS, RES, 2 * CHUNK, width), jnp.float32),
            pltpu.VMEM((8, width), jnp.float32),
            pltpu.SemaphoreType.DMA((RES // many,)),
            pltpu.SemaphoreType.DMA((2 * CHUNKS * row_total,)),
        ],
        compiler_params=params(36),
        name="column_inverse",
    )(place_row, lines, twist_col, inv_col)
    near = [near[:row_total], near[row_total:]]
    piece_shape = piece_shapes[-1]
    near[0] = exchange(near[0], "row")
    shift = 1
    while shift < col_total:
        partner = [(i, i ^ shift) for i in range(col_total)]
        peaks = [peak_sq, lax.ppermute(peak_sq, "col", partner)]
        shift *= 2
        if shift < col_total:
            peak_sq = jnp.maximum(*peaks)
    others = row_total - 1
    stamped = pl.pallas_call(
        partial(stamp_kernel, others),
        in_specs=[whole(pltpu.SMEM)] * 2 + [anywhere] * (others + CHUNKS),
        out_specs=[anywhere] * others + [whole()] * CHUNKS,
        out_shape=[piece_shape] * others + piece_shapes,
        scratch_shapes=[
            pltpu.VMEM((SPARE, width), jnp.float32),
            pltpu.SemaphoreType.DMA((others + CHUNKS,)),
        ],
        input_output_aliases={2 + j: j for j in range(others)},
        compiler_params=params(16),
        name="stamp",
    )(*peaks, *near[1][1:], near[0][0], near[1][0])
    near[1][1:] = stamped[:others]
    near[0][0], near[1][0] = stamped[others:]
    near[0][1:], near[1][1] = lax.optimization_barrier((near[0][1:], near[1][1]))
    near[1] = exchange(near[1], "row")
    if width != 128:
        peak_sq = jnp.maximum(*peaks)[0]
        for piece in near[1][1:]:
            peak_sq = jnp.maximum(peak_sq, piece[-1, 0])
        both = []
        for cells, pieces in zip(BACK, near):
            part = jnp.stack([piece[: 2 * blocks * cells] for piece in pieces])
            part = jnp.take(part, jnp.arange(row_total) ^ place_row[0], axis=0)
            both.append(part.reshape(row_total, 2, blocks, cells, width))
        near = jnp.concatenate(both, axis=3)
        near = near.transpose(1, 2, 3, 0, 4).reshape(2, height, tile_width)
        odd_cell = (jnp.arange(height)[:, None] + jnp.arange(tile_width)[None, :]) % 2
        cell_sign = (1 - 2 * odd_cell).astype(jnp.float32)
        return encode(near[0], near[1], peak_sq, cell_sign)
    tile_shape = jax.ShapeDtypeStruct((height, tile_width), jnp.float32)
    tile = pltpu.VMEM((blocks, INNER, tile_width), jnp.float32)
    return pl.pallas_call(
        partial(encode_kernel, row_total),
        in_specs=[whole(pltpu.SMEM)] * 3 + [whole()] * (2 * row_total),
        out_specs=[anywhere] * 2,
        out_shape=[tile_shape, tile_shape],
        scratch_shapes=[tile, tile, pltpu.SemaphoreType.DMA((2 * blocks,))],
        compiler_params=params(16),
        name="encode",
    )(place_row, *peaks, *near[0], *near[1])


def solution(mesh):
    in_specs = (P("row", "col"), P("row", "col"))
    out_specs = (P("row", "col"), P("row", "col"))
    return jax.shard_map(body, mesh=mesh, in_specs=in_specs, out_specs=out_specs, check_vma=False)
```

```python
from functools import partial
import math

import jax
import jax.numpy as jnp
import ml_dtypes
import numpy as np
from jax import lax
from jax.experimental import pallas as pl
from jax.experimental.pallas import tpu as pltpu
from jax.sharding import PartitionSpec as P

N = 4096
PAD = 2 * N
wavelength = 5.2e-07
distance = 0.2
INNER = 256
SLABS = N // INNER
RES = PAD // INNER
HALF = 40
CHUNKS = 2
CHUNK = INNER // CHUNKS
FRONT = ((0, 128), (128, 128))
SPARE = 8


def optics(padded_side):
    pitch = 2e-06 * math.sqrt(8192.0 / padded_side)
    extent = padded_side * pitch
    ratio_sq = (wavelength / extent) ** 2
    band_limit = extent / (wavelength * math.sqrt((2.0 * distance / extent) ** 2 + 1.0))
    return (ratio_sq, band_limit)


RATIO_SQ, LIMIT = optics(PAD)
assert RES * HALF - RES // 2 + RES > LIMIT and RES * HALF + RES // 2 > LIMIT


def residue(u):
    return u if u < RES // 2 else u - RES


def split16(table):
    table = np.asarray(table, np.float64)
    high = table.astype(np.float32).astype(ml_dtypes.bfloat16)
    low = (table - high.astype(np.float64)).astype(np.float32).astype(ml_dtypes.bfloat16)
    return high, low


def row_order(groups, tail):
    rows = []
    for group in range(groups):
        size = 4 if tail and group == groups - 1 else 8
        for part in range(2):
            for s in range(size):
                rows.append((part, group * 8 + s - HALF))
    return rows


def column_tables(groups, tail):
    q = np.arange(INNER)
    rows = row_order(groups, tail)
    forward = np.zeros((len(rows), 2, INNER))
    inverse = np.zeros((2, INNER, len(rows)))
    for at, (part, k1) in enumerate(rows):
        if abs(k1) > HALF:
            continue
        angle = 2.0 * np.pi * ((k1 * q) % INNER) / INNER
        c, s = np.cos(angle), np.sin(angle)
        forward[at] = (c, s) if part == 0 else (-s, c)
        inverse[:, :, at] = (c, s) if part == 0 else (-s, c)
    tables = []
    for start, size in FRONT:
        part = forward[:, :, start : start + size].reshape(-1, 2, size // 8, 8)
        part = part.transpose(0, 2, 1, 3).reshape(-1, 2 * size)
        tables.append(np.concatenate(split16(part), axis=0))
    inverse = inverse.reshape(2, CHUNKS, CHUNK, -1).transpose(1, 0, 2, 3)
    high, low = split16(inverse.reshape(CHUNKS, 2 * CHUNK, len(rows)))
    inverse = np.concatenate([high, high, low], axis=2)
    inverse = np.pad(inverse, ((0, 0), (0, 0), (0, -3 * len(rows) % 16)))
    return tables, inverse


def line_tables():
    q = np.arange(INNER)
    forward = np.zeros((2 * INNER, 256))
    inverse = np.zeros((256, 2 * INNER))
    for lane in range(2 * HALF + 1):
        angle = 2.0 * np.pi * (((lane - HALF) * q) % INNER) / INNER
        c, s = np.cos(angle), np.sin(angle)
        forward[:INNER, lane], forward[INNER:, lane] = c, s
        forward[:INNER, 128 + lane], forward[INNER:, 128 + lane] = -s, c
        inverse[lane, :INNER], inverse[lane, INNER:] = c, s
        inverse[128 + lane, :INNER], inverse[128 + lane, INNER:] = -s, c
    return split16(forward) + split16(inverse)


def twist_table():
    q = np.arange(INNER) + N // 2
    k0 = np.arange(RES // 2 + 1)
    angle = 2.0 * np.pi * ((k0[:, None] * q[None, :]) % PAD) / PAD
    return np.cos(angle).astype(np.float32), (-np.sin(angle)).astype(np.float32)


def turn(value, num, den):
    re, im = value
    num = num % den
    eighth = 8 * num
    if num == 0:
        return re, im
    if 2 * num == den:
        return -re, -im
    if 4 * num == den:
        return -im, re
    if 4 * num == 3 * den:
        return im, -re
    if eighth % den == 0:
        root = np.float32(math.sqrt(0.5))
        kind = eighth // den
        if kind == 1:
            return (re - im) * root, (re + im) * root
        if kind == 3:
            return (re + im) * (-root), (re - im) * root
        if kind == 5:
            return (im - re) * root, (re + im) * (-root)
        return (re + im) * root, (im - re) * root
    c = np.float32(math.cos(2.0 * math.pi * num / den))
    s = np.float32(math.sin(2.0 * math.pi * num / den))
    return re * c - im * s, re * s + im * c


def small_dft(get, ids, sign):
    count = len(ids)
    if count == 1:
        return [get(ids[0])]
    even = small_dft(get, ids[0::2], sign)
    odd = small_dft(get, ids[1::2], sign)
    half = count // 2
    first, second = [], []
    for j in range(half):
        re, im = even[j]
        t_re, t_im = turn(odd[j], sign * j, count)
        first.append((re + t_re, im + t_im))
        second.append((re - t_re, im - t_im))
    return first + second


def forward_slabs(get, put):
    ids = list(range(SLABS))
    for v, value in enumerate(small_dft(get, ids, -1)):
        put(2 * v, value)
    for v, value in enumerate(small_dft(lambda n: turn(get(n), -n, RES), ids, -1)):
        put(2 * v + 1, value)


def inverse_slabs(get, put):
    even = small_dft(get, list(range(0, RES, 2)), 1)
    odd = small_dft(get, list(range(1, RES, 2)), 1)
    for n in range(SLABS):
        t_re, t_im = turn(odd[n], n, RES)
        put(n, (even[n][0] + t_re, even[n][1] + t_im))


def twisted(value, u, sign, read):
    re, im = value
    k0 = residue(u)
    if k0 == 0:
        return value
    c, s = read(abs(k0))
    if (k0 < 0) == (sign > 0):
        return re * c + im * s, im * c - re * s
    return re * c - im * s, re * s + im * c


def high_low(value):
    high = value.astype(jnp.bfloat16)
    low = (value - high.astype(jnp.float32)).astype(jnp.bfloat16)
    return high, low


def dot16(left, right):
    return jnp.dot(left, right, preferred_element_type=jnp.float32)


def three_left(stacked, count, high, low):
    both = dot16(stacked[...], high)
    return both[:count] + both[count:] + dot16(stacked[:count], low)


def three_right(stacked, count, high, low):
    both = dot16(stacked, high)
    return both[:count] + both[count:] + dot16(stacked[:count], low)


def column_twist(twist, q0):
    seen = {}

    def read(k):
        if k not in seen:
            rows = pl.ds(q0, 8)
            seen[k] = twist[rows, k : k + 1], twist[rows, 64 + k : 65 + k]
        return seen[k]

    return read


def column_forward_kernel(count, place, twist, matrix, *refs):
    pieces, refs = refs[:count], refs[count:]
    before, (out, high, low) = refs[:-3], refs[-3:]
    width = pieces[0].shape[-1]
    per_source, size = pieces[0].shape[1:3]
    many = high.shape[-1] // width
    products = RES // many
    rows_out = out.shape[1]

    for here in range(count):

        @pl.when(place[0] == here)
        def _():
            @pl.loop(0, size // 8)
            def _(t):
                q0 = pl.multiple_of(t * 8, 8)
                read = column_twist(twist, q0)

                def get(n):
                    source, block = divmod(n, per_source)
                    piece = pieces[source ^ here]
                    rows = pl.ds(q0, 8)
                    return piece[0, block, rows, :], piece[1, block, rows, :]

                def put(u, value):
                    item = jnp.concatenate(twisted(value, u, 1, read), axis=0)
                    rows = pl.ds(pl.multiple_of(t * 16, 16), 16)
                    at = (u // many, rows, pl.ds((u % many) * width, width))
                    high[at], low[at] = high_low(item)

                forward_slabs(get, put)

    @pl.loop(0, products)
    def _(p):
        done = three_left(matrix, rows_out, high[p], low[p])
        for part in range(many):
            item = done[:, part * width : (part + 1) * width]
            at = p * many + part
            out[at] = before[0][at] + item if before else item


def column_inverse_kernel(count, place, source, twist, matrix, *refs):
    pieces, (peak_sq, near, lines, deep, back, top, sems, out_sems) = refs[:-8], refs[-8:]
    width = lines.shape[-1]
    rows_in = lines.shape[1]
    per_dest = near.shape[3]
    many = deep.shape[-1] // width
    products = RES // many

    def copy_in(p):
        part = pl.ds(p * many, many)
        return pltpu.make_async_copy(source.at[part], lines.at[part], sems.at[p])

    def copies_out(chunk, part):
        parts = 1 if chunk + 1 < CHUNKS else 2
        if part >= parts:
            return []
        rows = pl.ds(part * CHUNK // parts, CHUNK // parts)
        copies = []
        for j in range(count):
            piece = pieces[chunk * count + j].at[pl.ds(0, 2 * per_dest * CHUNK)]
            there = piece.reshape(2, per_dest, CHUNK, width).at[:, :, rows]
            here = near.at[chunk, place[0] ^ j, :, :, rows]
            copies.append(pltpu.make_async_copy(here, there, out_sems.at[(chunk * 2 + part) * count + j]))
        return copies

    def prepare(p):
        copy_in(p).wait()
        blocks = [lines[p * many + part] for part in range(many)]
        joined = jnp.concatenate(blocks, axis=1) if many > 1 else blocks[0]
        high = joined.astype(jnp.bfloat16).astype(jnp.float32)
        parts = [high, joined - high, high]
        if deep.shape[1] > 3 * rows_in:
            parts.append(jnp.zeros((deep.shape[1] - 3 * rows_in, many * width), jnp.float32))
        deep[p] = jnp.concatenate(parts, axis=0).astype(jnp.bfloat16)

    def product(p, chunk):
        done = dot16(matrix[chunk], deep[p])
        for part in range(many):
            back[chunk, p * many + part] = done[:, part * width : (part + 1) * width]

    def butterflies(t, chunk):
        q0 = pl.multiple_of(t * 8, 8)
        largest = []
        read = column_twist(twist, pl.multiple_of(chunk * CHUNK + q0, 8))

        def get(u):
            re = back[chunk, u, pl.ds(q0, 8), :]
            im = back[chunk, u, pl.ds(CHUNK + q0, 8), :]
            return twisted((re, im), u, -1, read)

        def put(n, value):
            dest, block = divmod(n, per_dest)
            rows = pl.ds(q0, 8)
            near[chunk, dest, 0, block, rows, :], near[chunk, dest, 1, block, rows, :] = value
            largest.append(value[0] * value[0] + value[1] * value[1])

        inverse_slabs(get, put)
        while len(largest) > 1:
            largest = [jnp.maximum(a, b) for a, b in zip(largest[0::2], largest[1::2])]
        top[...] = jnp.maximum(top[...], largest[0])

    for p in range(products):
        copy_in(p).start()
    top[...] = jnp.zeros_like(top)

    @pl.loop(0, products)
    def _(p):
        prepare(p)
        product(p, 0)

    tiles = CHUNK // 16
    steps = min(tiles, products // 2)
    for chunk in range(CHUNKS):
        for part in range(2):

            @pl.loop(part * steps, (part + 1) * steps)
            def _(t):
                for item in range(tiles // steps):
                    butterflies(t * (tiles // steps) + item, chunk)
                if chunk + 1 < CHUNKS:
                    for item in range(products // 2 // steps):
                        product(t * (products // 2 // steps) + item, chunk + 1)

            for copy in copies_out(chunk, part if chunk + 1 == CHUNKS else 1 - part):
                copy.start()
    peak_sq[0] = jnp.max(top[...])
    for chunk in range(CHUNKS):
        for part in range(2):
            for copy in copies_out(chunk, part):
                copy.wait()


def line_kernel(
    order, own, tail, lines, gain, twist, fwd_high, fwd_low, inv_high, inv_low, out, *scratch
):
    half = RES * 8
    at_end = pl.program_id(0) == pl.num_programs(0) - 1

    def line_twist(side):
        def read(k):
            lanes = pl.ds(side * 128, 128)
            return twist[0, k, :, lanes], twist[1, k, :, lanes]

        return read

    def forward(group, stacked, sides=(0, 1)):
        for side in sides:
            waiting = {}

            def get(m):
                block = order[2 * m + side]
                at = group * 16
                return lines[block, at : at + 8, :], lines[block, at + 8 : at + 16, :]

            def put(u, value):
                waiting[u] = twisted(value, u, 1, line_twist(side))
                v = (u + RES // 2) % RES
                if v in waiting:
                    first = min(u, v)
                    rows = pl.ds(first * 16, 16)
                    rows_low = pl.ds(half + first * 16, 16)
                    for part in range(2):
                        item = jnp.concatenate(
                            [waiting[first][part], waiting[first + RES // 2][part]], axis=0
                        )
                        at = pl.ds(part * INNER + side * 128, 128)
                        stacked[rows, at], stacked[rows_low, at] = high_low(item)

            forward_slabs(get, put)

    def filtered(group, stacked):
        spec = three_right(stacked[...], half, fwd_high[...], fwd_low[...])
        spec_re, spec_im = spec[:, :128], spec[:, 128:]
        g_re, g_im = gain[0, group], gain[1, group]
        mixed = jnp.concatenate(
            [spec_re * g_re - spec_im * g_im, spec_re * g_im + spec_im * g_re], axis=1
        )
        return jnp.concatenate(high_low(mixed), axis=0)

    def unfold(mixed, back):
        back[...] = three_right(mixed, half, inv_high[...], inv_low[...])

    def inverse(group, back, sides=(0, 1)):
        for side in sides:

            def get(u):
                rows = pl.ds((u % (RES // 2)) * 16 + (u // (RES // 2)) * 8, 8)
                re = back[rows, pl.ds(side * 128, 128)]
                im = back[rows, pl.ds(INNER + side * 128, 128)]
                return twisted((re, im), u, -1, line_twist(side))

            def put(m, value):
                block = order[2 * m + side]
                at = group * 16
                out[block, at : at + 8, :], out[block, at + 8 : at + 16, :] = value

            inverse_slabs(get, put)

    if tail:

        @pl.when(at_end)
        def _():
            for block in range(N // 128):
                lines[block, 8:12, :] = lines[block, 4:8, :]

    groups = len(scratch) // 2

    stacked, back = scratch[:groups], scratch[groups:]

    def run(count):
        forward(0, stacked[0])
        for group in range(count):
            mixed = filtered(group, stacked[group])
            if group + 1 < count:
                forward(group + 1, stacked[group + 1], (0,))
            if group > 0:
                inverse(group - 1, back[group - 1], (0,))
            unfold(mixed, back[group])
            if group + 1 < count:
                forward(group + 1, stacked[group + 1], (1,))
            if group > 0:
                inverse(group - 1, back[group - 1], (1,))
        inverse(count - 1, back[count - 1])

    rest = own % groups
    if rest:
        pl.when(jnp.logical_not(at_end))(lambda: run(groups))
        pl.when(at_end)(lambda: run(rest))
    else:
        run(groups)

    if tail:

        @pl.when(at_end)
        def _():
            for block in range(N // 128):
                out[block, 4:8, :] = out[block, 8:12, :]


def gain_kernel(place, gain):
    k0 = place[0]
    group = place[1] + pl.program_id(0)
    down = lax.broadcasted_iota(jnp.int32, (8, 128), 0)
    across = lax.broadcasted_iota(jnp.int32, (8, 128), 1)
    row = (k0 + RES * (group * 8 + down - HALF)).astype(jnp.float32)
    row_sq = row * row
    row_in = jnp.abs(row) < LIMIT
    for u in range(RES):
        col = (residue(u) + RES * (across - HALF)).astype(jnp.float32)
        square = row_sq + col * col
        scaled = RATIO_SQ * square
        phase = -2.0 * math.pi * distance / wavelength * scaled / (1.0 + jnp.sqrt(1.0 - scaled))
        total = jnp.where(
            row_in & (jnp.abs(col) < LIMIT), jnp.exp(square * (-2.0 / (LIMIT * LIMIT))), 0.0
        )
        quarter = jnp.floor(phase * (2.0 / math.pi) + 0.5)
        left = phase - quarter * 1.5703125
        left = left - quarter * 4.837512969970703125e-4
        left = left - quarter * 7.549789954891882e-8
        sq = left * left
        sine = ((-1.9515295891e-4 * sq + 8.3321608736e-3) * sq - 1.6666654611e-1) * sq * left + left
        cosine = (
            (2.443315711809948e-5 * sq - 1.388731625493765e-3) * sq + 4.166664568298827e-2
        ) * sq * sq - 0.5 * sq + 1.0
        which = quarter.astype(jnp.int32) & 3
        swap = (which & 1) == 1
        cos_part = jnp.where(swap, sine, cosine)
        sin_part = jnp.where(swap, cosine, sine)
        cos_part = jnp.where((which == 1) | (which == 2), -cos_part, cos_part)
        sin_part = jnp.where(which >= 2, -sin_part, sin_part)
        at = (u % (RES // 2)) * 16 + (u // (RES // 2)) * 8
        gain[0, 0, at : at + 8, :] = total * cos_part
        gain[1, 0, at : at + 8, :] = total * sin_part


def encode(near_real, near_imag, peak_sq, cell_sign):
    square = near_real * near_real + near_imag * near_imag
    root = lax.rsqrt(jnp.maximum(square, 1.2e-38))
    top = lax.rsqrt(peak_sq)
    amp_level = (square * root) * (0.8 * top)
    unit = jnp.minimum(root, 20.0 * top)
    rest = 1.0 - amp_level * amp_level
    level = unit * amp_level
    lift = (rest * lax.rsqrt(rest)) * (unit * cell_sign)
    return (near_real * level + near_imag * lift, near_imag * level - near_real * lift)


def stamp_kernel(others, peak_one, peak_two, *refs):
    refs = refs[others:]
    stay, pieces, refs = refs[:CHUNKS], refs[CHUNKS : CHUNKS + others], refs[CHUNKS + others :]
    fetched, (tile, sems) = refs[:CHUNKS], refs[CHUNKS:]
    tile[...] = jnp.full(tile.shape, jnp.maximum(peak_one[0], peak_two[0]), jnp.float32)
    copies = []
    for j, piece in enumerate(pieces):
        rows = pl.ds(piece.shape[0] - SPARE, SPARE)
        copies.append(pltpu.make_async_copy(tile, piece.at[rows], sems.at[j]))
    for chunk in range(CHUNKS):
        copies.append(pltpu.make_async_copy(stay[chunk], fetched[chunk], sems.at[others + chunk]))
    for copy in copies:
        copy.start()
    for copy in copies:
        copy.wait()


def encode_kernel(count, place, peak_one, peak_two, *refs):
    pieces, refs = refs[: CHUNKS * count], refs[CHUNKS * count :]
    slm_real, slm_imag, tile_real, tile_imag, sems = refs
    blocks, width = tile_real.shape[0], pieces[0].shape[-1]
    top = jnp.full((1, width), jnp.maximum(peak_one[0], peak_two[0]), jnp.float32)
    for piece in pieces[(CHUNKS - 1) * count + 1 :]:
        top = jnp.maximum(top, piece[pl.ds(piece.shape[0] - SPARE, 1), :])
    cell = lax.broadcasted_iota(jnp.int32, (CHUNK, width), 0)
    cell = cell + lax.broadcasted_iota(jnp.int32, (CHUNK, width), 1)
    cell_sign = (1 - 2 * (cell & 1)).astype(jnp.float32)

    def copies_out(block, chunk):
        part_rows = pl.ds(chunk * CHUNK, CHUNK)
        rows = pl.ds(block * INNER + chunk * CHUNK, CHUNK)
        first = 2 * (CHUNKS * block + chunk)
        return [
            pltpu.make_async_copy(tile.at[block, part_rows], slm.at[rows], sems.at[first + part])
            for part, (tile, slm) in enumerate(((tile_real, slm_real), (tile_imag, slm_imag)))
        ]

    @pl.loop(0, blocks)
    def _(block):
        for at in range(CHUNKS * count):
            chunk, j = divmod(at, count)
            piece = pieces[at]
            lanes = pl.ds(pl.multiple_of((place[0] ^ j) * width, width), width)
            rows = pl.ds(chunk * CHUNK, CHUNK)
            real = pl.ds(pl.multiple_of(block * CHUNK, CHUNK), CHUNK)
            imag = pl.ds(pl.multiple_of((blocks + block) * CHUNK, CHUNK), CHUNK)
            tile_real[block, rows, lanes], tile_imag[block, rows, lanes] = encode(
                piece[real, :], piece[imag, :], top, cell_sign
            )
            if j == count - 1:
                for copy in copies_out(block, chunk):
                    copy.start()

    for block in range(blocks):
        for chunk in range(CHUNKS):
            for copy in copies_out(block, chunk):
                copy.wait()


def pack_kernel(start, place, field_real, field_imag, *refs):
    pieces, (rows_in, in_sems, sems) = refs[:-3], refs[-3:]
    size, width = pieces[0].shape[2:]
    rows = pl.ds(start, size)
    fetches = [
        pltpu.make_async_copy(field.at[:, rows], rows_in.at[part], in_sems.at[part])
        for part, field in enumerate((field_real, field_imag))
    ]
    for fetch in fetches:
        fetch.start()
    copies = []
    for part, fetch in enumerate(fetches):
        fetch.wait()
        for j in list(range(1, len(pieces))) + [0]:
            lanes = pl.ds(pl.multiple_of((place[0] ^ j) * width, width), width)
            copy = pltpu.make_async_copy(
                rows_in.at[part, :, :, lanes], pieces[j].at[part], sems.at[2 * j + part]
            )
            copy.start()
            copies.append(copy)
    for copy in copies:
        copy.wait()


def exchange(pieces, axis):
    total = len(pieces)
    return [pieces[0]] + [
        lax.ppermute(pieces[j], axis, [(i, i ^ j) for i in range(total)]) for j in range(1, total)
    ]


def params(mebibytes):
    return pltpu.CompilerParams(vmem_limit_bytes=mebibytes << 20)


def cost(megabytes):
    return pl.CostEstimate(flops=0, bytes_accessed=megabytes << 20, transcendentals=0)


def whole(memory=pltpu.VMEM):
    return pl.BlockSpec(memory_space=memory)


def body(field_real, field_imag):
    row_total, col_total = lax.axis_size("row"), lax.axis_size("col")
    devices = row_total * col_total
    device = lax.axis_index("row") * col_total + lax.axis_index("col")
    height, tile_width = field_real.shape
    width = tile_width // row_total
    parts = max(1, devices // RES)
    groups = -(-(2 * HALF + 1) // (8 * parts)) * parts
    own = groups // parts
    tail = parts == 1
    total_rows = groups * 16 - (8 if tail else 0)
    own_rows = total_rows // parts
    many = 4 if width == 128 else 1

    fwd_col, inv_col = column_tables(groups, tail)
    line_fh, line_fl, line_ih, line_il = line_tables()
    twist = np.stack(twist_table())
    twist_line = np.ascontiguousarray(np.broadcast_to(twist[:, :, None], twist.shape[:2] + (8, INNER)))
    twist_col = np.pad(twist, ((0, 0), (0, 64 - twist.shape[1]), (0, 0)))
    twist_col = twist_col.reshape(128, INNER).T.copy()

    u = device // parts
    k0 = jnp.where(u >= RES // 2, u - RES, u)
    place = jnp.stack([k0, (device % parts) * own]).astype(jnp.int32)
    gain = pl.pallas_call(
        gain_kernel,
        grid=(own,),
        in_specs=[whole(pltpu.SMEM)],
        out_specs=pl.BlockSpec((2, 1, RES * 8, 128), lambda g: (0, g, 0, 0)),
        out_shape=jax.ShapeDtypeStruct((2, own, RES * 8, 128), jnp.float32),
        compiler_params=params(50),
        name="gain",
    )(place)

    place_row = lax.axis_index("row").reshape(1).astype(jnp.int32)
    blocks = height // INNER
    anywhere = whole(pl.ANY)
    if width != 128:
        packed = jnp.stack([field_real, field_imag]).reshape(2, blocks, INNER, row_total, width)
        packed = jnp.take(packed, jnp.arange(row_total) ^ place_row[0], axis=3)
    lines = []
    for chunk, (start, size) in enumerate(FRONT):
        piece_shape = jax.ShapeDtypeStruct((2, blocks, size, width), jnp.float32)
        if width == 128:
            pieces = pl.pallas_call(
                partial(pack_kernel, start),
                in_specs=[whole(pltpu.SMEM), anywhere, anywhere],
                out_specs=[anywhere] * row_total,
                out_shape=[piece_shape] * row_total,
                scratch_shapes=[
                    pltpu.VMEM((2, blocks, size, tile_width), jnp.float32),
                    pltpu.SemaphoreType.DMA((2,)),
                    pltpu.SemaphoreType.DMA((2 * row_total,)),
                ],
                compiler_params=params(56),
                cost_estimate=cost(4),
                name="pack",
            )(
                place_row,
                field_real.reshape(blocks, INNER, tile_width),
                field_imag.reshape(blocks, INNER, tile_width),
            )
        else:
            pieces = [packed[:, :, start : start + size, j] for j in range(row_total)]
        pieces = exchange(pieces, "row")
        if chunk == 0:
            pieces, gain = lax.optimization_barrier((pieces, gain))
        rows = slice(start, start + size)
        slab = pltpu.VMEM((RES // many, 2 * size, many * width), jnp.bfloat16)
        lines = [
            pl.pallas_call(
                partial(column_forward_kernel, row_total),
                in_specs=[whole(pltpu.SMEM)] + [whole()] * (2 + row_total + len(lines)),
                out_specs=whole(),
                out_shape=jax.ShapeDtypeStruct((RES, total_rows, width), jnp.float32),
                scratch_shapes=[slab, slab],
                compiler_params=params(20),
                cost_estimate=cost(20),
                name="column_forward",
            )(place_row, twist_col[rows], fwd_col[chunk], *pieces, *lines)
        ]
    (lines,) = lines

    lines = lines.reshape(devices, own_rows, width)
    lines = lax.all_to_all(lines, ("row", "col"), split_axis=0, concat_axis=0, tiled=True)
    if width == 128:
        order = tuple((b % row_total) * col_total + b // row_total for b in range(N // 128))
    else:
        order = tuple(range(N // 128))
        lines = lines.reshape(row_total, col_total, own_rows, width).transpose(2, 1, 0, 3)
        lines = lines.reshape(own_rows, N // 128, 128).transpose(1, 0, 2)

    at_once = 2
    line_grain = pl.BlockSpec((N // 128, 16 * at_once, 128), lambda i: (0, i, 0))
    gain_grain = pl.BlockSpec((2, at_once, RES * 8, 128), lambda i: (0, i, 0, 0))
    lines = pl.pallas_call(
        partial(line_kernel, order, own, tail),
        grid=(-(-own // at_once),),
        in_specs=[line_grain, gain_grain] + [whole()] * 5,
        out_specs=line_grain,
        out_shape=jax.ShapeDtypeStruct((N // 128, own_rows, 128), jnp.float32),
        scratch_shapes=[pltpu.VMEM((2 * RES * 8, 2 * INNER), jnp.bfloat16)] * at_once
        + [pltpu.VMEM((RES * 8, 2 * INNER), jnp.float32)] * at_once,
        compiler_params=params(44),
        name="line",
    )(lines, gain, twist_line, line_fh, line_fl, line_ih, line_il)

    if width != 128:
        lines = lines.transpose(1, 0, 2).reshape(own_rows, col_total, row_total, width)
        lines = lines.transpose(2, 1, 0, 3).reshape(devices, own_rows, width)
    lines = lax.all_to_all(lines, ("row", "col"), split_axis=0, concat_axis=0, tiled=True)
    lines = lines.reshape(RES, total_rows, width)

    piece_shapes = [
        jax.ShapeDtypeStruct((2 * blocks * CHUNK + spare, width), jnp.float32)
        for spare in (0,) * (CHUNKS - 1) + (SPARE,)
    ]
    *near, peak_sq = pl.pallas_call(
        partial(column_inverse_kernel, row_total),
        in_specs=[whole(pltpu.SMEM), anywhere, whole(), whole()],
        out_specs=[anywhere] * (CHUNKS * row_total) + [whole(pltpu.SMEM)],
        out_shape=[shape for shape in piece_shapes for _ in range(row_total)]
        + [jax.ShapeDtypeStruct((1,), jnp.float32)],
        scratch_shapes=[
            pltpu.VMEM((CHUNKS, row_total, 2, blocks, CHUNK, width), jnp.float32),
            pltpu.VMEM((RES, total_rows, width), jnp.float32),
            pltpu.VMEM((RES // many, inv_col.shape[2], many * width), jnp.bfloat16),
            pltpu.VMEM((CHUNKS, RES, 2 * CHUNK, width), jnp.float32),
            pltpu.VMEM((8, width), jnp.float32),
            pltpu.SemaphoreType.DMA((RES // many,)),
            pltpu.SemaphoreType.DMA((2 * CHUNKS * row_total,)),
        ],
        compiler_params=params(36),
        name="column_inverse",
    )(place_row, lines, twist_col, inv_col)
    near = [near[:row_total], near[row_total:]]
    piece_shape = piece_shapes[-1]
    near[0] = exchange(near[0], "row")
    shift = 1
    while shift < col_total:
        partner = [(i, i ^ shift) for i in range(col_total)]
        peaks = [peak_sq, lax.ppermute(peak_sq, "col", partner)]
        shift *= 2
        if shift < col_total:
            peak_sq = jnp.maximum(*peaks)
    others = row_total - 1
    stamped = pl.pallas_call(
        partial(stamp_kernel, others),
        in_specs=[whole(pltpu.SMEM)] * 2 + [anywhere] * (others + CHUNKS),
        out_specs=[anywhere] * others + [whole()] * CHUNKS,
        out_shape=[piece_shape] * others + piece_shapes,
        scratch_shapes=[
            pltpu.VMEM((SPARE, width), jnp.float32),
            pltpu.SemaphoreType.DMA((others + CHUNKS,)),
        ],
        input_output_aliases={2 + j: j for j in range(others)},
        compiler_params=params(16),
        name="stamp",
    )(*peaks, *near[1][1:], near[0][0], near[1][0])
    near[1][1:] = stamped[:others]
    near[0][0], near[1][0] = stamped[others:]
    near[0][1:], near[1][1] = lax.optimization_barrier((near[0][1:], near[1][1]))
    near[1] = exchange(near[1], "row")
    if width != 128:
        peak_sq = jnp.maximum(*peaks)[0]
        for piece in near[1][1:]:
            peak_sq = jnp.maximum(peak_sq, piece[-1, 0])
        near = jnp.stack([jnp.stack([piece[: 2 * blocks * CHUNK] for piece in pieces]) for pieces in near])
        near = jnp.take(near, jnp.arange(row_total) ^ place_row[0], axis=1)
        near = near.reshape(CHUNKS, row_total, 2, blocks, CHUNK, width)
        near = near.transpose(2, 3, 0, 4, 1, 5).reshape(2, height, tile_width)
        odd_cell = (jnp.arange(height)[:, None] + jnp.arange(tile_width)[None, :]) % 2
        cell_sign = (1 - 2 * odd_cell).astype(jnp.float32)
        return encode(near[0], near[1], peak_sq, cell_sign)
    tile_shape = jax.ShapeDtypeStruct((height, tile_width), jnp.float32)
    tile = pltpu.VMEM((blocks, INNER, tile_width), jnp.float32)
    return pl.pallas_call(
        partial(encode_kernel, row_total),
        in_specs=[whole(pltpu.SMEM)] * 3 + [whole()] * (CHUNKS * row_total),
        out_specs=[anywhere] * 2,
        out_shape=[tile_shape, tile_shape],
        scratch_shapes=[tile, tile, pltpu.SemaphoreType.DMA((2 * CHUNKS * blocks,))],
        compiler_params=params(16),
        name="encode",
    )(place_row, *peaks, *near[0], *near[1])


def solution(mesh):
    in_specs = (P("row", "col"), P("row", "col"))
    out_specs = (P("row", "col"), P("row", "col"))
    return jax.shard_map(body, mesh=mesh, in_specs=in_specs, out_specs=out_specs, check_vma=False)
```

```python
from functools import partial
import math

import jax
import jax.numpy as jnp
import ml_dtypes
import numpy as np
from jax import lax
from jax.experimental import pallas as pl
from jax.experimental.pallas import tpu as pltpu
from jax.sharding import PartitionSpec as P

N = 4096
PAD = 2 * N
wavelength = 5.2e-07
distance = 0.2
INNER = 256
SLABS = N // INNER
RES = PAD // INNER
HALF = 40
CHUNKS = 2
CHUNK = INNER // CHUNKS
FRONT = ((0, 128), (128, 128))
SPARE = 8


def optics(padded_side):
    pitch = 2e-06 * math.sqrt(8192.0 / padded_side)
    extent = padded_side * pitch
    ratio_sq = (wavelength / extent) ** 2
    band_limit = extent / (wavelength * math.sqrt((2.0 * distance / extent) ** 2 + 1.0))
    return (ratio_sq, band_limit)


RATIO_SQ, LIMIT = optics(PAD)
assert RES * HALF - RES // 2 + RES > LIMIT and RES * HALF + RES // 2 > LIMIT


def residue(u):
    return u if u < RES // 2 else u - RES


def split16(table):
    table = np.asarray(table, np.float64)
    high = table.astype(np.float32).astype(ml_dtypes.bfloat16)
    low = (table - high.astype(np.float64)).astype(np.float32).astype(ml_dtypes.bfloat16)
    return high, low


def row_order(groups, tail):
    rows = []
    for group in range(groups):
        size = 4 if tail and group == groups - 1 else 8
        for part in range(2):
            for s in range(size):
                rows.append((part, group * 8 + s - HALF))
    return rows


def column_tables(groups, tail):
    q = np.arange(INNER)
    rows = row_order(groups, tail)
    forward = np.zeros((len(rows), 2, INNER))
    inverse = np.zeros((2, INNER, len(rows)))
    for at, (part, k1) in enumerate(rows):
        if abs(k1) > HALF:
            continue
        angle = 2.0 * np.pi * ((k1 * q) % INNER) / INNER
        c, s = np.cos(angle), np.sin(angle)
        forward[at] = (c, s) if part == 0 else (-s, c)
        inverse[:, :, at] = (c, s) if part == 0 else (-s, c)
    tables = []
    for start, size in FRONT:
        part = forward[:, :, start : start + size].reshape(-1, 2, size // 8, 8)
        part = part.transpose(0, 2, 1, 3).reshape(-1, 2 * size)
        tables.append(np.concatenate(split16(part), axis=0))
    inverse = inverse.reshape(2, CHUNKS, CHUNK, -1).transpose(1, 0, 2, 3)
    high, low = split16(inverse.reshape(CHUNKS, 2 * CHUNK, len(rows)))
    inverse = np.concatenate([high, high, low], axis=2)
    inverse = np.pad(inverse, ((0, 0), (0, 0), (0, -3 * len(rows) % 16)))
    return tables, inverse


def line_tables():
    q = np.arange(INNER)
    forward = np.zeros((2 * INNER, 256))
    inverse = np.zeros((256, 2 * INNER))
    for lane in range(2 * HALF + 1):
        angle = 2.0 * np.pi * (((lane - HALF) * q) % INNER) / INNER
        c, s = np.cos(angle), np.sin(angle)
        forward[:INNER, lane], forward[INNER:, lane] = c, s
        forward[:INNER, 128 + lane], forward[INNER:, 128 + lane] = -s, c
        inverse[lane, :INNER], inverse[lane, INNER:] = c, s
        inverse[128 + lane, :INNER], inverse[128 + lane, INNER:] = -s, c
    return split16(forward) + split16(inverse)


def twist_table():
    q = np.arange(INNER) + N // 2
    k0 = np.arange(RES // 2 + 1)
    angle = 2.0 * np.pi * ((k0[:, None] * q[None, :]) % PAD) / PAD
    return np.cos(angle).astype(np.float32), (-np.sin(angle)).astype(np.float32)


def turn(value, num, den):
    re, im = value
    num = num % den
    eighth = 8 * num
    if num == 0:
        return re, im
    if 2 * num == den:
        return -re, -im
    if 4 * num == den:
        return -im, re
    if 4 * num == 3 * den:
        return im, -re
    if eighth % den == 0:
        root = np.float32(math.sqrt(0.5))
        kind = eighth // den
        if kind == 1:
            return (re - im) * root, (re + im) * root
        if kind == 3:
            return (re + im) * (-root), (re - im) * root
        if kind == 5:
            return (im - re) * root, (re + im) * (-root)
        return (re + im) * root, (im - re) * root
    c = np.float32(math.cos(2.0 * math.pi * num / den))
    s = np.float32(math.sin(2.0 * math.pi * num / den))
    return re * c - im * s, re * s + im * c


def small_dft(get, ids, sign):
    count = len(ids)
    if count == 1:
        return [get(ids[0])]
    even = small_dft(get, ids[0::2], sign)
    odd = small_dft(get, ids[1::2], sign)
    half = count // 2
    first, second = [], []
    for j in range(half):
        re, im = even[j]
        t_re, t_im = turn(odd[j], sign * j, count)
        first.append((re + t_re, im + t_im))
        second.append((re - t_re, im - t_im))
    return first + second


def forward_slabs(get, put):
    ids = list(range(SLABS))
    for v, value in enumerate(small_dft(get, ids, -1)):
        put(2 * v, value)
    for v, value in enumerate(small_dft(lambda n: turn(get(n), -n, RES), ids, -1)):
        put(2 * v + 1, value)


def inverse_slabs(get, put):
    even = small_dft(get, list(range(0, RES, 2)), 1)
    odd = small_dft(get, list(range(1, RES, 2)), 1)
    for n in range(SLABS):
        t_re, t_im = turn(odd[n], n, RES)
        put(n, (even[n][0] + t_re, even[n][1] + t_im))


def twisted(value, u, sign, read):
    re, im = value
    k0 = residue(u)
    if k0 == 0:
        return value
    c, s = read(abs(k0))
    if (k0 < 0) == (sign > 0):
        return re * c + im * s, im * c - re * s
    return re * c - im * s, re * s + im * c


def high_low(value):
    high = value.astype(jnp.bfloat16)
    low = (value - high.astype(jnp.float32)).astype(jnp.bfloat16)
    return high, low


def dot16(left, right):
    return jnp.dot(left, right, preferred_element_type=jnp.float32)


def three_left(stacked, count, high, low):
    both = dot16(stacked[...], high)
    return both[:count] + both[count:] + dot16(stacked[:count], low)


def three_right(stacked, count, high, low):
    both = dot16(stacked, high)
    return both[:count] + both[count:] + dot16(stacked[:count], low)


def column_twist(twist, q0):
    seen = {}

    def read(k):
        if k not in seen:
            rows = pl.ds(q0, 8)
            seen[k] = twist[rows, k : k + 1], twist[rows, 64 + k : 65 + k]
        return seen[k]

    return read


def column_forward_kernel(count, place, twist, matrix, *refs):
    pieces, refs = refs[:count], refs[count:]
    before, (out, high, low) = refs[:-3], refs[-3:]
    width = pieces[0].shape[-1]
    per_source, size = pieces[0].shape[1:3]
    many = high.shape[-1] // width
    products = RES // many
    rows_out = out.shape[1]

    for here in range(count):

        @pl.when(place[0] == here)
        def _():
            @pl.loop(0, size // 8)
            def _(t):
                q0 = pl.multiple_of(t * 8, 8)
                read = column_twist(twist, q0)

                def get(n):
                    source, block = divmod(n, per_source)
                    piece = pieces[source ^ here]
                    rows = pl.ds(q0, 8)
                    return piece[0, block, rows, :], piece[1, block, rows, :]

                def put(u, value):
                    item = jnp.concatenate(twisted(value, u, 1, read), axis=0)
                    rows = pl.ds(pl.multiple_of(t * 16, 16), 16)
                    at = (u // many, rows, pl.ds((u % many) * width, width))
                    high[at], low[at] = high_low(item)

                forward_slabs(get, put)

    @pl.loop(0, products)
    def _(p):
        done = three_left(matrix, rows_out, high[p], low[p])
        for part in range(many):
            item = done[:, part * width : (part + 1) * width]
            at = p * many + part
            out[at] = before[0][at] + item if before else item


def column_inverse_kernel(count, place, source, twist, matrix, *refs):
    pieces, (peak_sq, near, lines, deep, back, top, sems, out_sems) = refs[:-8], refs[-8:]
    width = lines.shape[-1]
    rows_in = lines.shape[1]
    per_dest = near.shape[3]
    many = deep.shape[-1] // width
    products = RES // many

    def copy_in(p):
        part = pl.ds(p * many, many)
        return pltpu.make_async_copy(source.at[part], lines.at[part], sems.at[p])

    def copies_out(chunk, part):
        parts = 1 if chunk + 1 < CHUNKS else 2
        if part >= parts:
            return []
        rows = pl.ds(part * CHUNK // parts, CHUNK // parts)
        copies = []
        for j in range(count):
            piece = pieces[chunk * count + j].at[pl.ds(0, 2 * per_dest * CHUNK)]
            there = piece.reshape(2, per_dest, CHUNK, width).at[:, :, rows]
            here = near.at[chunk, place[0] ^ j, :, :, rows]
            copies.append(pltpu.make_async_copy(here, there, out_sems.at[(chunk * 2 + part) * count + j]))
        return copies

    def prepare(p):
        copy_in(p).wait()
        blocks = [lines[p * many + part] for part in range(many)]
        joined = jnp.concatenate(blocks, axis=1) if many > 1 else blocks[0]
        high = joined.astype(jnp.bfloat16).astype(jnp.float32)
        parts = [high, joined - high, high]
        if deep.shape[1] > 3 * rows_in:
            parts.append(jnp.zeros((deep.shape[1] - 3 * rows_in, many * width), jnp.float32))
        deep[p] = jnp.concatenate(parts, axis=0).astype(jnp.bfloat16)

    def product(p, chunk):
        done = dot16(matrix[chunk], deep[p])
        for part in range(many):
            back[chunk, p * many + part] = done[:, part * width : (part + 1) * width]

    def butterflies(t, chunk):
        q0 = pl.multiple_of(t * 8, 8)
        largest = []
        read = column_twist(twist, pl.multiple_of(chunk * CHUNK + q0, 8))

        def get(u):
            re = back[chunk, u, pl.ds(q0, 8), :]
            im = back[chunk, u, pl.ds(CHUNK + q0, 8), :]
            return twisted((re, im), u, -1, read)

        def put(n, value):
            dest, block = divmod(n, per_dest)
            rows = pl.ds(q0, 8)
            near[chunk, dest, 0, block, rows, :], near[chunk, dest, 1, block, rows, :] = value
            largest.append(value[0] * value[0] + value[1] * value[1])

        inverse_slabs(get, put)
        while len(largest) > 1:
            largest = [jnp.maximum(a, b) for a, b in zip(largest[0::2], largest[1::2])]
        top[...] = jnp.maximum(top[...], largest[0])

    for p in range(products):
        copy_in(p).start()
    top[...] = jnp.zeros_like(top)

    prepare(0)

    @pl.loop(1, products)
    def _(p):
        product(p - 1, 0)
        prepare(p)

    product(products - 1, 0)

    tiles = CHUNK // 16
    steps = min(tiles, products // 2)
    for chunk in range(CHUNKS):
        for part in range(2):

            @pl.loop(part * steps, (part + 1) * steps)
            def _(t):
                for item in range(tiles // steps):
                    butterflies(t * (tiles // steps) + item, chunk)
                if chunk + 1 < CHUNKS:
                    for item in range(products // 2 // steps):
                        product(t * (products // 2 // steps) + item, chunk + 1)

            for copy in copies_out(chunk, part if chunk + 1 == CHUNKS else 1 - part):
                copy.start()
    peak_sq[0] = jnp.max(top[...])
    for chunk in range(CHUNKS):
        for part in range(2):
            for copy in copies_out(chunk, part):
                copy.wait()


def line_kernel(
    order, own, tail, lines, gain, twist, fwd_high, fwd_low, inv_high, inv_low, out, *scratch
):
    half = RES * 8
    at_end = pl.program_id(0) == pl.num_programs(0) - 1

    def line_twist(side):
        def read(k):
            lanes = pl.ds(side * 128, 128)
            return twist[0, k, :, lanes], twist[1, k, :, lanes]

        return read

    def forward(group, stacked, sides=(0, 1)):
        for side in sides:
            waiting = {}

            def get(m):
                block = order[2 * m + side]
                at = group * 16
                return lines[block, at : at + 8, :], lines[block, at + 8 : at + 16, :]

            def put(u, value):
                waiting[u] = twisted(value, u, 1, line_twist(side))
                v = (u + RES // 2) % RES
                if v in waiting:
                    first = min(u, v)
                    rows = pl.ds(first * 16, 16)
                    rows_low = pl.ds(half + first * 16, 16)
                    for part in range(2):
                        item = jnp.concatenate(
                            [waiting[first][part], waiting[first + RES // 2][part]], axis=0
                        )
                        at = pl.ds(part * INNER + side * 128, 128)
                        stacked[rows, at], stacked[rows_low, at] = high_low(item)

            forward_slabs(get, put)

    def filtered(group, stacked):
        spec = three_right(stacked[...], half, fwd_high[...], fwd_low[...])
        spec_re, spec_im = spec[:, :128], spec[:, 128:]
        g_re, g_im = gain[0, group], gain[1, group]
        mixed = jnp.concatenate(
            [spec_re * g_re - spec_im * g_im, spec_re * g_im + spec_im * g_re], axis=1
        )
        return jnp.concatenate(high_low(mixed), axis=0)

    def unfold(mixed, back):
        back[...] = three_right(mixed, half, inv_high[...], inv_low[...])

    def inverse(group, back, sides=(0, 1)):
        for side in sides:

            def get(u):
                rows = pl.ds((u % (RES // 2)) * 16 + (u // (RES // 2)) * 8, 8)
                re = back[rows, pl.ds(side * 128, 128)]
                im = back[rows, pl.ds(INNER + side * 128, 128)]
                return twisted((re, im), u, -1, line_twist(side))

            def put(m, value):
                block = order[2 * m + side]
                at = group * 16
                out[block, at : at + 8, :], out[block, at + 8 : at + 16, :] = value

            inverse_slabs(get, put)

    if tail:

        @pl.when(at_end)
        def _():
            for block in range(N // 128):
                lines[block, 8:12, :] = lines[block, 4:8, :]

    groups = len(scratch) // 2

    stacked, back = scratch[:groups], scratch[groups:]

    def run(count):
        forward(0, stacked[0])
        for group in range(count):
            mixed = filtered(group, stacked[group])
            if group + 1 < count:
                forward(group + 1, stacked[group + 1], (0,))
            if group > 0:
                inverse(group - 1, back[group - 1], (0,))
            unfold(mixed, back[group])
            if group + 1 < count:
                forward(group + 1, stacked[group + 1], (1,))
            if group > 0:
                inverse(group - 1, back[group - 1], (1,))
        inverse(count - 1, back[count - 1])

    rest = own % groups
    if rest:
        pl.when(jnp.logical_not(at_end))(lambda: run(groups))
        pl.when(at_end)(lambda: run(rest))
    else:
        run(groups)

    if tail:

        @pl.when(at_end)
        def _():
            for block in range(N // 128):
                out[block, 4:8, :] = out[block, 8:12, :]


def gain_kernel(place, gain):
    k0 = place[0]
    group = place[1] + pl.program_id(0)
    down = lax.broadcasted_iota(jnp.int32, (8, 128), 0)
    across = lax.broadcasted_iota(jnp.int32, (8, 128), 1)
    row = (k0 + RES * (group * 8 + down - HALF)).astype(jnp.float32)
    row_sq = row * row
    row_in = jnp.abs(row) < LIMIT
    for u in range(RES):
        col = (residue(u) + RES * (across - HALF)).astype(jnp.float32)
        square = row_sq + col * col
        scaled = RATIO_SQ * square
        phase = -2.0 * math.pi * distance / wavelength * scaled / (1.0 + jnp.sqrt(1.0 - scaled))
        total = jnp.where(
            row_in & (jnp.abs(col) < LIMIT), jnp.exp(square * (-2.0 / (LIMIT * LIMIT))), 0.0
        )
        quarter = jnp.floor(phase * (2.0 / math.pi) + 0.5)
        left = phase - quarter * 1.5703125
        left = left - quarter * 4.837512969970703125e-4
        left = left - quarter * 7.549789954891882e-8
        sq = left * left
        sine = ((-1.9515295891e-4 * sq + 8.3321608736e-3) * sq - 1.6666654611e-1) * sq * left + left
        cosine = (
            (2.443315711809948e-5 * sq - 1.388731625493765e-3) * sq + 4.166664568298827e-2
        ) * sq * sq - 0.5 * sq + 1.0
        which = quarter.astype(jnp.int32) & 3
        swap = (which & 1) == 1
        cos_part = jnp.where(swap, sine, cosine)
        sin_part = jnp.where(swap, cosine, sine)
        cos_part = jnp.where((which == 1) | (which == 2), -cos_part, cos_part)
        sin_part = jnp.where(which >= 2, -sin_part, sin_part)
        at = (u % (RES // 2)) * 16 + (u // (RES // 2)) * 8
        gain[0, 0, at : at + 8, :] = total * cos_part
        gain[1, 0, at : at + 8, :] = total * sin_part


def encode(near_real, near_imag, peak_sq, cell_sign):
    square = near_real * near_real + near_imag * near_imag
    root = lax.rsqrt(jnp.maximum(square, 1.2e-38))
    top = lax.rsqrt(peak_sq)
    amp_level = (square * root) * (0.8 * top)
    unit = jnp.minimum(root, 20.0 * top)
    rest = 1.0 - amp_level * amp_level
    level = unit * amp_level
    lift = (rest * lax.rsqrt(rest)) * (unit * cell_sign)
    return (near_real * level + near_imag * lift, near_imag * level - near_real * lift)


def stamp_kernel(others, peak_one, peak_two, *refs):
    refs = refs[others:]
    stay, pieces, refs = refs[:CHUNKS], refs[CHUNKS : CHUNKS + others], refs[CHUNKS + others :]
    fetched, (tile, sems) = refs[:CHUNKS], refs[CHUNKS:]
    tile[...] = jnp.full(tile.shape, jnp.maximum(peak_one[0], peak_two[0]), jnp.float32)
    copies = []
    for j, piece in enumerate(pieces):
        rows = pl.ds(piece.shape[0] - SPARE, SPARE)
        copies.append(pltpu.make_async_copy(tile, piece.at[rows], sems.at[j]))
    for chunk in range(CHUNKS):
        copies.append(pltpu.make_async_copy(stay[chunk], fetched[chunk], sems.at[others + chunk]))
    for copy in copies:
        copy.start()
    for copy in copies:
        copy.wait()


def encode_kernel(count, place, peak_one, peak_two, *refs):
    pieces, refs = refs[: CHUNKS * count], refs[CHUNKS * count :]
    slm_real, slm_imag, tile_real, tile_imag, sems = refs
    blocks, width = tile_real.shape[0], pieces[0].shape[-1]
    top = jnp.full((1, width), jnp.maximum(peak_one[0], peak_two[0]), jnp.float32)
    for piece in pieces[(CHUNKS - 1) * count + 1 :]:
        top = jnp.maximum(top, piece[pl.ds(piece.shape[0] - SPARE, 1), :])
    cell = lax.broadcasted_iota(jnp.int32, (CHUNK, width), 0)
    cell = cell + lax.broadcasted_iota(jnp.int32, (CHUNK, width), 1)
    cell_sign = (1 - 2 * (cell & 1)).astype(jnp.float32)

    def copies_out(block, chunk):
        part_rows = pl.ds(chunk * CHUNK, CHUNK)
        rows = pl.ds(block * INNER + chunk * CHUNK, CHUNK)
        first = 2 * (CHUNKS * block + chunk)
        return [
            pltpu.make_async_copy(tile.at[block, part_rows], slm.at[rows], sems.at[first + part])
            for part, (tile, slm) in enumerate(((tile_real, slm_real), (tile_imag, slm_imag)))
        ]

    @pl.loop(0, blocks)
    def _(block):
        for at in range(CHUNKS * count):
            chunk, j = divmod(at, count)
            piece = pieces[at]
            lanes = pl.ds(pl.multiple_of((place[0] ^ j) * width, width), width)
            rows = pl.ds(chunk * CHUNK, CHUNK)
            real = pl.ds(pl.multiple_of(block * CHUNK, CHUNK), CHUNK)
            imag = pl.ds(pl.multiple_of((blocks + block) * CHUNK, CHUNK), CHUNK)
            tile_real[block, rows, lanes], tile_imag[block, rows, lanes] = encode(
                piece[real, :], piece[imag, :], top, cell_sign
            )
            if j == count - 1:
                for copy in copies_out(block, chunk):
                    copy.start()

    for block in range(blocks):
        for chunk in range(CHUNKS):
            for copy in copies_out(block, chunk):
                copy.wait()


def pack_kernel(start, place, field_real, field_imag, *refs):
    pieces, (rows_in, in_sems, sems) = refs[:-3], refs[-3:]
    size, width = pieces[0].shape[2:]
    rows = pl.ds(start, size)
    fetches = [
        pltpu.make_async_copy(field.at[:, rows], rows_in.at[part], in_sems.at[part])
        for part, field in enumerate((field_real, field_imag))
    ]
    for fetch in fetches:
        fetch.start()
    copies = []
    for part, fetch in enumerate(fetches):
        fetch.wait()
        for j in list(range(1, len(pieces))) + [0]:
            lanes = pl.ds(pl.multiple_of((place[0] ^ j) * width, width), width)
            copy = pltpu.make_async_copy(
                rows_in.at[part, :, :, lanes], pieces[j].at[part], sems.at[2 * j + part]
            )
            copy.start()
            copies.append(copy)
    for copy in copies:
        copy.wait()


def exchange(pieces, axis):
    total = len(pieces)
    return [pieces[0]] + [
        lax.ppermute(pieces[j], axis, [(i, i ^ j) for i in range(total)]) for j in range(1, total)
    ]


def params(mebibytes):
    return pltpu.CompilerParams(vmem_limit_bytes=mebibytes << 20)


def cost(megabytes):
    return pl.CostEstimate(flops=0, bytes_accessed=megabytes << 20, transcendentals=0)


def whole(memory=pltpu.VMEM):
    return pl.BlockSpec(memory_space=memory)


def body(field_real, field_imag):
    row_total, col_total = lax.axis_size("row"), lax.axis_size("col")
    devices = row_total * col_total
    device = lax.axis_index("row") * col_total + lax.axis_index("col")
    height, tile_width = field_real.shape
    width = tile_width // row_total
    parts = max(1, devices // RES)
    groups = -(-(2 * HALF + 1) // (8 * parts)) * parts
    own = groups // parts
    tail = parts == 1
    total_rows = groups * 16 - (8 if tail else 0)
    own_rows = total_rows // parts
    many = 4 if width == 128 else 1

    fwd_col, inv_col = column_tables(groups, tail)
    line_fh, line_fl, line_ih, line_il = line_tables()
    twist = np.stack(twist_table())
    twist_line = np.ascontiguousarray(np.broadcast_to(twist[:, :, None], twist.shape[:2] + (8, INNER)))
    twist_col = np.pad(twist, ((0, 0), (0, 64 - twist.shape[1]), (0, 0)))
    twist_col = twist_col.reshape(128, INNER).T.copy()

    u = device // parts
    k0 = jnp.where(u >= RES // 2, u - RES, u)
    place = jnp.stack([k0, (device % parts) * own]).astype(jnp.int32)
    gain = pl.pallas_call(
        gain_kernel,
        grid=(own,),
        in_specs=[whole(pltpu.SMEM)],
        out_specs=pl.BlockSpec((2, 1, RES * 8, 128), lambda g: (0, g, 0, 0)),
        out_shape=jax.ShapeDtypeStruct((2, own, RES * 8, 128), jnp.float32),
        compiler_params=params(50),
        name="gain",
    )(place)

    place_row = lax.axis_index("row").reshape(1).astype(jnp.int32)
    blocks = height // INNER
    anywhere = whole(pl.ANY)
    if width != 128:
        packed = jnp.stack([field_real, field_imag]).reshape(2, blocks, INNER, row_total, width)
        packed = jnp.take(packed, jnp.arange(row_total) ^ place_row[0], axis=3)
    lines = []
    for chunk, (start, size) in enumerate(FRONT):
        piece_shape = jax.ShapeDtypeStruct((2, blocks, size, width), jnp.float32)
        if width == 128:
            pieces = pl.pallas_call(
                partial(pack_kernel, start),
                in_specs=[whole(pltpu.SMEM), anywhere, anywhere],
                out_specs=[anywhere] * row_total,
                out_shape=[piece_shape] * row_total,
                scratch_shapes=[
                    pltpu.VMEM((2, blocks, size, tile_width), jnp.float32),
                    pltpu.SemaphoreType.DMA((2,)),
                    pltpu.SemaphoreType.DMA((2 * row_total,)),
                ],
                compiler_params=params(56),
                cost_estimate=cost(4),
                name="pack",
            )(
                place_row,
                field_real.reshape(blocks, INNER, tile_width),
                field_imag.reshape(blocks, INNER, tile_width),
            )
        else:
            pieces = [packed[:, :, start : start + size, j] for j in range(row_total)]
        pieces = exchange(pieces, "row")
        if chunk == 0:
            pieces, gain = lax.optimization_barrier((pieces, gain))
        rows = slice(start, start + size)
        slab = pltpu.VMEM((RES // many, 2 * size, many * width), jnp.bfloat16)
        lines = [
            pl.pallas_call(
                partial(column_forward_kernel, row_total),
                in_specs=[whole(pltpu.SMEM)] + [whole()] * (2 + row_total + len(lines)),
                out_specs=whole(),
                out_shape=jax.ShapeDtypeStruct((RES, total_rows, width), jnp.float32),
                scratch_shapes=[slab, slab],
                compiler_params=params(20),
                cost_estimate=cost(20),
                name="column_forward",
            )(place_row, twist_col[rows], fwd_col[chunk], *pieces, *lines)
        ]
    (lines,) = lines

    lines = lines.reshape(devices, own_rows, width)
    lines = lax.all_to_all(lines, ("row", "col"), split_axis=0, concat_axis=0, tiled=True)
    if width == 128:
        order = tuple((b % row_total) * col_total + b // row_total for b in range(N // 128))
    else:
        order = tuple(range(N // 128))
        lines = lines.reshape(row_total, col_total, own_rows, width).transpose(2, 1, 0, 3)
        lines = lines.reshape(own_rows, N // 128, 128).transpose(1, 0, 2)

    at_once = 2
    line_grain = pl.BlockSpec((N // 128, 16 * at_once, 128), lambda i: (0, i, 0))
    gain_grain = pl.BlockSpec((2, at_once, RES * 8, 128), lambda i: (0, i, 0, 0))
    lines = pl.pallas_call(
        partial(line_kernel, order, own, tail),
        grid=(-(-own // at_once),),
        in_specs=[line_grain, gain_grain] + [whole()] * 5,
        out_specs=line_grain,
        out_shape=jax.ShapeDtypeStruct((N // 128, own_rows, 128), jnp.float32),
        scratch_shapes=[pltpu.VMEM((2 * RES * 8, 2 * INNER), jnp.bfloat16)] * at_once
        + [pltpu.VMEM((RES * 8, 2 * INNER), jnp.float32)] * at_once,
        compiler_params=params(44),
        name="line",
    )(lines, gain, twist_line, line_fh, line_fl, line_ih, line_il)

    if width != 128:
        lines = lines.transpose(1, 0, 2).reshape(own_rows, col_total, row_total, width)
        lines = lines.transpose(2, 1, 0, 3).reshape(devices, own_rows, width)
    lines = lax.all_to_all(lines, ("row", "col"), split_axis=0, concat_axis=0, tiled=True)
    lines = lines.reshape(RES, total_rows, width)

    piece_shapes = [
        jax.ShapeDtypeStruct((2 * blocks * CHUNK + spare, width), jnp.float32)
        for spare in (0,) * (CHUNKS - 1) + (SPARE,)
    ]
    *near, peak_sq = pl.pallas_call(
        partial(column_inverse_kernel, row_total),
        in_specs=[whole(pltpu.SMEM), anywhere, whole(), whole()],
        out_specs=[anywhere] * (CHUNKS * row_total) + [whole(pltpu.SMEM)],
        out_shape=[shape for shape in piece_shapes for _ in range(row_total)]
        + [jax.ShapeDtypeStruct((1,), jnp.float32)],
        scratch_shapes=[
            pltpu.VMEM((CHUNKS, row_total, 2, blocks, CHUNK, width), jnp.float32),
            pltpu.VMEM((RES, total_rows, width), jnp.float32),
            pltpu.VMEM((RES // many, inv_col.shape[2], many * width), jnp.bfloat16),
            pltpu.VMEM((CHUNKS, RES, 2 * CHUNK, width), jnp.float32),
            pltpu.VMEM((8, width), jnp.float32),
            pltpu.SemaphoreType.DMA((RES // many,)),
            pltpu.SemaphoreType.DMA((2 * CHUNKS * row_total,)),
        ],
        compiler_params=params(36),
        name="column_inverse",
    )(place_row, lines, twist_col, inv_col)
    near = [near[:row_total], near[row_total:]]
    piece_shape = piece_shapes[-1]
    near[0] = exchange(near[0], "row")
    shift = 1
    while shift < col_total:
        partner = [(i, i ^ shift) for i in range(col_total)]
        peaks = [peak_sq, lax.ppermute(peak_sq, "col", partner)]
        shift *= 2
        if shift < col_total:
            peak_sq = jnp.maximum(*peaks)
    others = row_total - 1
    stamped = pl.pallas_call(
        partial(stamp_kernel, others),
        in_specs=[whole(pltpu.SMEM)] * 2 + [anywhere] * (others + CHUNKS),
        out_specs=[anywhere] * others + [whole()] * CHUNKS,
        out_shape=[piece_shape] * others + piece_shapes,
        scratch_shapes=[
            pltpu.VMEM((SPARE, width), jnp.float32),
            pltpu.SemaphoreType.DMA((others + CHUNKS,)),
        ],
        input_output_aliases={2 + j: j for j in range(others)},
        compiler_params=params(16),
        name="stamp",
    )(*peaks, *near[1][1:], near[0][0], near[1][0])
    near[1][1:] = stamped[:others]
    near[0][0], near[1][0] = stamped[others:]
    near[0][1:], near[1][1] = lax.optimization_barrier((near[0][1:], near[1][1]))
    near[1] = exchange(near[1], "row")
    if width != 128:
        peak_sq = jnp.maximum(*peaks)[0]
        for piece in near[1][1:]:
            peak_sq = jnp.maximum(peak_sq, piece[-1, 0])
        near = jnp.stack([jnp.stack([piece[: 2 * blocks * CHUNK] for piece in pieces]) for pieces in near])
        near = jnp.take(near, jnp.arange(row_total) ^ place_row[0], axis=1)
        near = near.reshape(CHUNKS, row_total, 2, blocks, CHUNK, width)
        near = near.transpose(2, 3, 0, 4, 1, 5).reshape(2, height, tile_width)
        odd_cell = (jnp.arange(height)[:, None] + jnp.arange(tile_width)[None, :]) % 2
        cell_sign = (1 - 2 * odd_cell).astype(jnp.float32)
        return encode(near[0], near[1], peak_sq, cell_sign)
    tile_shape = jax.ShapeDtypeStruct((height, tile_width), jnp.float32)
    tile = pltpu.VMEM((blocks, INNER, tile_width), jnp.float32)
    return pl.pallas_call(
        partial(encode_kernel, row_total),
        in_specs=[whole(pltpu.SMEM)] * 3 + [whole()] * (CHUNKS * row_total),
        out_specs=[anywhere] * 2,
        out_shape=[tile_shape, tile_shape],
        scratch_shapes=[tile, tile, pltpu.SemaphoreType.DMA((2 * CHUNKS * blocks,))],
        compiler_params=params(16),
        name="encode",
    )(place_row, *peaks, *near[0], *near[1])


def solution(mesh):
    in_specs = (P("row", "col"), P("row", "col"))
    out_specs = (P("row", "col"), P("row", "col"))
    return jax.shard_map(body, mesh=mesh, in_specs=in_specs, out_specs=out_specs, check_vma=False)
```
